32 devices in a mesh: ctx: 8 (over z, y), tp: 4 (over x, core).
Axes of the slice: x: 2, y: 2, z: 4, core: 2. Of those that a mesh axis runs over, the one named last changes fastest.
Arguments:
- hidden_in: bfloat16 [4096, 1536], P('ctx'), may hold values from -6 to 6
- norm_one: bfloat16 [1536], P('ctx'), may hold values from 0.5 to 1.5
- w_query: bfloat16 [1536, 1536], P('ctx', 'tp'), may hold values from -0.15625 to 0.15625
- w_key: bfloat16 [1536, 1536], P('ctx', 'tp'), may hold values from -0.15625 to 0.15625
- w_value: bfloat16 [1536, 1536], P('ctx', 'tp'), may hold values from -0.15625 to 0.15625
- w_gate_out: bfloat16 [1536, 1536], P('ctx', 'tp'), may hold values from -0.15625 to 0.15625
- w_forget: bfloat16 [1536, 24], P('ctx', 'tp'), may hold values from -0.15625 to 0.15625
- forget_bias: float32 [24], P('tp'), may hold values from 3.5 to 11.5
- head_gains: bfloat16 [128, 24], P('ctx', 'tp'), may hold values from 0.5 to 1.5
- w_output: bfloat16 [1536, 1536], P('ctx', 'tp'), may hold values from -0.625 to 0.625
- norm_two: bfloat16 [1536], P('ctx'), may hold values from 0.5 to 1.5
- w_gate: bfloat16 [1536, 4096], P('ctx', 'tp'), may hold values from -0.15625 to 0.15625
- w_up: bfloat16 [1536, 4096], P('ctx', 'tp'), may hold values from -0.15625 to 0.15625
- w_down: bfloat16 [1536, 4096], P('ctx', 'tp'), may hold values from -0.1875 to 0.1875
- out_grad: bfloat16 [4096, 1536], P('ctx'), may hold values from -6 to 6
- doc_lengths: int32 [2], replicated, may hold values from 1024 to 2304, as said below
- group_map: int32 [16], replicated, may hold values from 0 to 15, as said below
- skip_list: int32 [16, 16], replicated, may hold values 0 or 1
Outputs:
- layer_out: float32 [4096, 1536], P('ctx', 'tp')
- input_grad: float32 [4096, 1536], P('ctx')
- norm_one_grad: float32 [1536], P('ctx')
- w_query_grad: float32 [1536, 1536], P('ctx', 'tp')
- w_key_grad: float32 [1536, 1536], P('ctx', 'tp')
- w_value_grad: float32 [1536, 1536], P('ctx', 'tp')
- w_gate_out_grad: float32 [1536, 1536], P('ctx', 'tp')
- w_forget_grad: float32 [1536, 24], P('ctx', 'tp')
- forget_bias_grad: float32 [24], P('tp')
- head_gains_grad: float32 [128, 24], P('ctx', 'tp')
- w_output_grad: float32 [1536, 1536], P('ctx', 'tp')
- norm_two_grad: float32 [1536], P('ctx')
- w_gate_grad: float32 [1536, 4096], P('ctx', 'tp')
- w_up_grad: float32 [1536, 4096], P('ctx', 'tp')
- w_down_grad: float32 [1536, 4096], P('ctx', 'tp')
The draws below stay inside these ranges and needn't reach their ends.
Inputs may be any that keep to these rules, and one draw needn't show every extreme that they name: `doc_lengths`: documents lie end to end in this order and fill the pack of 4096 tokens; one of them is 2304 tokens long and stands first or last, each other one has 1024 tokens or more. `group_map`: each group stands in one slot; slots 2i and 2i + 1 hold one group of the first half of the pack and one of the second half. `skip_list`: only entries below the diagonal are read.
All inputs are finite; a program needn't handle non-finite values.
Results may differ from the reference program's by a relative error of at most 0.02.
Values may be sent and summed in bfloat16 or wider, within the bound.
A program may use at most 192 MiB of HBM per device.

```python
import math
import jax
import jax.numpy as jnp
from jax import lax

D = 1536
H = 24
HD = 64
FF = 4096
GROUP = 256
MINLEN = 1024
GROUPS = 16
TOKENS = 4096
LONGEST = 2304
DOCS = 2


def draw_doc_lengths(key, part):
    key = jax.random.fold_in(key, 11)
    side_key, cut_key = jax.random.split(key)
    remain = (GROUPS // 2 - 1) * GROUP
    others = DOCS - 1
    spare_rows = remain - others * MINLEN
    cut_points = jnp.sort(jax.random.randint(cut_key, (others - 1,), 0, spare_rows + 1)).astype(jnp.int32)
    bounds = jnp.concatenate([jnp.zeros((1,), jnp.int32), cut_points, jnp.full((1,), spare_rows, jnp.int32)])
    pieces = bounds[1:] - bounds[:-1] + MINLEN
    longest = jnp.full((1,), LONGEST, jnp.int32)
    at_start = jnp.concatenate([longest, pieces])
    at_end = jnp.concatenate([pieces, longest])
    flipper = jax.random.randint(side_key, (), 0, 2)
    return jnp.where(flipper == 1, at_start, at_end).astype(jnp.int32)


def draw_group_map(key, part):
    key = jax.random.fold_in(key, 7)
    low_key, high_key, flip_key = jax.random.split(key, 3)
    half_count = GROUPS // 2
    early_groups = jax.random.permutation(low_key, half_count).astype(jnp.int32)
    later_groups = jax.random.permutation(high_key, half_count).astype(jnp.int32) + half_count
    flipped = jax.random.randint(flip_key, (half_count,), 0, 2)
    first_slot = jnp.where(flipped == 1, later_groups, early_groups)
    second_slot = jnp.where(flipped == 1, early_groups, later_groups)
    return jnp.stack([first_slot, second_slot], axis=1).reshape(GROUPS).astype(jnp.int32)


def touch_ends(values, stream_key, smallest, top_value):
    dims = values.shape
    spot = [jax.random.randint(jax.random.fold_in(stream_key, axis), (), 0, dims[axis]) for axis in range(len(dims))]
    values = values.at[tuple(spot)].set(smallest)
    longest = dims.index(max(dims))
    spot[longest] = (spot[longest] + 1) % dims[longest]
    return values.at[tuple(spot)].set(top_value)


def level_of(rng, extent, cuts, least, largest):
    loudness, own = 1.0, jax.random.fold_in(rng, 6)
    for dim, shards_of in cuts:
        heights = jnp.exp(jax.random.uniform(jax.random.fold_in(own, dim), (shards_of,), jnp.float32, least / len(cuts), largest / len(cuts)))
        loudness = loudness * jnp.repeat(heights, extent[dim] // shards_of).reshape([-1 if axis == dim else 1 for axis in range(len(extent))])
    return loudness


def normal_values(stream_key, extent, deviation, reach, shards=(), kind=jnp.bfloat16):
    entries = jax.random.normal(stream_key, extent, jnp.float32) * deviation
    if len(shards) > 0:
        entries = level_of(stream_key, extent, shards, -0.22, 0.18) * entries
    return jnp.clip(entries, min=-reach, max=reach).astype(kind)


def setup_inputs(seed: int = 0) -> dict:
    arg_keys = jax.random.split(jax.random.key(seed), 19)
    return {
        "hidden_in": normal_values(arg_keys[0], (TOKENS, D), 1.0, 6.0, ((0, 8),)),
        "norm_one": jnp.clip(1.0 + 0.1 * jax.random.normal(arg_keys[1], (D,), jnp.float32), 0.5, 1.5).astype(jnp.bfloat16),
        "w_query": normal_values(arg_keys[2], (D, H * HD), D ** -0.5, 0.15625, ((0, 8), (1, 4))),
        "w_key": normal_values(arg_keys[3], (D, H * HD), D ** -0.5, 0.15625, ((0, 8), (1, 4))),
        "w_value": normal_values(arg_keys[4], (D, H * HD), D ** -0.5, 0.15625, ((0, 8), (1, 4))),
        "w_gate_out": normal_values(arg_keys[5], (D, H * HD), D ** -0.5, 0.15625, ((0, 8), (1, 4))),
        "w_forget": normal_values(arg_keys[6], (D, H), D ** -0.5, 0.15625, ((0, 8), (1, 4))),
        "forget_bias": jnp.clip(3.5 + 8.0 * jax.random.uniform(arg_keys[7], (H,), jnp.float32) ** level_of(arg_keys[7], (H,), ((0, 4),), -0.2, 0.2), 3.5, 11.5),
        "head_gains": jnp.clip(1.0 + 0.1 * jax.random.normal(arg_keys[8], (2 * HD, H), jnp.float32), 0.5, 1.5).astype(jnp.bfloat16),
        "w_output": normal_values(arg_keys[9], (D, H * HD), (H * HD // 16) ** -0.5, 0.625, ((0, 8), (1, 4))),
        "norm_two": jnp.clip(1.0 + 0.1 * jax.random.normal(arg_keys[10], (D,), jnp.float32), 0.5, 1.5).astype(jnp.bfloat16),
        "w_gate": normal_values(arg_keys[11], (D, FF), D ** -0.5, 0.15625, ((0, 8), (1, 4))),
        "w_up": normal_values(arg_keys[12], (D, FF), D ** -0.5, 0.15625, ((0, 8), (1, 4))),
        "w_down": normal_values(arg_keys[13], (D, FF), (FF // 4) ** -0.5, 0.1875, ((0, 8), (1, 4))),
        "out_grad": normal_values(arg_keys[14], (TOKENS, D), 1.0, 6.0, ((0, 8),)),
        "doc_lengths": draw_doc_lengths(jax.random.fold_in(arg_keys[18], 71), 0),
        "group_map": draw_group_map(jax.random.fold_in(arg_keys[18], 71), 0),
        "skip_list": touch_ends((jax.random.randint(arg_keys[17], (GROUPS, GROUPS), 0, 4) < 1).astype(jnp.int32), jax.random.fold_in(arg_keys[17], 1), 0, 1),
    }


EPS = 1e-06
HIGH = lax.Precision.HIGHEST

@jax.custom_vjp
def low(v):
    return lax.optimization_barrier(v.astype(jnp.bfloat16)).astype(jnp.float32)

@jax.custom_vjp
def low_back(v):
    return v

def low_keep(v):
    return (low(v), None)

def low_pass(kept, grad):
    return (grad,)

def back_keep(v):
    return (v, None)

def back_low(kept, grad):
    return (low(grad),)
low.defvjp(low_keep, low_pass)
low_back.defvjp(back_keep, back_low)

def matmul_high(left, right):
    return jnp.dot(left, right, precision=HIGH, preferred_element_type=jnp.float32)

def rms_scale(value):
    return value * lax.rsqrt(lax.optimization_barrier(jnp.mean(value * value, axis=-1, keepdims=True)) + EPS)

def layer(inputs, norm_one, w_query, w_key, w_value, w_gate_out, w_forget, forget_bias, head_gains, w_output, norm_two, w_gate, w_up, w_down, position_doc, position_group, skip_list):
    normed = low(rms_scale(inputs) * norm_one)
    query_raw = low_back(matmul_high(normed, w_query)).reshape(TOKENS, H, HD)
    key_raw = low_back(matmul_high(normed, w_key)).reshape(TOKENS, H, HD)
    value_rows = low(low_back(matmul_high(normed, w_value))).reshape(TOKENS, H, HD)
    gate_logit = low_back(matmul_high(normed, w_gate_out))
    forget_logit = low_back(matmul_high(normed, w_forget) + forget_bias)
    query_rows = low(rms_scale(query_raw) * head_gains[:HD].T * 0.125)
    key_rows = low(rms_scale(key_raw) * head_gains[HD:].T)
    offsets = jnp.cumsum(jax.nn.log_sigmoid(forget_logit), axis=0)
    key_pos = jnp.arange(TOKENS, dtype=jnp.int32)
    block_rows = math.gcd(TOKENS, 512)
    block_count = TOKENS // block_rows

    def attend(members):
        query_block, offset_block, doc_block, group_block, pos_block = members
        scores = low_back(jnp.einsum('qhe,khe->qhk', query_block, key_rows, precision=HIGH))
        scores = scores + offset_block[:, :, None] - offsets.T[None, :, :]
        skip_pairs = skip_list[group_block][:, position_group] == 1
        skipped = skip_pairs & (position_group[None, :] < group_block[:, None])
        allowed = (doc_block[:, None] == position_doc[None, :]) & (key_pos[None, :] <= pos_block[:, None]) & jnp.logical_not(skipped)
        scores = jnp.where(allowed[:, None, :], scores, -1e+30)
        row_peak = lax.optimization_barrier(jnp.max(scores, axis=-1, keepdims=True))
        weights = jnp.where(allowed[:, None, :], jnp.exp(scores - row_peak), 0.0)
        normalized = weights / lax.optimization_barrier(jnp.sum(weights, axis=-1, keepdims=True))
        return jnp.einsum('qhk,khe->qhe', normalized, value_rows, precision=HIGH)
    mixed = lax.map(jax.checkpoint(attend), (query_rows.reshape(block_count, block_rows, H, HD), offsets.reshape(block_count, block_rows, H), position_doc.reshape(block_count, block_rows), position_group.reshape(block_count, block_rows), key_pos.reshape(block_count, block_rows)))
    attended = low_back(mixed.reshape(TOKENS, H * HD))
    gated = low(attended * jax.nn.sigmoid(gate_logit))
    middle = inputs + low_back(matmul_high(gated, w_output.T))
    normed_two = low(rms_scale(middle) * norm_two)
    gate_value = low_back(matmul_high(normed_two, w_gate))
    up_value = low_back(matmul_high(normed_two, w_up))
    hidden = low(jax.nn.silu(gate_value) * up_value)
    return middle + low_back(matmul_high(hidden, w_down.T))

def reference(hidden_in, norm_one, w_query, w_key, w_value, w_gate_out, w_forget, forget_bias, head_gains, w_output, norm_two, w_gate, w_up, w_down, out_grad, doc_lengths, group_map, skip_list):
    slot_of_group = jnp.argsort(group_map).astype(jnp.int32)

    def to_pack(array):
        return array.reshape(GROUPS, GROUP, D)[slot_of_group].reshape(TOKENS, D)

    def from_pack(array):
        return array.reshape(GROUPS, GROUP, D)[group_map].reshape(TOKENS, D)
    position = jnp.arange(TOKENS, dtype=jnp.int32)
    doc_ends = jnp.cumsum(doc_lengths).astype(jnp.int32)
    position_doc = lax.optimization_barrier(jnp.sum((position[:, None] >= doc_ends[None, :]).astype(jnp.int32), axis=1))
    position_group = position // GROUP

    def run(inputs, gain_one, query_w, key_w, value_w, gate_out_w, forget_w, bias_f, gains_h, output_w, gain_two, gate_w, up_w, down_w):
        return layer(inputs, gain_one, query_w, key_w, value_w, gate_out_w, forget_w, bias_f, gains_h, output_w, gain_two, gate_w, up_w, down_w, position_doc, position_group, skip_list)
    layer_out, pull_back = jax.vjp(run, to_pack(hidden_in.astype(jnp.float32)), norm_one.astype(jnp.float32), w_query.astype(jnp.float32), w_key.astype(jnp.float32), w_value.astype(jnp.float32), w_gate_out.astype(jnp.float32), w_forget.astype(jnp.float32), forget_bias.astype(jnp.float32), head_gains.astype(jnp.float32), w_output.astype(jnp.float32), norm_two.astype(jnp.float32), w_gate.astype(jnp.float32), w_up.astype(jnp.float32), w_down.astype(jnp.float32))
    grads = pull_back(to_pack(out_grad.astype(jnp.float32)))
    return (from_pack(layer_out), from_pack(grads[0]), grads[1], grads[2], grads[3], grads[4], grads[5], grads[6], grads[7], grads[8], grads[9], grads[10], grads[11], grads[12], grads[13])
```

```python
import functools

import jax
import jax.numpy as jnp
from jax import lax
from jax.experimental import pallas as pl
from jax.experimental.pallas import tpu as pltpu
from jax.sharding import PartitionSpec as P

EPS = 1e-06
HIGHEST = lax.Precision.HIGHEST
MESH = pl.DeviceIdType.MESH
VMEM = pltpu.VMEM
VMEM_LIMIT = 60 * 1024 * 1024
F32 = jnp.float32
BF16 = jnp.bfloat16


def rms_scale(value):
    return value * lax.rsqrt(jnp.mean(value * value, axis=-1, keepdims=True) + EPS)


def rms_back(grad_in, value):
    inverse = lax.rsqrt(jnp.mean(value * value, axis=-1, keepdims=True) + EPS)
    normal = value * inverse
    return inverse * (grad_in - normal * jnp.mean(grad_in * normal, axis=-1, keepdims=True))


def dot(left, right):
    return jnp.dot(left, right, preferred_element_type=F32)


def contract_cols(left, right):
    return lax.dot_general(left, right, (((1,), (1,)), ((), ())), preferred_element_type=F32)


def contract_cols_exact(left, right):
    return lax.dot_general(left, right, (((1,), (1,)), ((), ())), precision=HIGHEST)


def contract_rows(left, right):
    return lax.dot_general(left, right, (((0,), (0,)), ((), ())), preferred_element_type=F32)


def ring_place(ctx, n):
    odd = lax.rem(ctx, 2)
    half = lax.div(ctx, 2)
    return (1 - odd) * half + odd * (n - 1 - half)


def ring_owner(place, n):
    late = lax.div(place, n // 2)
    return (1 - late) * (2 * place) + late * (2 * (n - 1 - place) + 1)


def wrap(place, n):
    return lax.rem(place + 2 * n, n)


def ring_setup(n):
    me = lax.axis_index("ctx")
    tp = lax.axis_index("tp")
    place = ring_place(me, n)
    right = ring_owner(wrap(place + 1, n), n)
    left = ring_owner(wrap(place - 1, n), n)
    return me, tp, place, (right, left)


def greet(peers):
    barrier = pltpu.get_barrier_semaphore()
    for peer in peers:
        pl.semaphore_signal(barrier, inc=1, device_id=peer, device_id_type=MESH)
    pl.semaphore_wait(barrier, len(peers))


def ctx_peers(me, tp, n):
    return [(lax.rem(me + i, n), tp) for i in range(1, n)]


def remote(src, dst, send, recv, device):
    return pltpu.make_async_remote_copy(
        src_ref=src, dst_ref=dst, send_sem=send, recv_sem=recv, device_id=device, device_id_type=MESH
    )


class Gather:
    def __init__(self, n, place, sides, tp, chunks, send, recv):
        self.n, self.place, self.sides, self.tp = n, place, sides, tp
        self.chunks, self.send, self.recv = chunks, send, recv
        self.arrived = None

    def owner(self, side, back):
        return ring_owner(wrap(self.place - back if side == 0 else self.place + back, self.n), self.n)

    def copy(self, index, step, first):
        side, source, target = self.chunks[index]
        target = target(self.owner(side, step))
        return remote(
            source if first else target, target, self.send.at[index, step], self.recv.at[index, step],
            (self.sides[side], self.tp),
        )

    def arrive(self, index, step):
        side, _, target = self.chunks[index]
        target = target(self.owner(side, step + 1))
        remote(
            target, target, self.send.at[index, step], self.recv.at[index, step], (self.sides[side], self.tp)
        ).wait_recv()
        if self.arrived is not None:
            self.arrived(index, step)

    def begin(self, indices=None):
        for index in indices if indices is not None else range(len(self.chunks)):
            self.copy(index, 0, True).start()

    def forward(self, step):
        for index in range(len(self.chunks)):
            self.arrive(index, step - 1)
            self.copy(index, step, False).start()

    def last(self):
        for index in range(len(self.chunks)):
            self.arrive(index, self.n - 2)

    def sent(self):
        def finish(step, carry):
            for index in range(len(self.chunks)):
                self.copy(index, step, False).wait_send()
            return carry

        lax.fori_loop(0, self.n - 1, finish, 0)


class Moves:
    def __init__(self, semaphores):
        self.semaphores, self.count, self.open = semaphores, 0, {}

    def start(self, name, source, target):
        copy = pltpu.make_async_copy(source, target, self.semaphores.at[self.count])
        self.count += 1
        copy.start()
        self.open[name] = copy

    def wait(self, *names):
        for name in names or list(self.open):
            self.open.pop(name).wait()


def start_kernel(
    n, heads, group_map, doc_lengths, skip, earlier_ref, x_ref, small_in, bias_ref, wq_in, wk_in, wv_in, wg_in, wo_in,
    wq_out, wk_out, wv_out, wg_out, wo_ref, u_out, q_out, qr_out, kr_out, gl_out, fz_ref, k_out, v_out, aug_out,
    att_out, term_ref, gain_one, gain_two, qgain_ref, kgain_ref, wf_ref,
    x_vmem, wq_ref, wk_ref, wv_ref, wg_ref, u_ref, q_ref, k_all, v_all, aug_ref, att_ref, acc_ref, cat_ref,
    diff_ref, span_ref, tot_ref, before_ref, inside_all,
    small_all, acc_r, acc_l, inside_src,
    wsend, wrecv, osend, orecv, ksend, krecv, ssend, srecv, isend, irecv, spill, local,
):
    me, tp, place, sides = ring_setup(n)
    moves = Moves(local)
    moves.start("x", x_ref, x_vmem)
    greet(ctx_peers(me, tp, n))
    rows, cols = x_ref.shape
    shard, width = wq_in.shape
    half = rows // 2
    head_dim = width // heads

    def shard_rows(owner):
        return pl.ds(pl.multiple_of(owner * shard, 16), shard)

    def window(ref, c0, cw):
        return lambda owner: ref.at[shard_rows(owner), pl.ds(c0, cw)]

    def token_rows(owner):
        return pl.ds(pl.multiple_of(owner * rows, rows), rows)

    def block(ref, pair):
        return lambda owner: ref.at[pair, token_rows(owner), :]

    ring = (n, place, sides, tp)
    projections = Gather(
        *ring,
        [
            (side, source, window(target, 0, width))
            for side, source, target in ((0, wq_in, wq_ref), (1, wv_in, wv_ref), (0, wk_in, wk_ref), (1, wg_in, wg_ref))
        ],
        wsend, wrecv,
    )
    middle = width // 256 * 128
    outputs = Gather(
        *ring,
        [
            (side, wo_in.at[:, pl.ds(c0, cw)], window(wo_ref, c0, cw))
            for side, c0, cw in ((0, 0, middle), (1, middle, width - middle))
        ],
        osend, orecv,
    )
    members = [(0, k_all, k_out, 0), (1, k_all, k_out, 2), (0, v_all, v_out, 0), (1, v_all, v_out, 2)]
    members += [(0, k_all, k_out, 1), (1, v_all, v_out, 1)]
    pairs = Gather(
        *ring, [(side, block(ref, pair)(me), block(ref, pair)) for side, ref, _, pair in members], ksend, krecv
    )

    def spill_copy(index, step):
        side, ref, out, pair = members[index]
        owner = pairs.owner(side, step + 1)
        return pltpu.make_async_copy(
            block(ref, pair)(owner), block(out, pair)(owner), spill.at[index, step]
        )

    pairs.arrived = lambda index, step: spill_copy(index, step).start()

    projections.begin()
    exchange_start(n, me, tp, lambda peer: small_in, small_all, ssend, srecv)
    gathered = ((wq_in, wq_ref), (wk_in, wk_ref), (wv_in, wv_ref), (wg_in, wg_ref), (wo_in, wo_ref))
    for i, (source, target) in enumerate(gathered):
        moves.start(i, source, target.at[shard_rows(me)])
    moves.start("small", small_in, small_all.at[me])
    moves.wait("small")
    exchange_wait(n, me, tp, lambda peer: small_in, small_all, ssend, srecv)
    projections.forward(1)

    count = 2 * head_dim // n
    for i in range(n):
        block_small = small_all[i].astype(F32)
        gain_one[:, i * shard : (i + 1) * shard] = block_small[0:1, :shard]
        gain_two[:, i * shard : (i + 1) * shard] = block_small[1:2, :shard]
        wf_ref[:, i * shard : (i + 1) * shard] = block_small[8:16, :shard]
        target, at = (qgain_ref, i) if i < n // 2 else (kgain_ref, i - n // 2)
        for h in range(heads):
            lane = h * head_dim + at * count
            target[:, lane : lane + count] = block_small[2 + h : 3 + h, :count]

    size = 64

    def norm_rows(i, carry):
        here = pl.ds(pl.multiple_of(i * size, size), size)
        normed = (rms_scale(x_vmem[here, :].astype(F32)) * gain_one[...]).astype(BF16)
        for j in range(n):
            u_ref[j, here, :] = normed[:, j * shard : (j + 1) * shard]
        return carry

    moves.wait("x")
    lax.fori_loop(0, rows // size, norm_rows, 0)
    moves.start("u", u_ref, u_out)

    def grow(back):
        for side, acc, sources in ((0, acc_r, (wq_ref, wk_ref)), (1, acc_l, (wv_ref, wg_ref))):
            owner = projections.owner(side, back)
            for i, source in enumerate(sources):
                acc[:, i * width : (i + 1) * width] += dot(u_ref[owner], source[shard_rows(owner), :])

    acc_r[...] = jnp.zeros_like(acc_r)
    acc_l[...] = jnp.zeros_like(acc_l)
    moves.wait(0, 1, 2, 3, 4)
    grow(0)
    projections.forward(2)
    grow(1)
    grow(2)
    forget = jnp.zeros((16, rows), F32)
    for j in range(n):
        forget += contract_cols(small_all[j, :, :shard], u_ref[j])
    fz = forget[8:16] + bias_ref[:, 0:1]
    fz_ref[...] = fz
    logs = jnp.minimum(fz, 0.0) - jnp.log1p(jnp.exp(-jnp.abs(fz)))
    head = lax.broadcasted_iota(jnp.int32, logs.shape, 0)
    logs = jnp.where(head < heads, logs, 0.0)
    upto = (
        lax.broadcasted_iota(jnp.int32, (half, half), 0) <= lax.broadcasted_iota(jnp.int32, (half, half), 1)
    ).astype(F32)
    for g in range(2):
        inside_src[:, g * half : (g + 1) * half] = jnp.dot(
            logs[:, g * half : (g + 1) * half], upto, precision=HIGHEST, preferred_element_type=F32
        )
    exchange_start(n, me, tp, lambda peer: inside_src, inside_all, isend, irecv)
    moves.start("inside", inside_src, inside_all.at[me])

    def step_on(step, carry):
        projections.forward(step)
        grow(step)
        return carry

    lax.fori_loop(3, n - 2, step_on, 0)
    outputs.begin()
    projections.forward(n - 2)
    grow(n - 2)
    outputs.forward(1)
    projections.last()
    grow(n - 1)

    def head_norm(value):
        return value * lax.rsqrt(head_means(value * value, heads) + EPS)

    my_rows = token_rows(me)
    for pair in range(heads // 2):
        v_all[pair, my_rows, :] = acc_l[:, pair * LANES : (pair + 1) * LANES].astype(BF16)
    pairs.begin([2, 3, 5])
    keys = (head_norm(acc_r[:, width:]) * kgain_ref[...]).astype(BF16)
    for pair in range(heads // 2):
        k_all[pair, my_rows, :] = keys[:, pair * LANES : (pair + 1) * LANES]
    pairs.begin([0, 1, 4])
    for i, (source, target) in enumerate(
        ((wq_ref, wq_out), (wk_ref, wk_out), (wv_ref, wv_out), (wg_ref, wg_out))
    ):
        moves.start(i, source, target)
    moves.start("qr", acc_r.at[:, pl.ds(0, width)], qr_out)
    moves.start("kr", acc_r.at[:, pl.ds(width, width)], kr_out)
    moves.start("gl", acc_l.at[:, pl.ds(width, width)], gl_out)
    for i, (ref, out) in enumerate(((k_all, k_out), (v_all, v_out))):
        for pair in range(heads // 2):
            moves.start((i, pair), block(ref, pair)(me), block(out, pair)(me))
    q_ref[...] = (head_norm(acc_r[:, :width]) * qgain_ref[...] * 0.125).astype(BF16)
    moves.start("q", q_ref, q_out)

    moves.wait("inside")
    exchange_wait(n, me, tp, lambda peer: inside_src, inside_all, isend, irecv)
    tot_ref[...] = jnp.zeros_like(tot_ref)
    for i in range(n):
        for g in range(2):
            tot_ref[:, 2 * i + g : 2 * i + g + 1] = inside_all[i, :, (g + 1) * half - 1 : (g + 1) * half]
    before_ref[...] = jnp.dot(tot_ref[...], earlier_ref[...], precision=HIGHEST, preferred_element_type=F32)
    lane8 = lax.broadcasted_iota(jnp.int32, (8, LANES), 1)

    def offsets_of(shard_index):
        parts = []
        for g in range(2):
            before = jnp.sum(jnp.where(lane8 == 2 * shard_index + g, before_ref[...], 0.0), axis=1, keepdims=True)
            parts.append(inside_all[shard_index, :, g * half : (g + 1) * half] + before)
        return jnp.concatenate(parts, axis=1)

    def aug_rows(i, carry):
        aug_ref[token_rows(i), :] = key_pieces(offsets_of(i))
        return carry

    pairs.forward(1)
    lax.fori_loop(0, n, aug_rows, 0)
    moves.start("aug", aug_ref, aug_out)

    first, second = group_map[2 * me], group_map[2 * me + 1]
    in_order = first < second
    query_groups = (jnp.minimum(first, second), jnp.maximum(first, second))
    mine = turn(offsets_of(me))
    term_ref[...] = mine
    spread_heads(q_ref, row_pieces(mine, True), put_rows(cat_ref), heads, in_order)
    acc_ref[...] = jnp.zeros_like(acc_ref)
    query_at = lax.broadcasted_iota(jnp.int32, (half, half), 0)
    key_at = lax.broadcasted_iota(jnp.int32, (half, half), 1)
    diff_ref[...] = key_at - query_at
    for i, group in enumerate(query_groups):
        span_ref[i] = document_start(group * half + query_at, doc_lengths) - key_at
    ones = jnp.ones((half, LANES), BF16)

    def attend(i, back):
        late = lax.div(i, 2)
        pair = (1 - late) * 2 * i + late
        side = lax.rem(i, 2)
        owner = ring_owner(wrap(place + (2 * side - 1) * back, n), n)
        one, two = group_map[2 * owner], group_map[2 * owner + 1]
        forward = one < two
        key_groups = (jnp.minimum(one, two), jnp.maximum(one, two))
        top = pl.ds(pl.multiple_of(owner * rows, rows), half)
        bottom = pl.ds(pl.multiple_of(owner * rows + half, half), half)
        blocks = []
        for ref in (k_all.at[pair], v_all.at[pair], aug_ref):
            blocks.append(in_pack_order(forward, ref[top, :], ref[bottom, :]))
        for qi, ki in ((0, 0), (1, 0), (1, 1)):
            query_group, key_group = query_groups[qi], key_groups[ki]
            skipped = jnp.where(key_group < query_group, skip[query_group, key_group], 0)
            mask = (diff_ref[...] <= (query_group - key_group) * half) & (
                span_ref[qi] <= key_group * half - (skipped == 1).astype(jnp.int32) * (1 << 30)
            )
            here = pl.ds(qi * half, half)
            keys = jnp.concatenate([blocks[0][ki], blocks[2][ki]], axis=1)
            values = jnp.concatenate([blocks[1][ki], ones], axis=1)
            for e in range(2):
                h = 2 * pair + e
                weights = jnp.where(mask, jnp.exp(contract_cols(cat_ref[h, here, :], keys)), 0.0)
                acc_ref[h, here, :] += dot(weights.astype(BF16), values)

    def attend_all(count, back):
        def body(i, carry):
            attend(i, back)
            return carry

        lax.fori_loop(0, count, body, 0)

    attend_all(3, 0)
    attend_all(2, 1)

    def pair_step(step, count):
        outputs.forward(step)
        pairs.forward(step)
        attend_all(count, step)

    def early_step(step, carry):
        pair_step(step, 2)
        return carry

    def late_step(step, carry):
        pair_step(step, 4)
        return carry

    lax.fori_loop(2, n // 2, early_step, 0)
    pair_step(n // 2, 3)
    lax.fori_loop(n // 2 + 1, n - 1, late_step, 0)
    outputs.last()
    pairs.last()
    attend_all(4, n - 1)

    lane = lax.broadcasted_iota(jnp.int32, (rows, LANES), 1)
    low = low_lanes(rows)
    totals = jnp.ones((rows, LANES), F32)
    for pair in range(heads // 2):
        parts = []
        for h in (2 * pair, 2 * pair + 1):
            value = jnp.concatenate(in_pack_order(in_order, acc_ref[h, :half, :], acc_ref[h, half:, :]), axis=0)
            parts.append(value)
            totals = jnp.where(lane == h, value[:, LANES:], totals)
        att_ref[:, pair * LANES : (pair + 1) * LANES] = jnp.where(
            low, parts[0][:, :LANES], parts[1][:, :LANES]
        ) / jnp.where(low, parts[0][:, LANES:], parts[1][:, LANES:])
    moves.start("att", att_ref, att_out)
    term_ref[...] -= jnp.log(totals)

    def spilled(step, carry):
        for index in range(len(members)):
            spill_copy(index, step).wait()
        return carry

    lax.fori_loop(0, n - 1, spilled, 0)
    moves.wait()
    projections.sent()
    outputs.sent()
    pairs.sent()


def start_forward(n, collective_id, group_map, doc_lengths, skip, earlier, x, small, bias, weights, out_weight):
    rows, cols = x.shape
    shard, width = out_weight.shape
    heads = bias.shape[0]
    half = rows // 2
    dma = pltpu.SemaphoreType.DMA
    vmem = pl.BlockSpec(memory_space=VMEM)
    anywhere = pl.BlockSpec(memory_space=pl.ANY)
    bias = jnp.broadcast_to(jnp.pad(bias, (0, 8 - heads))[:, None], (8, LANES))
    by_pair = (heads // 2, n * rows, LANES)
    weight, wide, narrow = (n * shard, width), (rows, cols), (rows, width)
    shapes = (
        [(weight, BF16)] * 5
        + [((n, rows, shard), BF16), (narrow, BF16)]
        + [(narrow, F32)] * 3
        + [((8, rows), F32)]
        + [(by_pair, BF16)] * 2
        + [((n * rows, LANES), BF16), (narrow, F32), ((rows, LANES), F32)]
        + [((1, cols), F32)] * 2
        + [((1, width), F32)] * 2
        + [((8, cols), F32)]
    )
    return pl.pallas_call(
        functools.partial(start_kernel, n, heads),
        out_shape=[jax.ShapeDtypeStruct(*shape) for shape in shapes],
        in_specs=[smem(), smem(), smem(), vmem, anywhere, vmem, vmem] + [anywhere] * 5,
        out_specs=[anywhere if i < 10 or 11 <= i <= 14 else vmem for i in range(len(shapes))],
        scratch_shapes=[
            VMEM(wide, BF16),
            *[VMEM(weight, BF16)] * 4,
            VMEM((n, rows, shard), BF16),
            VMEM(narrow, BF16),
            *[VMEM(by_pair, BF16)] * 2,
            VMEM((n * rows, LANES), BF16),
            VMEM(narrow, F32),
            VMEM((heads, rows, 2 * LANES), F32),
            VMEM((heads, rows, 2 * LANES), BF16),
            VMEM((half, half), jnp.int32),
            VMEM((2, half, half), jnp.int32),
            VMEM((8, LANES), F32),
            VMEM((8, LANES), F32),
            VMEM((n, 8, rows), F32),
            VMEM((n, 16, 256), BF16),
            VMEM((rows, 2 * width), F32),
            VMEM((rows, 2 * width), F32),
            VMEM((8, rows), F32),
            *[dma((4, n - 1))] * 2,
            *[dma((2, n - 1))] * 2,
            *[dma((6, n - 1))] * 2,
            *[dma((n - 1,))] * 4,
            dma((6, n - 1)),
            dma((26,)),
        ],
        compiler_params=pltpu.CompilerParams(
            collective_id=collective_id, has_side_effects=True, vmem_limit_bytes=VMEM_LIMIT
        ),
    )(group_map, doc_lengths, skip, earlier, x, small, bias, *weights, out_weight)


class ScatterRing:
    def __init__(self, n, plan, local_term, slots, firsts, write, send, recv, place, sides, tp, source=None):
        self.n, self.place, self.sides, self.tp = n, place, sides, tp
        self.source, self.next = source, 1
        self.local_term, self.write = local_term, write
        self.slots, self.firsts, self.send, self.recv = slots, firsts, send, recv
        self.order = []
        starts = [0, 0]
        for index in range(max(len(plan[0]), len(plan[1]))):
            for side in (0, 1):
                if index < len(plan[side]):
                    width, tag = plan[side][index]
                    self.order.append((side, index, starts[side], width, tag))
                    starts[side] += width

    def target(self, side, step):
        step = -1 - step if side == 0 else 1 + step
        return ring_owner(wrap(self.place + step, self.n), self.n)

    def hop(self, side, index, start, width, step, first):
        cols = pl.ds(start, width)
        slots = self.slots[side]
        if not first:
            source = slots.at[step - 1, :, cols]
        elif self.source is None:
            source = self.firsts[side].at[:, cols]
        else:
            source = self.source(self.target(side, 0), side, cols)
        return remote(
            source,
            slots.at[step, :, cols],
            self.send.at[side, index, step],
            self.recv.at[side, index, step],
            (self.sides[side], self.tp),
        )

    def begin(self):
        for side, index, start, width, tag in self.order:
            if self.source is None:
                term = self.local_term(self.target(side, 0), tag)
                self.firsts[side][:, start : start + width] = term.astype(BF16)
            self.hop(side, index, start, width, 0, True).start()

    def forward(self, step):
        for side, index, start, width, tag in self.order:
            term = self.local_term(self.target(side, step), tag)
            slot = self.slots[side].at[step - 1, :, pl.ds(start, width)]
            self.hop(side, index, start, width, step - 1, True).wait_recv()
            slot[...] = (slot[...].astype(F32) + term).astype(BF16)
            self.hop(side, index, start, width, step, False).start()

    def span(self, first, last):
        def body(step, carry):
            self.forward(step)
            return carry

        if last > first:
            lax.fori_loop(first, last, body, 0)

    def advance(self, count):
        last = min(self.next + count, self.n - 1)
        self.span(self.next, last)
        self.next = last

    def end(self):
        n = self.n
        self.advance(n)
        for side, index, start, width, tag in self.order:
            term = self.local_term(self.target(side, n - 1), tag)
            self.hop(side, index, start, width, n - 2, True).wait_recv()
            self.write(tag, self.slots[side][n - 2, :, start : start + width].astype(F32) + term)
        if self.source is None:
            self.sent()

    def sent(self):
        for side, index, start, width, tag in self.order:
            self.hop(side, index, start, width, 0, True).wait_send()

        def finish(step, carry):
            for side, index, start, width, tag in self.order:
                self.hop(side, index, start, width, step, False).wait_send()
            return carry

        lax.fori_loop(1, self.n - 1, finish, 0)


def exchange_start(n, me, tp, source_of, landing, send, recv):
    for i in range(1, n):
        peer = lax.rem(me + i, n)
        remote(source_of(peer), landing.at[me], send.at[i - 1], recv.at[i - 1], (peer, tp)).start()


def exchange_wait(n, me, tp, source_of, landing, send, recv):
    for i in range(1, n):
        peer = lax.rem(me - i + n, n)
        remote(source_of(peer), landing.at[peer], send.at[i - 1], recv.at[i - 1], (peer, tp)).wait()


def ordered_sum(n, landing):
    total = landing[0]
    for i in range(1, n):
        total = total + landing[i]
    return total


def pair_scatter_kernel(
    n, key_ref, value_ref, col_ref, row_ref, key_out, value_out, off_out, tot_out,
    slot_r, slot_l, first_r, first_l, off_ref, tot_ref, off_land, tot_land,
    send, recv, osend, orecv, tsend, trecv, local,
):
    me, tp, place, sides = ring_setup(n)
    off_ref[...] = col_ref[...]
    off_ref[me] += row_ref[...]
    group_rows = row_ref.shape[1] // 2
    tot_ref[...] = jnp.zeros_like(tot_ref)
    for i in range(n):
        for g in range(2):
            tot_ref[:, 2 * i + g : 2 * i + g + 1] = jnp.sum(
                off_ref[i, :, g * group_rows : (g + 1) * group_rows], axis=1, keepdims=True
            )
    greet(ctx_peers(me, tp, n))
    exchange_start(n, me, tp, lambda peer: off_ref.at[peer], off_land, osend, orecv)
    exchange_start(n, me, tp, lambda peer: tot_ref, tot_land, tsend, trecv)
    mine = pltpu.make_async_copy(off_ref.at[me], off_land.at[me], local.at[0])
    mine_tot = pltpu.make_async_copy(tot_ref, tot_land.at[me], local.at[1])
    mine.start()
    mine_tot.start()
    width = key_ref.shape[2]
    plan = [
        [(w, (0, c)) for c, w in pieces(width, 128)],
        [(w, (1, c)) for c, w in pieces(width, 128)],
    ]

    def local_term(owner, tag):
        which, c0 = tag
        return (key_ref, value_ref)[which][owner, :, c0 : c0 + 128].astype(F32)

    def write(tag, value):
        which, c0 = tag
        (key_out, value_out)[which][:, c0 : c0 + 128] = value

    ring = ScatterRing(
        n, plan, local_term, (slot_r, slot_l), (first_r, first_l), write, send, recv, place, sides, tp
    )
    ring.begin()
    ring.end()
    mine.wait()
    mine_tot.wait()
    exchange_wait(n, me, tp, lambda peer: off_ref.at[peer], off_land, osend, orecv)
    exchange_wait(n, me, tp, lambda peer: tot_ref, tot_land, tsend, trecv)
    off_out[...] = ordered_sum(n, off_land)
    tot_out[...] = ordered_sum(n, tot_land)


def pieces(width, step):
    return [(c, min(step, width - c)) for c in range(0, width, step)]


def pair_scatter(n, collective_id, keys, values, columns, own_rows):
    _, rows, width = keys.shape
    offs, tots = columns, jax.ShapeDtypeStruct((8, LANES), F32)
    chunks = len(pieces(width, 128))
    return pl.pallas_call(
        functools.partial(pair_scatter_kernel, n),
        out_shape=[
            jax.ShapeDtypeStruct((rows, width), F32),
            jax.ShapeDtypeStruct((rows, width), F32),
            jax.ShapeDtypeStruct(offs.shape[1:], F32),
            jax.ShapeDtypeStruct(tots.shape, F32),
        ],
        in_specs=[pl.BlockSpec(memory_space=VMEM)] * 4,
        out_specs=[pl.BlockSpec(memory_space=VMEM)] * 4,
        scratch_shapes=[
            VMEM((n - 1, rows, width), BF16),
            VMEM((n - 1, rows, width), BF16),
            VMEM((rows, width), BF16),
            VMEM((rows, width), BF16),
            VMEM(offs.shape, F32),
            VMEM(tots.shape, F32),
            VMEM(offs.shape, F32),
            VMEM((n,) + tots.shape, F32),
            pltpu.SemaphoreType.DMA((2, chunks, n - 1)),
            pltpu.SemaphoreType.DMA((2, chunks, n - 1)),
            pltpu.SemaphoreType.DMA((n - 1,)),
            pltpu.SemaphoreType.DMA((n - 1,)),
            pltpu.SemaphoreType.DMA((n - 1,)),
            pltpu.SemaphoreType.DMA((n - 1,)),
            pltpu.SemaphoreType.DMA((2,)),
        ],
        compiler_params=pltpu.CompilerParams(
            collective_id=collective_id, has_side_effects=True, vmem_limit_bytes=VMEM_LIMIT
        ),
    )(keys, values, columns, own_rows)


def weight_scatter_kernel(n, plan, left_count, grads, *refs):
    lefts, refs = refs[:left_count], refs[left_count:]
    rights, refs = refs[:grads], refs[grads:]
    small_ref, part_ref, x_ref, gain_ref, dmid_ref, refs = *refs[:5], refs[5:]
    outs, refs = refs[:grads], refs[grads:]
    small_out, input_out, slot_r, slot_l, first_r, first_l, own_small, land, sum_out, refs = *refs[:9], refs[9:]
    tp_bufs, refs = refs[:4], refs[4:]
    send, recv, xsend, xrecv, tsend, trecv, local = refs
    me, tp, place, sides = ring_setup(n)
    chip, core, sibling, across = tp_setup()
    greet(ctx_peers(me, tp, n) + [sibling, across])
    shard = lefts[0].shape[2]
    half = part_ref.shape[0] // 2

    def local_term(owner, tag):
        left, right, c0, cw = tag
        return contract_rows(lefts[left][owner], rights[right][:, c0 : c0 + cw])

    def write(tag, value):
        _, right, c0, cw = tag
        outs[right][:, c0 : c0 + cw] = value

    ring = ScatterRing(
        n, plan, local_term, (slot_r, slot_l), (first_r, first_l), write, send, recv, place, sides, tp
    )

    def part(which, c):
        cols = part_ref.shape[1] // TP_CHUNKS
        return part_ref[pl.ds(pl.multiple_of(which * half, half), half), c * cols : (c + 1) * cols].astype(F32)

    total = TpSum(part, sum_out, tp_bufs, tsend, trecv, core, sibling, across)
    total.first()
    total.second()
    ring.begin()
    total.third()
    ring.advance(1)
    total.fourth()

    own_small[...] = small_ref[...]
    cols = part_ref.shape[1]
    size = 64

    def gain_rows(i, acc):
        rows = pl.ds(pl.multiple_of(i * size, size), size)
        value = x_ref[rows, :].astype(F32)
        inverse = lax.rsqrt(jnp.mean(value * value, axis=-1, keepdims=True) + EPS)
        normal = value * inverse
        grad = sum_out[rows, :].astype(F32)
        back = grad * gain_ref[...]
        back = inverse * (back - normal * jnp.mean(back * normal, axis=-1, keepdims=True))
        input_out[rows, :] = dmid_ref[rows, :] + back
        return acc + jnp.sum((grad * normal).reshape(size // 8, 8, cols), axis=0)

    gains = lax.fori_loop(0, 2 * half // size, gain_rows, jnp.zeros((8, cols), F32))
    gains = jnp.sum(gains, axis=0, keepdims=True)
    for i in range(n):
        own_small[i, 0:1, :shard] = gains[:, i * shard : (i + 1) * shard]
    exchange_start(n, me, tp, lambda peer: own_small.at[peer], land, xsend, xrecv)
    mine = pltpu.make_async_copy(own_small.at[me], land.at[me], local.at[0])
    mine.start()
    ring.end()
    mine.wait()
    exchange_wait(n, me, tp, lambda peer: own_small.at[peer], land, xsend, xrecv)
    small_out[...] = ordered_sum(n, land)


def weight_scatter(n, collective_id, plan, lefts, rights, small, part, x, gain, dmid):
    rows = lefts[0].shape[2]
    chunks = max(len(plan[0]), len(plan[1]))
    totals = [sum(width for width, _ in side) for side in plan]
    return pl.pallas_call(
        functools.partial(weight_scatter_kernel, n, plan, len(lefts), len(rights)),
        out_shape=[jax.ShapeDtypeStruct((rows, right.shape[1]), F32) for right in rights]
        + [jax.ShapeDtypeStruct(small.shape[1:], F32), jax.ShapeDtypeStruct(part.shape, F32)],
        in_specs=[pl.BlockSpec(memory_space=VMEM)] * (len(lefts) + len(rights) + 5),
        out_specs=[pl.BlockSpec(memory_space=VMEM)] * (len(rights) + 2),
        scratch_shapes=[
            VMEM((n - 1, rows, totals[0]), BF16),
            VMEM((n - 1, rows, totals[1]), BF16),
            VMEM((rows, totals[0]), BF16),
            VMEM((rows, totals[1]), BF16),
            VMEM(small.shape, F32),
            VMEM(small.shape, F32),
            VMEM(part.shape, BF16),
            *tp_buffers(*part.shape),
            pltpu.SemaphoreType.DMA((2, chunks, n - 1)),
            pltpu.SemaphoreType.DMA((2, chunks, n - 1)),
            pltpu.SemaphoreType.DMA((n - 1,)),
            pltpu.SemaphoreType.DMA((n - 1,)),
            pltpu.SemaphoreType.DMA((3, TP_CHUNKS)),
            pltpu.SemaphoreType.DMA((3, TP_CHUNKS)),
            pltpu.SemaphoreType.DMA((1,)),
        ],
        compiler_params=pltpu.CompilerParams(
            collective_id=collective_id, has_side_effects=True, vmem_limit_bytes=VMEM_LIMIT
        ),
    )(*lefts, *rights, small, part, x, gain, dmid)


def tp_setup():
    ctx = lax.axis_index("ctx")
    tp = lax.axis_index("tp")
    chip = lax.div(tp, 2)
    core = lax.rem(tp, 2)
    sibling = (ctx, 2 * chip + 1 - core)
    across = (ctx, 2 * (1 - chip) + core)
    return chip, core, sibling, across


TP_CHUNKS = 4


def tp_buffers(rows, width):
    return [VMEM((rows // 2, width), BF16) for _ in range(4)]


class TpSum:
    def __init__(self, part, out, bufs, send, recv, core, sibling, across):
        self.part, self.out, self.send, self.recv = part, out, send, recv
        self.away, self.land_a, self.half_b, self.land_b = bufs
        self.core, self.sibling, self.across = core, sibling, across
        self.half = self.away.shape[0]
        self.size = self.away.shape[1] // TP_CHUNKS

    def cols(self, c):
        return pl.ds(c * self.size, self.size)

    def copy(self, stage, c, which=None):
        cols = self.cols(c)
        if stage == 0:
            source, target, device = self.away.at[:, cols], self.land_a.at[:, cols], self.sibling
        elif stage == 1:
            source, target, device = self.half_b.at[:, cols], self.land_b.at[:, cols], self.across
        else:
            source = target = self.out.at[self.rows(which), cols]
            device = self.sibling
        return remote(source, target, self.send.at[stage, c], self.recv.at[stage, c], device)

    def rows(self, which):
        return pl.ds(pl.multiple_of(which * self.half, self.half), self.half)

    def first(self):
        for c in range(TP_CHUNKS):
            self.away[:, self.cols(c)] = self.part(1 - self.core, c).astype(BF16)
            self.copy(0, c).start()

    def second(self):
        for c in range(TP_CHUNKS):
            cols = self.cols(c)
            mine = self.part(self.core, c)
            self.copy(0, c).wait_recv()
            self.half_b[:, cols] = (mine + self.land_a[:, cols].astype(F32)).astype(BF16)
            self.copy(1, c).start()

    def third(self):
        for c in range(TP_CHUNKS):
            cols = self.cols(c)
            self.copy(1, c).wait_recv()
            both = self.half_b[:, cols].astype(F32) + self.land_b[:, cols].astype(F32)
            self.out[self.rows(self.core), cols] = both.astype(BF16)
            self.copy(2, c, self.core).start()

    def fourth(self):
        for c in range(TP_CHUNKS):
            self.copy(2, c, 1 - self.core).wait_recv()
            self.copy(0, c).wait_send()
            self.copy(1, c).wait_send()
            self.copy(2, c, self.core).wait_send()


class TpSplit:
    def __init__(self, part, bufs, send, recv, chip, core, sibling, across):
        self.part, self.send, self.recv = part, send, recv
        self.away, self.land_a, self.half_b, self.land_b = bufs
        self.chip, self.core, self.sibling, self.across = chip, core, sibling, across

    def copy(self, stage):
        if stage < 2:
            return remote(
                self.away.at[stage], self.land_a.at[stage], self.send.at[stage], self.recv.at[stage], self.sibling
            )
        return remote(self.half_b, self.land_b, self.send.at[2], self.recv.at[2], self.across)

    def first(self):
        for i, chip in enumerate((1 - self.chip, self.chip)):
            self.away[i] = self.part(chip, 1 - self.core).astype(BF16)
            self.copy(i).start()

    def second(self):
        mine = self.part(1 - self.chip, self.core)
        self.copy(0).wait_recv()
        self.half_b[...] = (mine + self.land_a[0].astype(F32)).astype(BF16)
        self.copy(2).start()

    def third(self):
        mine = self.part(self.chip, self.core)
        self.copy(1).wait_recv()
        self.copy(2).wait_recv()
        total = mine + self.land_a[1].astype(F32) + self.land_b[...].astype(F32)
        for stage in range(3):
            self.copy(stage).wait_send()
        return total


def feed_kernel(n, heads, attention, *refs):
    if attention:
        (group_map, doc_lengths, skip, q_in, term_in, k_in, v_in, aug_in), refs = refs[:8], refs[8:]
    (att_in, gl_in, outw_in, x_in, gain_ref, grad_in, wg_in, wu_in, wd_in), refs = refs[:9], refs[9:]
    (gated_out, layer_ref, down_out, gate_out, up_out, dmid_out, do_out, dgl_out, gain_out), refs = refs[:9], refs[9:]
    if attention:
        (dm_out, dq_out, drow_ref, dk_out, dv_out, dcol_ref), refs = refs[:6], refs[6:]
    (
        att_ref, gl_ref, outw_ref, x_ref, grad_ref, gated_ref, normed_ref, dgt_ref, dup_ref, do_ref, dgl_ref,
        gate_all, up_all, down_all, accs, dhid_acc, hid_ref, branch_ref, mid_ref, dw_ref, dy_ref,
        a0, a1, a2, a3, b3, s0, s1, s2, s3, dslot_r, dslot_l, dfirst_r, dfirst_l, eslot_r, eslot_l, efirst_r, efirst_l,
        gsend, grecv, hsend, hrecv, asend, arecv, bsend, brecv, ssend, srecv, dsend, drecv, esend, erecv, local,
    ), refs = refs[:53], refs[53:]
    if attention:
        term_ref, dm_ref, diff_ref, span_ref, stage, kv_sem, stage_sem = refs
    gate_acc, up_acc = accs.at[0], accs.at[1]
    me, tp, place, sides = ring_setup(n)
    chip, core, sibling, across = tp_setup()
    moves = Moves(local)
    for name, source, target in (
        ("att", att_in, att_ref), ("gl", gl_in, gl_ref), ("outw", outw_in, outw_ref), ("grad", grad_in, grad_ref),
        ("x", x_in, x_ref),
    ):
        moves.start(name, source, target)
    if attention:
        moves.start("term", term_in, term_ref)
    greet([(side, tp) for side in sides] + [sibling, across])
    shard, hidden = wg_in.shape
    rows, width = x_in.shape
    half = rows // 2
    hw = hidden // 2
    size = 64
    ring = (n, place, sides, tp)

    def rows_of(owner):
        return pl.ds(pl.multiple_of(owner * shard, 16), shard)

    def window(ref, c0, cw):
        return lambda owner: ref.at[rows_of(owner), pl.ds(c0, cw)]

    def chunks(members):
        return [(side, source.at[:, pl.ds(c0, cw)], window(target, c0, cw)) for side, source, target, c0, cw in members]

    gates = Gather(
        *ring,
        chunks(
            [
                (side, source, target, c0, hw)
                for c0 in (0, hw)
                for side, source, target in ((0, wg_in, gate_all), (1, wu_in, up_all))
            ]
        ),
        gsend, grecv,
    )
    downs = Gather(
        *ring,
        chunks([(side, wd_in, down_all, side * hw + c0, hw // 2) for c0 in (0, hw // 2) for side in (0, 1)]),
        hsend, hrecv,
    )
    gates.begin()
    for i, (source, target) in enumerate(((wg_in, gate_all), (wu_in, up_all), (wd_in, down_all))):
        moves.start(i, source, target.at[rows_of(me)])

    moves.wait("att", "gl")
    gated_ref[...] = (att_ref[...] * jax.nn.sigmoid(gl_ref[...])).astype(BF16)
    moves.start("gated", gated_ref, gated_out)
    moves.wait("outw")
    span = width // TP_CHUNKS

    def branch_part(which, c):
        mine = gated_ref[pl.ds(pl.multiple_of(which * half, half), half), :]
        return contract_cols(mine, outw_ref[c * span : (c + 1) * span, :])

    branch = TpSum(branch_part, branch_ref, (a0, a1, a2, a3), asend, arecv, core, sibling, across)
    branch.first()
    branch.second()
    gates.forward(1)
    moves.wait("grad")
    for j in range(n):
        dy_ref[j] = grad_ref[:, j * shard : (j + 1) * shard]
    dhid_acc[...] = jnp.zeros_like(dhid_acc)
    gate_acc[...] = jnp.zeros_like(gate_acc)
    up_acc[...] = jnp.zeros_like(up_acc)

    def grow_back(back):
        for side in (0, 1):
            owner = downs.owner(side, back)
            cols = pl.ds(side * hw, hw)
            dhid_acc[:, cols] += dot(dy_ref[owner], down_all[rows_of(owner), cols])

    def grow(back):
        for side, acc, source in ((0, gate_acc, gate_all), (1, up_acc, up_all)):
            owner = gates.owner(side, back)
            acc[...] += dot(normed_ref[owner], source[rows_of(owner), :])

    moves.wait(0, 1, 2)
    grow_back(0)
    gates.forward(2)
    branch.third()
    branch.fourth()
    moves.wait("x")

    def norm_rows(i, carry):
        here = pl.ds(pl.multiple_of(i * size, size), size)
        middle = x_ref[here, :].astype(F32) + branch_ref[here, :].astype(F32)
        mid_ref[here, :] = middle
        normed = (rms_scale(middle) * gain_ref[...]).astype(BF16)
        for j in range(n):
            normed_ref[j, here, :] = normed[:, j * shard : (j + 1) * shard]
        return carry

    lax.fori_loop(0, rows // size, norm_rows, 0)
    own = pl.ds(pl.multiple_of(tp * span, span), span)
    layer_ref[...] = mid_ref[:, own]
    if attention:
        narrow = q_in.shape[1]
        q_ref = x_ref.at[:, pl.ds(0, narrow)]
        moves.start("q", q_in, q_ref)
        for i in range(n):
            moves.start(
                ("aug", i),
                aug_in.at[pl.ds(i * rows, rows), :],
                x_ref.at[:, pl.ds(narrow + i * LANES, LANES)],
            )
    gates.forward(3)

    def grow_step(step, carry):
        grow(step)
        return carry

    lax.fori_loop(0, 4, grow_step, 0)

    def gate_step(step, carry):
        gates.forward(step)
        grow(step)
        return carry

    lax.fori_loop(4, n - 1, gate_step, 0)
    downs.begin()
    gates.last()
    grow(n - 1)

    def hid_rows(i, carry):
        here = pl.ds(pl.multiple_of(i * size, size), size)
        gate, up = gate_acc[here, :], up_acc[here, :]
        open_gate = jax.nn.sigmoid(gate)
        silu = gate * open_gate
        hid_ref[here, :] = (silu * up).astype(BF16)
        gate_acc[here, :] = up * open_gate * (1.0 + gate * (1.0 - open_gate))
        up_acc[here, :] = silu
        return carry

    lax.fori_loop(0, rows // size, hid_rows, 0)

    def down_step(step, carry):
        downs.forward(step)
        grow_back(step)
        return carry

    lax.fori_loop(1, n - 2, down_step, 0)
    downs.forward(n - 2)

    def down_term(owner, tag):
        return contract_rows(dy_ref[owner], hid_ref[:, tag * hw : (tag + 1) * hw])

    down_ref = accs.at[0, pl.ds(0, shard), :]
    gate_ref = accs.at[0, pl.ds(shard, shard), :]
    up_ref = accs.at[1, pl.ds(0, shard), :]

    def down_write(tag, value):
        down_ref[:, tag * hw : (tag + 1) * hw] = value

    def early_term(owner, tag):
        which, c0 = tag
        return contract_rows(normed_ref[owner], (dgt_ref, dup_ref)[which][:, c0 : c0 + hw])

    def early_write(tag, value):
        which, c0 = tag
        (gate_ref, up_ref)[which][:, c0 : c0 + hw] = value

    backs = ScatterRing(
        n, [[(hw, 0)], [(hw, 1)]], down_term, (dslot_r, dslot_l), (dfirst_r, dfirst_l), down_write,
        dsend, drecv, place, sides, tp,
    )
    earlies = ScatterRing(
        n, [[(hw, (i, 0)), (hw, (i, hw))] for i in range(2)], early_term, (eslot_r, eslot_l), (efirst_r, efirst_l),
        early_write, esend, erecv, place, sides, tp,
    )
    backs.begin()
    grow_back(n - 2)
    downs.last()
    grow_back(n - 1)

    def grad_rows(i, carry):
        here = pl.ds(pl.multiple_of(i * size, size), size)
        dhid = dhid_acc[here, :]
        dgt_ref[here, :] = (dhid * gate_acc[here, :]).astype(BF16)
        dup_ref[here, :] = (dhid * up_acc[here, :]).astype(BF16)
        return carry

    lax.fori_loop(0, rows // size, grad_rows, 0)

    def dw_part(which, c):
        mine = pl.ds(pl.multiple_of(which * half, half), half)
        back = pl.ds(c * span, span)
        return contract_cols(dgt_ref[mine, :], gate_all[back, :]) + contract_cols(dup_ref[mine, :], up_all[back, :])

    def layer_part(which_chip, which_core):
        back = pl.ds(pl.multiple_of((2 * which_chip + which_core) * span, span), span)
        return contract_cols(hid_ref[...], down_all[back, :])

    total = TpSum(dw_part, dw_ref, (a0, a1, a2, b3), bsend, brecv, core, sibling, across)
    layer = TpSplit(layer_part, (s0, s1, s2, s3), ssend, srecv, chip, core, sibling, across)
    total.first()
    backs.advance(1)
    earlies.begin()
    total.second()
    gates.sent()
    if attention:
        pairs = heads // 2

        def kv_copies(it):
            part, pair = lax.div(it, pairs), lax.rem(it, pairs)
            source = pl.ds(pl.multiple_of(part * rows, rows), rows)
            target = pl.ds(pl.multiple_of(pair * rows, rows), rows)
            lanes = pl.ds(pl.multiple_of(part * LANES, LANES), LANES)
            return [
                pltpu.make_async_copy(ref.at[pair, source, :], held.at[target, lanes], kv_sem.at[i, it])
                for i, (ref, held) in enumerate(((k_in, gate_all), (v_in, up_all)))
            ]

        def bring(it, carry):
            for copy in kv_copies(it):
                copy.start()
            return carry

        lax.fori_loop(0, n * pairs, bring, 0)
    layer.first()
    layer.second()
    backs.advance(1)
    earlies.advance(1)
    backs.advance(1)
    earlies.advance(1)
    total.third()
    total.fourth()

    def middle_rows(i, acc):
        here = pl.ds(pl.multiple_of(i * size, size), size)
        middle = mid_ref[here, :]
        inverse = lax.rsqrt(jnp.mean(middle * middle, axis=-1, keepdims=True) + EPS)
        normal = middle * inverse
        dw = dw_ref[here, :].astype(F32)
        back = dw * gain_ref[...]
        back = inverse * (back - normal * jnp.mean(back * normal, axis=-1, keepdims=True))
        dmid = grad_ref[here, :].astype(F32) + back
        mid_ref[here, :] = dmid
        low = dmid.astype(BF16)
        branch_ref[here, :] = low
        if attention:
            for j in range(n):
                dm_ref[j, here, :] = low[:, j * shard : (j + 1) * shard]
        return acc + jnp.sum((dw * normal).reshape(size // 8, 8, width), axis=0)

    gain_out[...] = lax.fori_loop(0, rows // size, middle_rows, jnp.zeros((8, width), F32))
    moves.start("dmid", mid_ref, dmid_out)
    if attention:
        moves.start("dm", dm_ref, dm_out)
    da = dot(branch_ref[...], outw_ref[...])
    open_gate = jax.nn.sigmoid(gl_ref[...])
    do_ref[...] = (da * open_gate).astype(BF16)
    dgl_ref[...] = (da * att_ref[...] * open_gate * (1.0 - open_gate)).astype(BF16)
    moves.start("do", do_ref, do_out)
    moves.start("dgl", dgl_ref, dgl_out)
    backs.advance(1)
    earlies.advance(1)
    layer_ref[...] += layer.third()

    if attention:
        moves.wait("q", "term", *[("aug", i) for i in range(n)])
        first, second = group_map[2 * me], group_map[2 * me + 1]
        in_order = first < second
        query_groups = (jnp.minimum(first, second), jnp.maximum(first, second))

        def put_in(ref):
            def put(h, value, extra):
                ref[:, 2 * h * LANES : (2 * h + 1) * LANES] = value
                ref[:, (2 * h + 1) * LANES : (2 * h + 2) * LANES] = extra

            return put

        spread_heads(q_ref, row_pieces(term_ref[...], True), put_in(dw_ref), heads, in_order)
        delta = head_sums(do_ref[...].astype(F32) * att_ref[...], heads)
        spread_heads(do_ref, row_pieces(-delta, False), put_in(branch_ref), heads, in_order)
        accs[...] = jnp.zeros_like(accs)
        query_at = lax.broadcasted_iota(jnp.int32, (half, half), 1)
        key_at = lax.broadcasted_iota(jnp.int32, (half, half), 0)
        diff_ref[...] = key_at - query_at
        for i, group in enumerate(query_groups):
            span_ref[i] = document_start(group * half + query_at, doc_lengths) - key_at
        dk_acc, dv_acc, dcol_acc = (dhid_acc.at[:, pl.ds(i * LANES, LANES)] for i in range(3))

        def stage_copies(it):
            part, pair = lax.div(it, pairs), lax.rem(it, pairs)
            lanes = pl.ds(pl.multiple_of(pair * LANES, LANES), LANES)
            slot = lax.rem(it, 2)
            return [
                pltpu.make_async_copy(stage.at[slot, i], out.at[part, :, lanes], stage_sem.at[slot, i])
                for i, out in enumerate((dk_out, dv_out))
            ]

        def attend(it, carry):
            part, pair = lax.div(it, pairs), lax.rem(it, pairs)
            for copy in kv_copies(it):
                copy.wait()
            one, two = group_map[2 * part], group_map[2 * part + 1]
            forward = one < two
            key_groups = (jnp.minimum(one, two), jnp.maximum(one, two))
            lanes = pl.ds(pl.multiple_of(part * LANES, LANES), LANES)

            def ordered(ref, base, where):
                top = pl.ds(pl.multiple_of(base * rows, rows), half)
                bottom = pl.ds(pl.multiple_of(base * rows + half, half), half)
                return in_pack_order(forward, ref[top, where], ref[bottom, where])

            key_blocks = ordered(gate_all, pair, lanes)
            value_blocks = ordered(up_all, pair, lanes)
            aug_lanes = pl.ds(pl.multiple_of(narrow + part * LANES, LANES), LANES)
            aug_blocks = ordered(x_ref, 0, aug_lanes)
            dk_acc[...] = jnp.zeros_like(dk_acc)
            dv_acc[...] = jnp.zeros_like(dv_acc)

            @pl.when(pair == 0)
            def _():
                dcol_acc[...] = jnp.zeros_like(dcol_acc)

            for qi, ki in ((0, 0), (1, 0), (1, 1)):
                query_group, key_group = query_groups[qi], key_groups[ki]
                skipped = jnp.where(key_group < query_group, skip[query_group, key_group], 0)
                mask = (diff_ref[...] <= (query_group - key_group) * half) & (
                    span_ref[qi] <= key_group * half - (skipped == 1).astype(jnp.int32) * (1 << 30)
                )
                q_rows, k_rows = pl.ds(qi * half, half), pl.ds(ki * half, half)
                keys = jnp.concatenate([key_blocks[ki], aug_blocks[ki]], axis=1)
                values = jnp.concatenate([value_blocks[ki], aug_blocks[ki]], axis=1)
                for e in range(2):
                    h = 2 * pair + e
                    spot = pl.ds(pl.multiple_of(h * 2 * LANES, 2 * LANES), 2 * LANES)
                    queries, grads_out = dw_ref[q_rows, spot], branch_ref[q_rows, spot]
                    probs = jnp.where(mask, jnp.exp(contract_cols(keys, queries)), 0.0)
                    grads = (probs * contract_cols(values, grads_out)).astype(BF16)
                    dv_acc[k_rows, :] += dot(probs.astype(BF16), grads_out[:, :LANES])
                    both = dot(grads, queries)
                    dk_acc[k_rows, :] += both[:, :LANES]
                    dcol_acc[k_rows, :] += both[:, LANES:]
                    quarter = pl.ds(pl.multiple_of(lax.rem(h, 4) * 2 * LANES, 2 * LANES), 2 * LANES)
                    accs[lax.div(h, 4), q_rows, quarter] += contract_rows(grads, keys)

            @pl.when(it >= 2)
            def _():
                for copy in stage_copies(it - 2):
                    copy.wait()

            slot = lax.rem(it, 2)
            for i, acc in enumerate((dk_acc, dv_acc)):
                stage[slot, i] = jnp.concatenate(
                    in_pack_order(forward, acc[pl.ds(0, half), :], acc[pl.ds(half, half), :]), axis=0
                ).astype(BF16)
            for copy in stage_copies(it):
                copy.start()

            @pl.when(pair == pairs - 1)
            def _():
                columns = jnp.concatenate(
                    in_pack_order(forward, dcol_acc[pl.ds(0, half), :], dcol_acc[pl.ds(half, half), :]), axis=0
                )
                dcol_ref[part] = -(columns.T[:8])

            return carry

        done = 0
        while earlies.next < n - 1:
            lax.fori_loop(done, done + 2 * pairs, attend, 0)
            done += 2 * pairs
            backs.advance(1)
            earlies.advance(1)
        lax.fori_loop(done, n * pairs, attend, 0)
        for it in (n * pairs - 2, n * pairs - 1):
            for copy in stage_copies(it):
                copy.wait()

        lane = lax.broadcasted_iota(jnp.int32, (rows, LANES), 1)
        low = low_lanes(rows)
        sums = jnp.zeros((rows, LANES), F32)
        for pair in range(pairs):
            parts = []
            for h in (2 * pair, 2 * pair + 1):
                spot = pl.ds((h % 4) * 2 * LANES, 2 * LANES)
                value = jnp.concatenate(
                    in_pack_order(in_order, accs[h // 4, :half, spot], accs[h // 4, half:, spot]), axis=0
                )
                parts.append(value)
                sums = jnp.where(lane == 24 + h, value[:, LANES:], sums)
            dhid_acc[:, (3 + pair) * LANES : (4 + pair) * LANES] = jnp.where(
                low, parts[0][:, :LANES], parts[1][:, :LANES]
            )
        moves.start("dq", dhid_acc.at[:, pl.ds(3 * LANES, pairs * LANES)], dq_out)
        drow_ref[...] = pltpu.roll(sums, LANES - 24, 1).T[:8]

        moves.wait("dq")
    backs.end()
    moves.start("down", down_ref, down_out)
    earlies.end()
    moves.start("gate", gate_ref, gate_out)
    moves.start("up", up_ref, up_out)
    downs.sent()
    moves.wait()


def feed_forward(
    n, collective_id, heads, attended, gate_logit, out_weight, x, gain, dy, w_gate, w_up, w_down, attention=None
):
    rows, width = x.shape
    shard, hidden = w_gate.shape
    heads_width = attended.shape[1]
    own = width // 4
    half = rows // 2
    dma = pltpu.SemaphoreType.DMA
    vmem = pl.BlockSpec(memory_space=VMEM)
    anywhere = pl.BlockSpec(memory_space=pl.ANY)
    wide, narrow, deep = (rows, width), (rows, heads_width), (rows, hidden)
    by_shard = (n, rows, shard)
    weight = (shard, hidden)
    shapes = [
        (narrow, BF16),
        ((rows, own), F32),
        (weight, F32),
        (weight, F32),
        (weight, F32),
        (wide, F32),
        (narrow, BF16),
        (narrow, BF16),
        ((8, width), F32),
    ]
    kept = [1, 8]
    extra_specs, extra_scratch = [], []
    if attention is not None:
        assert heads // 2 * rows == n * shard and n * LANES == hidden and heads_width + hidden <= width
        shapes += [
            (by_shard, BF16),
            (narrow, F32),
            ((8, rows), F32),
            ((n, rows, heads_width), BF16),
            ((n, rows, heads_width), BF16),
            ((n, 8, rows), F32),
        ]
        kept += [11, 14]
        extra_specs = [smem()] * 3 + [anywhere] * 5
        extra_scratch = [
            VMEM((rows, LANES), F32),
            VMEM(by_shard, BF16),
            VMEM((half, half), jnp.int32),
            VMEM((2, half, half), jnp.int32),
            VMEM((2, 2, rows, LANES), BF16),
            dma((2, n * heads // 2)),
            dma((2, 2)),
        ]
    return pl.pallas_call(
        functools.partial(feed_kernel, n, heads, attention is not None),
        out_shape=[jax.ShapeDtypeStruct(*shape) for shape in shapes],
        in_specs=extra_specs + [anywhere] * 4 + [vmem] + [anywhere] * 4,
        out_specs=[vmem if i in kept else anywhere for i in range(len(shapes))],
        scratch_shapes=[
            VMEM(narrow, F32),
            VMEM(narrow, F32),
            VMEM(out_weight.shape, BF16),
            VMEM(wide, BF16),
            VMEM(wide, BF16),
            VMEM(narrow, BF16),
            VMEM(by_shard, BF16),
            VMEM(deep, BF16),
            VMEM(deep, BF16),
            VMEM(narrow, BF16),
            VMEM(narrow, BF16),
            *[VMEM((n * shard, hidden), BF16)] * 3,
            VMEM((2,) + deep, F32),
            VMEM(deep, F32),
            VMEM(deep, BF16),
            VMEM(wide, BF16),
            VMEM(wide, F32),
            VMEM(wide, BF16),
            VMEM(by_shard, BF16),
            *tp_buffers(rows, width),
            VMEM((rows // 2, width), BF16),
            VMEM((2, rows, own), BF16),
            VMEM((2, rows, own), BF16),
            VMEM((rows, own), BF16),
            VMEM((rows, own), BF16),
            *ring_scratch(n, shard, [hidden // 2] * 2),
            *ring_scratch(n, shard, [hidden] * 2),
            *[dma((4, n - 1))] * 4,
            *[dma((3, TP_CHUNKS))] * 4,
            *[dma((3,))] * 2,
            *[dma((2, 1, n - 1))] * 2,
            *[dma((2, 2, n - 1))] * 2,
            dma((27,)),
            *extra_scratch,
        ],
        compiler_params=pltpu.CompilerParams(
            collective_id=collective_id, has_side_effects=True, vmem_limit_bytes=VMEM_LIMIT
        ),
    )(*(attention or ()), attended, gate_logit, out_weight, x, gain, dy, w_gate, w_up, w_down)


def ring_scratch(n, height, widths):
    return [VMEM((n - 1, height, w), BF16) for w in widths] + [VMEM((height, w), BF16) for w in widths]


def head_means(value, heads):
    width = value.shape[1]
    size = width // heads
    left = lax.div(lax.broadcasted_iota(jnp.int32, (width, width), 0), size)
    right = lax.div(lax.broadcasted_iota(jnp.int32, (width, width), 1), size)
    member = (left == right).astype(BF16)
    high = value.astype(BF16)
    return (dot(high, member) + dot((value - high.astype(F32)).astype(BF16), member)) * (1.0 / size)


STAGED = (0, 1, 4, 5, 16, 11, 14, 17, 18, 19, 6, 12, 13, 20)


def finish_kernel(n, heads, gate_plan, attn_plan, *refs):
    operands, refs = list(refs[:24]), refs[24:]
    (q_out, k_out, v_out, g_out, o_out, small_out, input_out), refs = refs[:7], refs[7:]
    staged, refs = refs[: len(STAGED)], refs[len(STAGED) :]
    (
        pslot_r, pslot_l, gslot_r, gslot_l, gfirst_r, gfirst_l, aslot_r, aslot_l, afirst_r, afirst_l,
        dk_sum, dv_sum, dqr_ref, dkr_ref, dvl_ref, du_ref, sum_ref, t0, t1, t2, t3,
        off_ref, tot_ref, off_land, tot_land, small_ref, small_land,
        psend, precv, gsend, grecv, asend, arecv, osend, orecv, qsend, qrecv, xsend, xrecv, tsend, trecv, local,
    ) = refs
    moves = Moves(local)
    dk_hbm, dv_hbm = operands[:2]
    for target, index in zip(staged, STAGED):
        moves.start(index, operands[index], target)
        operands[index] = target
    (
        dk_ref, dv_ref, col_ref, row_ref, dq_ref, qr_ref, kr_ref, qgain_ref, kgain_ref, fz_ref, later_ref,
        wq_ref, wk_ref, wv_ref, wg_ref, wf_ref, dgl_ref, u_ref, dm_ref, gated_ref,
        x_ref, gain_ref, dmid_ref, gain_two_ref,
    ) = operands
    me, tp, place, sides = ring_setup(n)
    chip, core, sibling, across = tp_setup()
    rows, width = dq_ref.shape
    cols = x_ref.shape[1]
    shard = u_ref.shape[2]
    half = rows // 2
    head_dim = width // heads
    small_ref[...] = jnp.zeros_like(small_ref)
    greet(ctx_peers(me, tp, n) + [sibling, across])

    def pair_term(owner, tag):
        which, c0 = tag
        return (dk_ref, dv_ref)[which][owner, :, c0 : c0 + LANES].astype(F32)

    def pair_write(tag, value):
        which, c0 = tag
        (dk_sum, dv_sum)[which][:, c0 : c0 + LANES] = value

    pairs = ScatterRing(
        n, [[(w, (i, c)) for c, w in pieces(width, LANES)] for i in range(2)], pair_term,
        (pslot_r, pslot_l), None, pair_write, psend, precv, place, sides, tp,
        source=lambda target, side, window: (dk_hbm, dv_hbm)[side].at[target, :, window],
    )
    pairs.begin()
    off_ref[...] = col_ref[...]
    off_ref[me] += row_ref[...]
    tot_ref[...] = jnp.zeros_like(tot_ref)
    for i in range(n):
        for g in range(2):
            tot_ref[:, 2 * i + g : 2 * i + g + 1] = jnp.sum(
                off_ref[i, :, g * half : (g + 1) * half], axis=1, keepdims=True
            )
    exchange_start(n, me, tp, lambda peer: off_ref.at[peer], off_land, osend, orecv)
    exchange_start(n, me, tp, lambda peer: tot_ref, tot_land, qsend, qrecv)
    moves.start("off", off_ref.at[me], off_land.at[me])
    moves.start("tot", tot_ref, tot_land.at[me])

    def raw_grad(grad, raw, gain):
        inverse = lax.rsqrt(head_means(raw * raw, heads) + EPS)
        normal = raw * inverse
        back = grad * gain
        back = inverse * (back - normal * head_means(back * normal, heads))
        return back.astype(BF16), jnp.sum(grad * normal, axis=0, keepdims=True)

    def gain_rows(row, first):
        count = 2 * head_dim // n
        for i in range(n // 2):
            for h in range(heads):
                lane = h * head_dim + i * count
                small_ref[first + i, 2 + h : 3 + h, 0:count] = row[:, lane : lane + count]

    moves.wait(0, 1, 4, 5)
    pairs.advance(1)
    dqr, row = raw_grad(dq_ref[...], qr_ref[...], qgain_ref[...] * 0.125)
    dqr_ref[...] = dqr
    gain_rows(row * 0.125, 0)
    pairs.advance(1)
    moves.wait(16, 11, 14)
    span = cols // TP_CHUNKS
    for c in range(TP_CHUNKS):
        back = pl.ds(c * span, span)
        du_ref[:, back] = contract_cols(dqr_ref[...], wq_ref[back, :]) + contract_cols(dgl_ref[...], wg_ref[back, :])
    pairs.advance(n)
    moves.wait(17, 18, 19)

    def gate_term(owner, tag):
        left, right, c0, cw = tag
        grads = (gated_ref, dqr_ref, dgl_ref)[right]
        return contract_rows((dm_ref, u_ref)[left][owner], grads[:, c0 : c0 + cw])

    def gate_write(tag, value):
        _, right, c0, cw = tag
        (o_out, q_out, g_out)[right][:, c0 : c0 + cw] = value

    gates = ScatterRing(
        n, gate_plan, gate_term, (gslot_r, gslot_l), (gfirst_r, gfirst_l), gate_write, gsend, grecv, place, sides, tp,
    )
    gates.begin()
    pairs.end()

    moves.wait(6)
    dkr, row = raw_grad(dk_sum[...], kr_ref[...], kgain_ref[...])
    dkr_ref[...] = dkr
    gain_rows(row, n // 2)
    dvl_ref[...] = dv_sum[...].astype(BF16)

    def attn_term(owner, tag):
        c0, cw = tag[1], tag[2]
        return contract_rows(u_ref[owner], (dkr_ref, dvl_ref)[tag[0]][:, c0 : c0 + cw])

    def attn_write(tag, value):
        c0, cw = tag[1], tag[2]
        (k_out, v_out)[tag[0]][:, c0 : c0 + cw] = value

    attns = ScatterRing(
        n, attn_plan, attn_term, (aslot_r, aslot_l), (afirst_r, afirst_l), attn_write, asend, arecv, place, sides, tp,
    )
    attns.begin()
    gates.advance(1)
    moves.wait("off", "tot")
    exchange_wait(n, me, tp, lambda peer: off_ref.at[peer], off_land, osend, orecv)
    exchange_wait(n, me, tp, lambda peer: tot_ref, tot_land, qsend, qrecv)
    off_sum = ordered_sum(n, off_land)
    tot_sum = ordered_sum(n, tot_land)
    onward = (
        lax.broadcasted_iota(jnp.int32, (half, half), 0) >= lax.broadcasted_iota(jnp.int32, (half, half), 1)
    ).astype(F32)
    parts = []
    for g in range(2):
        suffix = jnp.dot(
            off_sum[:, g * half : (g + 1) * half], onward, precision=HIGHEST, preferred_element_type=F32
        )
        parts.append(suffix + jnp.sum(tot_sum * later_ref[g : g + 1, :], axis=1, keepdims=True))
    dfz = (jnp.concatenate(parts, axis=1) * jax.nn.sigmoid(-fz_ref[...])).astype(BF16).astype(F32)
    head = lax.broadcasted_iota(jnp.int32, dfz.shape, 0)
    dfz = jnp.where(head < heads, dfz, 0.0)
    bias = jnp.sum(dfz, axis=1, keepdims=True)
    dfz_cols = turn(dfz).astype(BF16)
    dfz_low = dfz.astype(BF16)
    for i in range(n):
        small_ref[i, 8:16, :shard] = dot(dfz_low, u_ref[i])
        small_ref[i, 8:16, 224:225] = bias
        small_ref[i, 1:2, :shard] = jnp.sum(gain_two_ref[:, i * shard : (i + 1) * shard], axis=0, keepdims=True)

    moves.wait(12, 13)
    forget = jnp.concatenate([wf_ref[...], jnp.zeros((LANES - 8, cols), F32)], axis=0).astype(BF16)
    for c in range(TP_CHUNKS):
        back = pl.ds(c * span, span)
        du_ref[:, back] += (
            contract_cols(dkr_ref[...], wk_ref[back, :])
            + contract_cols(dvl_ref[...], wv_ref[back, :])
            + dot(dfz_cols, forget[:, c * span : (c + 1) * span])
        )

    def part(which, c):
        return du_ref[pl.ds(pl.multiple_of(which * half, half), half), c * span : (c + 1) * span]

    total = TpSum(part, sum_ref, (t0, t1, t2, t3), tsend, trecv, core, sibling, across)
    total.first()
    attns.advance(1)
    total.second()
    moves.start("dmid", dmid_ref, du_ref)
    gates.advance(1)
    attns.advance(1)
    gates.advance(1)
    total.third()
    attns.advance(1)
    total.fourth()
    moves.wait("dmid", 20)
    size = 64

    def input_rows(i, acc):
        here = pl.ds(pl.multiple_of(i * size, size), size)
        value = x_ref[here, :].astype(F32)
        inverse = lax.rsqrt(jnp.mean(value * value, axis=-1, keepdims=True) + EPS)
        normal = value * inverse
        grad = sum_ref[here, :].astype(F32)
        back = grad * gain_ref[...]
        back = inverse * (back - normal * jnp.mean(back * normal, axis=-1, keepdims=True))
        du_ref[here, :] += back
        return acc + jnp.sum((grad * normal).reshape(size // 8, 8, cols), axis=0)

    gains = lax.fori_loop(0, rows // size, input_rows, jnp.zeros((8, cols), F32))
    moves.start("input", du_ref, input_out)
    for i in range(n):
        small_ref[i, 0:1, :shard] = jnp.sum(gains[:, i * shard : (i + 1) * shard], axis=0, keepdims=True)
    exchange_start(n, me, tp, lambda peer: small_ref.at[peer], small_land, xsend, xrecv)
    moves.start("small", small_ref.at[me], small_land.at[me])
    while gates.next < n - 1:
        gates.advance(1)
        attns.advance(1)
    gates.end()
    attns.end()
    moves.wait("small")
    exchange_wait(n, me, tp, lambda peer: small_ref.at[peer], small_land, xsend, xrecv)
    small_out[...] = ordered_sum(n, small_land)
    pairs.sent()
    moves.wait()


def finish_backward(n, collective_id, heads, gate_plan, attn_plan, *operands):
    dq, u, x = operands[4], operands[17], operands[20]
    rows, width = dq.shape
    cols = x.shape[1]
    shard = u.shape[2]
    dma = pltpu.SemaphoreType.DMA
    vmem = pl.BlockSpec(memory_space=VMEM)
    anywhere = pl.BlockSpec(memory_space=pl.ANY)
    outside = STAGED + (22,)
    gate_widths = [sum(w for w, _ in side) for side in gate_plan]
    attn_widths = [sum(w for w, _ in side) for side in attn_plan]

    def ring_semaphores(plan):
        return [dma((2, max(len(side) for side in plan), n - 1))] * 2

    shapes = [(shard, width)] * 5 + [(16, 256), (rows, cols)]
    return pl.pallas_call(
        functools.partial(finish_kernel, n, heads, gate_plan, attn_plan),
        out_shape=[jax.ShapeDtypeStruct(shape, F32) for shape in shapes],
        in_specs=[anywhere if i in outside else vmem for i in range(len(operands))],
        out_specs=[vmem] * 6 + [anywhere],
        scratch_shapes=[
            *[VMEM(operands[i].shape, operands[i].dtype) for i in STAGED],
            *[VMEM((n - 1, rows, width), BF16)] * 2,
            *ring_scratch(n, shard, gate_widths),
            *ring_scratch(n, shard, attn_widths),
            VMEM((rows, width), F32),
            VMEM((rows, width), F32),
            *[VMEM((rows, width), BF16)] * 3,
            VMEM((rows, cols), F32),
            VMEM((rows, cols), BF16),
            *tp_buffers(rows, cols),
            VMEM((n, 8, rows), F32),
            VMEM((8, LANES), F32),
            VMEM((n, 8, rows), F32),
            VMEM((n, 8, LANES), F32),
            VMEM((n, 16, 256), F32),
            VMEM((n, 16, 256), F32),
            *[dma((2, len(pieces(width, LANES)), n - 1))] * 2,
            *ring_semaphores(gate_plan),
            *ring_semaphores(attn_plan),
            *[dma((n - 1,))] * 6,
            *[dma((3, TP_CHUNKS))] * 2,
            dma((len(STAGED) + 5,)),
        ],
        compiler_params=pltpu.CompilerParams(
            collective_id=collective_id, has_side_effects=True, vmem_limit_bytes=VMEM_LIMIT
        ),
    )(*operands)


LANES = 128


def block_state(group_map, doc_lengths, skip, query_group, key_group, rows, docs):
    first_q = query_group * rows
    last_q = first_q + rows - 1
    first_k = key_group * rows
    last_k = first_k + rows - 1
    zero = jnp.int32(0)
    doc_qf, doc_ql, doc_kf, doc_kl, end = zero, zero, zero, zero, zero
    for d in range(docs):
        end = end + doc_lengths[d]
        doc_qf += (first_q >= end).astype(jnp.int32)
        doc_ql += (last_q >= end).astype(jnp.int32)
        doc_kf += (first_k >= end).astype(jnp.int32)
        doc_kl += (last_k >= end).astype(jnp.int32)
    earlier = key_group < query_group
    same = key_group == query_group
    kept = skip[query_group, key_group] != 1
    active = jnp.logical_or(same, earlier & kept & (doc_kl == doc_qf))
    full = earlier & (doc_kf == doc_ql)
    return active, full


def block_mask(doc_lengths, query_group, key_group, rows, docs, query_dim):
    shape = (rows, rows)
    pos_q = query_group * rows + lax.broadcasted_iota(jnp.int32, shape, query_dim)
    pos_k = key_group * rows + lax.broadcasted_iota(jnp.int32, shape, 1 - query_dim)
    start = jnp.zeros(shape, jnp.int32)
    end = jnp.int32(0)
    for d in range(docs):
        end = end + doc_lengths[d]
        start = jnp.where(pos_q >= end, end, start)
    return (pos_k <= pos_q) & (pos_k >= start)


def document_start(position, doc_lengths):
    start, end = jnp.zeros_like(position), jnp.int32(0)
    for d in range(doc_lengths.shape[0]):
        end = end + doc_lengths[d]
        start = jnp.where(position >= end, end, start)
    return start


def in_pack_order(forward, one, two):
    return jnp.where(forward, one, two), jnp.where(forward, two, one)


def low_lanes(rows):
    return lax.broadcasted_iota(jnp.int32, (rows, LANES), 1) < LANES // 2


def three_pieces(value):
    high = value.astype(BF16).astype(F32)
    rest = value - high
    middle = rest.astype(BF16).astype(F32)
    return high, middle, rest - middle


def turn(value):
    rows = value.shape[1]
    return jnp.concatenate([value, jnp.zeros((LANES - 8, rows), F32)], axis=0).T


def row_pieces(term, with_ones):
    lane = lax.broadcasted_iota(jnp.int32, term.shape, 1)
    term = jnp.where(lane < 8, term, 0.0)
    high, middle, low = three_pieces(term)
    result = pltpu.roll(high, 24, 1) + pltpu.roll(middle, 32, 1) + pltpu.roll(low, 40, 1)
    if with_ones:
        result = jnp.where(lane < 24, 1.0, result)
    return result


def key_pieces(offsets):
    rows = offsets.shape[1]
    high, middle, low = three_pieces(offsets)
    stack = jnp.concatenate(
        [-high, -middle, -low, jnp.ones((24, rows), F32), jnp.zeros((LANES - 48, rows), F32)], axis=0
    )
    return stack.T.astype(BF16)


def spread_heads(wide_ref, common, put, heads, forward=None):
    rows = wide_ref.shape[0]
    low = low_lanes(rows)
    lane = lax.broadcasted_iota(jnp.int32, (rows, LANES), 1)

    def ordered(value):
        if forward is None:
            return value
        return jnp.concatenate(in_pack_order(forward, value[: rows // 2], value[rows // 2 :]), axis=0)

    common = ordered(common)
    for h in range(heads):
        pair = h // 2
        block = ordered(wide_ref[:, pair * LANES : (pair + 1) * LANES])
        keep = low if h % 2 == 0 else jnp.logical_not(low)
        put(
            h,
            jnp.where(keep, block, jnp.zeros_like(block)),
            jnp.where(lax.rem(lane, 8) == h, common, 0.0).astype(BF16),
        )


def put_rows(cat_ref):
    def put(h, value, extra):
        cat_ref[h, :, :LANES] = value
        cat_ref[h, :, LANES:] = extra

    return put


def smem():
    return pl.BlockSpec(memory_space=pltpu.SMEM)


def whole(shape):
    return pl.BlockSpec(shape, lambda i: (0,) * len(shape))


def head_sums(value, heads):
    width = value.shape[1]
    feature = lax.broadcasted_iota(jnp.int32, (width, LANES), 0)
    lane = lax.broadcasted_iota(jnp.int32, (width, LANES), 1)
    member = (lax.div(feature, width // heads) == lane).astype(BF16)
    high = value.astype(BF16)
    return dot(high, member) + dot((value - high.astype(F32)).astype(BF16), member)


def backward_kernel(
    heads, rows, docs, me, group_map, doc_lengths, skip, q_ref, d_ref, out_ref, term_ref, k_ref, v_ref, kaug_ref,
    dq_ref, drow_ref, dk_ref, dv_ref, dcol_ref, acc_ref, qcat_ref, dcat_ref, dk_acc, dv_acc, dcol_acc,
):
    step = pl.program_id(0)

    @pl.when(step == 0)
    def _():
        acc_ref[...] = jnp.zeros_like(acc_ref)
        spread_heads(q_ref, row_pieces(term_ref[...], True), put_rows(qcat_ref), heads)
        delta = head_sums(d_ref[...].astype(F32) * out_ref[...], heads)
        spread_heads(d_ref, row_pieces(-delta, False), put_rows(dcat_ref), heads)

    dk_acc[...] = jnp.zeros_like(dk_acc)
    dv_acc[...] = jnp.zeros_like(dv_acc)
    dcol_acc[...] = jnp.zeros_like(dcol_acc)

    def tile(qi, ki, mask):
        q_rows = pl.ds(qi * rows, rows)
        k_rows = pl.ds(ki * rows, rows)
        aug = kaug_ref[k_rows, :]
        for pair in range(heads // 2):
            lanes = pl.ds(pair * LANES, LANES)
            keys = jnp.concatenate([k_ref[pair, k_rows, :], aug], axis=1)
            values = jnp.concatenate([v_ref[pair, k_rows, :], aug], axis=1)
            for h in (2 * pair, 2 * pair + 1):
                probs = jnp.exp(contract_cols(keys, qcat_ref[h, q_rows, :]))
                if mask is not None:
                    probs = jnp.where(mask, probs, 0.0)
                grads = (probs * contract_cols(values, dcat_ref[h, q_rows, :])).astype(BF16)
                dv_acc[k_rows, lanes] += dot(probs.astype(BF16), dcat_ref[h, q_rows, :LANES])
                both = dot(grads, qcat_ref[h, q_rows, :])
                dk_acc[k_rows, lanes] += both[:, :LANES]
                dcol_acc[k_rows, :] += both[:, LANES:]
                acc_ref[h, q_rows, :] += contract_rows(grads, keys)

    for ki in range(2):
        key_group = group_map[2 * step + ki]
        for qi in range(2):
            query_group = group_map[2 * me[0] + qi]
            active, full = block_state(group_map, doc_lengths, skip, query_group, key_group, rows, docs)

            @pl.when(active & full)
            def _(qi=qi, ki=ki):
                tile(qi, ki, None)

            @pl.when(active & jnp.logical_not(full))
            def _(qi=qi, ki=ki, query_group=query_group, key_group=key_group):
                tile(qi, ki, block_mask(doc_lengths, query_group, key_group, rows, docs, 1))

    dk_ref[0] = dk_acc[...].astype(BF16)
    dv_ref[0] = dv_acc[...].astype(BF16)
    dcol_ref[0] = -(dcol_acc[...].T[:8])

    @pl.when(step == pl.num_programs(0) - 1)
    def _():
        total_rows = dq_ref.shape[0]
        low = low_lanes(total_rows)
        lane = lax.broadcasted_iota(jnp.int32, (total_rows, LANES), 1)
        sums = jnp.zeros((total_rows, LANES), F32)
        for pair in range(heads // 2):
            a, b = 2 * pair, 2 * pair + 1
            dq_ref[:, pair * LANES : (pair + 1) * LANES] = jnp.where(
                low, acc_ref[a, :, :LANES], acc_ref[b, :, :LANES]
            )
            sums = jnp.where(
                lane == 24 + a, acc_ref[a, :, LANES:], jnp.where(lane == 24 + b, acc_ref[b, :, LANES:], sums)
            )
        drow_ref[...] = pltpu.roll(sums, LANES - 24, 1).T[:8]


def backward_attention(me, group_map, doc_lengths, skip, queries, grads, attended, term, keys, values, key_aug, heads):
    total = keys.shape[1]
    own, width = queries.shape
    rows = own // 2
    n = total // own
    docs = doc_lengths.shape[0]
    return pl.pallas_call(
        functools.partial(backward_kernel, heads, rows, docs),
        grid=(n,),
        out_shape=[
            jax.ShapeDtypeStruct((own, width), F32),
            jax.ShapeDtypeStruct((8, own), F32),
            jax.ShapeDtypeStruct((n, own, width), BF16),
            jax.ShapeDtypeStruct((n, own, width), BF16),
            jax.ShapeDtypeStruct((n, 8, own), F32),
        ],
        in_specs=[smem(), smem(), smem(), smem()]
        + [
            whole((own, width)),
            whole((own, width)),
            whole((own, width)),
            whole((own, LANES)),
            pl.BlockSpec((heads // 2, own, LANES), lambda i: (0, i, 0)),
            pl.BlockSpec((heads // 2, own, LANES), lambda i: (0, i, 0)),
            pl.BlockSpec((own, LANES), lambda i: (i, 0)),
        ],
        out_specs=[
            whole((own, width)),
            whole((8, own)),
            pl.BlockSpec((1, own, width), lambda i: (i, 0, 0)),
            pl.BlockSpec((1, own, width), lambda i: (i, 0, 0)),
            pl.BlockSpec((1, 8, own), lambda i: (i, 0, 0)),
        ],
        scratch_shapes=[
            VMEM((heads, own, 2 * LANES), F32),
            VMEM((heads, own, 2 * LANES), BF16),
            VMEM((heads, own, 2 * LANES), BF16),
            VMEM((own, width), F32),
            VMEM((own, width), F32),
            VMEM((own, LANES), F32),
        ],
        compiler_params=pltpu.CompilerParams(vmem_limit_bytes=VMEM_LIMIT),
        cost_estimate=pl.CostEstimate(
            flops=own * total * width * 10, bytes_accessed=total * width * 8, transcendentals=own * total * heads
        ),
    )(me, group_map, doc_lengths, skip, queries, grads, attended, term, keys, values, key_aug)


def on_device(
    hidden_in,
    norm_one,
    w_query,
    w_key,
    w_value,
    w_gate_out,
    w_forget,
    forget_bias,
    head_gains,
    w_output,
    norm_two,
    w_gate,
    w_up,
    w_down,
    out_grad,
    doc_lengths,
    group_map,
    skip_list,
):
    device_ctx = lax.axis_index("ctx")
    device_tp = lax.axis_index("tp")
    n = lax.axis_size("ctx")
    row_count, model_width = hidden_in.shape
    group_rows = row_count // 2
    heads = forget_bias.shape[0]
    shard = norm_one.shape[0]
    gain_rows = head_gains.shape[0]
    head_dim = gain_rows * n // 2
    width = heads * head_dim
    hidden_width = w_gate.shape[1]

    slots = 2 * n
    earlier = jnp.pad(
        (group_map[:, None] < group_map[None, :]).astype(F32), ((0, LANES - slots), (0, LANES - slots))
    )

    def lanes_of(value, first_rows, last_rows):
        return jnp.pad(value, ((first_rows, last_rows), (0, 256 - value.shape[1])))

    small = jnp.concatenate(
        [
            lanes_of(jnp.stack([norm_one, norm_two]), 0, 0),
            lanes_of(head_gains.T, 0, 6 - heads),
            lanes_of(w_forget.T, 0, 8 - heads),
        ],
        axis=0,
    )
    (
        query_weight,
        key_weight,
        value_weight,
        gate_out_weight,
        output_weight,
        normed_shards,
        query_rows,
        query_raw,
        key_raw,
        gate_logit,
        forget_logit,
        keys_all,
        values_all,
        key_aug,
        attended_flat,
        row_term,
        gain_one,
        gain_two,
        query_gain,
        key_gain,
        forget_weight,
    ) = start_forward(
        n, 1, group_map, doc_lengths, skip_list, earlier, hidden_in, small, forget_bias, [w_query, w_key, w_value, w_gate_out], w_output
    )
    half = width // 256 * 128
    me_one = device_ctx.astype(jnp.int32).reshape(1)
    fused = n <= 8
    (
        gated,
        layer_out,
        down_share,
        gate_share,
        up_share,
        grad_middle,
        grad_attended,
        grad_gate_logit,
        gain_two_parts,
        *attention_grads,
    ) = feed_forward(
        n,
        3,
        heads,
        attended_flat,
        gate_logit,
        output_weight,
        hidden_in,
        gain_two,
        out_grad,
        w_gate,
        w_up,
        w_down,
        (group_map, doc_lengths, skip_list, query_rows, row_term, keys_all, values_all, key_aug) if fused else None,
    )
    if not fused:
        grad_branch = grad_middle.astype(BF16).reshape(row_count, n, shard).transpose(1, 0, 2)
        attention_grads = grad_branch, *backward_attention(
            me_one,
            group_map,
            doc_lengths,
            skip_list,
            query_rows,
            grad_attended,
            attended_flat,
            row_term,
            keys_all,
            values_all,
            key_aug,
            heads,
        )
    grad_branch, grad_query, row_sums, key_part, value_part, column_sums = attention_grads

    gate_plan = [
        [(width, (1, 1 + i, 0, width)), (w, (0, 0, c, w))] for i, (c, w) in enumerate([(0, half), (half, width - half)])
    ]
    attn_plan = [[(half, (i, 0, half)), (width - half, (i, half, width - half))] for i in (0, 1)]
    own_groups = lax.dynamic_slice_in_dim(group_map, device_ctx * 2, 2, 0)
    later = (group_map[None, :] > own_groups[:, None]).astype(F32)
    if fused:
        (
            query_share,
            key_share,
            value_share,
            gate_out_share,
            output_share,
            small_share,
            input_grad,
        ) = finish_backward(
            n,
            7,
            heads,
            gate_plan,
            attn_plan,
            key_part,
            value_part,
            column_sums,
            row_sums,
            grad_query,
            query_raw,
            key_raw,
            query_gain,
            key_gain,
            forget_logit,
            jnp.pad(later, ((0, 6), (0, LANES - slots))),
            query_weight,
            key_weight,
            value_weight,
            gate_out_weight,
            forget_weight,
            grad_gate_logit,
            normed_shards,
            grad_branch,
            gated,
            hidden_in,
            gain_one,
            grad_middle,
            gain_two_parts,
        )
    else:
        query_gain, key_gain = (gain.reshape(heads, head_dim) for gain in (query_gain, key_gain))
        query_raw, key_raw = (raw.reshape(row_count, heads, head_dim) for raw in (query_raw, key_raw))
        query_norm, key_norm = rms_scale(query_raw), rms_scale(key_raw)
        forget_logit = forget_logit[:heads].T
        forget_weight = forget_weight[:heads].astype(BF16)
        normed_one = normed_shards.transpose(1, 0, 2).reshape(row_count, model_width)
        place = jnp.arange(group_rows, dtype=jnp.int32)
        upper = (place[:, None] <= place[None, :]).astype(F32)
        grad_key, grad_value, off_sum, tot_sum = pair_scatter(n, 7, key_part, value_part, column_sums, row_sums)
        after = contract_cols_exact(tot_sum[:heads, :slots], later)
        suffix = lax.dot_general(
            off_sum[:heads].reshape(heads, 2, group_rows), upper, (((2,), (1,)), ((), ())), precision=HIGHEST
        )
        grad_log_forget = (suffix + after[:, :, None]).reshape(heads, row_count).T
        grad_key3 = grad_key.reshape(row_count, heads, head_dim)
        grad_query3 = grad_query.reshape(row_count, heads, head_dim)
        key_raw_grad = rms_back(grad_key3 * key_gain, key_raw).astype(BF16).reshape(row_count, width)
        query_raw_grad = (
            rms_back(grad_query3 * query_gain * 0.125, query_raw).astype(BF16).reshape(row_count, width)
        )
        value_low = grad_value.astype(BF16)
        query_gain_grad = jnp.sum(grad_query3 * query_norm * 0.125, axis=0)
        key_gain_grad = jnp.sum(grad_key3 * key_norm, axis=0)
        head_gain_grad = jnp.concatenate([query_gain_grad, key_gain_grad], axis=1)
        grad_forget_logit = (grad_log_forget * jax.nn.sigmoid(-forget_logit)).astype(BF16)
        bias_part = jnp.sum(grad_forget_logit.astype(F32), axis=0)
        normed_one_part = (
            contract_cols(query_raw_grad, query_weight)
            + contract_cols(key_raw_grad, key_weight)
            + contract_cols(value_low, value_weight)
            + contract_cols(grad_gate_logit, gate_out_weight)
            + dot(grad_forget_logit, forget_weight)
        )
        forget_grad = contract_rows(grad_forget_logit, normed_one)

        def wide(value):
            return jnp.pad(value, ((0, 0), (0, 0), (0, 256 - value.shape[2])))

        forget_rows = wide(forget_grad.reshape(heads, n, shard).transpose(1, 0, 2))
        forget_rows = forget_rows.at[:, :, 224].set(bias_part[None, :])
        small_grad = jnp.concatenate(
            [
                jnp.zeros((n, 1, 256), F32),
                wide(jnp.sum(gain_two_parts, axis=0).reshape(n, 1, shard)),
                wide(head_gain_grad.reshape(heads, n, gain_rows).transpose(1, 0, 2)),
                jnp.pad(forget_rows, ((0, 0), (0, 8 - heads), (0, 0))),
            ],
            axis=1,
        )
        lefts, rights = (1, 0), (4, 0, 3)
        plan = [
            [(w, (0, 1 + i, c0, cw)) for w, (i, c0, cw) in attn]
            + [(w, (lefts[left], rights[right], c0, cw)) for w, (left, right, c0, cw) in gate]
            for attn, gate in zip(attn_plan, gate_plan)
        ]
        (
            query_share,
            key_share,
            value_share,
            gate_out_share,
            output_share,
            small_share,
            input_grad,
        ) = weight_scatter(
            n,
            8,
            plan,
            [normed_shards, grad_branch],
            [query_raw_grad, key_raw_grad, value_low, grad_gate_logit, gated],
            small_grad,
            normed_one_part,
            hidden_in,
            gain_one,
            grad_middle,
        )
    return (
        layer_out,
        input_grad,
        small_share[0, :shard],
        query_share,
        key_share,
        value_share,
        gate_out_share,
        small_share[8 : 8 + heads, :shard].T,
        small_share[8 : 8 + heads, 224],
        small_share[2 : 2 + heads, :gain_rows].T,
        output_share,
        small_share[1, :shard],
        gate_share,
        up_share,
        down_share,
    )


def solution(mesh):
    split = P("ctx", "tp")
    in_specs = (
        P("ctx", None),
        P("ctx"),
        split,
        split,
        split,
        split,
        split,
        P("tp"),
        split,
        split,
        P("ctx"),
        split,
        split,
        split,
        P("ctx", None),
        P(),
        P(),
        P(),
    )
    out_specs = (
        split,
        P("ctx", None),
        P("ctx"),
        split,
        split,
        split,
        split,
        split,
        P("tp"),
        split,
        split,
        P("ctx"),
        split,
        split,
        split,
    )
    return jax.shard_map(on_device, mesh=mesh, in_specs=in_specs, out_specs=out_specs, check_vma=False)
```

```python
import functools

import jax
import jax.numpy as jnp
from jax import lax
from jax.experimental import pallas as pl
from jax.experimental.pallas import tpu as pltpu
from jax.sharding import PartitionSpec as P

EPS = 1e-06
HIGHEST = lax.Precision.HIGHEST
MESH = pl.DeviceIdType.MESH
VMEM = pltpu.VMEM
VMEM_LIMIT = 62 * 1024 * 1024
F32 = jnp.float32
BF16 = jnp.bfloat16


def rms_scale(value):
    return value * lax.rsqrt(jnp.mean(value * value, axis=-1, keepdims=True) + EPS)


def rms_back(grad_in, value):
    inverse = lax.rsqrt(jnp.mean(value * value, axis=-1, keepdims=True) + EPS)
    normal = value * inverse
    return inverse * (grad_in - normal * jnp.mean(grad_in * normal, axis=-1, keepdims=True))


def dot(left, right):
    return jnp.dot(left, right, preferred_element_type=F32)


def contract_cols(left, right):
    return lax.dot_general(left, right, (((1,), (1,)), ((), ())), preferred_element_type=F32)


def contract_cols_exact(left, right):
    return lax.dot_general(left, right, (((1,), (1,)), ((), ())), precision=HIGHEST)


def contract_rows(left, right):
    return lax.dot_general(left, right, (((0,), (0,)), ((), ())), preferred_element_type=F32)


def ring_place(ctx, n):
    odd = lax.rem(ctx, 2)
    half = lax.div(ctx, 2)
    return (1 - odd) * half + odd * (n - 1 - half)


def ring_owner(place, n):
    late = lax.div(place, n // 2)
    return (1 - late) * (2 * place) + late * (2 * (n - 1 - place) + 1)


def wrap(place, n):
    return lax.rem(place + 2 * n, n)


def ring_setup(n):
    me = lax.axis_index("ctx")
    tp = lax.axis_index("tp")
    place = ring_place(me, n)
    right = ring_owner(wrap(place + 1, n), n)
    left = ring_owner(wrap(place - 1, n), n)
    return me, tp, place, (right, left)


def greet(peers):
    barrier = pltpu.get_barrier_semaphore()
    for peer in peers:
        pl.semaphore_signal(barrier, inc=1, device_id=peer, device_id_type=MESH)
    pl.semaphore_wait(barrier, len(peers))


def ctx_peers(me, tp, n):
    return [(lax.rem(me + i, n), tp) for i in range(1, n)]


def remote(src, dst, send, recv, device):
    return pltpu.make_async_remote_copy(
        src_ref=src, dst_ref=dst, send_sem=send, recv_sem=recv, device_id=device, device_id_type=MESH
    )


class Gather:
    def __init__(self, n, place, sides, tp, chunks, send, recv):
        self.n, self.place, self.sides, self.tp = n, place, sides, tp
        self.chunks, self.send, self.recv = chunks, send, recv
        self.arrived = None

    def owner(self, side, back):
        return ring_owner(wrap(self.place - back if side == 0 else self.place + back, self.n), self.n)

    def copy(self, index, step, first):
        side, source, target = self.chunks[index]
        target = target(self.owner(side, step))
        return remote(
            source if first else target, target, self.send.at[index, step], self.recv.at[index, step],
            (self.sides[side], self.tp),
        )

    def arrive(self, index, step):
        side, _, target = self.chunks[index]
        target = target(self.owner(side, step + 1))
        remote(
            target, target, self.send.at[index, step], self.recv.at[index, step], (self.sides[side], self.tp)
        ).wait_recv()
        if self.arrived is not None:
            self.arrived(index, step)

    def begin(self, indices=None):
        for index in indices if indices is not None else range(len(self.chunks)):
            self.copy(index, 0, True).start()

    def forward(self, step):
        for index in range(len(self.chunks)):
            self.arrive(index, step - 1)
            self.copy(index, step, False).start()

    def last(self):
        for index in range(len(self.chunks)):
            self.arrive(index, self.n - 2)

    def sent(self):
        def finish(step, carry):
            for index in range(len(self.chunks)):
                self.copy(index, step, False).wait_send()
            return carry

        lax.fori_loop(0, self.n - 1, finish, 0)


class Moves:
    def __init__(self, semaphores):
        self.semaphores, self.count, self.open = semaphores, 0, {}

    def start(self, name, source, target):
        copy = pltpu.make_async_copy(source, target, self.semaphores.at[self.count])
        self.count += 1
        copy.start()
        self.open[name] = copy

    def wait(self, *names):
        for name in names or list(self.open):
            self.open.pop(name).wait()


def start_kernel(
    n, heads, group_map, doc_lengths, skip, earlier_ref, x_ref, small_in, bias_ref, wq_in, wk_in, wv_in, wg_in, wo_in,
    wq_out, wk_out, wv_out, wg_out, wo_ref, u_out, q_out, qr_out, kr_out, gl_out, fz_ref, k_out, v_out, aug_out,
    att_out, term_ref, gain_one, gain_two, qgain_ref, kgain_ref, wf_ref,
    x_vmem, wq_ref, wk_ref, wv_ref, wg_ref, u_ref, q_ref, k_all, v_all, aug_ref, att_ref, acc_ref, cat_ref,
    diff_ref, span_ref, tot_ref, before_ref, inside_all,
    small_all, acc_r, acc_l, inside_src,
    wsend, wrecv, osend, orecv, ksend, krecv, ssend, srecv, isend, irecv, spill, local,
):
    me, tp, place, sides = ring_setup(n)
    moves = Moves(local)
    moves.start("x", x_ref, x_vmem)
    greet(ctx_peers(me, tp, n))
    rows, cols = x_ref.shape
    shard, width = wq_in.shape
    half = rows // 2
    head_dim = width // heads

    def shard_rows(owner):
        return pl.ds(pl.multiple_of(owner * shard, 16), shard)

    def window(ref, c0, cw):
        return lambda owner: ref.at[shard_rows(owner), pl.ds(c0, cw)]

    def token_rows(owner):
        return pl.ds(pl.multiple_of(owner * rows, rows), rows)

    def block(ref, pair):
        return lambda owner: ref.at[pair, token_rows(owner), :]

    ring = (n, place, sides, tp)
    projections = Gather(
        *ring,
        [
            (side, source, window(target, 0, width))
            for side, source, target in ((0, wq_in, wq_ref), (1, wv_in, wv_ref), (0, wk_in, wk_ref), (1, wg_in, wg_ref))
        ],
        wsend, wrecv,
    )
    middle = width // 256 * 128
    outputs = Gather(
        *ring,
        [
            (side, wo_in.at[:, pl.ds(c0, cw)], window(wo_ref, c0, cw))
            for side, c0, cw in ((0, 0, middle), (1, middle, width - middle))
        ],
        osend, orecv,
    )
    members = [(0, k_all, k_out, 0), (1, k_all, k_out, 2), (0, v_all, v_out, 0), (1, v_all, v_out, 2)]
    members += [(0, k_all, k_out, 1), (1, v_all, v_out, 1)]
    pairs = Gather(
        *ring, [(side, block(ref, pair)(me), block(ref, pair)) for side, ref, _, pair in members], ksend, krecv
    )

    def spill_copy(index, step):
        side, ref, out, pair = members[index]
        owner = pairs.owner(side, step + 1)
        return pltpu.make_async_copy(
            block(ref, pair)(owner), block(out, pair)(owner), spill.at[index, step]
        )

    pairs.arrived = lambda index, step: spill_copy(index, step).start()

    projections.begin()
    exchange_start(n, me, tp, lambda peer: small_in, small_all, ssend, srecv)
    gathered = ((wq_in, wq_ref), (wk_in, wk_ref), (wv_in, wv_ref), (wg_in, wg_ref), (wo_in, wo_ref))
    for i, (source, target) in enumerate(gathered):
        moves.start(i, source, target.at[shard_rows(me)])
    moves.start("small", small_in, small_all.at[me])
    moves.wait("small")
    exchange_wait(n, me, tp, lambda peer: small_in, small_all, ssend, srecv)
    projections.forward(1)

    count = 2 * head_dim // n
    for i in range(n):
        block_small = small_all[i].astype(F32)
        gain_one[:, i * shard : (i + 1) * shard] = block_small[0:1, :shard]
        gain_two[:, i * shard : (i + 1) * shard] = block_small[1:2, :shard]
        wf_ref[:, i * shard : (i + 1) * shard] = block_small[8:16, :shard]
        target, at = (qgain_ref, i) if i < n // 2 else (kgain_ref, i - n // 2)
        for h in range(heads):
            lane = h * head_dim + at * count
            target[:, lane : lane + count] = block_small[2 + h : 3 + h, :count]

    size = 64

    def norm_rows(i, carry):
        here = pl.ds(pl.multiple_of(i * size, size), size)
        normed = (rms_scale(x_vmem[here, :].astype(F32)) * gain_one[...]).astype(BF16)
        for j in range(n):
            u_ref[j, here, :] = normed[:, j * shard : (j + 1) * shard]
        return carry

    moves.wait("x")
    lax.fori_loop(0, rows // size, norm_rows, 0)
    moves.start("u", u_ref, u_out)

    def grow(back):
        for side, acc, sources in ((0, acc_r, (wq_ref, wk_ref)), (1, acc_l, (wv_ref, wg_ref))):
            owner = projections.owner(side, back)
            for i, source in enumerate(sources):
                acc[:, i * width : (i + 1) * width] += dot(u_ref[owner], source[shard_rows(owner), :])

    acc_r[...] = jnp.zeros_like(acc_r)
    acc_l[...] = jnp.zeros_like(acc_l)
    moves.wait(0, 1, 2, 3, 4)
    grow(0)
    projections.forward(2)
    grow(1)
    grow(2)
    forget = jnp.zeros((16, rows), F32)
    for j in range(n):
        forget += contract_cols(small_all[j, :, :shard], u_ref[j])
    fz = forget[8:16] + bias_ref[:, 0:1]
    fz_ref[...] = fz
    logs = jnp.minimum(fz, 0.0) - jnp.log1p(jnp.exp(-jnp.abs(fz)))
    head = lax.broadcasted_iota(jnp.int32, logs.shape, 0)
    logs = jnp.where(head < heads, logs, 0.0)
    upto = (
        lax.broadcasted_iota(jnp.int32, (half, half), 0) <= lax.broadcasted_iota(jnp.int32, (half, half), 1)
    ).astype(F32)
    for g in range(2):
        inside_src[:, g * half : (g + 1) * half] = jnp.dot(
            logs[:, g * half : (g + 1) * half], upto, precision=HIGHEST, preferred_element_type=F32
        )
    exchange_start(n, me, tp, lambda peer: inside_src, inside_all, isend, irecv)
    moves.start("inside", inside_src, inside_all.at[me])

    def step_on(step, carry):
        projections.forward(step)
        grow(step)
        return carry

    lax.fori_loop(3, n - 2, step_on, 0)
    outputs.begin()
    projections.forward(n - 2)
    grow(n - 2)
    outputs.forward(1)
    projections.last()
    grow(n - 1)

    def head_norm(value):
        return value * lax.rsqrt(head_means(value * value, heads) + EPS)

    my_rows = token_rows(me)
    for pair in range(heads // 2):
        v_all[pair, my_rows, :] = acc_l[:, pair * LANES : (pair + 1) * LANES].astype(BF16)
    pairs.begin([2, 3, 5])
    keys = (head_norm(acc_r[:, width:]) * kgain_ref[...]).astype(BF16)
    for pair in range(heads // 2):
        k_all[pair, my_rows, :] = keys[:, pair * LANES : (pair + 1) * LANES]
    pairs.begin([0, 1, 4])
    for i, (source, target) in enumerate(
        ((wq_ref, wq_out), (wk_ref, wk_out), (wv_ref, wv_out), (wg_ref, wg_out))
    ):
        moves.start(i, source, target)
    moves.start("qr", acc_r.at[:, pl.ds(0, width)], qr_out)
    moves.start("kr", acc_r.at[:, pl.ds(width, width)], kr_out)
    moves.start("gl", acc_l.at[:, pl.ds(width, width)], gl_out)
    for i, (ref, out) in enumerate(((k_all, k_out), (v_all, v_out))):
        for pair in range(heads // 2):
            moves.start((i, pair), block(ref, pair)(me), block(out, pair)(me))
    q_ref[...] = (head_norm(acc_r[:, :width]) * qgain_ref[...] * 0.125).astype(BF16)
    moves.start("q", q_ref, q_out)

    moves.wait("inside")
    exchange_wait(n, me, tp, lambda peer: inside_src, inside_all, isend, irecv)
    tot_ref[...] = jnp.zeros_like(tot_ref)
    for i in range(n):
        for g in range(2):
            tot_ref[:, 2 * i + g : 2 * i + g + 1] = inside_all[i, :, (g + 1) * half - 1 : (g + 1) * half]
    before_ref[...] = jnp.dot(tot_ref[...], earlier_ref[...], precision=HIGHEST, preferred_element_type=F32)
    lane8 = lax.broadcasted_iota(jnp.int32, (8, LANES), 1)

    def offsets_of(shard_index):
        parts = []
        for g in range(2):
            before = jnp.sum(jnp.where(lane8 == 2 * shard_index + g, before_ref[...], 0.0), axis=1, keepdims=True)
            parts.append(inside_all[shard_index, :, g * half : (g + 1) * half] + before)
        return jnp.concatenate(parts, axis=1)

    def aug_rows(i, carry):
        aug_ref[token_rows(i), :] = key_pieces(offsets_of(i))
        return carry

    pairs.forward(1)
    lax.fori_loop(0, n, aug_rows, 0)
    moves.start("aug", aug_ref, aug_out)

    first, second = group_map[2 * me], group_map[2 * me + 1]
    in_order = first < second
    query_groups = (jnp.minimum(first, second), jnp.maximum(first, second))
    mine = turn(offsets_of(me))
    term_ref[...] = mine
    spread_heads(q_ref, row_pieces(mine, True), put_rows(cat_ref), heads, in_order)
    acc_ref[...] = jnp.zeros_like(acc_ref)
    query_at = lax.broadcasted_iota(jnp.int32, (half, half), 0)
    key_at = lax.broadcasted_iota(jnp.int32, (half, half), 1)
    diff_ref[...] = key_at - query_at
    for i, group in enumerate(query_groups):
        span_ref[i] = document_start(group * half + query_at, doc_lengths) - key_at
    ones = jnp.ones((half, LANES), BF16)

    def attend(i, back):
        late = lax.div(i, 2)
        pair = (1 - late) * 2 * i + late
        side = lax.rem(i, 2)
        owner = ring_owner(wrap(place + (2 * side - 1) * back, n), n)
        one, two = group_map[2 * owner], group_map[2 * owner + 1]
        forward = one < two
        key_groups = (jnp.minimum(one, two), jnp.maximum(one, two))
        top = pl.ds(pl.multiple_of(owner * rows, rows), half)
        bottom = pl.ds(pl.multiple_of(owner * rows + half, half), half)
        blocks = []
        for ref in (k_all.at[pair], v_all.at[pair], aug_ref):
            blocks.append(in_pack_order(forward, ref[top, :], ref[bottom, :]))
        masks = block_masks(diff_ref, span_ref, skip, query_groups, key_groups, half)
        keys = [jnp.concatenate([blocks[0][ki], blocks[2][ki]], axis=1) for ki in range(2)]
        values = [jnp.concatenate([blocks[1][ki], ones], axis=1) for ki in range(2)]
        both_values = jnp.concatenate(values, axis=0)
        for e in range(2):
            h = 2 * pair + e
            queries = cat_ref[h]
            early = contract_cols(queries, keys[0])
            weights = [
                jnp.where(mask, jnp.exp(score), 0.0).astype(BF16)
                for mask, score in zip(masks, (early[:half], early[half:], contract_cols(queries[half:], keys[1])))
            ]
            acc_ref[h, :half, :] += dot(weights[0], values[0])
            acc_ref[h, half:, :] += dot(jnp.concatenate(weights[1:], axis=1), both_values)

    def attend_all(count, back):
        def body(i, carry):
            attend(i, back)
            return carry

        lax.fori_loop(0, count, body, 0)

    attend_all(3, 0)
    attend_all(2, 1)

    def pair_step(step, count):
        outputs.forward(step)
        pairs.forward(step)
        attend_all(count, step)

    def early_step(step, carry):
        pair_step(step, 2)
        return carry

    def late_step(step, carry):
        pair_step(step, 4)
        return carry

    lax.fori_loop(2, n // 2, early_step, 0)
    pair_step(n // 2, 3)
    lax.fori_loop(n // 2 + 1, n - 1, late_step, 0)
    outputs.last()
    pairs.last()
    attend_all(4, n - 1)

    lane = lax.broadcasted_iota(jnp.int32, (rows, LANES), 1)
    low = low_lanes(rows)
    totals = jnp.ones((rows, LANES), F32)
    for pair in range(heads // 2):
        parts = []
        for h in (2 * pair, 2 * pair + 1):
            value = jnp.concatenate(in_pack_order(in_order, acc_ref[h, :half, :], acc_ref[h, half:, :]), axis=0)
            parts.append(value)
            totals = jnp.where(lane == h, value[:, LANES:], totals)
        att_ref[:, pair * LANES : (pair + 1) * LANES] = jnp.where(
            low, parts[0][:, :LANES], parts[1][:, :LANES]
        ) / jnp.where(low, parts[0][:, LANES:], parts[1][:, LANES:])
    moves.start("att", att_ref, att_out)
    term_ref[...] -= jnp.log(totals)

    def spilled(step, carry):
        for index in range(len(members)):
            spill_copy(index, step).wait()
        return carry

    lax.fori_loop(0, n - 1, spilled, 0)
    moves.wait()
    projections.sent()
    outputs.sent()
    pairs.sent()


def start_forward(n, collective_id, group_map, doc_lengths, skip, earlier, x, small, bias, weights, out_weight):
    rows, cols = x.shape
    shard, width = out_weight.shape
    heads = bias.shape[0]
    half = rows // 2
    dma = pltpu.SemaphoreType.DMA
    vmem = pl.BlockSpec(memory_space=VMEM)
    anywhere = pl.BlockSpec(memory_space=pl.ANY)
    bias = jnp.broadcast_to(jnp.pad(bias, (0, 8 - heads))[:, None], (8, LANES))
    by_pair = (heads // 2, n * rows, LANES)
    weight, wide, narrow = (n * shard, width), (rows, cols), (rows, width)
    shapes = (
        [(weight, BF16)] * 5
        + [((n, rows, shard), BF16), (narrow, BF16)]
        + [(narrow, F32)] * 3
        + [((8, rows), F32)]
        + [(by_pair, BF16)] * 2
        + [((n * rows, LANES), BF16), (narrow, F32), ((rows, LANES), F32)]
        + [((1, cols), F32)] * 2
        + [((1, width), F32)] * 2
        + [((8, cols), F32)]
    )
    return pl.pallas_call(
        functools.partial(start_kernel, n, heads),
        out_shape=[jax.ShapeDtypeStruct(*shape) for shape in shapes],
        in_specs=[smem(), smem(), smem(), vmem, anywhere, vmem, vmem] + [anywhere] * 5,
        out_specs=[anywhere if i < 10 or 11 <= i <= 14 else vmem for i in range(len(shapes))],
        scratch_shapes=[
            VMEM(wide, BF16),
            *[VMEM(weight, BF16)] * 4,
            VMEM((n, rows, shard), BF16),
            VMEM(narrow, BF16),
            *[VMEM(by_pair, BF16)] * 2,
            VMEM((n * rows, LANES), BF16),
            VMEM(narrow, F32),
            VMEM((heads, rows, 2 * LANES), F32),
            VMEM((heads, rows, 2 * LANES), BF16),
            VMEM((half, half), jnp.int32),
            VMEM((2, half, half), jnp.int32),
            VMEM((8, LANES), F32),
            VMEM((8, LANES), F32),
            VMEM((n, 8, rows), F32),
            VMEM((n, 16, 256), BF16),
            VMEM((rows, 2 * width), F32),
            VMEM((rows, 2 * width), F32),
            VMEM((8, rows), F32),
            *[dma((4, n - 1))] * 2,
            *[dma((2, n - 1))] * 2,
            *[dma((6, n - 1))] * 2,
            *[dma((n - 1,))] * 4,
            dma((6, n - 1)),
            dma((26,)),
        ],
        compiler_params=pltpu.CompilerParams(
            collective_id=collective_id, has_side_effects=True, vmem_limit_bytes=VMEM_LIMIT
        ),
    )(group_map, doc_lengths, skip, earlier, x, small, bias, *weights, out_weight)


class ScatterRing:
    def __init__(self, n, plan, local_term, slots, firsts, write, send, recv, place, sides, tp, source=None):
        self.n, self.place, self.sides, self.tp = n, place, sides, tp
        self.source, self.next = source, 1
        self.local_term, self.write = local_term, write
        self.slots, self.firsts, self.send, self.recv = slots, firsts, send, recv
        self.order = []
        starts = [0, 0]
        for index in range(max(len(plan[0]), len(plan[1]))):
            for side in (0, 1):
                if index < len(plan[side]):
                    width, tag = plan[side][index]
                    self.order.append((side, index, starts[side], width, tag))
                    starts[side] += width

    def target(self, side, step):
        step = -1 - step if side == 0 else 1 + step
        return ring_owner(wrap(self.place + step, self.n), self.n)

    def hop(self, side, index, start, width, step, first):
        cols = pl.ds(start, width)
        slots = self.slots[side]
        if not first:
            source = slots.at[step - 1, :, cols]
        elif self.source is None:
            source = self.firsts[side].at[:, cols]
        else:
            source = self.source(self.target(side, 0), side, cols)
        return remote(
            source,
            slots.at[step, :, cols],
            self.send.at[side, index, step],
            self.recv.at[side, index, step],
            (self.sides[side], self.tp),
        )

    def begin(self):
        for side, index, start, width, tag in self.order:
            if self.source is None:
                term = self.local_term(self.target(side, 0), tag)
                self.firsts[side][:, start : start + width] = term.astype(BF16)
            self.hop(side, index, start, width, 0, True).start()

    def forward(self, step):
        for side, index, start, width, tag in self.order:
            term = self.local_term(self.target(side, step), tag)
            slot = self.slots[side].at[step - 1, :, pl.ds(start, width)]
            self.hop(side, index, start, width, step - 1, True).wait_recv()
            slot[...] = (slot[...].astype(F32) + term).astype(BF16)
            self.hop(side, index, start, width, step, False).start()

    def span(self, first, last):
        def body(step, carry):
            self.forward(step)
            return carry

        if last > first:
            lax.fori_loop(first, last, body, 0)

    def advance(self, count):
        last = min(self.next + count, self.n - 1)
        self.span(self.next, last)
        self.next = last

    def end(self):
        n = self.n
        self.advance(n)
        for side, index, start, width, tag in self.order:
            term = self.local_term(self.target(side, n - 1), tag)
            self.hop(side, index, start, width, n - 2, True).wait_recv()
            self.write(tag, self.slots[side][n - 2, :, start : start + width].astype(F32) + term)
        if self.source is None:
            self.sent()

    def sent(self):
        for side, index, start, width, tag in self.order:
            self.hop(side, index, start, width, 0, True).wait_send()

        def finish(step, carry):
            for side, index, start, width, tag in self.order:
                self.hop(side, index, start, width, step, False).wait_send()
            return carry

        lax.fori_loop(1, self.n - 1, finish, 0)


def exchange_start(n, me, tp, source_of, landing, send, recv):
    for i in range(1, n):
        peer = lax.rem(me + i, n)
        remote(source_of(peer), landing.at[me], send.at[i - 1], recv.at[i - 1], (peer, tp)).start()


def exchange_wait(n, me, tp, source_of, landing, send, recv):
    for i in range(1, n):
        peer = lax.rem(me - i + n, n)
        remote(source_of(peer), landing.at[peer], send.at[i - 1], recv.at[i - 1], (peer, tp)).wait()


def ordered_sum(n, landing):
    total = landing[0]
    for i in range(1, n):
        total = total + landing[i]
    return total


def pair_scatter_kernel(
    n, key_ref, value_ref, col_ref, row_ref, key_out, value_out, off_out, tot_out,
    slot_r, slot_l, first_r, first_l, off_ref, tot_ref, off_land, tot_land,
    send, recv, osend, orecv, tsend, trecv, local,
):
    me, tp, place, sides = ring_setup(n)
    off_ref[...] = col_ref[...]
    off_ref[me] += row_ref[...]
    group_rows = row_ref.shape[1] // 2
    tot_ref[...] = jnp.zeros_like(tot_ref)
    for i in range(n):
        for g in range(2):
            tot_ref[:, 2 * i + g : 2 * i + g + 1] = jnp.sum(
                off_ref[i, :, g * group_rows : (g + 1) * group_rows], axis=1, keepdims=True
            )
    greet(ctx_peers(me, tp, n))
    exchange_start(n, me, tp, lambda peer: off_ref.at[peer], off_land, osend, orecv)
    exchange_start(n, me, tp, lambda peer: tot_ref, tot_land, tsend, trecv)
    mine = pltpu.make_async_copy(off_ref.at[me], off_land.at[me], local.at[0])
    mine_tot = pltpu.make_async_copy(tot_ref, tot_land.at[me], local.at[1])
    mine.start()
    mine_tot.start()
    width = key_ref.shape[2]
    plan = [
        [(w, (0, c)) for c, w in pieces(width, 128)],
        [(w, (1, c)) for c, w in pieces(width, 128)],
    ]

    def local_term(owner, tag):
        which, c0 = tag
        return (key_ref, value_ref)[which][owner, :, c0 : c0 + 128].astype(F32)

    def write(tag, value):
        which, c0 = tag
        (key_out, value_out)[which][:, c0 : c0 + 128] = value

    ring = ScatterRing(
        n, plan, local_term, (slot_r, slot_l), (first_r, first_l), write, send, recv, place, sides, tp
    )
    ring.begin()
    ring.end()
    mine.wait()
    mine_tot.wait()
    exchange_wait(n, me, tp, lambda peer: off_ref.at[peer], off_land, osend, orecv)
    exchange_wait(n, me, tp, lambda peer: tot_ref, tot_land, tsend, trecv)
    off_out[...] = ordered_sum(n, off_land)
    tot_out[...] = ordered_sum(n, tot_land)


def pieces(width, step):
    return [(c, min(step, width - c)) for c in range(0, width, step)]


def pair_scatter(n, collective_id, keys, values, columns, own_rows):
    _, rows, width = keys.shape
    offs, tots = columns, jax.ShapeDtypeStruct((8, LANES), F32)
    chunks = len(pieces(width, 128))
    return pl.pallas_call(
        functools.partial(pair_scatter_kernel, n),
        out_shape=[
            jax.ShapeDtypeStruct((rows, width), F32),
            jax.ShapeDtypeStruct((rows, width), F32),
            jax.ShapeDtypeStruct(offs.shape[1:], F32),
            jax.ShapeDtypeStruct(tots.shape, F32),
        ],
        in_specs=[pl.BlockSpec(memory_space=VMEM)] * 4,
        out_specs=[pl.BlockSpec(memory_space=VMEM)] * 4,
        scratch_shapes=[
            VMEM((n - 1, rows, width), BF16),
            VMEM((n - 1, rows, width), BF16),
            VMEM((rows, width), BF16),
            VMEM((rows, width), BF16),
            VMEM(offs.shape, F32),
            VMEM(tots.shape, F32),
            VMEM(offs.shape, F32),
            VMEM((n,) + tots.shape, F32),
            pltpu.SemaphoreType.DMA((2, chunks, n - 1)),
            pltpu.SemaphoreType.DMA((2, chunks, n - 1)),
            pltpu.SemaphoreType.DMA((n - 1,)),
            pltpu.SemaphoreType.DMA((n - 1,)),
            pltpu.SemaphoreType.DMA((n - 1,)),
            pltpu.SemaphoreType.DMA((n - 1,)),
            pltpu.SemaphoreType.DMA((2,)),
        ],
        compiler_params=pltpu.CompilerParams(
            collective_id=collective_id, has_side_effects=True, vmem_limit_bytes=VMEM_LIMIT
        ),
    )(keys, values, columns, own_rows)


def weight_scatter_kernel(n, plan, left_count, grads, *refs):
    lefts, refs = refs[:left_count], refs[left_count:]
    rights, refs = refs[:grads], refs[grads:]
    small_ref, part_ref, x_ref, gain_ref, dmid_ref, refs = *refs[:5], refs[5:]
    outs, refs = refs[:grads], refs[grads:]
    small_out, input_out, slot_r, slot_l, first_r, first_l, own_small, land, sum_out, refs = *refs[:9], refs[9:]
    tp_bufs, refs = refs[:4], refs[4:]
    send, recv, xsend, xrecv, tsend, trecv, local = refs
    me, tp, place, sides = ring_setup(n)
    chip, core, sibling, across = tp_setup()
    greet(ctx_peers(me, tp, n) + [sibling, across])
    shard = lefts[0].shape[2]
    half = part_ref.shape[0] // 2

    def local_term(owner, tag):
        left, right, c0, cw = tag
        return contract_rows(lefts[left][owner], rights[right][:, c0 : c0 + cw])

    def write(tag, value):
        _, right, c0, cw = tag
        outs[right][:, c0 : c0 + cw] = value

    ring = ScatterRing(
        n, plan, local_term, (slot_r, slot_l), (first_r, first_l), write, send, recv, place, sides, tp
    )

    def part(which, c):
        cols = part_ref.shape[1] // TP_CHUNKS
        return part_ref[pl.ds(pl.multiple_of(which * half, half), half), c * cols : (c + 1) * cols].astype(F32)

    total = TpSum(part, sum_out, tp_bufs, tsend, trecv, core, sibling, across)
    total.first()
    total.second()
    ring.begin()
    total.third()
    ring.advance(1)
    total.fourth()

    own_small[...] = small_ref[...]
    cols = part_ref.shape[1]
    size = 64

    def gain_rows(i, acc):
        rows = pl.ds(pl.multiple_of(i * size, size), size)
        value = x_ref[rows, :].astype(F32)
        inverse = lax.rsqrt(jnp.mean(value * value, axis=-1, keepdims=True) + EPS)
        normal = value * inverse
        grad = sum_out[rows, :].astype(F32)
        back = grad * gain_ref[...]
        back = inverse * (back - normal * jnp.mean(back * normal, axis=-1, keepdims=True))
        input_out[rows, :] = dmid_ref[rows, :] + back
        return acc + jnp.sum((grad * normal).reshape(size // 8, 8, cols), axis=0)

    gains = lax.fori_loop(0, 2 * half // size, gain_rows, jnp.zeros((8, cols), F32))
    gains = jnp.sum(gains, axis=0, keepdims=True)
    for i in range(n):
        own_small[i, 0:1, :shard] = gains[:, i * shard : (i + 1) * shard]
    exchange_start(n, me, tp, lambda peer: own_small.at[peer], land, xsend, xrecv)
    mine = pltpu.make_async_copy(own_small.at[me], land.at[me], local.at[0])
    mine.start()
    ring.end()
    mine.wait()
    exchange_wait(n, me, tp, lambda peer: own_small.at[peer], land, xsend, xrecv)
    small_out[...] = ordered_sum(n, land)


def weight_scatter(n, collective_id, plan, lefts, rights, small, part, x, gain, dmid):
    rows = lefts[0].shape[2]
    chunks = max(len(plan[0]), len(plan[1]))
    totals = [sum(width for width, _ in side) for side in plan]
    return pl.pallas_call(
        functools.partial(weight_scatter_kernel, n, plan, len(lefts), len(rights)),
        out_shape=[jax.ShapeDtypeStruct((rows, right.shape[1]), F32) for right in rights]
        + [jax.ShapeDtypeStruct(small.shape[1:], F32), jax.ShapeDtypeStruct(part.shape, F32)],
        in_specs=[pl.BlockSpec(memory_space=VMEM)] * (len(lefts) + len(rights) + 5),
        out_specs=[pl.BlockSpec(memory_space=VMEM)] * (len(rights) + 2),
        scratch_shapes=[
            VMEM((n - 1, rows, totals[0]), BF16),
            VMEM((n - 1, rows, totals[1]), BF16),
            VMEM((rows, totals[0]), BF16),
            VMEM((rows, totals[1]), BF16),
            VMEM(small.shape, F32),
            VMEM(small.shape, F32),
            VMEM(part.shape, BF16),
            *tp_buffers(*part.shape),
            pltpu.SemaphoreType.DMA((2, chunks, n - 1)),
            pltpu.SemaphoreType.DMA((2, chunks, n - 1)),
            pltpu.SemaphoreType.DMA((n - 1,)),
            pltpu.SemaphoreType.DMA((n - 1,)),
            pltpu.SemaphoreType.DMA((3, TP_CHUNKS)),
            pltpu.SemaphoreType.DMA((3, TP_CHUNKS)),
            pltpu.SemaphoreType.DMA((1,)),
        ],
        compiler_params=pltpu.CompilerParams(
            collective_id=collective_id, has_side_effects=True, vmem_limit_bytes=VMEM_LIMIT
        ),
    )(*lefts, *rights, small, part, x, gain, dmid)


def tp_setup():
    ctx = lax.axis_index("ctx")
    tp = lax.axis_index("tp")
    chip = lax.div(tp, 2)
    core = lax.rem(tp, 2)
    sibling = (ctx, 2 * chip + 1 - core)
    across = (ctx, 2 * (1 - chip) + core)
    return chip, core, sibling, across


TP_CHUNKS = 4


def tp_buffers(rows, width):
    return [VMEM((rows // 2, width), BF16) for _ in range(4)]


class TpSum:
    def __init__(self, part, out, bufs, send, recv, core, sibling, across):
        self.part, self.out, self.send, self.recv = part, out, send, recv
        self.away, self.land_a, self.half_b, self.land_b = bufs
        self.core, self.sibling, self.across = core, sibling, across
        self.half = self.away.shape[0]
        self.size = self.away.shape[1] // TP_CHUNKS

    def cols(self, c):
        return pl.ds(c * self.size, self.size)

    def copy(self, stage, c, which=None):
        cols = self.cols(c)
        if stage == 0:
            source, target, device = self.away.at[:, cols], self.land_a.at[:, cols], self.sibling
        elif stage == 1:
            source, target, device = self.half_b.at[:, cols], self.land_b.at[:, cols], self.across
        else:
            source = target = self.out.at[self.rows(which), cols]
            device = self.sibling
        return remote(source, target, self.send.at[stage, c], self.recv.at[stage, c], device)

    def rows(self, which):
        return pl.ds(pl.multiple_of(which * self.half, self.half), self.half)

    def first(self):
        for c in range(TP_CHUNKS):
            self.away[:, self.cols(c)] = self.part(1 - self.core, c).astype(BF16)
            self.copy(0, c).start()

    def second(self):
        for c in range(TP_CHUNKS):
            cols = self.cols(c)
            mine = self.part(self.core, c)
            self.copy(0, c).wait_recv()
            self.half_b[:, cols] = (mine + self.land_a[:, cols].astype(F32)).astype(BF16)
            self.copy(1, c).start()

    def third(self):
        for c in range(TP_CHUNKS):
            cols = self.cols(c)
            self.copy(1, c).wait_recv()
            both = self.half_b[:, cols].astype(F32) + self.land_b[:, cols].astype(F32)
            self.out[self.rows(self.core), cols] = both.astype(BF16)
            self.copy(2, c, self.core).start()

    def fourth(self):
        for c in range(TP_CHUNKS):
            self.copy(2, c, 1 - self.core).wait_recv()
            self.copy(0, c).wait_send()
            self.copy(1, c).wait_send()
            self.copy(2, c, self.core).wait_send()


class TpSplit:
    def __init__(self, part, bufs, send, recv, chip, core, sibling, across):
        self.part, self.send, self.recv = part, send, recv
        self.away, self.land_a, self.half_b, self.land_b = bufs
        self.chip, self.core, self.sibling, self.across = chip, core, sibling, across

    def copy(self, stage):
        if stage < 2:
            return remote(
                self.away.at[stage], self.land_a.at[stage], self.send.at[stage], self.recv.at[stage], self.sibling
            )
        return remote(self.half_b, self.land_b, self.send.at[2], self.recv.at[2], self.across)

    def first(self):
        for i, chip in enumerate((1 - self.chip, self.chip)):
            self.away[i] = self.part(chip, 1 - self.core).astype(BF16)
            self.copy(i).start()

    def second(self):
        mine = self.part(1 - self.chip, self.core)
        self.copy(0).wait_recv()
        self.half_b[...] = (mine + self.land_a[0].astype(F32)).astype(BF16)
        self.copy(2).start()

    def third(self):
        mine = self.part(self.chip, self.core)
        self.copy(1).wait_recv()
        self.copy(2).wait_recv()
        total = mine + self.land_a[1].astype(F32) + self.land_b[...].astype(F32)
        for stage in range(3):
            self.copy(stage).wait_send()
        return total


def feed_kernel(n, heads, attention, *refs):
    if attention:
        (group_map, doc_lengths, skip, q_in, term_in, k_in, v_in, aug_in), refs = refs[:8], refs[8:]
    (att_in, gl_in, outw_in, x_in, gain_ref, grad_in, wg_in, wu_in, wd_in), refs = refs[:9], refs[9:]
    (gated_out, layer_ref, down_out, gate_out, up_out, dmid_out, do_out, dgl_out, gain_out), refs = refs[:9], refs[9:]
    if attention:
        (dm_out, dq_out, drow_ref, dk_out, dv_out, dcol_ref), refs = refs[:6], refs[6:]
    (
        att_ref, gl_ref, outw_ref, x_ref, gated_ref, normed_ref, dgt_ref, dup_ref, do_ref, dgl_ref,
        gate_all, up_all, down_all, accs, dhid_acc, hid_ref, branch_ref, mid_ref, dw_ref, dy_ref,
        a0, a1, a2, a3, b3, s0, s1, s2, s3, dslot_r, dslot_l, dfirst_r, dfirst_l, eslot_r, eslot_l, efirst_r, efirst_l,
        gsend, grecv, hsend, hrecv, asend, arecv, bsend, brecv, ssend, srecv, dsend, drecv, esend, erecv, local,
    ), refs = refs[:52], refs[52:]
    if attention:
        term_ref, dm_ref, diff_ref, span_ref, stage, kv_sem, stage_sem = refs
    gate_acc, up_acc = accs.at[0], accs.at[1]
    me, tp, place, sides = ring_setup(n)
    chip, core, sibling, across = tp_setup()
    moves = Moves(local)
    for name, source, target in (
        ("att", att_in, att_ref), ("gl", gl_in, gl_ref), ("outw", outw_in, outw_ref), ("grad", grad_in, dw_ref),
        ("x", x_in, x_ref),
    ):
        moves.start(name, source, target)
    if attention:
        moves.start("term", term_in, term_ref)
    greet([(side, tp) for side in sides] + [sibling, across])
    shard, hidden = wg_in.shape
    rows, width = x_in.shape
    half = rows // 2
    hw = hidden // 2
    size = 64
    ring = (n, place, sides, tp)

    def rows_of(owner):
        return pl.ds(pl.multiple_of(owner * shard, 16), shard)

    def window(ref, c0, cw):
        return lambda owner: ref.at[rows_of(owner), pl.ds(c0, cw)]

    def chunks(members):
        return [(side, source.at[:, pl.ds(c0, cw)], window(target, c0, cw)) for side, source, target, c0, cw in members]

    gates = Gather(
        *ring,
        chunks(
            [
                (side, source, target, c0, hw)
                for c0 in (0, hw)
                for side, source, target in ((0, wg_in, gate_all), (1, wu_in, up_all))
            ]
        ),
        gsend, grecv,
    )
    downs = Gather(
        *ring,
        chunks([(side, wd_in, down_all, side * hw + c0, hw // 2) for c0 in (0, hw // 2) for side in (0, 1)]),
        hsend, hrecv,
    )
    gates.begin()
    for i, (source, target) in enumerate(((wg_in, gate_all), (wu_in, up_all), (wd_in, down_all))):
        moves.start(i, source, target.at[rows_of(me)])

    moves.wait("att", "gl")
    gated_ref[...] = (att_ref[...] * jax.nn.sigmoid(gl_ref[...])).astype(BF16)
    moves.start("gated", gated_ref, gated_out)
    moves.wait("outw")
    span = width // TP_CHUNKS

    def branch_part(which, c):
        mine = gated_ref[pl.ds(pl.multiple_of(which * half, half), half), :]
        return contract_cols(mine, outw_ref[c * span : (c + 1) * span, :])

    branch = TpSum(branch_part, branch_ref, (a0, a1, a2, a3), asend, arecv, core, sibling, across)
    branch.first()
    branch.second()
    gates.forward(1)
    moves.wait("grad")
    for j in range(n):
        dy_ref[j] = dw_ref[:, j * shard : (j + 1) * shard]
    dhid_acc[...] = jnp.zeros_like(dhid_acc)
    gate_acc[...] = jnp.zeros_like(gate_acc)
    up_acc[...] = jnp.zeros_like(up_acc)

    def grow_back(back):
        for side in (0, 1):
            owner = downs.owner(side, back)
            cols = pl.ds(side * hw, hw)
            dhid_acc[:, cols] += dot(dy_ref[owner], down_all[rows_of(owner), cols])

    def grow(back):
        for side, acc, source in ((0, gate_acc, gate_all), (1, up_acc, up_all)):
            owner = gates.owner(side, back)
            acc[...] += dot(normed_ref[owner], source[rows_of(owner), :])

    moves.wait(0, 1, 2)
    grow_back(0)
    gates.forward(2)
    branch.third()
    branch.fourth()
    moves.wait("x")

    def norm_rows(i, carry):
        here = pl.ds(pl.multiple_of(i * size, size), size)
        middle = x_ref[here, :].astype(F32) + branch_ref[here, :].astype(F32)
        mid_ref[here, :] = middle
        normed = (rms_scale(middle) * gain_ref[...]).astype(BF16)
        for j in range(n):
            normed_ref[j, here, :] = normed[:, j * shard : (j + 1) * shard]
        return carry

    lax.fori_loop(0, rows // size, norm_rows, 0)
    own = pl.ds(pl.multiple_of(tp * span, span), span)
    layer_ref[...] = mid_ref[:, own]
    moves.start("again", grad_in, x_ref)
    gates.forward(3)

    def grow_step(step, carry):
        grow(step)
        return carry

    lax.fori_loop(0, 4, grow_step, 0)

    def gate_step(step, carry):
        gates.forward(step)
        grow(step)
        return carry

    lax.fori_loop(4, n - 1, gate_step, 0)
    downs.begin()
    gates.last()
    grow(n - 1)

    def hid_rows(i, carry):
        here = pl.ds(pl.multiple_of(i * size, size), size)
        gate, up = gate_acc[here, :], up_acc[here, :]
        open_gate = jax.nn.sigmoid(gate)
        silu = gate * open_gate
        hid_ref[here, :] = (silu * up).astype(BF16)
        gate_acc[here, :] = up * open_gate * (1.0 + gate * (1.0 - open_gate))
        up_acc[here, :] = silu
        return carry

    lax.fori_loop(0, rows // size, hid_rows, 0)

    def down_step(step, carry):
        downs.forward(step)
        grow_back(step)
        return carry

    lax.fori_loop(1, n - 2, down_step, 0)
    downs.forward(n - 2)

    def down_term(owner, tag):
        return contract_rows(dy_ref[owner], hid_ref[:, tag * hw : (tag + 1) * hw])

    down_ref = accs.at[0, pl.ds(0, shard), :]
    gate_ref = accs.at[0, pl.ds(shard, shard), :]
    up_ref = accs.at[1, pl.ds(0, shard), :]

    def down_write(tag, value):
        down_ref[:, tag * hw : (tag + 1) * hw] = value

    def early_term(owner, tag):
        which, c0 = tag
        return contract_rows(normed_ref[owner], (dgt_ref, dup_ref)[which][:, c0 : c0 + hw])

    def early_write(tag, value):
        which, c0 = tag
        (gate_ref, up_ref)[which][:, c0 : c0 + hw] = value

    backs = ScatterRing(
        n, [[(hw, 0)], [(hw, 1)]], down_term, (dslot_r, dslot_l), (dfirst_r, dfirst_l), down_write,
        dsend, drecv, place, sides, tp,
    )
    earlies = ScatterRing(
        n, [[(hw, (i, 0)), (hw, (i, hw))] for i in range(2)], early_term, (eslot_r, eslot_l), (efirst_r, efirst_l),
        early_write, esend, erecv, place, sides, tp,
    )
    backs.begin()
    grow_back(n - 2)
    downs.last()
    grow_back(n - 1)

    def grad_rows(i, carry):
        here = pl.ds(pl.multiple_of(i * size, size), size)
        dhid = dhid_acc[here, :]
        dgt_ref[here, :] = (dhid * gate_acc[here, :]).astype(BF16)
        dup_ref[here, :] = (dhid * up_acc[here, :]).astype(BF16)
        return carry

    lax.fori_loop(0, rows // size, grad_rows, 0)

    def dw_part(which, c):
        mine = pl.ds(pl.multiple_of(which * half, half), half)
        back = pl.ds(c * span, span)
        return contract_cols(dgt_ref[mine, :], gate_all[back, :]) + contract_cols(dup_ref[mine, :], up_all[back, :])

    def layer_part(which_chip, which_core):
        back = pl.ds(pl.multiple_of((2 * which_chip + which_core) * span, span), span)
        return contract_cols(hid_ref[...], down_all[back, :])

    total = TpSum(dw_part, dw_ref, (a0, a1, a2, b3), bsend, brecv, core, sibling, across)
    layer = TpSplit(layer_part, (s0, s1, s2, s3), ssend, srecv, chip, core, sibling, across)
    total.first()
    backs.advance(1)
    earlies.begin()
    total.second()
    gates.sent()
    if attention:
        pairs = heads // 2

        def kv_copies(it):
            part, pair = lax.div(it, pairs), lax.rem(it, pairs)
            source = pl.ds(pl.multiple_of(part * rows, rows), rows)
            target = pl.ds(pl.multiple_of(pair * rows, rows), rows)
            lanes = pl.ds(pl.multiple_of(part * LANES, LANES), LANES)
            return [
                pltpu.make_async_copy(ref.at[pair, source, :], held.at[target, lanes], kv_sem.at[i, it])
                for i, (ref, held) in enumerate(((k_in, gate_all), (v_in, up_all)))
            ]

        def bring(it, carry):
            for copy in kv_copies(it):
                copy.start()
            return carry

        lax.fori_loop(0, n * pairs, bring, 0)
    layer.first()
    layer.second()
    backs.advance(1)
    earlies.advance(1)
    backs.advance(1)
    earlies.advance(1)
    total.third()
    total.fourth()

    def middle_rows(i, acc):
        here = pl.ds(pl.multiple_of(i * size, size), size)
        middle = mid_ref[here, :]
        inverse = lax.rsqrt(jnp.mean(middle * middle, axis=-1, keepdims=True) + EPS)
        normal = middle * inverse
        dw = dw_ref[here, :].astype(F32)
        back = dw * gain_ref[...]
        back = inverse * (back - normal * jnp.mean(back * normal, axis=-1, keepdims=True))
        dmid = x_ref[here, :].astype(F32) + back
        mid_ref[here, :] = dmid
        low = dmid.astype(BF16)
        branch_ref[here, :] = low
        if attention:
            for j in range(n):
                dm_ref[j, here, :] = low[:, j * shard : (j + 1) * shard]
        return acc + jnp.sum((dw * normal).reshape(size // 8, 8, width), axis=0)

    moves.wait("again")
    gain_out[...] = lax.fori_loop(0, rows // size, middle_rows, jnp.zeros((8, width), F32))
    if attention:
        narrow = q_in.shape[1]
        q_ref = x_ref.at[:, pl.ds(0, narrow)]
        moves.start("q", q_in, q_ref)
        for i in range(n):
            moves.start(
                ("aug", i),
                aug_in.at[pl.ds(i * rows, rows), :],
                x_ref.at[:, pl.ds(narrow + i * LANES, LANES)],
            )
    moves.start("dmid", mid_ref, dmid_out)
    if attention:
        moves.start("dm", dm_ref, dm_out)
    da = dot(branch_ref[...], outw_ref[...])
    open_gate = jax.nn.sigmoid(gl_ref[...])
    do_ref[...] = (da * open_gate).astype(BF16)
    dgl_ref[...] = (da * att_ref[...] * open_gate * (1.0 - open_gate)).astype(BF16)
    moves.start("do", do_ref, do_out)
    moves.start("dgl", dgl_ref, dgl_out)
    backs.advance(1)
    earlies.advance(1)
    layer_ref[...] += layer.third()

    if attention:
        moves.wait("q", "term", *[("aug", i) for i in range(n)])
        first, second = group_map[2 * me], group_map[2 * me + 1]
        in_order = first < second
        query_groups = (jnp.minimum(first, second), jnp.maximum(first, second))

        def put_in(ref):
            def put(h, value, extra):
                ref[:, 2 * h * LANES : (2 * h + 1) * LANES] = value
                ref[:, (2 * h + 1) * LANES : (2 * h + 2) * LANES] = extra

            return put

        spread_heads(q_ref, row_pieces(term_ref[...], True), put_in(dw_ref), heads, in_order)
        delta = head_sums(do_ref[...].astype(F32) * att_ref[...], heads)
        spread_heads(do_ref, row_pieces(-delta, False), put_in(branch_ref), heads, in_order)
        accs[...] = jnp.zeros_like(accs)
        query_at = lax.broadcasted_iota(jnp.int32, (half, half), 1)
        key_at = lax.broadcasted_iota(jnp.int32, (half, half), 0)
        diff_ref[...] = key_at - query_at
        for i, group in enumerate(query_groups):
            span_ref[i] = document_start(group * half + query_at, doc_lengths) - key_at
        dcol_acc = dhid_acc.at[:, pl.ds(0, LANES)]

        def stage_copies(it):
            part, pair = lax.div(it, pairs), lax.rem(it, pairs)
            lanes = pl.ds(pl.multiple_of(pair * LANES, LANES), LANES)
            slot = lax.rem(it, 2)
            return [
                pltpu.make_async_copy(stage.at[slot, i], out.at[part, :, lanes], stage_sem.at[slot, i])
                for i, out in enumerate((dk_out, dv_out))
            ]

        def attend(it, carry):
            part, pair = lax.div(it, pairs), lax.rem(it, pairs)
            for copy in kv_copies(it):
                copy.wait()
            one, two = group_map[2 * part], group_map[2 * part + 1]
            forward = one < two
            key_groups = (jnp.minimum(one, two), jnp.maximum(one, two))
            lanes = pl.ds(pl.multiple_of(part * LANES, LANES), LANES)

            def ordered(ref, base, where):
                top = pl.ds(pl.multiple_of(base * rows, rows), half)
                bottom = pl.ds(pl.multiple_of(base * rows + half, half), half)
                return in_pack_order(forward, ref[top, where], ref[bottom, where])

            key_blocks = ordered(gate_all, pair, lanes)
            value_blocks = ordered(up_all, pair, lanes)
            aug_lanes = pl.ds(pl.multiple_of(narrow + part * LANES, LANES), LANES)
            aug_blocks = ordered(x_ref, 0, aug_lanes)
            masks = block_masks(diff_ref, span_ref, skip, query_groups, key_groups, half)
            keys = [jnp.concatenate([key_blocks[ki], aug_blocks[ki]], axis=1) for ki in range(2)]
            values = [jnp.concatenate([value_blocks[ki], aug_blocks[ki]], axis=1) for ki in range(2)]
            both_keys = jnp.concatenate(keys, axis=0)
            queries, douts, probs, grads = [], [], ([], []), ([], [])
            for e in range(2):
                h = 2 * pair + e
                spot = pl.ds(pl.multiple_of(h * 2 * LANES, 2 * LANES), 2 * LANES)
                query, dout = dw_ref[:, spot], branch_ref[:, spot]
                early = contract_cols(keys[0], query)
                scores = (early[:, :half], early[:, half:], contract_cols(keys[1], query[half:]))
                early = contract_cols(values[0], dout)
                backs_out = (early[:, :half], early[:, half:], contract_cols(values[1], dout[half:]))
                prob = [jnp.where(mask, jnp.exp(score), 0.0) for mask, score in zip(masks, scores)]
                grad = [(p * back).astype(BF16) for p, back in zip(prob, backs_out)]
                prob = [p.astype(BF16) for p in prob]
                queries.append(query)
                douts.append(dout[:, :LANES])
                probs[0].extend(prob[:2])
                probs[1].append(prob[2])
                grads[0].extend(grad[:2])
                grads[1].append(grad[2])
                quarter = pl.ds(pl.multiple_of(lax.rem(h, 4) * 2 * LANES, 2 * LANES), 2 * LANES)
                accs[lax.div(h, 4), :half, quarter] += contract_rows(grad[0], keys[0])
                accs[lax.div(h, 4), half:, quarter] += contract_rows(jnp.concatenate(grad[1:], axis=0), both_keys)
            late_queries = jnp.concatenate([query[half:] for query in queries], axis=0)
            late_douts = jnp.concatenate([dout[half:] for dout in douts], axis=0)
            queries, douts = jnp.concatenate(queries, axis=0), jnp.concatenate(douts, axis=0)
            sums = [
                dot(jnp.concatenate(grads[0], axis=1), queries),
                dot(jnp.concatenate(grads[1], axis=1), late_queries),
            ]
            value_sums = [
                dot(jnp.concatenate(probs[0], axis=1), douts),
                dot(jnp.concatenate(probs[1], axis=1), late_douts),
            ]
            columns = jnp.concatenate([part_sum[:, LANES:] for part_sum in sums], axis=0)
            dcol_acc[...] = jnp.where(pair == 0, 0.0, dcol_acc[...]) + columns

            @pl.when(it >= 2)
            def _():
                for copy in stage_copies(it - 2):
                    copy.wait()

            slot = lax.rem(it, 2)
            for i, part_sums in enumerate(([part_sum[:, :LANES] for part_sum in sums], value_sums)):
                stage[slot, i] = jnp.concatenate(in_pack_order(forward, *part_sums), axis=0).astype(BF16)
            for copy in stage_copies(it):
                copy.start()

            @pl.when(pair == pairs - 1)
            def _():
                columns = jnp.concatenate(
                    in_pack_order(forward, dcol_acc[pl.ds(0, half), :], dcol_acc[pl.ds(half, half), :]), axis=0
                )
                dcol_ref[part] = -(columns.T[:8])

            return carry

        done = 0
        while earlies.next < n - 1:
            lax.fori_loop(done, done + 2 * pairs, attend, 0)
            done += 2 * pairs
            backs.advance(1)
            earlies.advance(1)
        lax.fori_loop(done, n * pairs, attend, 0)
        for it in (n * pairs - 2, n * pairs - 1):
            for copy in stage_copies(it):
                copy.wait()

        lane = lax.broadcasted_iota(jnp.int32, (rows, LANES), 1)
        low = low_lanes(rows)
        sums = jnp.zeros((rows, LANES), F32)
        for pair in range(pairs):
            parts = []
            for h in (2 * pair, 2 * pair + 1):
                spot = pl.ds((h % 4) * 2 * LANES, 2 * LANES)
                value = jnp.concatenate(
                    in_pack_order(in_order, accs[h // 4, :half, spot], accs[h // 4, half:, spot]), axis=0
                )
                parts.append(value)
                sums = jnp.where(lane == 24 + h, value[:, LANES:], sums)
            dhid_acc[:, (3 + pair) * LANES : (4 + pair) * LANES] = jnp.where(
                low, parts[0][:, :LANES], parts[1][:, :LANES]
            )
        moves.start("dq", dhid_acc.at[:, pl.ds(3 * LANES, pairs * LANES)], dq_out)
        drow_ref[...] = pltpu.roll(sums, LANES - 24, 1).T[:8]

        moves.wait("dq")
    backs.end()
    moves.start("down", down_ref, down_out)
    earlies.end()
    moves.start("gate", gate_ref, gate_out)
    moves.start("up", up_ref, up_out)
    downs.sent()
    moves.wait()


def feed_forward(
    n, collective_id, heads, attended, gate_logit, out_weight, x, gain, dy, w_gate, w_up, w_down, attention=None
):
    rows, width = x.shape
    shard, hidden = w_gate.shape
    heads_width = attended.shape[1]
    own = width // 4
    half = rows // 2
    dma = pltpu.SemaphoreType.DMA
    vmem = pl.BlockSpec(memory_space=VMEM)
    anywhere = pl.BlockSpec(memory_space=pl.ANY)
    wide, narrow, deep = (rows, width), (rows, heads_width), (rows, hidden)
    by_shard = (n, rows, shard)
    weight = (shard, hidden)
    shapes = [
        (narrow, BF16),
        ((rows, own), F32),
        (weight, F32),
        (weight, F32),
        (weight, F32),
        (wide, F32),
        (narrow, BF16),
        (narrow, BF16),
        ((8, width), F32),
    ]
    kept = [1, 8]
    extra_specs, extra_scratch = [], []
    if attention is not None:
        assert heads // 2 * rows == n * shard and n * LANES == hidden and heads_width + hidden <= width
        shapes += [
            (by_shard, BF16),
            (narrow, F32),
            ((8, rows), F32),
            ((n, rows, heads_width), BF16),
            ((n, rows, heads_width), BF16),
            ((n, 8, rows), F32),
        ]
        kept += [11, 14]
        extra_specs = [smem()] * 3 + [anywhere] * 5
        extra_scratch = [
            VMEM((rows, LANES), F32),
            VMEM(by_shard, BF16),
            VMEM((half, half), jnp.int32),
            VMEM((2, half, half), jnp.int32),
            VMEM((2, 2, rows, LANES), BF16),
            dma((2, n * heads // 2)),
            dma((2, 2)),
        ]
    return pl.pallas_call(
        functools.partial(feed_kernel, n, heads, attention is not None),
        out_shape=[jax.ShapeDtypeStruct(*shape) for shape in shapes],
        in_specs=extra_specs + [anywhere] * 4 + [vmem] + [anywhere] * 4,
        out_specs=[vmem if i in kept else anywhere for i in range(len(shapes))],
        scratch_shapes=[
            VMEM(narrow, F32),
            VMEM(narrow, F32),
            VMEM(out_weight.shape, BF16),
            VMEM(wide, BF16),
            VMEM(narrow, BF16),
            VMEM(by_shard, BF16),
            VMEM(deep, BF16),
            VMEM(deep, BF16),
            VMEM(narrow, BF16),
            VMEM(narrow, BF16),
            *[VMEM((n * shard, hidden), BF16)] * 3,
            VMEM((2,) + deep, F32),
            VMEM(deep, F32),
            VMEM(deep, BF16),
            VMEM(wide, BF16),
            VMEM(wide, F32),
            VMEM(wide, BF16),
            VMEM(by_shard, BF16),
            *tp_buffers(rows, width),
            VMEM((rows // 2, width), BF16),
            VMEM((2, rows, own), BF16),
            VMEM((2, rows, own), BF16),
            VMEM((rows, own), BF16),
            VMEM((rows, own), BF16),
            *ring_scratch(n, shard, [hidden // 2] * 2),
            *ring_scratch(n, shard, [hidden] * 2),
            *[dma((4, n - 1))] * 4,
            *[dma((3, TP_CHUNKS))] * 4,
            *[dma((3,))] * 2,
            *[dma((2, 1, n - 1))] * 2,
            *[dma((2, 2, n - 1))] * 2,
            dma((28,)),
            *extra_scratch,
        ],
        compiler_params=pltpu.CompilerParams(
            collective_id=collective_id, has_side_effects=True, vmem_limit_bytes=VMEM_LIMIT
        ),
    )(*(attention or ()), attended, gate_logit, out_weight, x, gain, dy, w_gate, w_up, w_down)


def ring_scratch(n, height, widths):
    return [VMEM((n - 1, height, w), BF16) for w in widths] + [VMEM((height, w), BF16) for w in widths]


def head_means(value, heads):
    width = value.shape[1]
    size = width // heads
    left = lax.div(lax.broadcasted_iota(jnp.int32, (width, width), 0), size)
    right = lax.div(lax.broadcasted_iota(jnp.int32, (width, width), 1), size)
    member = (left == right).astype(BF16)
    high = value.astype(BF16)
    return (dot(high, member) + dot((value - high.astype(F32)).astype(BF16), member)) * (1.0 / size)


STAGED = (0, 1, 4, 5, 16, 11, 14, 17, 18, 19, 6, 12, 13, 20)


def finish_kernel(n, heads, gate_plan, attn_plan, *refs):
    operands, refs = list(refs[:24]), refs[24:]
    (q_out, k_out, v_out, g_out, o_out, small_out, input_out), refs = refs[:7], refs[7:]
    staged, refs = refs[: len(STAGED)], refs[len(STAGED) :]
    (
        pslot_r, pslot_l, gslot_r, gslot_l, gfirst_r, gfirst_l, aslot_r, aslot_l, afirst_r, afirst_l,
        dk_sum, dv_sum, dqr_ref, dkr_ref, dvl_ref, du_ref, sum_ref, t0, t1, t2, t3,
        off_ref, tot_ref, off_land, tot_land, small_ref, small_land,
        psend, precv, gsend, grecv, asend, arecv, osend, orecv, qsend, qrecv, xsend, xrecv, tsend, trecv, local,
    ) = refs
    moves = Moves(local)
    dk_hbm, dv_hbm = operands[:2]
    for target, index in zip(staged, STAGED):
        moves.start(index, operands[index], target)
        operands[index] = target
    (
        dk_ref, dv_ref, col_ref, row_ref, dq_ref, qr_ref, kr_ref, qgain_ref, kgain_ref, fz_ref, later_ref,
        wq_ref, wk_ref, wv_ref, wg_ref, wf_ref, dgl_ref, u_ref, dm_ref, gated_ref,
        x_ref, gain_ref, dmid_ref, gain_two_ref,
    ) = operands
    me, tp, place, sides = ring_setup(n)
    chip, core, sibling, across = tp_setup()
    rows, width = dq_ref.shape
    cols = x_ref.shape[1]
    shard = u_ref.shape[2]
    half = rows // 2
    head_dim = width // heads
    small_ref[...] = jnp.zeros_like(small_ref)
    greet(ctx_peers(me, tp, n) + [sibling, across])

    def pair_term(owner, tag):
        which, c0 = tag
        return (dk_ref, dv_ref)[which][owner, :, c0 : c0 + LANES].astype(F32)

    def pair_write(tag, value):
        which, c0 = tag
        (dk_sum, dv_sum)[which][:, c0 : c0 + LANES] = value

    pairs = ScatterRing(
        n, [[(w, (i, c)) for c, w in pieces(width, LANES)] for i in range(2)], pair_term,
        (pslot_r, pslot_l), None, pair_write, psend, precv, place, sides, tp,
        source=lambda target, side, window: (dk_hbm, dv_hbm)[side].at[target, :, window],
    )
    pairs.begin()
    off_ref[...] = col_ref[...]
    off_ref[me] += row_ref[...]
    tot_ref[...] = jnp.zeros_like(tot_ref)
    for i in range(n):
        for g in range(2):
            tot_ref[:, 2 * i + g : 2 * i + g + 1] = jnp.sum(
                off_ref[i, :, g * half : (g + 1) * half], axis=1, keepdims=True
            )
    exchange_start(n, me, tp, lambda peer: off_ref.at[peer], off_land, osend, orecv)
    exchange_start(n, me, tp, lambda peer: tot_ref, tot_land, qsend, qrecv)
    moves.start("off", off_ref.at[me], off_land.at[me])
    moves.start("tot", tot_ref, tot_land.at[me])

    def raw_grad(grad, raw, gain):
        inverse = lax.rsqrt(head_means(raw * raw, heads) + EPS)
        normal = raw * inverse
        back = grad * gain
        back = inverse * (back - normal * head_means(back * normal, heads))
        return back.astype(BF16), jnp.sum(grad * normal, axis=0, keepdims=True)

    def gain_rows(row, first):
        count = 2 * head_dim // n
        for i in range(n // 2):
            for h in range(heads):
                lane = h * head_dim + i * count
                small_ref[first + i, 2 + h : 3 + h, 0:count] = row[:, lane : lane + count]

    moves.wait(0, 1, 4, 5)
    pairs.advance(1)
    dqr, row = raw_grad(dq_ref[...], qr_ref[...], qgain_ref[...] * 0.125)
    dqr_ref[...] = dqr
    gain_rows(row * 0.125, 0)
    pairs.advance(1)
    moves.wait(16, 11, 14)
    span = cols // TP_CHUNKS
    for c in range(TP_CHUNKS):
        back = pl.ds(c * span, span)
        du_ref[:, back] = contract_cols(dqr_ref[...], wq_ref[back, :]) + contract_cols(dgl_ref[...], wg_ref[back, :])
    pairs.advance(n)
    moves.wait(17, 18, 19)

    def gate_term(owner, tag):
        left, right, c0, cw = tag
        grads = (gated_ref, dqr_ref, dgl_ref)[right]
        return contract_rows((dm_ref, u_ref)[left][owner], grads[:, c0 : c0 + cw])

    def gate_write(tag, value):
        _, right, c0, cw = tag
        (o_out, q_out, g_out)[right][:, c0 : c0 + cw] = value

    gates = ScatterRing(
        n, gate_plan, gate_term, (gslot_r, gslot_l), (gfirst_r, gfirst_l), gate_write, gsend, grecv, place, sides, tp,
    )
    gates.begin()
    pairs.end()

    moves.wait(6)
    dkr, row = raw_grad(dk_sum[...], kr_ref[...], kgain_ref[...])
    dkr_ref[...] = dkr
    gain_rows(row, n // 2)
    dvl_ref[...] = dv_sum[...].astype(BF16)

    def attn_term(owner, tag):
        c0, cw = tag[1], tag[2]
        return contract_rows(u_ref[owner], (dkr_ref, dvl_ref)[tag[0]][:, c0 : c0 + cw])

    def attn_write(tag, value):
        c0, cw = tag[1], tag[2]
        (k_out, v_out)[tag[0]][:, c0 : c0 + cw] = value

    attns = ScatterRing(
        n, attn_plan, attn_term, (aslot_r, aslot_l), (afirst_r, afirst_l), attn_write, asend, arecv, place, sides, tp,
    )
    attns.begin()
    gates.advance(1)
    moves.wait("off", "tot")
    exchange_wait(n, me, tp, lambda peer: off_ref.at[peer], off_land, osend, orecv)
    exchange_wait(n, me, tp, lambda peer: tot_ref, tot_land, qsend, qrecv)
    off_sum = ordered_sum(n, off_land)
    tot_sum = ordered_sum(n, tot_land)
    onward = (
        lax.broadcasted_iota(jnp.int32, (half, half), 0) >= lax.broadcasted_iota(jnp.int32, (half, half), 1)
    ).astype(F32)
    parts = []
    for g in range(2):
        suffix = jnp.dot(
            off_sum[:, g * half : (g + 1) * half], onward, precision=HIGHEST, preferred_element_type=F32
        )
        parts.append(suffix + jnp.sum(tot_sum * later_ref[g : g + 1, :], axis=1, keepdims=True))
    dfz = (jnp.concatenate(parts, axis=1) * jax.nn.sigmoid(-fz_ref[...])).astype(BF16).astype(F32)
    head = lax.broadcasted_iota(jnp.int32, dfz.shape, 0)
    dfz = jnp.where(head < heads, dfz, 0.0)
    bias = jnp.sum(dfz, axis=1, keepdims=True)
    dfz_cols = turn(dfz).astype(BF16)
    dfz_low = dfz.astype(BF16)
    for i in range(n):
        small_ref[i, 8:16, :shard] = dot(dfz_low, u_ref[i])
        small_ref[i, 8:16, 224:225] = bias
        small_ref[i, 1:2, :shard] = jnp.sum(gain_two_ref[:, i * shard : (i + 1) * shard], axis=0, keepdims=True)

    moves.wait(12, 13)
    forget = jnp.concatenate([wf_ref[...], jnp.zeros((LANES - 8, cols), F32)], axis=0).astype(BF16)
    for c in range(TP_CHUNKS):
        back = pl.ds(c * span, span)
        du_ref[:, back] += (
            contract_cols(dkr_ref[...], wk_ref[back, :])
            + contract_cols(dvl_ref[...], wv_ref[back, :])
            + dot(dfz_cols, forget[:, c * span : (c + 1) * span])
        )

    def part(which, c):
        return du_ref[pl.ds(pl.multiple_of(which * half, half), half), c * span : (c + 1) * span]

    total = TpSum(part, sum_ref, (t0, t1, t2, t3), tsend, trecv, core, sibling, across)
    total.first()
    attns.advance(1)
    total.second()
    moves.start("dmid", dmid_ref, du_ref)
    gates.advance(1)
    attns.advance(1)
    gates.advance(1)
    total.third()
    attns.advance(1)
    total.fourth()
    moves.wait("dmid", 20)
    size = 64

    def input_rows(i, acc):
        here = pl.ds(pl.multiple_of(i * size, size), size)
        value = x_ref[here, :].astype(F32)
        inverse = lax.rsqrt(jnp.mean(value * value, axis=-1, keepdims=True) + EPS)
        normal = value * inverse
        grad = sum_ref[here, :].astype(F32)
        back = grad * gain_ref[...]
        back = inverse * (back - normal * jnp.mean(back * normal, axis=-1, keepdims=True))
        du_ref[here, :] += back
        return acc + jnp.sum((grad * normal).reshape(size // 8, 8, cols), axis=0)

    gains = lax.fori_loop(0, rows // size, input_rows, jnp.zeros((8, cols), F32))
    moves.start("input", du_ref, input_out)
    for i in range(n):
        small_ref[i, 0:1, :shard] = jnp.sum(gains[:, i * shard : (i + 1) * shard], axis=0, keepdims=True)
    exchange_start(n, me, tp, lambda peer: small_ref.at[peer], small_land, xsend, xrecv)
    moves.start("small", small_ref.at[me], small_land.at[me])
    while gates.next < n - 1:
        gates.advance(1)
        attns.advance(1)
    gates.end()
    attns.end()
    moves.wait("small")
    exchange_wait(n, me, tp, lambda peer: small_ref.at[peer], small_land, xsend, xrecv)
    small_out[...] = ordered_sum(n, small_land)
    pairs.sent()
    moves.wait()


def finish_backward(n, collective_id, heads, gate_plan, attn_plan, *operands):
    dq, u, x = operands[4], operands[17], operands[20]
    rows, width = dq.shape
    cols = x.shape[1]
    shard = u.shape[2]
    dma = pltpu.SemaphoreType.DMA
    vmem = pl.BlockSpec(memory_space=VMEM)
    anywhere = pl.BlockSpec(memory_space=pl.ANY)
    outside = STAGED + (22,)
    gate_widths = [sum(w for w, _ in side) for side in gate_plan]
    attn_widths = [sum(w for w, _ in side) for side in attn_plan]

    def ring_semaphores(plan):
        return [dma((2, max(len(side) for side in plan), n - 1))] * 2

    shapes = [(shard, width)] * 5 + [(16, 256), (rows, cols)]
    return pl.pallas_call(
        functools.partial(finish_kernel, n, heads, gate_plan, attn_plan),
        out_shape=[jax.ShapeDtypeStruct(shape, F32) for shape in shapes],
        in_specs=[anywhere if i in outside else vmem for i in range(len(operands))],
        out_specs=[vmem] * 6 + [anywhere],
        scratch_shapes=[
            *[VMEM(operands[i].shape, operands[i].dtype) for i in STAGED],
            *[VMEM((n - 1, rows, width), BF16)] * 2,
            *ring_scratch(n, shard, gate_widths),
            *ring_scratch(n, shard, attn_widths),
            VMEM((rows, width), F32),
            VMEM((rows, width), F32),
            *[VMEM((rows, width), BF16)] * 3,
            VMEM((rows, cols), F32),
            VMEM((rows, cols), BF16),
            *tp_buffers(rows, cols),
            VMEM((n, 8, rows), F32),
            VMEM((8, LANES), F32),
            VMEM((n, 8, rows), F32),
            VMEM((n, 8, LANES), F32),
            VMEM((n, 16, 256), F32),
            VMEM((n, 16, 256), F32),
            *[dma((2, len(pieces(width, LANES)), n - 1))] * 2,
            *ring_semaphores(gate_plan),
            *ring_semaphores(attn_plan),
            *[dma((n - 1,))] * 6,
            *[dma((3, TP_CHUNKS))] * 2,
            dma((len(STAGED) + 5,)),
        ],
        compiler_params=pltpu.CompilerParams(
            collective_id=collective_id, has_side_effects=True, vmem_limit_bytes=VMEM_LIMIT
        ),
    )(*operands)


LANES = 128


def block_state(group_map, doc_lengths, skip, query_group, key_group, rows, docs):
    first_q = query_group * rows
    last_q = first_q + rows - 1
    first_k = key_group * rows
    last_k = first_k + rows - 1
    zero = jnp.int32(0)
    doc_qf, doc_ql, doc_kf, doc_kl, end = zero, zero, zero, zero, zero
    for d in range(docs):
        end = end + doc_lengths[d]
        doc_qf += (first_q >= end).astype(jnp.int32)
        doc_ql += (last_q >= end).astype(jnp.int32)
        doc_kf += (first_k >= end).astype(jnp.int32)
        doc_kl += (last_k >= end).astype(jnp.int32)
    earlier = key_group < query_group
    same = key_group == query_group
    kept = skip[query_group, key_group] != 1
    active = jnp.logical_or(same, earlier & kept & (doc_kl == doc_qf))
    full = earlier & (doc_kf == doc_ql)
    return active, full


def block_mask(doc_lengths, query_group, key_group, rows, docs, query_dim):
    shape = (rows, rows)
    pos_q = query_group * rows + lax.broadcasted_iota(jnp.int32, shape, query_dim)
    pos_k = key_group * rows + lax.broadcasted_iota(jnp.int32, shape, 1 - query_dim)
    start = jnp.zeros(shape, jnp.int32)
    end = jnp.int32(0)
    for d in range(docs):
        end = end + doc_lengths[d]
        start = jnp.where(pos_q >= end, end, start)
    return (pos_k <= pos_q) & (pos_k >= start)


def document_start(position, doc_lengths):
    start, end = jnp.zeros_like(position), jnp.int32(0)
    for d in range(doc_lengths.shape[0]):
        end = end + doc_lengths[d]
        start = jnp.where(position >= end, end, start)
    return start


def block_masks(diff_ref, span_ref, skip, query_groups, key_groups, rows):
    masks = []
    for qi, ki in ((0, 0), (1, 0), (1, 1)):
        query_group, key_group = query_groups[qi], key_groups[ki]
        skipped = jnp.where(key_group < query_group, skip[query_group, key_group], 0)
        reach = key_group * rows - (skipped == 1).astype(jnp.int32) * (1 << 30)
        mask = span_ref[qi] <= reach
        if qi == ki:
            mask = mask & (diff_ref[...] <= (query_group - key_group) * rows)
        masks.append(mask)
    return masks


def in_pack_order(forward, one, two):
    return jnp.where(forward, one, two), jnp.where(forward, two, one)


def low_lanes(rows):
    return lax.broadcasted_iota(jnp.int32, (rows, LANES), 1) < LANES // 2


def three_pieces(value):
    high = value.astype(BF16).astype(F32)
    rest = value - high
    middle = rest.astype(BF16).astype(F32)
    return high, middle, rest - middle


def turn(value):
    rows = value.shape[1]
    return jnp.concatenate([value, jnp.zeros((LANES - 8, rows), F32)], axis=0).T


def row_pieces(term, with_ones):
    lane = lax.broadcasted_iota(jnp.int32, term.shape, 1)
    term = jnp.where(lane < 8, term, 0.0)
    high, middle, low = three_pieces(term)
    result = pltpu.roll(high, 24, 1) + pltpu.roll(middle, 32, 1) + pltpu.roll(low, 40, 1)
    if with_ones:
        result = jnp.where(lane < 24, 1.0, result)
    return result


def key_pieces(offsets):
    rows = offsets.shape[1]
    high, middle, low = three_pieces(offsets)
    stack = jnp.concatenate(
        [-high, -middle, -low, jnp.ones((24, rows), F32), jnp.zeros((LANES - 48, rows), F32)], axis=0
    )
    return stack.T.astype(BF16)


def spread_heads(wide_ref, common, put, heads, forward=None):
    rows = wide_ref.shape[0]
    low = low_lanes(rows)
    lane = lax.broadcasted_iota(jnp.int32, (rows, LANES), 1)

    def ordered(value):
        if forward is None:
            return value
        return jnp.concatenate(in_pack_order(forward, value[: rows // 2], value[rows // 2 :]), axis=0)

    common = ordered(common)
    for h in range(heads):
        pair = h // 2
        block = ordered(wide_ref[:, pair * LANES : (pair + 1) * LANES])
        keep = low if h % 2 == 0 else jnp.logical_not(low)
        put(
            h,
            jnp.where(keep, block, jnp.zeros_like(block)),
            jnp.where(lax.rem(lane, 8) == h, common, 0.0).astype(BF16),
        )


def put_rows(cat_ref):
    def put(h, value, extra):
        cat_ref[h, :, :LANES] = value
        cat_ref[h, :, LANES:] = extra

    return put


def smem():
    return pl.BlockSpec(memory_space=pltpu.SMEM)


def whole(shape):
    return pl.BlockSpec(shape, lambda i: (0,) * len(shape))


def head_sums(value, heads):
    width = value.shape[1]
    feature = lax.broadcasted_iota(jnp.int32, (width, LANES), 0)
    lane = lax.broadcasted_iota(jnp.int32, (width, LANES), 1)
    member = (lax.div(feature, width // heads) == lane).astype(BF16)
    high = value.astype(BF16)
    return dot(high, member) + dot((value - high.astype(F32)).astype(BF16), member)


def backward_kernel(
    heads, rows, docs, me, group_map, doc_lengths, skip, q_ref, d_ref, out_ref, term_ref, k_ref, v_ref, kaug_ref,
    dq_ref, drow_ref, dk_ref, dv_ref, dcol_ref, acc_ref, qcat_ref, dcat_ref, dk_acc, dv_acc, dcol_acc,
):
    step = pl.program_id(0)

    @pl.when(step == 0)
    def _():
        acc_ref[...] = jnp.zeros_like(acc_ref)
        spread_heads(q_ref, row_pieces(term_ref[...], True), put_rows(qcat_ref), heads)
        delta = head_sums(d_ref[...].astype(F32) * out_ref[...], heads)
        spread_heads(d_ref, row_pieces(-delta, False), put_rows(dcat_ref), heads)

    dk_acc[...] = jnp.zeros_like(dk_acc)
    dv_acc[...] = jnp.zeros_like(dv_acc)
    dcol_acc[...] = jnp.zeros_like(dcol_acc)

    def tile(qi, ki, mask):
        q_rows = pl.ds(qi * rows, rows)
        k_rows = pl.ds(ki * rows, rows)
        aug = kaug_ref[k_rows, :]
        for pair in range(heads // 2):
            lanes = pl.ds(pair * LANES, LANES)
            keys = jnp.concatenate([k_ref[pair, k_rows, :], aug], axis=1)
            values = jnp.concatenate([v_ref[pair, k_rows, :], aug], axis=1)
            for h in (2 * pair, 2 * pair + 1):
                probs = jnp.exp(contract_cols(keys, qcat_ref[h, q_rows, :]))
                if mask is not None:
                    probs = jnp.where(mask, probs, 0.0)
                grads = (probs * contract_cols(values, dcat_ref[h, q_rows, :])).astype(BF16)
                dv_acc[k_rows, lanes] += dot(probs.astype(BF16), dcat_ref[h, q_rows, :LANES])
                both = dot(grads, qcat_ref[h, q_rows, :])
                dk_acc[k_rows, lanes] += both[:, :LANES]
                dcol_acc[k_rows, :] += both[:, LANES:]
                acc_ref[h, q_rows, :] += contract_rows(grads, keys)

    for ki in range(2):
        key_group = group_map[2 * step + ki]
        for qi in range(2):
            query_group = group_map[2 * me[0] + qi]
            active, full = block_state(group_map, doc_lengths, skip, query_group, key_group, rows, docs)

            @pl.when(active & full)
            def _(qi=qi, ki=ki):
                tile(qi, ki, None)

            @pl.when(active & jnp.logical_not(full))
            def _(qi=qi, ki=ki, query_group=query_group, key_group=key_group):
                tile(qi, ki, block_mask(doc_lengths, query_group, key_group, rows, docs, 1))

    dk_ref[0] = dk_acc[...].astype(BF16)
    dv_ref[0] = dv_acc[...].astype(BF16)
    dcol_ref[0] = -(dcol_acc[...].T[:8])

    @pl.when(step == pl.num_programs(0) - 1)
    def _():
        total_rows = dq_ref.shape[0]
        low = low_lanes(total_rows)
        lane = lax.broadcasted_iota(jnp.int32, (total_rows, LANES), 1)
        sums = jnp.zeros((total_rows, LANES), F32)
        for pair in range(heads // 2):
            a, b = 2 * pair, 2 * pair + 1
            dq_ref[:, pair * LANES : (pair + 1) * LANES] = jnp.where(
                low, acc_ref[a, :, :LANES], acc_ref[b, :, :LANES]
            )
            sums = jnp.where(
                lane == 24 + a, acc_ref[a, :, LANES:], jnp.where(lane == 24 + b, acc_ref[b, :, LANES:], sums)
            )
        drow_ref[...] = pltpu.roll(sums, LANES - 24, 1).T[:8]


def backward_attention(me, group_map, doc_lengths, skip, queries, grads, attended, term, keys, values, key_aug, heads):
    total = keys.shape[1]
    own, width = queries.shape
    rows = own // 2
    n = total // own
    docs = doc_lengths.shape[0]
    return pl.pallas_call(
        functools.partial(backward_kernel, heads, rows, docs),
        grid=(n,),
        out_shape=[
            jax.ShapeDtypeStruct((own, width), F32),
            jax.ShapeDtypeStruct((8, own), F32),
            jax.ShapeDtypeStruct((n, own, width), BF16),
            jax.ShapeDtypeStruct((n, own, width), BF16),
            jax.ShapeDtypeStruct((n, 8, own), F32),
        ],
        in_specs=[smem(), smem(), smem(), smem()]
        + [
            whole((own, width)),
            whole((own, width)),
            whole((own, width)),
            whole((own, LANES)),
            pl.BlockSpec((heads // 2, own, LANES), lambda i: (0, i, 0)),
            pl.BlockSpec((heads // 2, own, LANES), lambda i: (0, i, 0)),
            pl.BlockSpec((own, LANES), lambda i: (i, 0)),
        ],
        out_specs=[
            whole((own, width)),
            whole((8, own)),
            pl.BlockSpec((1, own, width), lambda i: (i, 0, 0)),
            pl.BlockSpec((1, own, width), lambda i: (i, 0, 0)),
            pl.BlockSpec((1, 8, own), lambda i: (i, 0, 0)),
        ],
        scratch_shapes=[
            VMEM((heads, own, 2 * LANES), F32),
            VMEM((heads, own, 2 * LANES), BF16),
            VMEM((heads, own, 2 * LANES), BF16),
            VMEM((own, width), F32),
            VMEM((own, width), F32),
            VMEM((own, LANES), F32),
        ],
        compiler_params=pltpu.CompilerParams(vmem_limit_bytes=VMEM_LIMIT),
        cost_estimate=pl.CostEstimate(
            flops=own * total * width * 10, bytes_accessed=total * width * 8, transcendentals=own * total * heads
        ),
    )(me, group_map, doc_lengths, skip, queries, grads, attended, term, keys, values, key_aug)


def on_device(
    hidden_in,
    norm_one,
    w_query,
    w_key,
    w_value,
    w_gate_out,
    w_forget,
    forget_bias,
    head_gains,
    w_output,
    norm_two,
    w_gate,
    w_up,
    w_down,
    out_grad,
    doc_lengths,
    group_map,
    skip_list,
):
    device_ctx = lax.axis_index("ctx")
    device_tp = lax.axis_index("tp")
    n = lax.axis_size("ctx")
    row_count, model_width = hidden_in.shape
    group_rows = row_count // 2
    heads = forget_bias.shape[0]
    shard = norm_one.shape[0]
    gain_rows = head_gains.shape[0]
    head_dim = gain_rows * n // 2
    width = heads * head_dim
    hidden_width = w_gate.shape[1]

    slots = 2 * n
    earlier = jnp.pad(
        (group_map[:, None] < group_map[None, :]).astype(F32), ((0, LANES - slots), (0, LANES - slots))
    )

    def lanes_of(value, first_rows, last_rows):
        return jnp.pad(value, ((first_rows, last_rows), (0, 256 - value.shape[1])))

    small = jnp.concatenate(
        [
            lanes_of(jnp.stack([norm_one, norm_two]), 0, 0),
            lanes_of(head_gains.T, 0, 6 - heads),
            lanes_of(w_forget.T, 0, 8 - heads),
        ],
        axis=0,
    )
    (
        query_weight,
        key_weight,
        value_weight,
        gate_out_weight,
        output_weight,
        normed_shards,
        query_rows,
        query_raw,
        key_raw,
        gate_logit,
        forget_logit,
        keys_all,
        values_all,
        key_aug,
        attended_flat,
        row_term,
        gain_one,
        gain_two,
        query_gain,
        key_gain,
        forget_weight,
    ) = start_forward(
        n, 1, group_map, doc_lengths, skip_list, earlier, hidden_in, small, forget_bias, [w_query, w_key, w_value, w_gate_out], w_output
    )
    half = width // 256 * 128
    me_one = device_ctx.astype(jnp.int32).reshape(1)
    fused = n <= 8
    (
        gated,
        layer_out,
        down_share,
        gate_share,
        up_share,
        grad_middle,
        grad_attended,
        grad_gate_logit,
        gain_two_parts,
        *attention_grads,
    ) = feed_forward(
        n,
        3,
        heads,
        attended_flat,
        gate_logit,
        output_weight,
        hidden_in,
        gain_two,
        out_grad,
        w_gate,
        w_up,
        w_down,
        (group_map, doc_lengths, skip_list, query_rows, row_term, keys_all, values_all, key_aug) if fused else None,
    )
    if not fused:
        grad_branch = grad_middle.astype(BF16).reshape(row_count, n, shard).transpose(1, 0, 2)
        attention_grads = grad_branch, *backward_attention(
            me_one,
            group_map,
            doc_lengths,
            skip_list,
            query_rows,
            grad_attended,
            attended_flat,
            row_term,
            keys_all,
            values_all,
            key_aug,
            heads,
        )
    grad_branch, grad_query, row_sums, key_part, value_part, column_sums = attention_grads

    gate_plan = [
        [(width, (1, 1 + i, 0, width)), (w, (0, 0, c, w))] for i, (c, w) in enumerate([(0, half), (half, width - half)])
    ]
    attn_plan = [[(half, (i, 0, half)), (width - half, (i, half, width - half))] for i in (0, 1)]
    own_groups = lax.dynamic_slice_in_dim(group_map, device_ctx * 2, 2, 0)
    later = (group_map[None, :] > own_groups[:, None]).astype(F32)
    if fused:
        (
            query_share,
            key_share,
            value_share,
            gate_out_share,
            output_share,
            small_share,
            input_grad,
        ) = finish_backward(
            n,
            7,
            heads,
            gate_plan,
            attn_plan,
            key_part,
            value_part,
            column_sums,
            row_sums,
            grad_query,
            query_raw,
            key_raw,
            query_gain,
            key_gain,
            forget_logit,
            jnp.pad(later, ((0, 6), (0, LANES - slots))),
            query_weight,
            key_weight,
            value_weight,
            gate_out_weight,
            forget_weight,
            grad_gate_logit,
            normed_shards,
            grad_branch,
            gated,
            hidden_in,
            gain_one,
            grad_middle,
            gain_two_parts,
        )
    else:
        query_gain, key_gain = (gain.reshape(heads, head_dim) for gain in (query_gain, key_gain))
        query_raw, key_raw = (raw.reshape(row_count, heads, head_dim) for raw in (query_raw, key_raw))
        query_norm, key_norm = rms_scale(query_raw), rms_scale(key_raw)
        forget_logit = forget_logit[:heads].T
        forget_weight = forget_weight[:heads].astype(BF16)
        normed_one = normed_shards.transpose(1, 0, 2).reshape(row_count, model_width)
        place = jnp.arange(group_rows, dtype=jnp.int32)
        upper = (place[:, None] <= place[None, :]).astype(F32)
        grad_key, grad_value, off_sum, tot_sum = pair_scatter(n, 7, key_part, value_part, column_sums, row_sums)
        after = contract_cols_exact(tot_sum[:heads, :slots], later)
        suffix = lax.dot_general(
            off_sum[:heads].reshape(heads, 2, group_rows), upper, (((2,), (1,)), ((), ())), precision=HIGHEST
        )
        grad_log_forget = (suffix + after[:, :, None]).reshape(heads, row_count).T
        grad_key3 = grad_key.reshape(row_count, heads, head_dim)
        grad_query3 = grad_query.reshape(row_count, heads, head_dim)
        key_raw_grad = rms_back(grad_key3 * key_gain, key_raw).astype(BF16).reshape(row_count, width)
        query_raw_grad = (
            rms_back(grad_query3 * query_gain * 0.125, query_raw).astype(BF16).reshape(row_count, width)
        )
        value_low = grad_value.astype(BF16)
        query_gain_grad = jnp.sum(grad_query3 * query_norm * 0.125, axis=0)
        key_gain_grad = jnp.sum(grad_key3 * key_norm, axis=0)
        head_gain_grad = jnp.concatenate([query_gain_grad, key_gain_grad], axis=1)
        grad_forget_logit = (grad_log_forget * jax.nn.sigmoid(-forget_logit)).astype(BF16)
        bias_part = jnp.sum(grad_forget_logit.astype(F32), axis=0)
        normed_one_part = (
            contract_cols(query_raw_grad, query_weight)
            + contract_cols(key_raw_grad, key_weight)
            + contract_cols(value_low, value_weight)
            + contract_cols(grad_gate_logit, gate_out_weight)
            + dot(grad_forget_logit, forget_weight)
        )
        forget_grad = contract_rows(grad_forget_logit, normed_one)

        def wide(value):
            return jnp.pad(value, ((0, 0), (0, 0), (0, 256 - value.shape[2])))

        forget_rows = wide(forget_grad.reshape(heads, n, shard).transpose(1, 0, 2))
        forget_rows = forget_rows.at[:, :, 224].set(bias_part[None, :])
        small_grad = jnp.concatenate(
            [
                jnp.zeros((n, 1, 256), F32),
                wide(jnp.sum(gain_two_parts, axis=0).reshape(n, 1, shard)),
                wide(head_gain_grad.reshape(heads, n, gain_rows).transpose(1, 0, 2)),
                jnp.pad(forget_rows, ((0, 0), (0, 8 - heads), (0, 0))),
            ],
            axis=1,
        )
        lefts, rights = (1, 0), (4, 0, 3)
        plan = [
            [(w, (0, 1 + i, c0, cw)) for w, (i, c0, cw) in attn]
            + [(w, (lefts[left], rights[right], c0, cw)) for w, (left, right, c0, cw) in gate]
            for attn, gate in zip(attn_plan, gate_plan)
        ]
        (
            query_share,
            key_share,
            value_share,
            gate_out_share,
            output_share,
            small_share,
            input_grad,
        ) = weight_scatter(
            n,
            8,
            plan,
            [normed_shards, grad_branch],
            [query_raw_grad, key_raw_grad, value_low, grad_gate_logit, gated],
            small_grad,
            normed_one_part,
            hidden_in,
            gain_one,
            grad_middle,
        )
    return (
        layer_out,
        input_grad,
        small_share[0, :shard],
        query_share,
        key_share,
        value_share,
        gate_out_share,
        small_share[8 : 8 + heads, :shard].T,
        small_share[8 : 8 + heads, 224],
        small_share[2 : 2 + heads, :gain_rows].T,
        output_share,
        small_share[1, :shard],
        gate_share,
        up_share,
        down_share,
    )


def solution(mesh):
    split = P("ctx", "tp")
    in_specs = (
        P("ctx", None),
        P("ctx"),
        split,
        split,
        split,
        split,
        split,
        P("tp"),
        split,
        split,
        P("ctx"),
        split,
        split,
        split,
        P("ctx", None),
        P(),
        P(),
        P(),
    )
    out_specs = (
        split,
        P("ctx", None),
        P("ctx"),
        split,
        split,
        split,
        split,
        split,
        P("tp"),
        split,
        split,
        P("ctx"),
        split,
        split,
        split,
    )
    return jax.shard_map(on_device, mesh=mesh, in_specs=in_specs, out_specs=out_specs, check_vma=False)
```

```python
import functools

import jax
import jax.numpy as jnp
from jax import lax
from jax.experimental import pallas as pl
from jax.experimental.pallas import tpu as pltpu
from jax.sharding import PartitionSpec as P

EPS = 1e-06
HIGHEST = lax.Precision.HIGHEST
MESH = pl.DeviceIdType.MESH
VMEM = pltpu.VMEM
VMEM_LIMIT = 62 * 1024 * 1024
F32 = jnp.float32
BF16 = jnp.bfloat16


def rms_scale(value):
    return value * lax.rsqrt(jnp.mean(value * value, axis=-1, keepdims=True) + EPS)


def rms_back(grad_in, value):
    inverse = lax.rsqrt(jnp.mean(value * value, axis=-1, keepdims=True) + EPS)
    normal = value * inverse
    return inverse * (grad_in - normal * jnp.mean(grad_in * normal, axis=-1, keepdims=True))


def dot(left, right):
    return jnp.dot(left, right, preferred_element_type=F32)


def contract_cols(left, right):
    return lax.dot_general(left, right, (((1,), (1,)), ((), ())), preferred_element_type=F32)


def contract_cols_exact(left, right):
    return lax.dot_general(left, right, (((1,), (1,)), ((), ())), precision=HIGHEST)


def contract_rows(left, right):
    return lax.dot_general(left, right, (((0,), (0,)), ((), ())), preferred_element_type=F32)


def ring_place(ctx, n):
    odd = lax.rem(ctx, 2)
    half = lax.div(ctx, 2)
    return (1 - odd) * half + odd * (n - 1 - half)


def ring_owner(place, n):
    late = lax.div(place, n // 2)
    return (1 - late) * (2 * place) + late * (2 * (n - 1 - place) + 1)


def wrap(place, n):
    return lax.rem(place + 2 * n, n)


def ring_setup(n):
    me = lax.axis_index("ctx")
    tp = lax.axis_index("tp")
    place = ring_place(me, n)
    right = ring_owner(wrap(place + 1, n), n)
    left = ring_owner(wrap(place - 1, n), n)
    return me, tp, place, (right, left)


def greet(peers):
    barrier = pltpu.get_barrier_semaphore()
    for peer in peers:
        pl.semaphore_signal(barrier, inc=1, device_id=peer, device_id_type=MESH)
    pl.semaphore_wait(barrier, len(peers))


def ctx_peers(me, tp, n):
    return [(lax.rem(me + i, n), tp) for i in range(1, n)]


def remote(src, dst, send, recv, device):
    return pltpu.make_async_remote_copy(
        src_ref=src, dst_ref=dst, send_sem=send, recv_sem=recv, device_id=device, device_id_type=MESH
    )


class Gather:
    def __init__(self, n, place, sides, tp, chunks, send, recv):
        self.n, self.place, self.sides, self.tp = n, place, sides, tp
        self.chunks, self.send, self.recv = chunks, send, recv
        self.arrived = None

    def owner(self, side, back):
        return ring_owner(wrap(self.place - back if side == 0 else self.place + back, self.n), self.n)

    def copy(self, index, step, first):
        side, source, target = self.chunks[index]
        target = target(self.owner(side, step))
        return remote(
            source if first else target, target, self.send.at[index, step], self.recv.at[index, step],
            (self.sides[side], self.tp),
        )

    def arrive(self, index, step):
        side, _, target = self.chunks[index]
        target = target(self.owner(side, step + 1))
        remote(
            target, target, self.send.at[index, step], self.recv.at[index, step], (self.sides[side], self.tp)
        ).wait_recv()
        if self.arrived is not None:
            self.arrived(index, step)

    def begin(self, indices=None):
        for index in indices if indices is not None else range(len(self.chunks)):
            self.copy(index, 0, True).start()

    def forward(self, step):
        for index in range(len(self.chunks)):
            self.arrive(index, step - 1)
            self.copy(index, step, False).start()

    def last(self):
        for index in range(len(self.chunks)):
            self.arrive(index, self.n - 2)

    def sent(self):
        def finish(step, carry):
            for index in range(len(self.chunks)):
                self.copy(index, step, False).wait_send()
            return carry

        lax.fori_loop(0, self.n - 1, finish, 0)


class Moves:
    def __init__(self, semaphores):
        self.semaphores, self.count, self.open = semaphores, 0, {}

    def start(self, name, source, target):
        copy = pltpu.make_async_copy(source, target, self.semaphores.at[self.count])
        self.count += 1
        copy.start()
        self.open[name] = copy

    def wait(self, *names):
        for name in names or list(self.open):
            self.open.pop(name).wait()


def start_kernel(
    n, heads, group_map, doc_lengths, skip, bias_ref, x_ref, norm_one, norm_two, gains_in, forget_in,
    wq_in, wk_in, wv_in, wg_in, wo_in,
    wq_out, wk_out, wv_out, wg_out, wo_ref, u_out, q_out, qr_out, kr_out, gl_out, fz_ref, k_out, v_out, aug_out,
    att_out, term_ref, gain_one, gain_two, qgain_ref, kgain_ref, wf_ref,
    x_vmem, wq_ref, wk_ref, wv_ref, wg_ref, u_ref, q_ref, k_all, v_all, aug_ref, att_ref, acc_ref, cat_ref,
    diff_ref, span_ref, tot_ref, before_ref, inside_all, small_wide, small_in,
    small_all, acc_r, acc_l, inside_src,
    wsend, wrecv, osend, orecv, ksend, krecv, ssend, srecv, isend, irecv, spill, local,
):
    me, tp, place, sides = ring_setup(n)
    moves = Moves(local)
    moves.start("x", x_ref, x_vmem)
    shard, width = wq_in.shape
    small_wide[...] = jnp.zeros_like(small_wide)
    small_wide[0:1, :shard] = norm_one[...].astype(F32).reshape(1, shard)
    small_wide[1:2, :shard] = norm_two[...].astype(F32).reshape(1, shard)
    for ref, first in ((gains_in, 2), (forget_in, 8)):
        size = ref.shape[0]
        same = lax.broadcasted_iota(jnp.int32, (size, size), 0) == lax.broadcasted_iota(jnp.int32, (size, size), 1)
        small_wide[first : first + heads, :size] = contract_rows(ref[...], same.astype(BF16))
    small_in[...] = small_wide[...].astype(BF16)
    greet(ctx_peers(me, tp, n))
    rows, cols = x_ref.shape
    half = rows // 2
    head_dim = width // heads

    def shard_rows(owner):
        return pl.ds(pl.multiple_of(owner * shard, 16), shard)

    def window(ref, c0, cw):
        return lambda owner: ref.at[shard_rows(owner), pl.ds(c0, cw)]

    def token_rows(owner):
        return pl.ds(pl.multiple_of(owner * rows, rows), rows)

    def block(ref, pair):
        return lambda owner: ref.at[pair, token_rows(owner), :]

    ring = (n, place, sides, tp)
    projections = Gather(
        *ring,
        [
            (side, source, window(target, 0, width))
            for side, source, target in ((0, wq_in, wq_ref), (1, wv_in, wv_ref), (0, wk_in, wk_ref), (1, wg_in, wg_ref))
        ],
        wsend, wrecv,
    )
    middle = width // 256 * 128
    outputs = Gather(
        *ring,
        [
            (side, wo_in.at[:, pl.ds(c0, cw)], window(wo_ref, c0, cw))
            for side, c0, cw in ((0, 0, middle), (1, middle, width - middle))
        ],
        osend, orecv,
    )
    members = [(0, k_all, k_out, 0), (1, k_all, k_out, 2), (0, v_all, v_out, 0), (1, v_all, v_out, 2)]
    members += [(0, k_all, k_out, 1), (1, v_all, v_out, 1)]
    pairs = Gather(
        *ring, [(side, block(ref, pair)(me), block(ref, pair)) for side, ref, _, pair in members], ksend, krecv
    )

    def spill_copy(index, step):
        side, ref, out, pair = members[index]
        owner = pairs.owner(side, step + 1)
        return pltpu.make_async_copy(
            block(ref, pair)(owner), block(out, pair)(owner), spill.at[index, step]
        )

    pairs.arrived = lambda index, step: spill_copy(index, step).start()

    projections.begin()
    exchange_start(n, me, tp, lambda peer: small_in, small_all, ssend, srecv)
    gathered = ((wq_in, wq_ref), (wk_in, wk_ref), (wv_in, wv_ref), (wg_in, wg_ref), (wo_in, wo_ref))
    for i, (source, target) in enumerate(gathered):
        moves.start(i, source, target.at[shard_rows(me)])
    moves.start("small", small_in, small_all.at[me])
    moves.wait("small")
    exchange_wait(n, me, tp, lambda peer: small_in, small_all, ssend, srecv)
    projections.forward(1)

    count = 2 * head_dim // n
    for i in range(n):
        block_small = small_all[i].astype(F32)
        gain_one[:, i * shard : (i + 1) * shard] = block_small[0:1, :shard]
        gain_two[:, i * shard : (i + 1) * shard] = block_small[1:2, :shard]
        wf_ref[:, i * shard : (i + 1) * shard] = block_small[8:16, :shard]
        target, at = (qgain_ref, i) if i < n // 2 else (kgain_ref, i - n // 2)
        for h in range(heads):
            lane = h * head_dim + at * count
            target[:, lane : lane + count] = block_small[2 + h : 3 + h, :count]

    size = 64

    def norm_rows(i, carry):
        here = pl.ds(pl.multiple_of(i * size, size), size)
        normed = (rms_scale(x_vmem[here, :].astype(F32)) * gain_one[...]).astype(BF16)
        for j in range(n):
            u_ref[j, here, :] = normed[:, j * shard : (j + 1) * shard]
        return carry

    moves.wait("x")
    lax.fori_loop(0, rows // size, norm_rows, 0)
    moves.start("u", u_ref, u_out)

    def grow(back):
        for side, acc, sources in ((0, acc_r, (wq_ref, wk_ref)), (1, acc_l, (wv_ref, wg_ref))):
            owner = projections.owner(side, back)
            for i, source in enumerate(sources):
                acc[:, i * width : (i + 1) * width] += dot(u_ref[owner], source[shard_rows(owner), :])

    acc_r[...] = jnp.zeros_like(acc_r)
    acc_l[...] = jnp.zeros_like(acc_l)
    moves.wait(0, 1, 2, 3, 4)
    grow(0)
    projections.forward(2)
    grow(1)
    grow(2)
    forget = jnp.zeros((16, rows), F32)
    for j in range(n):
        forget += contract_cols(small_all[j, :, :shard], u_ref[j])
    head = lax.broadcasted_iota(jnp.int32, (8, rows), 0)
    fz = forget[8:16]
    for h in range(heads):
        fz = jnp.where(head == h, fz + bias_ref[h], fz)
    fz_ref[...] = fz
    logs = jnp.minimum(fz, 0.0) - jnp.log1p(jnp.exp(-jnp.abs(fz)))
    logs = jnp.where(head < heads, logs, 0.0)
    upto = (
        lax.broadcasted_iota(jnp.int32, (half, half), 0) <= lax.broadcasted_iota(jnp.int32, (half, half), 1)
    ).astype(F32)
    for g in range(2):
        inside_src[:, g * half : (g + 1) * half] = jnp.dot(
            logs[:, g * half : (g + 1) * half], upto, precision=HIGHEST, preferred_element_type=F32
        )
    exchange_start(n, me, tp, lambda peer: inside_src, inside_all, isend, irecv)
    moves.start("inside", inside_src, inside_all.at[me])

    def step_on(step, carry):
        projections.forward(step)
        grow(step)
        return carry

    lax.fori_loop(3, n - 2, step_on, 0)
    outputs.begin()
    projections.forward(n - 2)
    grow(n - 2)
    outputs.forward(1)
    projections.last()
    grow(n - 1)

    def head_norm(value):
        return value * lax.rsqrt(head_means(value * value, heads) + EPS)

    my_rows = token_rows(me)
    for pair in range(heads // 2):
        v_all[pair, my_rows, :] = acc_l[:, pair * LANES : (pair + 1) * LANES].astype(BF16)
    pairs.begin([2, 3, 5])
    keys = (head_norm(acc_r[:, width:]) * kgain_ref[...]).astype(BF16)
    for pair in range(heads // 2):
        k_all[pair, my_rows, :] = keys[:, pair * LANES : (pair + 1) * LANES]
    pairs.begin([0, 1, 4])
    for i, (source, target) in enumerate(
        ((wq_ref, wq_out), (wk_ref, wk_out), (wv_ref, wv_out), (wg_ref, wg_out))
    ):
        moves.start(i, source, target)
    moves.start("qr", acc_r.at[:, pl.ds(0, width)], qr_out)
    moves.start("kr", acc_r.at[:, pl.ds(width, width)], kr_out)
    moves.start("gl", acc_l.at[:, pl.ds(width, width)], gl_out)
    for i, (ref, out) in enumerate(((k_all, k_out), (v_all, v_out))):
        for pair in range(heads // 2):
            moves.start((i, pair), block(ref, pair)(me), block(out, pair)(me))
    q_ref[...] = (head_norm(acc_r[:, :width]) * qgain_ref[...] * 0.125).astype(BF16)
    moves.start("q", q_ref, q_out)

    moves.wait("inside")
    exchange_wait(n, me, tp, lambda peer: inside_src, inside_all, isend, irecv)
    tot_ref[...] = jnp.zeros_like(tot_ref)
    for i in range(n):
        for g in range(2):
            tot_ref[:, 2 * i + g : 2 * i + g + 1] = inside_all[i, :, (g + 1) * half - 1 : (g + 1) * half]
    earlier = groups_along(group_map, 0, 1 << 20) < groups_along(group_map, 1, 1 << 20)
    before_ref[...] = jnp.dot(
        tot_ref[...], earlier.astype(F32), precision=HIGHEST, preferred_element_type=F32
    )
    lane8 = lax.broadcasted_iota(jnp.int32, (8, LANES), 1)

    def offsets_of(shard_index):
        parts = []
        for g in range(2):
            before = jnp.sum(jnp.where(lane8 == 2 * shard_index + g, before_ref[...], 0.0), axis=1, keepdims=True)
            parts.append(inside_all[shard_index, :, g * half : (g + 1) * half] + before)
        return jnp.concatenate(parts, axis=1)

    def aug_rows(i, carry):
        aug_ref[token_rows(i), :] = key_pieces(offsets_of(i))
        return carry

    pairs.forward(1)
    lax.fori_loop(0, n, aug_rows, 0)
    moves.start("aug", aug_ref, aug_out)

    first, second = group_map[2 * me], group_map[2 * me + 1]
    in_order = first < second
    query_groups = (jnp.minimum(first, second), jnp.maximum(first, second))
    mine = turn(offsets_of(me))
    term_ref[...] = mine
    spread_heads(q_ref, row_pieces(mine, True), put_rows(cat_ref), heads, in_order)
    acc_ref[...] = jnp.zeros_like(acc_ref)
    query_at = lax.broadcasted_iota(jnp.int32, (half, half), 0)
    key_at = lax.broadcasted_iota(jnp.int32, (half, half), 1)
    diff_ref[...] = key_at - query_at
    for i, group in enumerate(query_groups):
        span_ref[i] = document_start(group * half + query_at, doc_lengths) - key_at
    ones = jnp.ones((half, LANES), BF16)

    def attend(i, back):
        late = lax.div(i, 2)
        pair = (1 - late) * 2 * i + late
        side = lax.rem(i, 2)
        owner = ring_owner(wrap(place + (2 * side - 1) * back, n), n)
        one, two = group_map[2 * owner], group_map[2 * owner + 1]
        forward = one < two
        key_groups = (jnp.minimum(one, two), jnp.maximum(one, two))
        top = pl.ds(pl.multiple_of(owner * rows, rows), half)
        bottom = pl.ds(pl.multiple_of(owner * rows + half, half), half)
        blocks = []
        for ref in (k_all.at[pair], v_all.at[pair], aug_ref):
            blocks.append(in_pack_order(forward, ref[top, :], ref[bottom, :]))
        masks = block_masks(diff_ref, span_ref, skip, query_groups, key_groups, half)
        keys = [jnp.concatenate([blocks[0][ki], blocks[2][ki]], axis=1) for ki in range(2)]
        values = [jnp.concatenate([blocks[1][ki], ones], axis=1) for ki in range(2)]
        both_values = jnp.concatenate(values, axis=0)
        for e in range(2):
            h = 2 * pair + e
            queries = cat_ref[h]
            early = contract_cols(queries, keys[0])
            weights = [
                jnp.where(mask, jnp.exp(score), 0.0).astype(BF16)
                for mask, score in zip(masks, (early[:half], early[half:], contract_cols(queries[half:], keys[1])))
            ]
            acc_ref[h, :half, :] += dot(weights[0], values[0])
            acc_ref[h, half:, :] += dot(jnp.concatenate(weights[1:], axis=1), both_values)

    def attend_all(count, back):
        def body(i, carry):
            attend(i, back)
            return carry

        lax.fori_loop(0, count, body, 0)

    attend_all(3, 0)
    attend_all(2, 1)

    def pair_step(step, count):
        outputs.forward(step)
        pairs.forward(step)
        attend_all(count, step)

    def early_step(step, carry):
        pair_step(step, 2)
        return carry

    def late_step(step, carry):
        pair_step(step, 4)
        return carry

    lax.fori_loop(2, n // 2, early_step, 0)
    pair_step(n // 2, 3)
    lax.fori_loop(n // 2 + 1, n - 1, late_step, 0)
    outputs.last()
    pairs.last()
    attend_all(4, n - 1)

    lane = lax.broadcasted_iota(jnp.int32, (rows, LANES), 1)
    low = low_lanes(rows)
    totals = jnp.ones((rows, LANES), F32)
    for pair in range(heads // 2):
        parts = []
        for h in (2 * pair, 2 * pair + 1):
            value = jnp.concatenate(in_pack_order(in_order, acc_ref[h, :half, :], acc_ref[h, half:, :]), axis=0)
            parts.append(value)
            totals = jnp.where(lane == h, value[:, LANES:], totals)
        att_ref[:, pair * LANES : (pair + 1) * LANES] = jnp.where(
            low, parts[0][:, :LANES], parts[1][:, :LANES]
        ) / jnp.where(low, parts[0][:, LANES:], parts[1][:, LANES:])
    moves.start("att", att_ref, att_out)
    term_ref[...] -= jnp.log(totals)

    def spilled(step, carry):
        for index in range(len(members)):
            spill_copy(index, step).wait()
        return carry

    lax.fori_loop(0, n - 1, spilled, 0)
    moves.wait()
    projections.sent()
    outputs.sent()
    pairs.sent()


def groups_along(group_map, dim, fill, shape=(128, 128)):
    slot = lax.broadcasted_iota(jnp.int32, shape, dim)
    groups = jnp.full(shape, fill, jnp.int32)
    for i in range(group_map.shape[0]):
        groups = jnp.where(slot == i, group_map[i], groups)
    return groups


def start_forward(n, collective_id, group_map, doc_lengths, skip, bias, x, vectors, weights, out_weight):
    rows, cols = x.shape
    shard, width = out_weight.shape
    heads = bias.shape[0]
    half = rows // 2
    dma = pltpu.SemaphoreType.DMA
    vmem = pl.BlockSpec(memory_space=VMEM)
    anywhere = pl.BlockSpec(memory_space=pl.ANY)
    by_pair = (heads // 2, n * rows, LANES)
    weight, wide, narrow = (n * shard, width), (rows, cols), (rows, width)
    shapes = (
        [(weight, BF16)] * 5
        + [((n, rows, shard), BF16), (narrow, BF16)]
        + [(narrow, F32)] * 3
        + [((8, rows), F32)]
        + [(by_pair, BF16)] * 2
        + [((n * rows, LANES), BF16), (narrow, F32), ((rows, LANES), F32)]
        + [((1, cols), F32)] * 2
        + [((1, width), F32)] * 2
        + [((8, cols), F32)]
    )
    return pl.pallas_call(
        functools.partial(start_kernel, n, heads),
        out_shape=[jax.ShapeDtypeStruct(*shape) for shape in shapes],
        in_specs=[smem(), smem(), smem(), smem(), anywhere] + [vmem] * 4 + [anywhere] * 5,
        out_specs=[anywhere if i < 10 or 11 <= i <= 14 else vmem for i in range(len(shapes))],
        scratch_shapes=[
            VMEM(wide, BF16),
            *[VMEM(weight, BF16)] * 4,
            VMEM((n, rows, shard), BF16),
            VMEM(narrow, BF16),
            *[VMEM(by_pair, BF16)] * 2,
            VMEM((n * rows, LANES), BF16),
            VMEM(narrow, F32),
            VMEM((heads, rows, 2 * LANES), F32),
            VMEM((heads, rows, 2 * LANES), BF16),
            VMEM((half, half), jnp.int32),
            VMEM((2, half, half), jnp.int32),
            VMEM((8, LANES), F32),
            VMEM((8, LANES), F32),
            VMEM((n, 8, rows), F32),
            VMEM((16, 256), F32),
            VMEM((16, 256), BF16),
            VMEM((n, 16, 256), BF16),
            VMEM((rows, 2 * width), F32),
            VMEM((rows, 2 * width), F32),
            VMEM((8, rows), F32),
            *[dma((4, n - 1))] * 2,
            *[dma((2, n - 1))] * 2,
            *[dma((6, n - 1))] * 2,
            *[dma((n - 1,))] * 4,
            dma((6, n - 1)),
            dma((26,)),
        ],
        compiler_params=pltpu.CompilerParams(
            collective_id=collective_id, has_side_effects=True, vmem_limit_bytes=VMEM_LIMIT
        ),
    )(group_map, doc_lengths, skip, bias, x, *vectors, *weights, out_weight)


class ScatterRing:
    def __init__(self, n, plan, local_term, slots, firsts, write, send, recv, place, sides, tp, source=None):
        self.n, self.place, self.sides, self.tp = n, place, sides, tp
        self.source, self.next = source, 1
        self.local_term, self.write = local_term, write
        self.slots, self.firsts, self.send, self.recv = slots, firsts, send, recv
        self.order = []
        starts = [0, 0]
        for index in range(max(len(plan[0]), len(plan[1]))):
            for side in (0, 1):
                if index < len(plan[side]):
                    width, tag = plan[side][index]
                    self.order.append((side, index, starts[side], width, tag))
                    starts[side] += width

    def target(self, side, step):
        step = -1 - step if side == 0 else 1 + step
        return ring_owner(wrap(self.place + step, self.n), self.n)

    def hop(self, side, index, start, width, step, first):
        cols = pl.ds(start, width)
        slots = self.slots[side]
        if not first:
            source = slots.at[step - 1, :, cols]
        elif self.source is None:
            source = self.firsts[side].at[:, cols]
        else:
            source = self.source(self.target(side, 0), side, cols)
        return remote(
            source,
            slots.at[step, :, cols],
            self.send.at[side, index, step],
            self.recv.at[side, index, step],
            (self.sides[side], self.tp),
        )

    def begin(self):
        for side, index, start, width, tag in self.order:
            if self.source is None:
                term = self.local_term(self.target(side, 0), tag)
                self.firsts[side][:, start : start + width] = term.astype(BF16)
            self.hop(side, index, start, width, 0, True).start()

    def forward(self, step):
        for side, index, start, width, tag in self.order:
            term = self.local_term(self.target(side, step), tag)
            slot = self.slots[side].at[step - 1, :, pl.ds(start, width)]
            self.hop(side, index, start, width, step - 1, True).wait_recv()
            slot[...] = (slot[...].astype(F32) + term).astype(BF16)
            self.hop(side, index, start, width, step, False).start()

    def span(self, first, last):
        def body(step, carry):
            self.forward(step)
            return carry

        if last > first:
            lax.fori_loop(first, last, body, 0)

    def advance(self, count):
        last = min(self.next + count, self.n - 1)
        self.span(self.next, last)
        self.next = last

    def end(self):
        n = self.n
        self.advance(n)
        for side, index, start, width, tag in self.order:
            term = self.local_term(self.target(side, n - 1), tag)
            self.hop(side, index, start, width, n - 2, True).wait_recv()
            self.write(tag, self.slots[side][n - 2, :, start : start + width].astype(F32) + term)
        if self.source is None:
            self.sent()

    def sent(self):
        for side, index, start, width, tag in self.order:
            self.hop(side, index, start, width, 0, True).wait_send()

        def finish(step, carry):
            for side, index, start, width, tag in self.order:
                self.hop(side, index, start, width, step, False).wait_send()
            return carry

        lax.fori_loop(1, self.n - 1, finish, 0)


def exchange_start(n, me, tp, source_of, landing, send, recv):
    for i in range(1, n):
        peer = lax.rem(me + i, n)
        remote(source_of(peer), landing.at[me], send.at[i - 1], recv.at[i - 1], (peer, tp)).start()


def exchange_wait(n, me, tp, source_of, landing, send, recv):
    for i in range(1, n):
        peer = lax.rem(me - i + n, n)
        remote(source_of(peer), landing.at[peer], send.at[i - 1], recv.at[i - 1], (peer, tp)).wait()


def ordered_sum(n, landing):
    total = landing[0]
    for i in range(1, n):
        total = total + landing[i]
    return total


def pair_scatter_kernel(
    n, key_ref, value_ref, col_ref, row_ref, key_out, value_out, off_out, tot_out,
    slot_r, slot_l, first_r, first_l, off_ref, tot_ref, off_land, tot_land,
    send, recv, osend, orecv, tsend, trecv, local,
):
    me, tp, place, sides = ring_setup(n)
    off_ref[...] = col_ref[...]
    off_ref[me] += row_ref[...]
    group_rows = row_ref.shape[1] // 2
    tot_ref[...] = jnp.zeros_like(tot_ref)
    for i in range(n):
        for g in range(2):
            tot_ref[:, 2 * i + g : 2 * i + g + 1] = jnp.sum(
                off_ref[i, :, g * group_rows : (g + 1) * group_rows], axis=1, keepdims=True
            )
    greet(ctx_peers(me, tp, n))
    exchange_start(n, me, tp, lambda peer: off_ref.at[peer], off_land, osend, orecv)
    exchange_start(n, me, tp, lambda peer: tot_ref, tot_land, tsend, trecv)
    mine = pltpu.make_async_copy(off_ref.at[me], off_land.at[me], local.at[0])
    mine_tot = pltpu.make_async_copy(tot_ref, tot_land.at[me], local.at[1])
    mine.start()
    mine_tot.start()
    width = key_ref.shape[2]
    plan = [
        [(w, (0, c)) for c, w in pieces(width, 128)],
        [(w, (1, c)) for c, w in pieces(width, 128)],
    ]

    def local_term(owner, tag):
        which, c0 = tag
        return (key_ref, value_ref)[which][owner, :, c0 : c0 + 128].astype(F32)

    def write(tag, value):
        which, c0 = tag
        (key_out, value_out)[which][:, c0 : c0 + 128] = value

    ring = ScatterRing(
        n, plan, local_term, (slot_r, slot_l), (first_r, first_l), write, send, recv, place, sides, tp
    )
    ring.begin()
    ring.end()
    mine.wait()
    mine_tot.wait()
    exchange_wait(n, me, tp, lambda peer: off_ref.at[peer], off_land, osend, orecv)
    exchange_wait(n, me, tp, lambda peer: tot_ref, tot_land, tsend, trecv)
    off_out[...] = ordered_sum(n, off_land)
    tot_out[...] = ordered_sum(n, tot_land)


def pieces(width, step):
    return [(c, min(step, width - c)) for c in range(0, width, step)]


def pair_scatter(n, collective_id, keys, values, columns, own_rows):
    _, rows, width = keys.shape
    offs, tots = columns, jax.ShapeDtypeStruct((8, LANES), F32)
    chunks = len(pieces(width, 128))
    return pl.pallas_call(
        functools.partial(pair_scatter_kernel, n),
        out_shape=[
            jax.ShapeDtypeStruct((rows, width), F32),
            jax.ShapeDtypeStruct((rows, width), F32),
            jax.ShapeDtypeStruct(offs.shape[1:], F32),
            jax.ShapeDtypeStruct(tots.shape, F32),
        ],
        in_specs=[pl.BlockSpec(memory_space=VMEM)] * 4,
        out_specs=[pl.BlockSpec(memory_space=VMEM)] * 4,
        scratch_shapes=[
            VMEM((n - 1, rows, width), BF16),
            VMEM((n - 1, rows, width), BF16),
            VMEM((rows, width), BF16),
            VMEM((rows, width), BF16),
            VMEM(offs.shape, F32),
            VMEM(tots.shape, F32),
            VMEM(offs.shape, F32),
            VMEM((n,) + tots.shape, F32),
            pltpu.SemaphoreType.DMA((2, chunks, n - 1)),
            pltpu.SemaphoreType.DMA((2, chunks, n - 1)),
            pltpu.SemaphoreType.DMA((n - 1,)),
            pltpu.SemaphoreType.DMA((n - 1,)),
            pltpu.SemaphoreType.DMA((n - 1,)),
            pltpu.SemaphoreType.DMA((n - 1,)),
            pltpu.SemaphoreType.DMA((2,)),
        ],
        compiler_params=pltpu.CompilerParams(
            collective_id=collective_id, has_side_effects=True, vmem_limit_bytes=VMEM_LIMIT
        ),
    )(keys, values, columns, own_rows)


def weight_scatter_kernel(n, plan, left_count, grads, *refs):
    lefts, refs = refs[:left_count], refs[left_count:]
    rights, refs = refs[:grads], refs[grads:]
    small_ref, part_ref, x_ref, gain_ref, dmid_ref, refs = *refs[:5], refs[5:]
    outs, refs = refs[:grads], refs[grads:]
    small_out, input_out, slot_r, slot_l, first_r, first_l, own_small, land, sum_out, refs = *refs[:9], refs[9:]
    tp_bufs, refs = refs[:4], refs[4:]
    send, recv, xsend, xrecv, tsend, trecv, local = refs
    me, tp, place, sides = ring_setup(n)
    chip, core, sibling, across = tp_setup()
    greet(ctx_peers(me, tp, n) + [sibling, across])
    shard = lefts[0].shape[2]
    half = part_ref.shape[0] // 2

    def local_term(owner, tag):
        left, right, c0, cw = tag
        return contract_rows(lefts[left][owner], rights[right][:, c0 : c0 + cw])

    def write(tag, value):
        _, right, c0, cw = tag
        outs[right][:, c0 : c0 + cw] = value

    ring = ScatterRing(
        n, plan, local_term, (slot_r, slot_l), (first_r, first_l), write, send, recv, place, sides, tp
    )

    def part(which, c):
        cols = part_ref.shape[1] // TP_CHUNKS
        return part_ref[pl.ds(pl.multiple_of(which * half, half), half), c * cols : (c + 1) * cols].astype(F32)

    total = TpSum(part, sum_out, tp_bufs, tsend, trecv, core, sibling, across)
    total.first()
    total.second()
    ring.begin()
    total.third()
    ring.advance(1)
    total.fourth()

    own_small[...] = small_ref[...]
    cols = part_ref.shape[1]
    size = 64

    def gain_rows(i, acc):
        rows = pl.ds(pl.multiple_of(i * size, size), size)
        value = x_ref[rows, :].astype(F32)
        inverse = lax.rsqrt(jnp.mean(value * value, axis=-1, keepdims=True) + EPS)
        normal = value * inverse
        grad = sum_out[rows, :].astype(F32)
        back = grad * gain_ref[...]
        back = inverse * (back - normal * jnp.mean(back * normal, axis=-1, keepdims=True))
        input_out[rows, :] = dmid_ref[rows, :] + back
        return acc + jnp.sum((grad * normal).reshape(size // 8, 8, cols), axis=0)

    gains = lax.fori_loop(0, 2 * half // size, gain_rows, jnp.zeros((8, cols), F32))
    gains = jnp.sum(gains, axis=0, keepdims=True)
    for i in range(n):
        own_small[i, 0:1, :shard] = gains[:, i * shard : (i + 1) * shard]
    exchange_start(n, me, tp, lambda peer: own_small.at[peer], land, xsend, xrecv)
    mine = pltpu.make_async_copy(own_small.at[me], land.at[me], local.at[0])
    mine.start()
    ring.end()
    mine.wait()
    exchange_wait(n, me, tp, lambda peer: own_small.at[peer], land, xsend, xrecv)
    small_out[...] = ordered_sum(n, land)


def weight_scatter(n, collective_id, plan, lefts, rights, small, part, x, gain, dmid):
    rows = lefts[0].shape[2]
    chunks = max(len(plan[0]), len(plan[1]))
    totals = [sum(width for width, _ in side) for side in plan]
    return pl.pallas_call(
        functools.partial(weight_scatter_kernel, n, plan, len(lefts), len(rights)),
        out_shape=[jax.ShapeDtypeStruct((rows, right.shape[1]), F32) for right in rights]
        + [jax.ShapeDtypeStruct(small.shape[1:], F32), jax.ShapeDtypeStruct(part.shape, F32)],
        in_specs=[pl.BlockSpec(memory_space=VMEM)] * (len(lefts) + len(rights) + 5),
        out_specs=[pl.BlockSpec(memory_space=VMEM)] * (len(rights) + 2),
        scratch_shapes=[
            VMEM((n - 1, rows, totals[0]), BF16),
            VMEM((n - 1, rows, totals[1]), BF16),
            VMEM((rows, totals[0]), BF16),
            VMEM((rows, totals[1]), BF16),
            VMEM(small.shape, F32),
            VMEM(small.shape, F32),
            VMEM(part.shape, BF16),
            *tp_buffers(*part.shape),
            pltpu.SemaphoreType.DMA((2, chunks, n - 1)),
            pltpu.SemaphoreType.DMA((2, chunks, n - 1)),
            pltpu.SemaphoreType.DMA((n - 1,)),
            pltpu.SemaphoreType.DMA((n - 1,)),
            pltpu.SemaphoreType.DMA((3, TP_CHUNKS)),
            pltpu.SemaphoreType.DMA((3, TP_CHUNKS)),
            pltpu.SemaphoreType.DMA((1,)),
        ],
        compiler_params=pltpu.CompilerParams(
            collective_id=collective_id, has_side_effects=True, vmem_limit_bytes=VMEM_LIMIT
        ),
    )(*lefts, *rights, small, part, x, gain, dmid)


def tp_setup():
    ctx = lax.axis_index("ctx")
    tp = lax.axis_index("tp")
    chip = lax.div(tp, 2)
    core = lax.rem(tp, 2)
    sibling = (ctx, 2 * chip + 1 - core)
    across = (ctx, 2 * (1 - chip) + core)
    return chip, core, sibling, across


TP_CHUNKS = 4


def tp_buffers(rows, width):
    return [VMEM((rows // 2, width), BF16) for _ in range(4)]


class TpSum:
    def __init__(self, part, out, bufs, send, recv, core, sibling, across):
        self.part, self.out, self.send, self.recv = part, out, send, recv
        self.away, self.land_a, self.half_b, self.land_b = bufs
        self.core, self.sibling, self.across = core, sibling, across
        self.half = self.away.shape[0]
        self.size = self.away.shape[1] // TP_CHUNKS

    def cols(self, c):
        return pl.ds(c * self.size, self.size)

    def copy(self, stage, c, which=None):
        cols = self.cols(c)
        if stage == 0:
            source, target, device = self.away.at[:, cols], self.land_a.at[:, cols], self.sibling
        elif stage == 1:
            source, target, device = self.half_b.at[:, cols], self.land_b.at[:, cols], self.across
        else:
            source = target = self.out.at[self.rows(which), cols]
            device = self.sibling
        return remote(source, target, self.send.at[stage, c], self.recv.at[stage, c], device)

    def rows(self, which):
        return pl.ds(pl.multiple_of(which * self.half, self.half), self.half)

    def first(self):
        for c in range(TP_CHUNKS):
            self.away[:, self.cols(c)] = self.part(1 - self.core, c).astype(BF16)
            self.copy(0, c).start()

    def second(self):
        for c in range(TP_CHUNKS):
            cols = self.cols(c)
            mine = self.part(self.core, c)
            self.copy(0, c).wait_recv()
            self.half_b[:, cols] = (mine + self.land_a[:, cols].astype(F32)).astype(BF16)
            self.copy(1, c).start()

    def third(self):
        for c in range(TP_CHUNKS):
            cols = self.cols(c)
            self.copy(1, c).wait_recv()
            both = self.half_b[:, cols].astype(F32) + self.land_b[:, cols].astype(F32)
            self.out[self.rows(self.core), cols] = both.astype(BF16)
            self.copy(2, c, self.core).start()

    def fourth(self):
        for c in range(TP_CHUNKS):
            self.copy(2, c, 1 - self.core).wait_recv()
            self.copy(0, c).wait_send()
            self.copy(1, c).wait_send()
            self.copy(2, c, self.core).wait_send()


class TpSplit:
    def __init__(self, part, bufs, send, recv, chip, core, sibling, across):
        self.part, self.send, self.recv = part, send, recv
        self.away, self.land_a, self.half_b, self.land_b = bufs
        self.chip, self.core, self.sibling, self.across = chip, core, sibling, across

    def copy(self, stage):
        if stage < 2:
            return remote(
                self.away.at[stage], self.land_a.at[stage], self.send.at[stage], self.recv.at[stage], self.sibling
            )
        return remote(self.half_b, self.land_b, self.send.at[2], self.recv.at[2], self.across)

    def first(self):
        for i, chip in enumerate((1 - self.chip, self.chip)):
            self.away[i] = self.part(chip, 1 - self.core).astype(BF16)
            self.copy(i).start()

    def second(self):
        mine = self.part(1 - self.chip, self.core)
        self.copy(0).wait_recv()
        self.half_b[...] = (mine + self.land_a[0].astype(F32)).astype(BF16)
        self.copy(2).start()

    def third(self):
        mine = self.part(self.chip, self.core)
        self.copy(1).wait_recv()
        self.copy(2).wait_recv()
        total = mine + self.land_a[1].astype(F32) + self.land_b[...].astype(F32)
        for stage in range(3):
            self.copy(stage).wait_send()
        return total


def feed_kernel(n, heads, attention, *refs):
    if attention:
        (group_map, doc_lengths, skip, q_in, term_in, k_in, v_in, aug_in), refs = refs[:8], refs[8:]
    (att_in, gl_in, outw_in, x_in, gain_ref, grad_in, wg_in, wu_in, wd_in), refs = refs[:9], refs[9:]
    (gated_out, layer_ref, down_out, gate_out, up_out, dmid_out, do_out, dgl_out, gain_out), refs = refs[:9], refs[9:]
    if attention:
        (dm_out, dq_out, drow_ref, dk_out, dv_out, dcol_ref), refs = refs[:6], refs[6:]
    (
        att_ref, gl_ref, outw_ref, x_ref, gated_ref, normed_ref, dgt_ref, dup_ref, do_ref, dgl_ref,
        gate_all, up_all, down_all, accs, dhid_acc, hid_ref, branch_ref, mid_ref, dw_ref, dy_ref,
        a0, a1, a2, a3, b3, s0, s1, s2, s3, dslot_r, dslot_l, dfirst_r, dfirst_l, eslot_r, eslot_l, efirst_r, efirst_l,
        gsend, grecv, hsend, hrecv, asend, arecv, bsend, brecv, ssend, srecv, dsend, drecv, esend, erecv, local,
    ), refs = refs[:52], refs[52:]
    if attention:
        term_ref, dm_ref, diff_ref, span_ref, stage, kv_sem, stage_sem = refs
    gate_acc, up_acc = accs.at[0], accs.at[1]
    me, tp, place, sides = ring_setup(n)
    chip, core, sibling, across = tp_setup()
    moves = Moves(local)
    for name, source, target in (
        ("att", att_in, att_ref), ("gl", gl_in, gl_ref), ("outw", outw_in, outw_ref), ("grad", grad_in, dw_ref),
        ("x", x_in, x_ref),
    ):
        moves.start(name, source, target)
    if attention:
        moves.start("term", term_in, term_ref)
    greet([(side, tp) for side in sides] + [sibling, across])
    shard, hidden = wg_in.shape
    rows, width = x_in.shape
    half = rows // 2
    hw = hidden // 2
    size = 64
    ring = (n, place, sides, tp)

    def rows_of(owner):
        return pl.ds(pl.multiple_of(owner * shard, 16), shard)

    def window(ref, c0, cw):
        return lambda owner: ref.at[rows_of(owner), pl.ds(c0, cw)]

    def chunks(members):
        return [(side, source.at[:, pl.ds(c0, cw)], window(target, c0, cw)) for side, source, target, c0, cw in members]

    gates = Gather(
        *ring,
        chunks(
            [
                (side, source, target, c0, hw)
                for c0 in (0, hw)
                for side, source, target in ((0, wg_in, gate_all), (1, wu_in, up_all))
            ]
        ),
        gsend, grecv,
    )
    downs = Gather(
        *ring,
        chunks([(side, wd_in, down_all, side * hw + c0, hw // 2) for c0 in (0, hw // 2) for side in (0, 1)]),
        hsend, hrecv,
    )
    gates.begin()
    for i, (source, target) in enumerate(((wg_in, gate_all), (wu_in, up_all), (wd_in, down_all))):
        moves.start(i, source, target.at[rows_of(me)])

    moves.wait("att", "gl")
    gated_ref[...] = (att_ref[...] * jax.nn.sigmoid(gl_ref[...])).astype(BF16)
    moves.start("gated", gated_ref, gated_out)
    moves.wait("outw")
    span = width // TP_CHUNKS

    def branch_part(which, c):
        mine = gated_ref[pl.ds(pl.multiple_of(which * half, half), half), :]
        return contract_cols(mine, outw_ref[c * span : (c + 1) * span, :])

    branch = TpSum(branch_part, branch_ref, (a0, a1, a2, a3), asend, arecv, core, sibling, across)
    branch.first()
    branch.second()
    gates.forward(1)
    moves.wait("grad")
    for j in range(n):
        dy_ref[j] = dw_ref[:, j * shard : (j + 1) * shard]
    dhid_acc[...] = jnp.zeros_like(dhid_acc)
    gate_acc[...] = jnp.zeros_like(gate_acc)
    up_acc[...] = jnp.zeros_like(up_acc)

    def grow_back(back):
        for side in (0, 1):
            owner = downs.owner(side, back)
            cols = pl.ds(side * hw, hw)
            dhid_acc[:, cols] += dot(dy_ref[owner], down_all[rows_of(owner), cols])

    def grow(back):
        for side, acc, source in ((0, gate_acc, gate_all), (1, up_acc, up_all)):
            owner = gates.owner(side, back)
            acc[...] += dot(normed_ref[owner], source[rows_of(owner), :])

    moves.wait(0, 1, 2)
    grow_back(0)
    gates.forward(2)
    branch.third()
    branch.fourth()
    moves.wait("x")

    def norm_rows(i, carry):
        here = pl.ds(pl.multiple_of(i * size, size), size)
        middle = x_ref[here, :].astype(F32) + branch_ref[here, :].astype(F32)
        mid_ref[here, :] = middle
        normed = (rms_scale(middle) * gain_ref[...]).astype(BF16)
        for j in range(n):
            normed_ref[j, here, :] = normed[:, j * shard : (j + 1) * shard]
        return carry

    lax.fori_loop(0, rows // size, norm_rows, 0)
    own = pl.ds(pl.multiple_of(tp * span, span), span)
    layer_ref[...] = mid_ref[:, own]
    moves.start("again", grad_in, x_ref)
    gates.forward(3)

    def grow_step(step, carry):
        grow(step)
        return carry

    lax.fori_loop(0, 4, grow_step, 0)

    def gate_step(step, carry):
        gates.forward(step)
        grow(step)
        return carry

    lax.fori_loop(4, n - 1, gate_step, 0)
    downs.begin()
    gates.last()
    grow(n - 1)

    def hid_rows(i, carry):
        here = pl.ds(pl.multiple_of(i * size, size), size)
        gate, up = gate_acc[here, :], up_acc[here, :]
        open_gate = jax.nn.sigmoid(gate)
        silu = gate * open_gate
        hid_ref[here, :] = (silu * up).astype(BF16)
        gate_acc[here, :] = up * open_gate * (1.0 + gate * (1.0 - open_gate))
        up_acc[here, :] = silu
        return carry

    lax.fori_loop(0, rows // size, hid_rows, 0)

    def down_step(step, carry):
        downs.forward(step)
        grow_back(step)
        return carry

    lax.fori_loop(1, n - 2, down_step, 0)
    downs.forward(n - 2)

    def down_term(owner, tag):
        return contract_rows(dy_ref[owner], hid_ref[:, tag * hw : (tag + 1) * hw])

    down_ref = accs.at[0, pl.ds(0, shard), :]
    gate_ref = accs.at[0, pl.ds(shard, shard), :]
    up_ref = accs.at[1, pl.ds(0, shard), :]

    def down_write(tag, value):
        down_ref[:, tag * hw : (tag + 1) * hw] = value

    def early_term(owner, tag):
        which, c0 = tag
        return contract_rows(normed_ref[owner], (dgt_ref, dup_ref)[which][:, c0 : c0 + hw])

    def early_write(tag, value):
        which, c0 = tag
        (gate_ref, up_ref)[which][:, c0 : c0 + hw] = value

    backs = ScatterRing(
        n, [[(hw, 0)], [(hw, 1)]], down_term, (dslot_r, dslot_l), (dfirst_r, dfirst_l), down_write,
        dsend, drecv, place, sides, tp,
    )
    earlies = [
        ScatterRing(
            n, [[(hw, (i, part * hw))] for i in range(2)], early_term, (eslot_r.at[part], eslot_l.at[part]),
            (efirst_r.at[part], efirst_l.at[part]), early_write, esend.at[part], erecv.at[part], place, sides, tp,
        )
        for part in range(2)
    ]
    backs.begin()
    grow_back(n - 2)
    downs.last()
    grow_back(n - 1)

    def grad_rows(i, carry):
        here = pl.ds(pl.multiple_of(i * size, size), size)
        dhid = dhid_acc[here, :]
        dgt_ref[here, :] = (dhid * gate_acc[here, :]).astype(BF16)
        dup_ref[here, :] = (dhid * up_acc[here, :]).astype(BF16)
        return carry

    lax.fori_loop(0, rows // size, grad_rows, 0)

    def dw_part(which, c):
        mine = pl.ds(pl.multiple_of(which * half, half), half)
        back = pl.ds(c * span, span)
        return contract_cols(dgt_ref[mine, :], gate_all[back, :]) + contract_cols(dup_ref[mine, :], up_all[back, :])

    def layer_part(which_chip, which_core):
        back = pl.ds(pl.multiple_of((2 * which_chip + which_core) * span, span), span)
        return contract_cols(hid_ref[...], down_all[back, :])

    total = TpSum(dw_part, dw_ref, (a0, a1, a2, b3), bsend, brecv, core, sibling, across)
    layer = TpSplit(layer_part, (s0, s1, s2, s3), ssend, srecv, chip, core, sibling, across)
    total.first()
    backs.advance(1)
    earlies[0].begin()
    earlies[1].begin()
    total.second()
    gates.sent()
    if attention:
        pairs = heads // 2

        def kv_copies(it):
            part, pair = lax.div(it, pairs), lax.rem(it, pairs)
            source = pl.ds(pl.multiple_of(part * rows, rows), rows)
            target = pl.ds(pl.multiple_of(pair * rows, rows), rows)
            lanes = pl.ds(pl.multiple_of(part * LANES, LANES), LANES)
            return [
                pltpu.make_async_copy(ref.at[pair, source, :], held.at[target, lanes], kv_sem.at[i, it])
                for i, (ref, held) in enumerate(((k_in, gate_all), (v_in, up_all)))
            ]

        def bring(it, carry):
            for copy in kv_copies(it):
                copy.start()
            return carry

        lax.fori_loop(0, n * pairs, bring, 0)
    layer.first()
    layer.second()
    for _ in range(2):
        backs.advance(1)
        earlies[0].advance(1)
        earlies[1].advance(1)
    total.third()
    total.fourth()

    def middle_rows(i, acc):
        here = pl.ds(pl.multiple_of(i * size, size), size)
        middle = mid_ref[here, :]
        inverse = lax.rsqrt(jnp.mean(middle * middle, axis=-1, keepdims=True) + EPS)
        normal = middle * inverse
        dw = dw_ref[here, :].astype(F32)
        back = dw * gain_ref[...]
        back = inverse * (back - normal * jnp.mean(back * normal, axis=-1, keepdims=True))
        dmid = x_ref[here, :].astype(F32) + back
        mid_ref[here, :] = dmid
        low = dmid.astype(BF16)
        branch_ref[here, :] = low
        if attention:
            for j in range(n):
                dm_ref[j, here, :] = low[:, j * shard : (j + 1) * shard]
        return acc + jnp.sum((dw * normal).reshape(size // 8, 8, width), axis=0)

    moves.wait("again")
    gain_out[...] = lax.fori_loop(0, rows // size, middle_rows, jnp.zeros((8, width), F32))
    if attention:
        narrow = q_in.shape[1]
        q_ref = x_ref.at[:, pl.ds(0, narrow)]
        moves.start("q", q_in, q_ref)
        for i in range(n):
            moves.start(
                ("aug", i),
                aug_in.at[pl.ds(i * rows, rows), :],
                x_ref.at[:, pl.ds(narrow + i * LANES, LANES)],
            )
    moves.start("dmid", mid_ref, dmid_out)
    if attention:
        moves.start("dm", dm_ref, dm_out)
    da = dot(branch_ref[...], outw_ref[...])
    open_gate = jax.nn.sigmoid(gl_ref[...])
    do_ref[...] = (da * open_gate).astype(BF16)
    dgl_ref[...] = (da * att_ref[...] * open_gate * (1.0 - open_gate)).astype(BF16)
    moves.start("do", do_ref, do_out)
    moves.start("dgl", dgl_ref, dgl_out)
    backs.advance(1)
    earlies[0].advance(1)
    earlies[1].advance(1)
    layer_ref[...] += layer.third()

    if attention:
        moves.wait("q", "term", *[("aug", i) for i in range(n)])
        first, second = group_map[2 * me], group_map[2 * me + 1]
        in_order = first < second
        query_groups = (jnp.minimum(first, second), jnp.maximum(first, second))

        def put_in(ref):
            def put(h, value, extra):
                ref[:, 2 * h * LANES : (2 * h + 1) * LANES] = value
                ref[:, (2 * h + 1) * LANES : (2 * h + 2) * LANES] = extra

            return put

        spread_heads(q_ref, row_pieces(term_ref[...], True), put_in(dw_ref), heads, in_order)
        delta = head_sums(do_ref[...].astype(F32) * att_ref[...], heads)
        spread_heads(do_ref, row_pieces(-delta, False), put_in(branch_ref), heads, in_order)
        accs[...] = jnp.zeros_like(accs)
        query_at = lax.broadcasted_iota(jnp.int32, (half, half), 1)
        key_at = lax.broadcasted_iota(jnp.int32, (half, half), 0)
        diff_ref[...] = key_at - query_at
        for i, group in enumerate(query_groups):
            span_ref[i] = document_start(group * half + query_at, doc_lengths) - key_at
        dcol_acc = dhid_acc.at[:, pl.ds(0, LANES)]

        def stage_copies(it):
            part, pair = lax.div(it, pairs), lax.rem(it, pairs)
            lanes = pl.ds(pl.multiple_of(pair * LANES, LANES), LANES)
            slot = lax.rem(it, 2)
            return [
                pltpu.make_async_copy(stage.at[slot, i], out.at[part, :, lanes], stage_sem.at[slot, i])
                for i, out in enumerate((dk_out, dv_out))
            ]

        def attend(it, carry):
            part, pair = lax.div(it, pairs), lax.rem(it, pairs)
            for copy in kv_copies(it):
                copy.wait()
            one, two = group_map[2 * part], group_map[2 * part + 1]
            forward = one < two
            key_groups = (jnp.minimum(one, two), jnp.maximum(one, two))
            lanes = pl.ds(pl.multiple_of(part * LANES, LANES), LANES)

            def ordered(ref, base, where):
                top = pl.ds(pl.multiple_of(base * rows, rows), half)
                bottom = pl.ds(pl.multiple_of(base * rows + half, half), half)
                return in_pack_order(forward, ref[top, where], ref[bottom, where])

            key_blocks = ordered(gate_all, pair, lanes)
            value_blocks = ordered(up_all, pair, lanes)
            aug_lanes = pl.ds(pl.multiple_of(narrow + part * LANES, LANES), LANES)
            aug_blocks = ordered(x_ref, 0, aug_lanes)
            masks = block_masks(diff_ref, span_ref, skip, query_groups, key_groups, half)
            keys = [jnp.concatenate([key_blocks[ki], aug_blocks[ki]], axis=1) for ki in range(2)]
            values = [jnp.concatenate([value_blocks[ki], aug_blocks[ki]], axis=1) for ki in range(2)]
            both_keys = jnp.concatenate(keys, axis=0)
            queries, douts, probs, grads = [], [], ([], []), ([], [])
            for e in range(2):
                h = 2 * pair + e
                spot = pl.ds(pl.multiple_of(h * 2 * LANES, 2 * LANES), 2 * LANES)
                query, dout = dw_ref[:, spot], branch_ref[:, spot]
                early = contract_cols(keys[0], query)
                scores = (early[:, :half], early[:, half:], contract_cols(keys[1], query[half:]))
                early = contract_cols(values[0], dout)
                backs_out = (early[:, :half], early[:, half:], contract_cols(values[1], dout[half:]))
                prob = [jnp.where(mask, jnp.exp(score), 0.0) for mask, score in zip(masks, scores)]
                grad = [(p * back).astype(BF16) for p, back in zip(prob, backs_out)]
                prob = [p.astype(BF16) for p in prob]
                queries.append(query)
                douts.append(dout[:, :LANES])
                probs[0].extend(prob[:2])
                probs[1].append(prob[2])
                grads[0].extend(grad[:2])
                grads[1].append(grad[2])
                quarter = pl.ds(pl.multiple_of(lax.rem(h, 4) * 2 * LANES, 2 * LANES), 2 * LANES)
                accs[lax.div(h, 4), :half, quarter] += contract_rows(grad[0], keys[0])
                accs[lax.div(h, 4), half:, quarter] += contract_rows(jnp.concatenate(grad[1:], axis=0), both_keys)
            late_queries = jnp.concatenate([query[half:] for query in queries], axis=0)
            late_douts = jnp.concatenate([dout[half:] for dout in douts], axis=0)
            queries, douts = jnp.concatenate(queries, axis=0), jnp.concatenate(douts, axis=0)
            sums = [
                dot(jnp.concatenate(grads[0], axis=1), queries),
                dot(jnp.concatenate(grads[1], axis=1), late_queries),
            ]
            value_sums = [
                dot(jnp.concatenate(probs[0], axis=1), douts),
                dot(jnp.concatenate(probs[1], axis=1), late_douts),
            ]
            columns = jnp.concatenate([part_sum[:, LANES:] for part_sum in sums], axis=0)
            dcol_acc[...] = jnp.where(pair == 0, 0.0, dcol_acc[...]) + columns

            @pl.when(it >= 2)
            def _():
                for copy in stage_copies(it - 2):
                    copy.wait()

            slot = lax.rem(it, 2)
            for i, part_sums in enumerate(([part_sum[:, :LANES] for part_sum in sums], value_sums)):
                stage[slot, i] = jnp.concatenate(in_pack_order(forward, *part_sums), axis=0).astype(BF16)
            for copy in stage_copies(it):
                copy.start()

            @pl.when(pair == pairs - 1)
            def _():
                columns = jnp.concatenate(
                    in_pack_order(forward, dcol_acc[pl.ds(0, half), :], dcol_acc[pl.ds(half, half), :]), axis=0
                )
                dcol_ref[part] = -(columns.T[:8])

            return carry

        turns = (*earlies, backs)
        starts = [ring.next for ring in turns]
        services = sum(n - 1 - start for start in starts)
        assert starts[0] == starts[1] == starts[2] - 1
        share = n * pairs // services

        def serve(k, carry):
            lax.fori_loop(k * share, (k + 1) * share, attend, 0)
            for i, ring in enumerate(turns):

                @pl.when(lax.rem(k, 3) == i)
                def _(i=i, ring=ring):
                    ring.forward(starts[i] + lax.div(k, 3))

            return carry

        lax.fori_loop(0, services, serve, 0)
        for ring in turns:
            ring.next = n - 1
        if services * share < n * pairs:
            lax.fori_loop(services * share, n * pairs, attend, 0)
        for it in (n * pairs - 2, n * pairs - 1):
            for copy in stage_copies(it):
                copy.wait()

        lane = lax.broadcasted_iota(jnp.int32, (rows, LANES), 1)
        low = low_lanes(rows)
        sums = jnp.zeros((rows, LANES), F32)
        for pair in range(pairs):
            parts = []
            for h in (2 * pair, 2 * pair + 1):
                spot = pl.ds((h % 4) * 2 * LANES, 2 * LANES)
                value = jnp.concatenate(
                    in_pack_order(in_order, accs[h // 4, :half, spot], accs[h // 4, half:, spot]), axis=0
                )
                parts.append(value)
                sums = jnp.where(lane == 24 + h, value[:, LANES:], sums)
            dhid_acc[:, (3 + pair) * LANES : (4 + pair) * LANES] = jnp.where(
                low, parts[0][:, :LANES], parts[1][:, :LANES]
            )
        moves.start("dq", dhid_acc.at[:, pl.ds(3 * LANES, pairs * LANES)], dq_out)
        drow_ref[...] = pltpu.roll(sums, LANES - 24, 1).T[:8]

        moves.wait("dq")
    backs.end()
    moves.start("down", down_ref, down_out)
    earlies[0].end()
    earlies[1].end()
    moves.start("gate", gate_ref, gate_out)
    moves.start("up", up_ref, up_out)
    downs.sent()
    moves.wait()


def feed_forward(
    n, collective_id, heads, attended, gate_logit, out_weight, x, gain, dy, w_gate, w_up, w_down, attention=None
):
    rows, width = x.shape
    shard, hidden = w_gate.shape
    heads_width = attended.shape[1]
    own = width // 4
    half = rows // 2
    dma = pltpu.SemaphoreType.DMA
    vmem = pl.BlockSpec(memory_space=VMEM)
    anywhere = pl.BlockSpec(memory_space=pl.ANY)
    wide, narrow, deep = (rows, width), (rows, heads_width), (rows, hidden)
    by_shard = (n, rows, shard)
    weight = (shard, hidden)
    shapes = [
        (narrow, BF16),
        ((rows, own), F32),
        (weight, F32),
        (weight, F32),
        (weight, F32),
        (wide, F32),
        (narrow, BF16),
        (narrow, BF16),
        ((8, width), F32),
    ]
    kept = [1, 8]
    extra_specs, extra_scratch = [], []
    if attention is not None:
        assert heads // 2 * rows == n * shard and n * LANES == hidden and heads_width + hidden <= width
        shapes += [
            (by_shard, BF16),
            (narrow, F32),
            ((8, rows), F32),
            ((n, rows, heads_width), BF16),
            ((n, rows, heads_width), BF16),
            ((n, 8, rows), F32),
        ]
        kept += [11, 14]
        extra_specs = [smem()] * 3 + [anywhere] * 5
        extra_scratch = [
            VMEM((rows, LANES), F32),
            VMEM(by_shard, BF16),
            VMEM((half, half), jnp.int32),
            VMEM((2, half, half), jnp.int32),
            VMEM((2, 2, rows, LANES), BF16),
            dma((2, n * heads // 2)),
            dma((2, 2)),
        ]
    return pl.pallas_call(
        functools.partial(feed_kernel, n, heads, attention is not None),
        out_shape=[jax.ShapeDtypeStruct(*shape) for shape in shapes],
        in_specs=extra_specs + [anywhere] * 4 + [vmem] + [anywhere] * 4,
        out_specs=[vmem if i in kept else anywhere for i in range(len(shapes))],
        scratch_shapes=[
            VMEM(narrow, F32),
            VMEM(narrow, F32),
            VMEM(out_weight.shape, BF16),
            VMEM(wide, BF16),
            VMEM(narrow, BF16),
            VMEM(by_shard, BF16),
            VMEM(deep, BF16),
            VMEM(deep, BF16),
            VMEM(narrow, BF16),
            VMEM(narrow, BF16),
            *[VMEM((n * shard, hidden), BF16)] * 3,
            VMEM((2,) + deep, F32),
            VMEM(deep, F32),
            VMEM(deep, BF16),
            VMEM(wide, BF16),
            VMEM(wide, F32),
            VMEM(wide, BF16),
            VMEM(by_shard, BF16),
            *tp_buffers(rows, width),
            VMEM((rows // 2, width), BF16),
            VMEM((2, rows, own), BF16),
            VMEM((2, rows, own), BF16),
            VMEM((rows, own), BF16),
            VMEM((rows, own), BF16),
            *ring_scratch(n, shard, [hidden // 2] * 2),
            *[VMEM((2, n - 1, shard, hidden // 2), BF16)] * 2,
            *[VMEM((2, shard, hidden // 2), BF16)] * 2,
            *[dma((4, n - 1))] * 4,
            *[dma((3, TP_CHUNKS))] * 4,
            *[dma((3,))] * 2,
            *[dma((2, 1, n - 1))] * 2,
            *[dma((2, 2, 1, n - 1))] * 2,
            dma((28,)),
            *extra_scratch,
        ],
        compiler_params=pltpu.CompilerParams(
            collective_id=collective_id, has_side_effects=True, vmem_limit_bytes=VMEM_LIMIT
        ),
    )(*(attention or ()), attended, gate_logit, out_weight, x, gain, dy, w_gate, w_up, w_down)


def ring_scratch(n, height, widths):
    return [VMEM((n - 1, height, w), BF16) for w in widths] + [VMEM((height, w), BF16) for w in widths]


def head_means(value, heads):
    width = value.shape[1]
    size = width // heads
    left = lax.div(lax.broadcasted_iota(jnp.int32, (width, width), 0), size)
    right = lax.div(lax.broadcasted_iota(jnp.int32, (width, width), 1), size)
    member = (left == right).astype(BF16)
    high = value.astype(BF16)
    return (dot(high, member) + dot((value - high.astype(F32)).astype(BF16), member)) * (1.0 / size)


STAGED = (0, 1, 4, 5, 16, 11, 14, 17, 18, 19, 6, 12, 13, 20)


def finish_kernel(n, heads, gate_plan, attn_plan, *refs):
    operands, refs = list(refs[:24]), refs[24:]
    (q_out, k_out, v_out, g_out, o_out, small_out, input_out), refs = refs[:7], refs[7:]
    staged, refs = refs[: len(STAGED)], refs[len(STAGED) :]
    (
        pslot_r, pslot_l, gslot_r, gslot_l, gfirst_r, gfirst_l, aslot_r, aslot_l, afirst_r, afirst_l,
        dk_sum, dv_sum, dqr_ref, dkr_ref, dvl_ref, du_ref, sum_ref, t0, t1, t2, t3,
        off_ref, tot_ref, off_land, tot_land, small_ref, small_land,
        psend, precv, gsend, grecv, asend, arecv, osend, orecv, qsend, qrecv, xsend, xrecv, tsend, trecv, local,
    ) = refs
    moves = Moves(local)
    dk_hbm, dv_hbm = operands[:2]
    for target, index in zip(staged, STAGED):
        moves.start(index, operands[index], target)
        operands[index] = target
    (
        dk_ref, dv_ref, col_ref, row_ref, dq_ref, qr_ref, kr_ref, qgain_ref, kgain_ref, fz_ref, group_map,
        wq_ref, wk_ref, wv_ref, wg_ref, wf_ref, dgl_ref, u_ref, dm_ref, gated_ref,
        x_ref, gain_ref, dmid_ref, gain_two_ref,
    ) = operands
    me, tp, place, sides = ring_setup(n)
    chip, core, sibling, across = tp_setup()
    rows, width = dq_ref.shape
    cols = x_ref.shape[1]
    shard = u_ref.shape[2]
    half = rows // 2
    head_dim = width // heads
    small_ref[...] = jnp.zeros_like(small_ref)
    greet(ctx_peers(me, tp, n) + [sibling, across])

    def pair_term(owner, tag):
        which, c0 = tag
        return (dk_ref, dv_ref)[which][owner, :, c0 : c0 + LANES].astype(F32)

    def pair_write(tag, value):
        which, c0 = tag
        (dk_sum, dv_sum)[which][:, c0 : c0 + LANES] = value

    pairs = ScatterRing(
        n, [[(w, (i, c)) for c, w in pieces(width, LANES)] for i in range(2)], pair_term,
        (pslot_r, pslot_l), None, pair_write, psend, precv, place, sides, tp,
        source=lambda target, side, window: (dk_hbm, dv_hbm)[side].at[target, :, window],
    )
    pairs.begin()
    off_ref[...] = col_ref[...]
    off_ref[me] += row_ref[...]
    tot_ref[...] = jnp.zeros_like(tot_ref)
    for i in range(n):
        for g in range(2):
            tot_ref[:, 2 * i + g : 2 * i + g + 1] = jnp.sum(
                off_ref[i, :, g * half : (g + 1) * half], axis=1, keepdims=True
            )
    exchange_start(n, me, tp, lambda peer: off_ref.at[peer], off_land, osend, orecv)
    exchange_start(n, me, tp, lambda peer: tot_ref, tot_land, qsend, qrecv)
    moves.start("off", off_ref.at[me], off_land.at[me])
    moves.start("tot", tot_ref, tot_land.at[me])

    def raw_grad(grad, raw, gain):
        inverse = lax.rsqrt(head_means(raw * raw, heads) + EPS)
        normal = raw * inverse
        back = grad * gain
        back = inverse * (back - normal * head_means(back * normal, heads))
        return back.astype(BF16), jnp.sum(grad * normal, axis=0, keepdims=True)

    def gain_rows(row, first):
        count = 2 * head_dim // n
        for i in range(n // 2):
            for h in range(heads):
                lane = h * head_dim + i * count
                small_ref[first + i, 2 + h : 3 + h, 0:count] = row[:, lane : lane + count]

    moves.wait(0, 1, 4, 5)
    pairs.advance(1)
    dqr, row = raw_grad(dq_ref[...], qr_ref[...], qgain_ref[...] * 0.125)
    dqr_ref[...] = dqr
    gain_rows(row * 0.125, 0)
    pairs.advance(1)
    moves.wait(16, 11, 14)
    span = cols // TP_CHUNKS
    for c in range(TP_CHUNKS):
        back = pl.ds(c * span, span)
        du_ref[:, back] = contract_cols(dqr_ref[...], wq_ref[back, :]) + contract_cols(dgl_ref[...], wg_ref[back, :])
    pairs.advance(n)
    moves.wait(17, 18, 19)

    def gate_term(owner, tag):
        right, c0, cw = tag
        left = dm_ref if right == 2 else u_ref
        return contract_rows(left[owner], (dqr_ref, dgl_ref, gated_ref)[right][:, c0 : c0 + cw])

    def gate_write(tag, value):
        right, c0, cw = tag
        (q_out, g_out, o_out)[right][:, c0 : c0 + cw] = value

    gates = ScatterRing(
        n, gate_plan, gate_term, (gslot_r, gslot_l), (gfirst_r, gfirst_l), gate_write, gsend, grecv, place, sides, tp,
    )
    gates.begin()
    pairs.end()

    moves.wait(6)
    dkr, row = raw_grad(dk_sum[...], kr_ref[...], kgain_ref[...])
    dkr_ref[...] = dkr
    gain_rows(row, n // 2)
    dvl_ref[...] = dv_sum[...].astype(BF16)

    def attn_term(owner, tag):
        c0, cw = tag[1], tag[2]
        return contract_rows(u_ref[owner], (dkr_ref, dvl_ref)[tag[0]][:, c0 : c0 + cw])

    def attn_write(tag, value):
        c0, cw = tag[1], tag[2]
        (k_out, v_out)[tag[0]][:, c0 : c0 + cw] = value

    attns = ScatterRing(
        n, attn_plan, attn_term, (aslot_r, aslot_l), (afirst_r, afirst_l), attn_write, asend, arecv, place, sides, tp,
    )
    attns.begin()
    gates.advance(1)
    moves.wait("off", "tot")
    exchange_wait(n, me, tp, lambda peer: off_ref.at[peer], off_land, osend, orecv)
    exchange_wait(n, me, tp, lambda peer: tot_ref, tot_land, qsend, qrecv)
    off_sum = ordered_sum(n, off_land)
    tot_sum = ordered_sum(n, tot_land)
    onward = (
        lax.broadcasted_iota(jnp.int32, (half, half), 0) >= lax.broadcasted_iota(jnp.int32, (half, half), 1)
    ).astype(F32)
    parts = []
    for g in range(2):
        suffix = jnp.dot(
            off_sum[:, g * half : (g + 1) * half], onward, precision=HIGHEST, preferred_element_type=F32
        )
        later = groups_along(group_map, 1, -1, (8, LANES)) > group_map[2 * me + g]
        parts.append(suffix + jnp.sum(jnp.where(later, tot_sum, 0.0), axis=1, keepdims=True))
    dfz = (jnp.concatenate(parts, axis=1) * jax.nn.sigmoid(-fz_ref[...])).astype(BF16).astype(F32)
    head = lax.broadcasted_iota(jnp.int32, dfz.shape, 0)
    dfz = jnp.where(head < heads, dfz, 0.0)
    bias = jnp.sum(dfz, axis=1, keepdims=True)
    dfz_cols = turn(dfz).astype(BF16)
    dfz_low = dfz.astype(BF16)
    for i in range(n):
        small_ref[i, 8:16, :shard] = dot(dfz_low, u_ref[i])
        small_ref[i, 8:16, 224:225] = bias
        small_ref[i, 1:2, :shard] = jnp.sum(gain_two_ref[:, i * shard : (i + 1) * shard], axis=0, keepdims=True)

    moves.wait(12, 13)
    forget = jnp.concatenate([wf_ref[...], jnp.zeros((LANES - 8, cols), F32)], axis=0).astype(BF16)
    for c in range(TP_CHUNKS):
        back = pl.ds(c * span, span)
        du_ref[:, back] += (
            contract_cols(dkr_ref[...], wk_ref[back, :])
            + contract_cols(dvl_ref[...], wv_ref[back, :])
            + dot(dfz_cols, forget[:, c * span : (c + 1) * span])
        )

    def part(which, c):
        return du_ref[pl.ds(pl.multiple_of(which * half, half), half), c * span : (c + 1) * span]

    total = TpSum(part, sum_ref, (t0, t1, t2, t3), tsend, trecv, core, sibling, across)
    total.first()
    attns.advance(1)
    total.second()
    moves.start("dmid", dmid_ref, du_ref)
    gates.advance(1)
    attns.advance(1)
    gates.advance(1)
    total.third()
    attns.advance(1)
    total.fourth()
    moves.wait("dmid", 20)
    size = 64

    def input_rows(i, acc):
        here = pl.ds(pl.multiple_of(i * size, size), size)
        value = x_ref[here, :].astype(F32)
        inverse = lax.rsqrt(jnp.mean(value * value, axis=-1, keepdims=True) + EPS)
        normal = value * inverse
        grad = sum_ref[here, :].astype(F32)
        back = grad * gain_ref[...]
        back = inverse * (back - normal * jnp.mean(back * normal, axis=-1, keepdims=True))
        du_ref[here, :] += back
        return acc + jnp.sum((grad * normal).reshape(size // 8, 8, cols), axis=0)

    gains = lax.fori_loop(0, rows // size, input_rows, jnp.zeros((8, cols), F32))
    moves.start("input", du_ref, input_out)
    for i in range(n):
        small_ref[i, 0:1, :shard] = jnp.sum(gains[:, i * shard : (i + 1) * shard], axis=0, keepdims=True)
    exchange_start(n, me, tp, lambda peer: small_ref.at[peer], small_land, xsend, xrecv)
    moves.start("small", small_ref.at[me], small_land.at[me])
    while gates.next < n - 1:
        gates.advance(1)
        attns.advance(1)
    gates.end()
    attns.end()
    moves.wait("small")
    exchange_wait(n, me, tp, lambda peer: small_ref.at[peer], small_land, xsend, xrecv)
    small_out[...] = ordered_sum(n, small_land)
    pairs.sent()
    moves.wait()


def finish_backward(n, collective_id, heads, gate_plan, attn_plan, *operands):
    dq, u, x = operands[4], operands[17], operands[20]
    rows, width = dq.shape
    cols = x.shape[1]
    shard = u.shape[2]
    dma = pltpu.SemaphoreType.DMA
    vmem = pl.BlockSpec(memory_space=VMEM)
    anywhere = pl.BlockSpec(memory_space=pl.ANY)
    outside = STAGED + (22,)
    gate_widths = [sum(w for w, _ in side) for side in gate_plan]
    attn_widths = [sum(w for w, _ in side) for side in attn_plan]

    def ring_semaphores(plan):
        return [dma((2, max(len(side) for side in plan), n - 1))] * 2

    shapes = [(shard, width)] * 5 + [(16, 256), (rows, cols)]
    return pl.pallas_call(
        functools.partial(finish_kernel, n, heads, gate_plan, attn_plan),
        out_shape=[jax.ShapeDtypeStruct(shape, F32) for shape in shapes],
        in_specs=[anywhere if i in outside else smem() if i == 10 else vmem for i in range(len(operands))],
        out_specs=[vmem] * 6 + [anywhere],
        scratch_shapes=[
            *[VMEM(operands[i].shape, operands[i].dtype) for i in STAGED],
            *[VMEM((n - 1, rows, width), BF16)] * 2,
            *ring_scratch(n, shard, gate_widths),
            *ring_scratch(n, shard, attn_widths),
            VMEM((rows, width), F32),
            VMEM((rows, width), F32),
            *[VMEM((rows, width), BF16)] * 3,
            VMEM((rows, cols), F32),
            VMEM((rows, cols), BF16),
            *tp_buffers(rows, cols),
            VMEM((n, 8, rows), F32),
            VMEM((8, LANES), F32),
            VMEM((n, 8, rows), F32),
            VMEM((n, 8, LANES), F32),
            VMEM((n, 16, 256), F32),
            VMEM((n, 16, 256), F32),
            *[dma((2, len(pieces(width, LANES)), n - 1))] * 2,
            *ring_semaphores(gate_plan),
            *ring_semaphores(attn_plan),
            *[dma((n - 1,))] * 6,
            *[dma((3, TP_CHUNKS))] * 2,
            dma((len(STAGED) + 5,)),
        ],
        compiler_params=pltpu.CompilerParams(
            collective_id=collective_id, has_side_effects=True, vmem_limit_bytes=VMEM_LIMIT
        ),
    )(*operands)


LANES = 128


def block_state(group_map, doc_lengths, skip, query_group, key_group, rows, docs):
    first_q = query_group * rows
    last_q = first_q + rows - 1
    first_k = key_group * rows
    last_k = first_k + rows - 1
    zero = jnp.int32(0)
    doc_qf, doc_ql, doc_kf, doc_kl, end = zero, zero, zero, zero, zero
    for d in range(docs):
        end = end + doc_lengths[d]
        doc_qf += (first_q >= end).astype(jnp.int32)
        doc_ql += (last_q >= end).astype(jnp.int32)
        doc_kf += (first_k >= end).astype(jnp.int32)
        doc_kl += (last_k >= end).astype(jnp.int32)
    earlier = key_group < query_group
    same = key_group == query_group
    kept = skip[query_group, key_group] != 1
    active = jnp.logical_or(same, earlier & kept & (doc_kl == doc_qf))
    full = earlier & (doc_kf == doc_ql)
    return active, full


def block_mask(doc_lengths, query_group, key_group, rows, docs, query_dim):
    shape = (rows, rows)
    pos_q = query_group * rows + lax.broadcasted_iota(jnp.int32, shape, query_dim)
    pos_k = key_group * rows + lax.broadcasted_iota(jnp.int32, shape, 1 - query_dim)
    start = jnp.zeros(shape, jnp.int32)
    end = jnp.int32(0)
    for d in range(docs):
        end = end + doc_lengths[d]
        start = jnp.where(pos_q >= end, end, start)
    return (pos_k <= pos_q) & (pos_k >= start)


def document_start(position, doc_lengths):
    start, end = jnp.zeros_like(position), jnp.int32(0)
    for d in range(doc_lengths.shape[0]):
        end = end + doc_lengths[d]
        start = jnp.where(position >= end, end, start)
    return start


def block_masks(diff_ref, span_ref, skip, query_groups, key_groups, rows):
    masks = []
    for qi, ki in ((0, 0), (1, 0), (1, 1)):
        query_group, key_group = query_groups[qi], key_groups[ki]
        skipped = jnp.where(key_group < query_group, skip[query_group, key_group], 0)
        reach = key_group * rows - (skipped == 1).astype(jnp.int32) * (1 << 30)
        mask = span_ref[qi] <= reach
        if qi == ki:
            mask = mask & (diff_ref[...] <= (query_group - key_group) * rows)
        masks.append(mask)
    return masks


def in_pack_order(forward, one, two):
    return jnp.where(forward, one, two), jnp.where(forward, two, one)


def low_lanes(rows):
    return lax.broadcasted_iota(jnp.int32, (rows, LANES), 1) < LANES // 2


def three_pieces(value):
    high = value.astype(BF16).astype(F32)
    rest = value - high
    middle = rest.astype(BF16).astype(F32)
    return high, middle, rest - middle


def turn(value):
    rows = value.shape[1]
    return jnp.concatenate([value, jnp.zeros((LANES - 8, rows), F32)], axis=0).T


def row_pieces(term, with_ones):
    lane = lax.broadcasted_iota(jnp.int32, term.shape, 1)
    term = jnp.where(lane < 8, term, 0.0)
    high, middle, low = three_pieces(term)
    result = pltpu.roll(high, 24, 1) + pltpu.roll(middle, 32, 1) + pltpu.roll(low, 40, 1)
    if with_ones:
        result = jnp.where(lane < 24, 1.0, result)
    return result


def key_pieces(offsets):
    rows = offsets.shape[1]
    high, middle, low = three_pieces(offsets)
    stack = jnp.concatenate(
        [-high, -middle, -low, jnp.ones((24, rows), F32), jnp.zeros((LANES - 48, rows), F32)], axis=0
    )
    return stack.T.astype(BF16)


def spread_heads(wide_ref, common, put, heads, forward=None):
    rows = wide_ref.shape[0]
    low = low_lanes(rows)
    lane = lax.broadcasted_iota(jnp.int32, (rows, LANES), 1)

    def ordered(value):
        if forward is None:
            return value
        return jnp.concatenate(in_pack_order(forward, value[: rows // 2], value[rows // 2 :]), axis=0)

    common = ordered(common)
    for h in range(heads):
        pair = h // 2
        block = ordered(wide_ref[:, pair * LANES : (pair + 1) * LANES])
        keep = low if h % 2 == 0 else jnp.logical_not(low)
        put(
            h,
            jnp.where(keep, block, jnp.zeros_like(block)),
            jnp.where(lax.rem(lane, 8) == h, common, 0.0).astype(BF16),
        )


def put_rows(cat_ref):
    def put(h, value, extra):
        cat_ref[h, :, :LANES] = value
        cat_ref[h, :, LANES:] = extra

    return put


def smem():
    return pl.BlockSpec(memory_space=pltpu.SMEM)


def whole(shape):
    return pl.BlockSpec(shape, lambda i: (0,) * len(shape))


def head_sums(value, heads):
    width = value.shape[1]
    feature = lax.broadcasted_iota(jnp.int32, (width, LANES), 0)
    lane = lax.broadcasted_iota(jnp.int32, (width, LANES), 1)
    member = (lax.div(feature, width // heads) == lane).astype(BF16)
    high = value.astype(BF16)
    return dot(high, member) + dot((value - high.astype(F32)).astype(BF16), member)


def backward_kernel(
    heads, rows, docs, me, group_map, doc_lengths, skip, q_ref, d_ref, out_ref, term_ref, k_ref, v_ref, kaug_ref,
    dq_ref, drow_ref, dk_ref, dv_ref, dcol_ref, acc_ref, qcat_ref, dcat_ref, dk_acc, dv_acc, dcol_acc,
):
    step = pl.program_id(0)

    @pl.when(step == 0)
    def _():
        acc_ref[...] = jnp.zeros_like(acc_ref)
        spread_heads(q_ref, row_pieces(term_ref[...], True), put_rows(qcat_ref), heads)
        delta = head_sums(d_ref[...].astype(F32) * out_ref[...], heads)
        spread_heads(d_ref, row_pieces(-delta, False), put_rows(dcat_ref), heads)

    dk_acc[...] = jnp.zeros_like(dk_acc)
    dv_acc[...] = jnp.zeros_like(dv_acc)
    dcol_acc[...] = jnp.zeros_like(dcol_acc)

    def tile(qi, ki, mask):
        q_rows = pl.ds(qi * rows, rows)
        k_rows = pl.ds(ki * rows, rows)
        aug = kaug_ref[k_rows, :]
        for pair in range(heads // 2):
            lanes = pl.ds(pair * LANES, LANES)
            keys = jnp.concatenate([k_ref[pair, k_rows, :], aug], axis=1)
            values = jnp.concatenate([v_ref[pair, k_rows, :], aug], axis=1)
            for h in (2 * pair, 2 * pair + 1):
                probs = jnp.exp(contract_cols(keys, qcat_ref[h, q_rows, :]))
                if mask is not None:
                    probs = jnp.where(mask, probs, 0.0)
                grads = (probs * contract_cols(values, dcat_ref[h, q_rows, :])).astype(BF16)
                dv_acc[k_rows, lanes] += dot(probs.astype(BF16), dcat_ref[h, q_rows, :LANES])
                both = dot(grads, qcat_ref[h, q_rows, :])
                dk_acc[k_rows, lanes] += both[:, :LANES]
                dcol_acc[k_rows, :] += both[:, LANES:]
                acc_ref[h, q_rows, :] += contract_rows(grads, keys)

    for ki in range(2):
        key_group = group_map[2 * step + ki]
        for qi in range(2):
            query_group = group_map[2 * me[0] + qi]
            active, full = block_state(group_map, doc_lengths, skip, query_group, key_group, rows, docs)

            @pl.when(active & full)
            def _(qi=qi, ki=ki):
                tile(qi, ki, None)

            @pl.when(active & jnp.logical_not(full))
            def _(qi=qi, ki=ki, query_group=query_group, key_group=key_group):
                tile(qi, ki, block_mask(doc_lengths, query_group, key_group, rows, docs, 1))

    dk_ref[0] = dk_acc[...].astype(BF16)
    dv_ref[0] = dv_acc[...].astype(BF16)
    dcol_ref[0] = -(dcol_acc[...].T[:8])

    @pl.when(step == pl.num_programs(0) - 1)
    def _():
        total_rows = dq_ref.shape[0]
        low = low_lanes(total_rows)
        lane = lax.broadcasted_iota(jnp.int32, (total_rows, LANES), 1)
        sums = jnp.zeros((total_rows, LANES), F32)
        for pair in range(heads // 2):
            a, b = 2 * pair, 2 * pair + 1
            dq_ref[:, pair * LANES : (pair + 1) * LANES] = jnp.where(
                low, acc_ref[a, :, :LANES], acc_ref[b, :, :LANES]
            )
            sums = jnp.where(
                lane == 24 + a, acc_ref[a, :, LANES:], jnp.where(lane == 24 + b, acc_ref[b, :, LANES:], sums)
            )
        drow_ref[...] = pltpu.roll(sums, LANES - 24, 1).T[:8]


def backward_attention(me, group_map, doc_lengths, skip, queries, grads, attended, term, keys, values, key_aug, heads):
    total = keys.shape[1]
    own, width = queries.shape
    rows = own // 2
    n = total // own
    docs = doc_lengths.shape[0]
    return pl.pallas_call(
        functools.partial(backward_kernel, heads, rows, docs),
        grid=(n,),
        out_shape=[
            jax.ShapeDtypeStruct((own, width), F32),
            jax.ShapeDtypeStruct((8, own), F32),
            jax.ShapeDtypeStruct((n, own, width), BF16),
            jax.ShapeDtypeStruct((n, own, width), BF16),
            jax.ShapeDtypeStruct((n, 8, own), F32),
        ],
        in_specs=[smem(), smem(), smem(), smem()]
        + [
            whole((own, width)),
            whole((own, width)),
            whole((own, width)),
            whole((own, LANES)),
            pl.BlockSpec((heads // 2, own, LANES), lambda i: (0, i, 0)),
            pl.BlockSpec((heads // 2, own, LANES), lambda i: (0, i, 0)),
            pl.BlockSpec((own, LANES), lambda i: (i, 0)),
        ],
        out_specs=[
            whole((own, width)),
            whole((8, own)),
            pl.BlockSpec((1, own, width), lambda i: (i, 0, 0)),
            pl.BlockSpec((1, own, width), lambda i: (i, 0, 0)),
            pl.BlockSpec((1, 8, own), lambda i: (i, 0, 0)),
        ],
        scratch_shapes=[
            VMEM((heads, own, 2 * LANES), F32),
            VMEM((heads, own, 2 * LANES), BF16),
            VMEM((heads, own, 2 * LANES), BF16),
            VMEM((own, width), F32),
            VMEM((own, width), F32),
            VMEM((own, LANES), F32),
        ],
        compiler_params=pltpu.CompilerParams(vmem_limit_bytes=VMEM_LIMIT),
        cost_estimate=pl.CostEstimate(
            flops=own * total * width * 10, bytes_accessed=total * width * 8, transcendentals=own * total * heads
        ),
    )(me, group_map, doc_lengths, skip, queries, grads, attended, term, keys, values, key_aug)


def deliver_kernel(heads, count, small_ref, *refs):
    sources, refs = refs[:count], refs[count:]
    targets, refs = refs[:count], refs[count:]
    (first_ref, second_ref, forget_ref, bias_ref, gains_ref), refs = refs[:5], refs[5:]
    held, local = refs[:count], refs[count]
    moves = Moves(local)
    for i in range(count):
        moves.start(i, sources[i], held[i])
    shard, gain_rows = first_ref.shape[0], gains_ref.shape[0]
    first_ref[...] = small_ref[0:1, :shard].reshape(shard)
    second_ref[...] = small_ref[1:2, :shard].reshape(shard)
    turned = jnp.concatenate([small_ref[...], jnp.zeros((LANES - 16, 256), F32)], axis=0).T
    forget_ref[...] = turned[:shard, 8 : 8 + heads]
    gains_ref[...] = turned[:gain_rows, 2 : 2 + heads]
    bias_ref[...] = turned[224:225, 8 : 8 + heads].reshape(heads)
    for i in range(count):
        moves.wait(i)
        moves.start(i, held[i], targets[i])
    moves.wait()


def deliver(heads, shard, gain_rows, small, arrays):
    vmem = pl.BlockSpec(memory_space=VMEM)
    anywhere = pl.BlockSpec(memory_space=pl.ANY)
    shapes = [array.shape for array in arrays]
    shapes += [(shard,), (shard,), (shard, heads), (heads,), (gain_rows, heads)]
    (layer, input_grad, query, key, value, gate_out, output, gate, up, down, one, two, forget, bias, gains) = (
        pl.pallas_call(
            functools.partial(deliver_kernel, heads, len(arrays)),
            out_shape=[jax.ShapeDtypeStruct(shape, F32) for shape in shapes],
            in_specs=[vmem] + [anywhere] * len(arrays),
            out_specs=[anywhere] * len(arrays) + [vmem] * 5,
            scratch_shapes=[VMEM(array.shape, F32) for array in arrays]
            + [pltpu.SemaphoreType.DMA((2 * len(arrays),))],
            compiler_params=pltpu.CompilerParams(vmem_limit_bytes=VMEM_LIMIT),
        )(small, *arrays)
    )
    return (
        layer, input_grad, one, query, key, value, gate_out, forget, bias, gains, output, two, gate, up, down,
    )


def on_device(
    hidden_in,
    norm_one,
    w_query,
    w_key,
    w_value,
    w_gate_out,
    w_forget,
    forget_bias,
    head_gains,
    w_output,
    norm_two,
    w_gate,
    w_up,
    w_down,
    out_grad,
    doc_lengths,
    group_map,
    skip_list,
):
    device_ctx = lax.axis_index("ctx")
    device_tp = lax.axis_index("tp")
    n = lax.axis_size("ctx")
    row_count, model_width = hidden_in.shape
    group_rows = row_count // 2
    heads = forget_bias.shape[0]
    shard = norm_one.shape[0]
    gain_rows = head_gains.shape[0]
    head_dim = gain_rows * n // 2
    width = heads * head_dim
    hidden_width = w_gate.shape[1]

    slots = 2 * n
    (
        query_weight,
        key_weight,
        value_weight,
        gate_out_weight,
        output_weight,
        normed_shards,
        query_rows,
        query_raw,
        key_raw,
        gate_logit,
        forget_logit,
        keys_all,
        values_all,
        key_aug,
        attended_flat,
        row_term,
        gain_one,
        gain_two,
        query_gain,
        key_gain,
        forget_weight,
    ) = start_forward(
        n,
        1,
        group_map,
        doc_lengths,
        skip_list,
        forget_bias,
        hidden_in,
        [norm_one, norm_two, head_gains, w_forget],
        [w_query, w_key, w_value, w_gate_out],
        w_output,
    )
    half = width // 256 * 128
    fused = n <= 8
    (
        gated,
        layer_out,
        down_share,
        gate_share,
        up_share,
        grad_middle,
        grad_attended,
        grad_gate_logit,
        gain_two_parts,
        *attention_grads,
    ) = feed_forward(
        n,
        3,
        heads,
        attended_flat,
        gate_logit,
        output_weight,
        hidden_in,
        gain_two,
        out_grad,
        w_gate,
        w_up,
        w_down,
        (group_map, doc_lengths, skip_list, query_rows, row_term, keys_all, values_all, key_aug) if fused else None,
    )
    halves = [(0, half), (half, width - half)]
    attn_plan = [[(cw, (i, c0, cw)) for c0, cw in halves] for i in (0, 1)]
    if fused:
        grad_branch, grad_query, row_sums, key_part, value_part, column_sums = attention_grads
        early_plan = [side + [(cw, (2, c0, cw))] for side, (c0, cw) in zip(attn_plan, halves)]
        query_share, key_share, value_share, gate_out_share, output_share, small_share, input_grad = finish_backward(
            n,
            7,
            heads,
            early_plan,
            attn_plan,
            key_part,
            value_part,
            column_sums,
            row_sums,
            grad_query,
            query_raw,
            key_raw,
            query_gain,
            key_gain,
            forget_logit,
            group_map,
            query_weight,
            key_weight,
            value_weight,
            gate_out_weight,
            forget_weight,
            grad_gate_logit,
            normed_shards,
            grad_branch,
            gated,
            hidden_in,
            gain_one,
            grad_middle,
            gain_two_parts,
        )
    else:
        grad_branch = grad_middle.astype(BF16).reshape(row_count, n, shard).transpose(1, 0, 2)
        grad_query, row_sums, key_part, value_part, column_sums = backward_attention(
            device_ctx.astype(jnp.int32).reshape(1),
            group_map,
            doc_lengths,
            skip_list,
            query_rows,
            grad_attended,
            attended_flat,
            row_term,
            keys_all,
            values_all,
            key_aug,
            heads,
        )
        own_groups = lax.dynamic_slice_in_dim(group_map, device_ctx * 2, 2, 0)
        later = (group_map[None, :] > own_groups[:, None]).astype(F32)
        query_gain, key_gain = (gain.reshape(heads, head_dim) for gain in (query_gain, key_gain))
        query_raw, key_raw = (raw.reshape(row_count, heads, head_dim) for raw in (query_raw, key_raw))
        query_norm, key_norm = rms_scale(query_raw), rms_scale(key_raw)
        forget_logit = forget_logit[:heads].T
        forget_weight = forget_weight[:heads].astype(BF16)
        normed_one = normed_shards.transpose(1, 0, 2).reshape(row_count, model_width)
        place = jnp.arange(group_rows, dtype=jnp.int32)
        upper = (place[:, None] <= place[None, :]).astype(F32)
        grad_key, grad_value, off_sum, tot_sum = pair_scatter(n, 7, key_part, value_part, column_sums, row_sums)
        after = contract_cols_exact(tot_sum[:heads, :slots], later)
        suffix = lax.dot_general(
            off_sum[:heads].reshape(heads, 2, group_rows), upper, (((2,), (1,)), ((), ())), precision=HIGHEST
        )
        grad_log_forget = (suffix + after[:, :, None]).reshape(heads, row_count).T
        grad_key3 = grad_key.reshape(row_count, heads, head_dim)
        grad_query3 = grad_query.reshape(row_count, heads, head_dim)
        key_raw_grad = rms_back(grad_key3 * key_gain, key_raw).astype(BF16).reshape(row_count, width)
        query_raw_grad = (
            rms_back(grad_query3 * query_gain * 0.125, query_raw).astype(BF16).reshape(row_count, width)
        )
        value_low = grad_value.astype(BF16)
        query_gain_grad = jnp.sum(grad_query3 * query_norm * 0.125, axis=0)
        key_gain_grad = jnp.sum(grad_key3 * key_norm, axis=0)
        head_gain_grad = jnp.concatenate([query_gain_grad, key_gain_grad], axis=1)
        grad_forget_logit = (grad_log_forget * jax.nn.sigmoid(-forget_logit)).astype(BF16)
        bias_part = jnp.sum(grad_forget_logit.astype(F32), axis=0)
        normed_one_part = (
            contract_cols(query_raw_grad, query_weight)
            + contract_cols(key_raw_grad, key_weight)
            + contract_cols(value_low, value_weight)
            + contract_cols(grad_gate_logit, gate_out_weight)
            + dot(grad_forget_logit, forget_weight)
        )
        forget_grad = contract_rows(grad_forget_logit, normed_one)

        def wide(value):
            return jnp.pad(value, ((0, 0), (0, 0), (0, 256 - value.shape[2])))

        forget_rows = wide(forget_grad.reshape(heads, n, shard).transpose(1, 0, 2))
        forget_rows = forget_rows.at[:, :, 224].set(bias_part[None, :])
        small_grad = jnp.concatenate(
            [
                jnp.zeros((n, 1, 256), F32),
                wide(jnp.sum(gain_two_parts, axis=0).reshape(n, 1, shard)),
                wide(head_gain_grad.reshape(heads, n, gain_rows).transpose(1, 0, 2)),
                jnp.pad(forget_rows, ((0, 0), (0, 8 - heads), (0, 0))),
            ],
            axis=1,
        )
        plan = [
            [(cw, (0, right, c0, cw)) for right in rights for c0, cw in halves] + [(cw, (1, 4, c0, cw))]
            for rights, (c0, cw) in zip(((0, 1), (2, 3)), halves)
        ]
        (
            query_share,
            key_share,
            value_share,
            gate_out_share,
            output_share,
            small_share,
            input_grad,
        ) = weight_scatter(
            n,
            8,
            plan,
            [normed_shards, grad_branch],
            [query_raw_grad, key_raw_grad, value_low, grad_gate_logit, gated],
            small_grad,
            normed_one_part,
            hidden_in,
            gain_one,
            grad_middle,
        )
    return deliver(
        heads,
        shard,
        gain_rows,
        small_share,
        [
            layer_out,
            input_grad,
            query_share,
            key_share,
            value_share,
            gate_out_share,
            output_share,
            gate_share,
            up_share,
            down_share,
        ],
    )


def solution(mesh):
    split = P("ctx", "tp")
    in_specs = (
        P("ctx", None),
        P("ctx"),
        split,
        split,
        split,
        split,
        split,
        P("tp"),
        split,
        split,
        P("ctx"),
        split,
        split,
        split,
        P("ctx", None),
        P(),
        P(),
        P(),
    )
    out_specs = (
        split,
        P("ctx", None),
        P("ctx"),
        split,
        split,
        split,
        split,
        split,
        P("tp"),
        split,
        split,
        P("ctx"),
        split,
        split,
        split,
    )
    return jax.shard_map(on_device, mesh=mesh, in_specs=in_specs, out_specs=out_specs, check_vma=False)
```

```python
import functools

import jax
import jax.numpy as jnp
from jax import lax
from jax.experimental import pallas as pl
from jax.experimental.pallas import tpu as pltpu
from jax.sharding import PartitionSpec as P

EPS = 1e-06
HIGHEST = lax.Precision.HIGHEST
MESH = pl.DeviceIdType.MESH
VMEM = pltpu.VMEM
VMEM_LIMIT = 62 * 1024 * 1024
F32 = jnp.float32
BF16 = jnp.bfloat16


def rms_scale(value):
    return value * lax.rsqrt(jnp.mean(value * value, axis=-1, keepdims=True) + EPS)


def rms_back(grad_in, value):
    inverse = lax.rsqrt(jnp.mean(value * value, axis=-1, keepdims=True) + EPS)
    normal = value * inverse
    return inverse * (grad_in - normal * jnp.mean(grad_in * normal, axis=-1, keepdims=True))


def dot(left, right):
    return jnp.dot(left, right, preferred_element_type=F32)


def contract_cols(left, right):
    return lax.dot_general(left, right, (((1,), (1,)), ((), ())), preferred_element_type=F32)


def contract_cols_exact(left, right):
    return lax.dot_general(left, right, (((1,), (1,)), ((), ())), precision=HIGHEST)


def contract_rows(left, right):
    return lax.dot_general(left, right, (((0,), (0,)), ((), ())), preferred_element_type=F32)


def ring_place(ctx, n):
    odd = lax.rem(ctx, 2)
    half = lax.div(ctx, 2)
    return (1 - odd) * half + odd * (n - 1 - half)


def ring_owner(place, n):
    late = lax.div(place, n // 2)
    return (1 - late) * (2 * place) + late * (2 * (n - 1 - place) + 1)


def wrap(place, n):
    return lax.rem(place + 2 * n, n)


def ring_setup(n):
    me = lax.axis_index("ctx")
    tp = lax.axis_index("tp")
    place = ring_place(me, n)
    right = ring_owner(wrap(place + 1, n), n)
    left = ring_owner(wrap(place - 1, n), n)
    return me, tp, place, (right, left)


def greet(peers):
    barrier = pltpu.get_barrier_semaphore()
    for peer in peers:
        pl.semaphore_signal(barrier, inc=1, device_id=peer, device_id_type=MESH)
    pl.semaphore_wait(barrier, len(peers))


def ctx_peers(me, tp, n):
    return [(lax.rem(me + i, n), tp) for i in range(1, n)]


def remote(src, dst, send, recv, device):
    return pltpu.make_async_remote_copy(
        src_ref=src, dst_ref=dst, send_sem=send, recv_sem=recv, device_id=device, device_id_type=MESH
    )


class Gather:
    def __init__(self, n, place, sides, tp, chunks, send, recv):
        self.n, self.place, self.sides, self.tp = n, place, sides, tp
        self.chunks, self.send, self.recv = chunks, send, recv
        self.arrived = None

    def owner(self, side, back):
        return ring_owner(wrap(self.place - back if side == 0 else self.place + back, self.n), self.n)

    def copy(self, index, step, first):
        side, source, target = self.chunks[index]
        target = target(self.owner(side, step))
        return remote(
            source if first else target, target, self.send.at[index, step], self.recv.at[index, step],
            (self.sides[side], self.tp),
        )

    def arrive(self, index, step):
        side, _, target = self.chunks[index]
        target = target(self.owner(side, step + 1))
        remote(
            target, target, self.send.at[index, step], self.recv.at[index, step], (self.sides[side], self.tp)
        ).wait_recv()
        if self.arrived is not None:
            self.arrived(index, step)

    def begin(self, indices=None):
        for index in indices if indices is not None else range(len(self.chunks)):
            self.copy(index, 0, True).start()

    def forward(self, step):
        for index in range(len(self.chunks)):
            self.arrive(index, step - 1)
            self.copy(index, step, False).start()

    def last(self):
        for index in range(len(self.chunks)):
            self.arrive(index, self.n - 2)

    def sent(self):
        def finish(step, carry):
            for index in range(len(self.chunks)):
                self.copy(index, step, False).wait_send()
            return carry

        lax.fori_loop(0, self.n - 1, finish, 0)


class Moves:
    def __init__(self, semaphores):
        self.semaphores, self.count, self.open = semaphores, 0, {}

    def start(self, name, source, target):
        copy = pltpu.make_async_copy(source, target, self.semaphores.at[self.count])
        self.count += 1
        copy.start()
        self.open[name] = copy

    def wait(self, *names):
        for name in names or list(self.open):
            self.open.pop(name).wait()


def start_kernel(
    n, heads, group_map, doc_lengths, skip, bias_ref, x_ref, norm_one, norm_two, gains_in, forget_in,
    wq_in, wk_in, wv_in, wg_in, wo_in,
    wq_out, wk_out, wv_out, wg_out, wo_ref, u_out, q_out, qr_out, kr_out, gl_out, fz_ref, k_out, v_out, aug_out,
    att_out, term_ref, gain_one, gain_two, qgain_ref, kgain_ref, wf_ref,
    x_vmem, wq_ref, wk_ref, wv_ref, wg_ref, u_ref, turned_ref, q_ref, k_all, v_all, aug_ref, att_ref, acc_ref, cat_ref,
    diff_ref, span_ref, tot_ref, before_ref, inside_all, small_wide, small_in,
    small_all, acc_r, acc_l, inside_src,
    wsend, wrecv, osend, orecv, ksend, krecv, ssend, srecv, isend, irecv, spill, local,
):
    me, tp, place, sides = ring_setup(n)
    moves = Moves(local)
    moves.start("x", x_ref, x_vmem)
    shard, width = wq_in.shape
    small_wide[...] = jnp.zeros_like(small_wide)
    small_wide[0:1, :shard] = norm_one[...].astype(F32).reshape(1, shard)
    small_wide[1:2, :shard] = norm_two[...].astype(F32).reshape(1, shard)
    for ref, first in ((gains_in, 2), (forget_in, 8)):
        small_wide[first : first + heads, : ref.shape[1]] = ref[...].astype(F32)
    small_in[...] = small_wide[...].astype(BF16)
    greet(ctx_peers(me, tp, n))
    rows, cols = x_ref.shape
    half = rows // 2
    head_dim = width // heads

    def shard_rows(owner):
        return pl.ds(pl.multiple_of(owner * shard, 16), shard)

    def window(ref, c0, cw):
        return lambda owner: ref.at[shard_rows(owner), pl.ds(c0, cw)]

    def token_rows(owner):
        return pl.ds(pl.multiple_of(owner * rows, rows), rows)

    def block(ref, pair):
        return lambda owner: ref.at[pair, token_rows(owner), :]

    ring = (n, place, sides, tp)
    projections = Gather(
        *ring,
        [
            (side, source, window(target, 0, width))
            for side, source, target in ((0, wq_in, wq_ref), (1, wv_in, wv_ref), (0, wk_in, wk_ref), (1, wg_in, wg_ref))
        ],
        wsend, wrecv,
    )
    middle = width // 256 * 128
    outputs = Gather(
        *ring,
        [
            (side, wo_in.at[:, pl.ds(c0, cw)], window(wo_ref, c0, cw))
            for side, c0, cw in ((0, 0, middle), (1, middle, width - middle))
        ],
        osend, orecv,
    )
    members = [(0, k_all, k_out, 0), (1, k_all, k_out, 2), (0, v_all, v_out, 0), (1, v_all, v_out, 2)]
    members += [(0, k_all, k_out, 1), (1, v_all, v_out, 1)]
    pairs = Gather(
        *ring, [(side, block(ref, pair)(me), block(ref, pair)) for side, ref, _, pair in members], ksend, krecv
    )

    def spill_copy(index, step):
        side, ref, out, pair = members[index]
        owner = pairs.owner(side, step + 1)
        return pltpu.make_async_copy(
            block(ref, pair)(owner), block(out, pair)(owner), spill.at[index, step]
        )

    pairs.arrived = lambda index, step: spill_copy(index, step).start()

    projections.begin()
    exchange_start(n, me, tp, lambda peer: small_in, small_all, ssend, srecv)
    gathered = ((wq_in, wq_ref), (wk_in, wk_ref), (wv_in, wv_ref), (wg_in, wg_ref), (wo_in, wo_ref))
    for i, (source, target) in enumerate(gathered):
        moves.start(i, source, target.at[shard_rows(me)])
    moves.start("small", small_in, small_all.at[me])
    moves.wait("small")
    exchange_wait(n, me, tp, lambda peer: small_in, small_all, ssend, srecv)
    projections.forward(1)

    count = 2 * head_dim // n
    for i in range(n):
        block_small = small_all[i].astype(F32)
        gain_one[:, i * shard : (i + 1) * shard] = block_small[0:1, :shard]
        gain_two[:, i * shard : (i + 1) * shard] = block_small[1:2, :shard]
        wf_ref[:, i * shard : (i + 1) * shard] = block_small[8:16, :shard]
        target, at = (qgain_ref, i) if i < n // 2 else (kgain_ref, i - n // 2)
        for h in range(heads):
            lane = h * head_dim + at * count
            target[:, lane : lane + count] = block_small[2 + h : 3 + h, :count]

    size = LANES

    def norm_rows(i, carry):
        here = pl.ds(pl.multiple_of(i * size, size), size)
        normed = (rms_scale(x_vmem[here, :].astype(F32)) * gain_one[...]).astype(BF16)
        for j in range(n):
            u_ref[j, here, :] = normed[:, j * shard : (j + 1) * shard]
        turned_ref[:, here] = normed.astype(F32).T.astype(BF16)
        return carry

    moves.wait("x")
    lax.fori_loop(0, rows // size, norm_rows, 0)
    moves.start("u", turned_ref, u_out)

    def grow(back):
        for side, acc, sources in ((0, acc_r, (wq_ref, wk_ref)), (1, acc_l, (wv_ref, wg_ref))):
            owner = projections.owner(side, back)
            for i, source in enumerate(sources):
                acc[:, i * width : (i + 1) * width] += dot(u_ref[owner], source[shard_rows(owner), :])

    acc_r[...] = jnp.zeros_like(acc_r)
    acc_l[...] = jnp.zeros_like(acc_l)
    moves.wait(0, 1, 2, 3, 4)
    grow(0)
    projections.forward(2)
    grow(1)
    grow(2)
    forget = jnp.zeros((16, rows), F32)
    for j in range(n):
        forget += contract_cols(small_all[j, :, :shard], u_ref[j])
    head = lax.broadcasted_iota(jnp.int32, (8, rows), 0)
    fz = forget[8:16]
    for h in range(heads):
        fz = jnp.where(head == h, fz + bias_ref[h], fz)
    fz_ref[...] = fz
    logs = jnp.minimum(fz, 0.0) - jnp.log1p(jnp.exp(-jnp.abs(fz)))
    logs = jnp.where(head < heads, logs, 0.0)
    upto = (
        lax.broadcasted_iota(jnp.int32, (half, half), 0) <= lax.broadcasted_iota(jnp.int32, (half, half), 1)
    ).astype(F32)
    for g in range(2):
        inside_src[:, g * half : (g + 1) * half] = jnp.dot(
            logs[:, g * half : (g + 1) * half], upto, precision=HIGHEST, preferred_element_type=F32
        )
    exchange_start(n, me, tp, lambda peer: inside_src, inside_all, isend, irecv)
    moves.start("inside", inside_src, inside_all.at[me])

    def step_on(step, carry):
        projections.forward(step)
        grow(step)
        return carry

    lax.fori_loop(3, n - 2, step_on, 0)
    outputs.begin()
    projections.forward(n - 2)
    grow(n - 2)
    outputs.forward(1)
    projections.last()
    grow(n - 1)

    def head_norm(value):
        return value * lax.rsqrt(head_means(value * value, heads) + EPS)

    my_rows = token_rows(me)
    for pair in range(heads // 2):
        v_all[pair, my_rows, :] = acc_l[:, pair * LANES : (pair + 1) * LANES].astype(BF16)
    pairs.begin([2, 3, 5])
    keys = (head_norm(acc_r[:, width:]) * kgain_ref[...]).astype(BF16)
    for pair in range(heads // 2):
        k_all[pair, my_rows, :] = keys[:, pair * LANES : (pair + 1) * LANES]
    pairs.begin([0, 1, 4])
    for i, (source, target) in enumerate(
        ((wq_ref, wq_out), (wk_ref, wk_out), (wv_ref, wv_out), (wg_ref, wg_out))
    ):
        moves.start(i, source, target)
    moves.start("qr", acc_r.at[:, pl.ds(0, width)], qr_out)
    moves.start("kr", acc_r.at[:, pl.ds(width, width)], kr_out)
    moves.start("gl", acc_l.at[:, pl.ds(width, width)], gl_out)
    for i, (ref, out) in enumerate(((k_all, k_out), (v_all, v_out))):
        for pair in range(heads // 2):
            moves.start((i, pair), block(ref, pair)(me), block(out, pair)(me))
    q_ref[...] = (head_norm(acc_r[:, :width]) * qgain_ref[...] * 0.125).astype(BF16)
    moves.start("q", q_ref, q_out)

    moves.wait("inside")
    exchange_wait(n, me, tp, lambda peer: inside_src, inside_all, isend, irecv)
    tot_ref[...] = jnp.zeros_like(tot_ref)
    for i in range(n):
        for g in range(2):
            tot_ref[:, 2 * i + g : 2 * i + g + 1] = inside_all[i, :, (g + 1) * half - 1 : (g + 1) * half]
    earlier = groups_along(group_map, 0, 1 << 20) < groups_along(group_map, 1, 1 << 20)
    before_ref[...] = jnp.dot(
        tot_ref[...], earlier.astype(F32), precision=HIGHEST, preferred_element_type=F32
    )
    lane8 = lax.broadcasted_iota(jnp.int32, (8, LANES), 1)

    def offsets_of(shard_index):
        parts = []
        for g in range(2):
            before = jnp.sum(jnp.where(lane8 == 2 * shard_index + g, before_ref[...], 0.0), axis=1, keepdims=True)
            parts.append(inside_all[shard_index, :, g * half : (g + 1) * half] + before)
        return jnp.concatenate(parts, axis=1)

    def aug_rows(i, carry):
        aug_ref[token_rows(i), :] = key_pieces(offsets_of(i))
        return carry

    pairs.forward(1)
    lax.fori_loop(0, n, aug_rows, 0)
    moves.start("aug", aug_ref, aug_out)

    first, second = group_map[2 * me], group_map[2 * me + 1]
    in_order = first < second
    query_groups = (jnp.minimum(first, second), jnp.maximum(first, second))
    mine = turn(offsets_of(me))
    term_ref[...] = mine
    spread_heads(q_ref, row_pieces(mine, True), put_rows(cat_ref), heads, in_order)
    acc_ref[...] = jnp.zeros_like(acc_ref)
    query_at = lax.broadcasted_iota(jnp.int32, (half, half), 0)
    key_at = lax.broadcasted_iota(jnp.int32, (half, half), 1)
    diff_ref[...] = key_at - query_at
    for i, group in enumerate(query_groups):
        span_ref[i] = document_start(group * half + query_at, doc_lengths) - key_at
    ones = jnp.ones((half, LANES), BF16)

    def attend(i, back):
        late = lax.div(i, 2)
        pair = (1 - late) * 2 * i + late
        side = lax.rem(i, 2)
        owner = ring_owner(wrap(place + (2 * side - 1) * back, n), n)
        one, two = group_map[2 * owner], group_map[2 * owner + 1]
        forward = one < two
        key_groups = (jnp.minimum(one, two), jnp.maximum(one, two))
        top = pl.ds(pl.multiple_of(owner * rows, rows), half)
        bottom = pl.ds(pl.multiple_of(owner * rows + half, half), half)
        blocks = []
        for ref in (k_all.at[pair], v_all.at[pair], aug_ref):
            blocks.append(in_pack_order(forward, ref[top, :], ref[bottom, :]))
        masks = block_masks(diff_ref, span_ref, skip, query_groups, key_groups, half)
        keys = [jnp.concatenate([blocks[0][ki], blocks[2][ki]], axis=1) for ki in range(2)]
        values = [jnp.concatenate([blocks[1][ki], ones], axis=1) for ki in range(2)]
        both_values = jnp.concatenate(values, axis=0)
        for e in range(2):
            h = 2 * pair + e
            queries = cat_ref[h]
            early = contract_cols(queries, keys[0])
            weights = [
                jnp.where(mask, jnp.exp(score), 0.0).astype(BF16)
                for mask, score in zip(masks, (early[:half], early[half:], contract_cols(queries[half:], keys[1])))
            ]
            acc_ref[h, :half, :] += dot(weights[0], values[0])
            acc_ref[h, half:, :] += dot(jnp.concatenate(weights[1:], axis=1), both_values)

    def attend_all(count, back):
        def body(i, carry):
            attend(i, back)
            return carry

        lax.fori_loop(0, count, body, 0)

    attend_all(3, 0)
    attend_all(2, 1)

    def pair_step(step, count):
        outputs.forward(step)
        pairs.forward(step)
        attend_all(count, step)

    def early_step(step, carry):
        pair_step(step, 2)
        return carry

    def late_step(step, carry):
        pair_step(step, 4)
        return carry

    lax.fori_loop(2, n // 2, early_step, 0)
    pair_step(n // 2, 3)
    lax.fori_loop(n // 2 + 1, n - 1, late_step, 0)
    outputs.last()
    pairs.last()
    attend_all(4, n - 1)

    lane = lax.broadcasted_iota(jnp.int32, (rows, LANES), 1)
    low = low_lanes(rows)
    totals = jnp.ones((rows, LANES), F32)
    for pair in range(heads // 2):
        parts = []
        for h in (2 * pair, 2 * pair + 1):
            value = jnp.concatenate(in_pack_order(in_order, acc_ref[h, :half, :], acc_ref[h, half:, :]), axis=0)
            parts.append(value)
            totals = jnp.where(lane == h, value[:, LANES:], totals)
        att_ref[:, pair * LANES : (pair + 1) * LANES] = jnp.where(
            low, parts[0][:, :LANES], parts[1][:, :LANES]
        ) / jnp.where(low, parts[0][:, LANES:], parts[1][:, LANES:])
    moves.start("att", att_ref, att_out)
    term_ref[...] -= jnp.log(totals)

    def spilled(step, carry):
        for index in range(len(members)):
            spill_copy(index, step).wait()
        return carry

    lax.fori_loop(0, n - 1, spilled, 0)
    moves.wait()
    projections.sent()
    outputs.sent()
    pairs.sent()


def groups_along(group_map, dim, fill, shape=(128, 128)):
    slot = lax.broadcasted_iota(jnp.int32, shape, dim)
    groups = jnp.full(shape, fill, jnp.int32)
    for i in range(group_map.shape[0]):
        groups = jnp.where(slot == i, group_map[i], groups)
    return groups


def start_forward(n, collective_id, group_map, doc_lengths, skip, bias, x, vectors, weights, out_weight):
    rows, cols = x.shape
    shard, width = out_weight.shape
    heads = bias.shape[0]
    half = rows // 2
    dma = pltpu.SemaphoreType.DMA
    vmem = pl.BlockSpec(memory_space=VMEM)
    anywhere = pl.BlockSpec(memory_space=pl.ANY)
    by_pair = (heads // 2, n * rows, LANES)
    weight, wide, narrow = (n * shard, width), (rows, cols), (rows, width)
    shapes = (
        [(weight, BF16)] * 5
        + [((n * shard, rows), BF16), (narrow, BF16)]
        + [(narrow, F32)] * 3
        + [((8, rows), F32)]
        + [(by_pair, BF16)] * 2
        + [((n * rows, LANES), BF16), (narrow, F32), ((rows, LANES), F32)]
        + [((1, cols), F32)] * 2
        + [((1, width), F32)] * 2
        + [((8, cols), F32)]
    )
    return pl.pallas_call(
        functools.partial(start_kernel, n, heads),
        out_shape=[jax.ShapeDtypeStruct(*shape) for shape in shapes],
        in_specs=[smem(), smem(), smem(), smem(), anywhere] + [vmem] * 4 + [anywhere] * 5,
        out_specs=[anywhere if i < 10 or 11 <= i <= 14 else vmem for i in range(len(shapes))],
        scratch_shapes=[
            VMEM(wide, BF16),
            *[VMEM(weight, BF16)] * 4,
            VMEM((n, rows, shard), BF16),
            VMEM((n * shard, rows), BF16),
            VMEM(narrow, BF16),
            *[VMEM(by_pair, BF16)] * 2,
            VMEM((n * rows, LANES), BF16),
            VMEM(narrow, F32),
            VMEM((heads, rows, 2 * LANES), F32),
            VMEM((heads, rows, 2 * LANES), BF16),
            VMEM((half, half), jnp.int32),
            VMEM((2, half, half), jnp.int32),
            VMEM((8, LANES), F32),
            VMEM((8, LANES), F32),
            VMEM((n, 8, rows), F32),
            VMEM((16, 256), F32),
            VMEM((16, 256), BF16),
            VMEM((n, 16, 256), BF16),
            VMEM((rows, 2 * width), F32),
            VMEM((rows, 2 * width), F32),
            VMEM((8, rows), F32),
            *[dma((4, n - 1))] * 2,
            *[dma((2, n - 1))] * 2,
            *[dma((6, n - 1))] * 2,
            *[dma((n - 1,))] * 4,
            dma((6, n - 1)),
            dma((26,)),
        ],
        compiler_params=pltpu.CompilerParams(
            collective_id=collective_id, has_side_effects=True, vmem_limit_bytes=VMEM_LIMIT
        ),
    )(group_map, doc_lengths, skip, bias, x, *vectors, *weights, out_weight)


class ScatterRing:
    def __init__(self, n, plan, local_term, slots, firsts, write, send, recv, place, sides, tp, source=None):
        self.n, self.place, self.sides, self.tp = n, place, sides, tp
        self.source, self.next = source, 1
        self.local_term, self.write = local_term, write
        self.slots, self.firsts, self.send, self.recv = slots, firsts, send, recv
        self.order = []
        starts = [0, 0]
        for index in range(max(len(plan[0]), len(plan[1]))):
            for side in (0, 1):
                if index < len(plan[side]):
                    width, tag = plan[side][index]
                    self.order.append((side, index, starts[side], width, tag))
                    starts[side] += width

    def target(self, side, step):
        step = -1 - step if side == 0 else 1 + step
        return ring_owner(wrap(self.place + step, self.n), self.n)

    def hop(self, side, index, start, width, step, first):
        cols = pl.ds(start, width)
        slots = self.slots[side]
        if not first:
            source = slots.at[step - 1, :, cols]
        elif self.source is None:
            source = self.firsts[side].at[:, cols]
        else:
            source = self.source(self.target(side, 0), side, cols)
        return remote(
            source,
            slots.at[step, :, cols],
            self.send.at[side, index, step],
            self.recv.at[side, index, step],
            (self.sides[side], self.tp),
        )

    def begin(self):
        for side, index, start, width, tag in self.order:
            if self.source is None:
                term = self.local_term(self.target(side, 0), tag)
                self.firsts[side][:, start : start + width] = term.astype(BF16)
            self.hop(side, index, start, width, 0, True).start()

    def forward(self, step):
        for side, index, start, width, tag in self.order:
            term = self.local_term(self.target(side, step), tag)
            slot = self.slots[side].at[step - 1, :, pl.ds(start, width)]
            self.hop(side, index, start, width, step - 1, True).wait_recv()
            slot[...] = (slot[...].astype(F32) + term).astype(BF16)
            self.hop(side, index, start, width, step, False).start()

    def span(self, first, last):
        def body(step, carry):
            self.forward(step)
            return carry

        if last > first:
            lax.fori_loop(first, last, body, 0)

    def advance(self, count):
        last = min(self.next + count, self.n - 1)
        self.span(self.next, last)
        self.next = last

    def end(self):
        n = self.n
        self.advance(n)
        for side, index, start, width, tag in self.order:
            term = self.local_term(self.target(side, n - 1), tag)
            self.hop(side, index, start, width, n - 2, True).wait_recv()
            self.write(tag, self.slots[side][n - 2, :, start : start + width].astype(F32) + term)
        if self.source is None:
            self.sent()

    def sent(self):
        for side, index, start, width, tag in self.order:
            self.hop(side, index, start, width, 0, True).wait_send()

        def finish(step, carry):
            for side, index, start, width, tag in self.order:
                self.hop(side, index, start, width, step, False).wait_send()
            return carry

        lax.fori_loop(1, self.n - 1, finish, 0)


def exchange_start(n, me, tp, source_of, landing, send, recv):
    for i in range(1, n):
        peer = lax.rem(me + i, n)
        remote(source_of(peer), landing.at[me], send.at[i - 1], recv.at[i - 1], (peer, tp)).start()


def exchange_wait(n, me, tp, source_of, landing, send, recv):
    for i in range(1, n):
        peer = lax.rem(me - i + n, n)
        remote(source_of(peer), landing.at[peer], send.at[i - 1], recv.at[i - 1], (peer, tp)).wait()


def ordered_sum(n, landing):
    total = landing[0]
    for i in range(1, n):
        total = total + landing[i]
    return total


def pair_scatter_kernel(
    n, key_ref, value_ref, col_ref, row_ref, key_out, value_out, off_out, tot_out,
    slot_r, slot_l, first_r, first_l, off_ref, tot_ref, off_land, tot_land,
    send, recv, osend, orecv, tsend, trecv, local,
):
    me, tp, place, sides = ring_setup(n)
    off_ref[...] = col_ref[...]
    off_ref[me] += row_ref[...]
    group_rows = row_ref.shape[1] // 2
    tot_ref[...] = jnp.zeros_like(tot_ref)
    for i in range(n):
        for g in range(2):
            tot_ref[:, 2 * i + g : 2 * i + g + 1] = jnp.sum(
                off_ref[i, :, g * group_rows : (g + 1) * group_rows], axis=1, keepdims=True
            )
    greet(ctx_peers(me, tp, n))
    exchange_start(n, me, tp, lambda peer: off_ref.at[peer], off_land, osend, orecv)
    exchange_start(n, me, tp, lambda peer: tot_ref, tot_land, tsend, trecv)
    mine = pltpu.make_async_copy(off_ref.at[me], off_land.at[me], local.at[0])
    mine_tot = pltpu.make_async_copy(tot_ref, tot_land.at[me], local.at[1])
    mine.start()
    mine_tot.start()
    width = key_ref.shape[2]
    plan = [
        [(w, (0, c)) for c, w in pieces(width, 128)],
        [(w, (1, c)) for c, w in pieces(width, 128)],
    ]

    def local_term(owner, tag):
        which, c0 = tag
        return (key_ref, value_ref)[which][owner, :, c0 : c0 + 128].astype(F32)

    def write(tag, value):
        which, c0 = tag
        (key_out, value_out)[which][:, c0 : c0 + 128] = value

    ring = ScatterRing(
        n, plan, local_term, (slot_r, slot_l), (first_r, first_l), write, send, recv, place, sides, tp
    )
    ring.begin()
    ring.end()
    mine.wait()
    mine_tot.wait()
    exchange_wait(n, me, tp, lambda peer: off_ref.at[peer], off_land, osend, orecv)
    exchange_wait(n, me, tp, lambda peer: tot_ref, tot_land, tsend, trecv)
    off_out[...] = ordered_sum(n, off_land)
    tot_out[...] = ordered_sum(n, tot_land)


def pieces(width, step):
    return [(c, min(step, width - c)) for c in range(0, width, step)]


def pair_scatter(n, collective_id, keys, values, columns, own_rows):
    _, rows, width = keys.shape
    offs, tots = columns, jax.ShapeDtypeStruct((8, LANES), F32)
    chunks = len(pieces(width, 128))
    return pl.pallas_call(
        functools.partial(pair_scatter_kernel, n),
        out_shape=[
            jax.ShapeDtypeStruct((rows, width), F32),
            jax.ShapeDtypeStruct((rows, width), F32),
            jax.ShapeDtypeStruct(offs.shape[1:], F32),
            jax.ShapeDtypeStruct(tots.shape, F32),
        ],
        in_specs=[pl.BlockSpec(memory_space=VMEM)] * 4,
        out_specs=[pl.BlockSpec(memory_space=VMEM)] * 4,
        scratch_shapes=[
            VMEM((n - 1, rows, width), BF16),
            VMEM((n - 1, rows, width), BF16),
            VMEM((rows, width), BF16),
            VMEM((rows, width), BF16),
            VMEM(offs.shape, F32),
            VMEM(tots.shape, F32),
            VMEM(offs.shape, F32),
            VMEM((n,) + tots.shape, F32),
            pltpu.SemaphoreType.DMA((2, chunks, n - 1)),
            pltpu.SemaphoreType.DMA((2, chunks, n - 1)),
            pltpu.SemaphoreType.DMA((n - 1,)),
            pltpu.SemaphoreType.DMA((n - 1,)),
            pltpu.SemaphoreType.DMA((n - 1,)),
            pltpu.SemaphoreType.DMA((n - 1,)),
            pltpu.SemaphoreType.DMA((2,)),
        ],
        compiler_params=pltpu.CompilerParams(
            collective_id=collective_id, has_side_effects=True, vmem_limit_bytes=VMEM_LIMIT
        ),
    )(keys, values, columns, own_rows)


def weight_scatter_kernel(n, plan, left_count, grads, *refs):
    lefts, refs = refs[:left_count], refs[left_count:]
    rights, refs = refs[:grads], refs[grads:]
    small_ref, part_ref, x_ref, gain_ref, dmid_ref, refs = *refs[:5], refs[5:]
    outs, refs = refs[:grads], refs[grads:]
    small_out, input_out, slot_r, slot_l, first_r, first_l, own_small, land, sum_out, refs = *refs[:9], refs[9:]
    tp_bufs, refs = refs[:4], refs[4:]
    send, recv, xsend, xrecv, tsend, trecv, local = refs
    me, tp, place, sides = ring_setup(n)
    chip, core, sibling, across = tp_setup()
    greet(ctx_peers(me, tp, n) + [sibling, across])
    shard = lefts[0].shape[2]
    half = part_ref.shape[0] // 2

    def local_term(owner, tag):
        left, right, c0, cw = tag
        return contract_rows(lefts[left][owner], rights[right][:, c0 : c0 + cw])

    def write(tag, value):
        _, right, c0, cw = tag
        outs[right][:, c0 : c0 + cw] = value

    ring = ScatterRing(
        n, plan, local_term, (slot_r, slot_l), (first_r, first_l), write, send, recv, place, sides, tp
    )

    def part(which, c):
        cols = part_ref.shape[1] // TP_CHUNKS
        return part_ref[pl.ds(pl.multiple_of(which * half, half), half), c * cols : (c + 1) * cols].astype(F32)

    total = TpSum(part, sum_out, tp_bufs, tsend, trecv, core, sibling, across)
    total.first()
    total.second()
    ring.begin()
    total.third()
    ring.advance(1)
    total.fourth()

    own_small[...] = small_ref[...]
    cols = part_ref.shape[1]
    size = 64

    def gain_rows(i, acc):
        rows = pl.ds(pl.multiple_of(i * size, size), size)
        value = x_ref[rows, :].astype(F32)
        inverse = lax.rsqrt(jnp.mean(value * value, axis=-1, keepdims=True) + EPS)
        normal = value * inverse
        grad = sum_out[rows, :].astype(F32)
        back = grad * gain_ref[...]
        back = inverse * (back - normal * jnp.mean(back * normal, axis=-1, keepdims=True))
        input_out[rows, :] = dmid_ref[rows, :] + back
        return acc + jnp.sum((grad * normal).reshape(size // 8, 8, cols), axis=0)

    gains = lax.fori_loop(0, 2 * half // size, gain_rows, jnp.zeros((8, cols), F32))
    gains = jnp.sum(gains, axis=0, keepdims=True)
    for i in range(n):
        own_small[i, 0:1, :shard] = gains[:, i * shard : (i + 1) * shard]
    exchange_start(n, me, tp, lambda peer: own_small.at[peer], land, xsend, xrecv)
    mine = pltpu.make_async_copy(own_small.at[me], land.at[me], local.at[0])
    mine.start()
    ring.end()
    mine.wait()
    exchange_wait(n, me, tp, lambda peer: own_small.at[peer], land, xsend, xrecv)
    small_out[...] = ordered_sum(n, land)


def weight_scatter(n, collective_id, plan, lefts, rights, small, part, x, gain, dmid):
    rows = lefts[0].shape[2]
    chunks = max(len(plan[0]), len(plan[1]))
    totals = [sum(width for width, _ in side) for side in plan]
    return pl.pallas_call(
        functools.partial(weight_scatter_kernel, n, plan, len(lefts), len(rights)),
        out_shape=[jax.ShapeDtypeStruct((rows, right.shape[1]), F32) for right in rights]
        + [jax.ShapeDtypeStruct(small.shape[1:], F32), jax.ShapeDtypeStruct(part.shape, F32)],
        in_specs=[pl.BlockSpec(memory_space=VMEM)] * (len(lefts) + len(rights) + 5),
        out_specs=[pl.BlockSpec(memory_space=VMEM)] * (len(rights) + 2),
        scratch_shapes=[
            VMEM((n - 1, rows, totals[0]), BF16),
            VMEM((n - 1, rows, totals[1]), BF16),
            VMEM((rows, totals[0]), BF16),
            VMEM((rows, totals[1]), BF16),
            VMEM(small.shape, F32),
            VMEM(small.shape, F32),
            VMEM(part.shape, BF16),
            *tp_buffers(*part.shape),
            pltpu.SemaphoreType.DMA((2, chunks, n - 1)),
            pltpu.SemaphoreType.DMA((2, chunks, n - 1)),
            pltpu.SemaphoreType.DMA((n - 1,)),
            pltpu.SemaphoreType.DMA((n - 1,)),
            pltpu.SemaphoreType.DMA((3, TP_CHUNKS)),
            pltpu.SemaphoreType.DMA((3, TP_CHUNKS)),
            pltpu.SemaphoreType.DMA((1,)),
        ],
        compiler_params=pltpu.CompilerParams(
            collective_id=collective_id, has_side_effects=True, vmem_limit_bytes=VMEM_LIMIT
        ),
    )(*lefts, *rights, small, part, x, gain, dmid)


def tp_setup():
    ctx = lax.axis_index("ctx")
    tp = lax.axis_index("tp")
    chip = lax.div(tp, 2)
    core = lax.rem(tp, 2)
    sibling = (ctx, 2 * chip + 1 - core)
    across = (ctx, 2 * (1 - chip) + core)
    return chip, core, sibling, across


TP_CHUNKS = 4


def tp_buffers(rows, width):
    return [VMEM((rows // 2, width), BF16) for _ in range(4)]


class TpSum:
    def __init__(self, part, out, bufs, send, recv, core, sibling, across):
        self.part, self.out, self.send, self.recv = part, out, send, recv
        self.away, self.land_a, self.half_b, self.land_b = bufs
        self.core, self.sibling, self.across = core, sibling, across
        self.half = self.away.shape[0]
        self.size = self.away.shape[1] // TP_CHUNKS

    def cols(self, c):
        return pl.ds(c * self.size, self.size)

    def copy(self, stage, c, which=None):
        cols = self.cols(c)
        if stage == 0:
            source, target, device = self.away.at[:, cols], self.land_a.at[:, cols], self.sibling
        elif stage == 1:
            source, target, device = self.half_b.at[:, cols], self.land_b.at[:, cols], self.across
        else:
            source = target = self.out.at[self.rows(which), cols]
            device = self.sibling
        return remote(source, target, self.send.at[stage, c], self.recv.at[stage, c], device)

    def rows(self, which):
        return pl.ds(pl.multiple_of(which * self.half, self.half), self.half)

    def first(self):
        for c in range(TP_CHUNKS):
            self.away[:, self.cols(c)] = self.part(1 - self.core, c).astype(BF16)
            self.copy(0, c).start()

    def second(self):
        for c in range(TP_CHUNKS):
            cols = self.cols(c)
            mine = self.part(self.core, c)
            self.copy(0, c).wait_recv()
            self.half_b[:, cols] = (mine + self.land_a[:, cols].astype(F32)).astype(BF16)
            self.copy(1, c).start()

    def third(self):
        for c in range(TP_CHUNKS):
            cols = self.cols(c)
            self.copy(1, c).wait_recv()
            both = self.half_b[:, cols].astype(F32) + self.land_b[:, cols].astype(F32)
            self.out[self.rows(self.core), cols] = both.astype(BF16)
            self.copy(2, c, self.core).start()

    def fourth(self):
        for c in range(TP_CHUNKS):
            self.copy(2, c, 1 - self.core).wait_recv()
            self.copy(0, c).wait_send()
            self.copy(1, c).wait_send()
            self.copy(2, c, self.core).wait_send()


class TpSplit:
    def __init__(self, part, bufs, send, recv, chip, core, sibling, across):
        self.part, self.send, self.recv = part, send, recv
        self.away, self.land_a, self.half_b, self.land_b = bufs
        self.chip, self.core, self.sibling, self.across = chip, core, sibling, across

    def copy(self, stage):
        if stage < 2:
            return remote(
                self.away.at[stage], self.land_a.at[stage], self.send.at[stage], self.recv.at[stage], self.sibling
            )
        return remote(self.half_b, self.land_b, self.send.at[2], self.recv.at[2], self.across)

    def first(self):
        for i, chip in enumerate((1 - self.chip, self.chip)):
            self.away[i] = self.part(chip, 1 - self.core).astype(BF16)
            self.copy(i).start()

    def second(self):
        mine = self.part(1 - self.chip, self.core)
        self.copy(0).wait_recv()
        self.half_b[...] = (mine + self.land_a[0].astype(F32)).astype(BF16)
        self.copy(2).start()

    def third(self):
        mine = self.part(self.chip, self.core)
        self.copy(1).wait_recv()
        self.copy(2).wait_recv()
        total = mine + self.land_a[1].astype(F32) + self.land_b[...].astype(F32)
        for stage in range(3):
            self.copy(stage).wait_send()
        return total


def feed_kernel(n, heads, attention, *refs):
    if attention:
        (group_map, doc_lengths, skip, q_in, term_in, k_in, v_in, aug_in), refs = refs[:8], refs[8:]
    (att_in, gl_in, outw_in, x_in, gain_ref, grad_in, wg_in, wu_in, wd_in), refs = refs[:9], refs[9:]
    (gated_out, layer_ref, down_out, gate_out, up_out, dmid_out, do_out, dgl_out, gain_out), refs = refs[:9], refs[9:]
    if attention:
        (dm_out, dq_out, drow_ref, dk_out, dv_out, dcol_ref), refs = refs[:6], refs[6:]
    (
        att_ref, gl_ref, outw_ref, x_ref, gated_ref, normed_ref, dgt_ref, dup_ref, do_ref, dgl_ref,
        gate_all, up_all, down_all, accs, dhid_acc, hid_ref, branch_ref, mid_ref, dw_ref, dy_ref,
        a0, a1, a2, a3, b3, s0, s1, s2, s3, dslot_r, dslot_l, dfirst_r, dfirst_l, eslot_r, eslot_l, efirst_r, efirst_l,
        gsend, grecv, hsend, hrecv, asend, arecv, bsend, brecv, ssend, srecv, dsend, drecv, esend, erecv, local,
    ), refs = refs[:52], refs[52:]
    if attention:
        term_ref, diff_ref, span_ref, stage, kv_sem, stage_sem = refs
    gate_acc, up_acc = accs.at[0], accs.at[1]
    me, tp, place, sides = ring_setup(n)
    chip, core, sibling, across = tp_setup()
    moves = Moves(local)
    for name, source, target in (
        ("att", att_in, att_ref), ("gl", gl_in, gl_ref), ("outw", outw_in, outw_ref), ("grad", grad_in, dw_ref),
        ("x", x_in, x_ref),
    ):
        moves.start(name, source, target)
    if attention:
        moves.start("term", term_in, term_ref)
    greet([(side, tp) for side in sides] + [sibling, across])
    shard, hidden = wg_in.shape
    rows, width = x_in.shape
    half = rows // 2
    hw = hidden // 2
    size = 64
    ring = (n, place, sides, tp)

    def rows_of(owner):
        return pl.ds(pl.multiple_of(owner * shard, 16), shard)

    def window(ref, c0, cw):
        return lambda owner: ref.at[rows_of(owner), pl.ds(c0, cw)]

    def chunks(members):
        return [(side, source.at[:, pl.ds(c0, cw)], window(target, c0, cw)) for side, source, target, c0, cw in members]

    gates = Gather(
        *ring,
        chunks(
            [
                (side, source, target, c0, hw)
                for c0 in (0, hw)
                for side, source, target in ((0, wg_in, gate_all), (1, wu_in, up_all))
            ]
        ),
        gsend, grecv,
    )
    downs = Gather(
        *ring,
        chunks([(side, wd_in, down_all, side * hw + c0, hw // 2) for c0 in (0, hw // 2) for side in (0, 1)]),
        hsend, hrecv,
    )
    gates.begin()
    for i, (source, target) in enumerate(((wg_in, gate_all), (wu_in, up_all), (wd_in, down_all))):
        moves.start(i, source, target.at[rows_of(me)])

    moves.wait("att", "gl")
    gated_ref[...] = (att_ref[...] * jax.nn.sigmoid(gl_ref[...])).astype(BF16)
    moves.start("gated", gated_ref, gated_out)
    moves.wait("outw")
    span = width // TP_CHUNKS

    def branch_part(which, c):
        mine = gated_ref[pl.ds(pl.multiple_of(which * half, half), half), :]
        return contract_cols(mine, outw_ref[c * span : (c + 1) * span, :])

    branch = TpSum(branch_part, branch_ref, (a0, a1, a2, a3), asend, arecv, core, sibling, across)
    branch.first()
    branch.second()
    gates.forward(1)
    moves.wait("grad")
    for c in range(TP_CHUNKS):
        back = pl.ds(c * span, span)
        dy_ref[back, :] = dw_ref[:, back].astype(F32).T.astype(BF16)
    dhid_acc[...] = jnp.zeros_like(dhid_acc)
    gate_acc[...] = jnp.zeros_like(gate_acc)
    up_acc[...] = jnp.zeros_like(up_acc)

    def grow_back(back):
        for side in (0, 1):
            owner = downs.owner(side, back)
            cols = pl.ds(side * hw, hw)
            dhid_acc[:, cols] += contract_rows(dy_ref[rows_of(owner), :], down_all[rows_of(owner), cols])

    def grow(back):
        for side, acc, source in ((0, gate_acc, gate_all), (1, up_acc, up_all)):
            owner = gates.owner(side, back)
            acc[...] += contract_rows(normed_ref[rows_of(owner), :], source[rows_of(owner), :])

    moves.wait(0, 1, 2)
    grow_back(0)
    gates.forward(2)
    branch.third()
    branch.fourth()
    moves.wait("x")

    def norm_rows(i, carry):
        here = pl.ds(pl.multiple_of(i * LANES, LANES), LANES)
        middle = x_ref[here, :].astype(F32) + branch_ref[here, :].astype(F32)
        mid_ref[here, :] = middle
        normed_ref[:, here] = (rms_scale(middle) * gain_ref[...]).T.astype(BF16)
        return carry

    lax.fori_loop(0, rows // LANES, norm_rows, 0)
    own = pl.ds(pl.multiple_of(tp * span, span), span)
    layer_ref[...] = mid_ref[:, own]
    moves.start("again", grad_in, x_ref)
    gates.forward(3)

    def grow_step(step, carry):
        grow(step)
        return carry

    lax.fori_loop(0, 4, grow_step, 0)

    def gate_step(step, carry):
        gates.forward(step)
        grow(step)
        return carry

    lax.fori_loop(4, n - 1, gate_step, 0)
    downs.begin()
    gates.last()
    grow(n - 1)

    def hid_rows(i, carry):
        here = pl.ds(pl.multiple_of(i * size, size), size)
        gate, up = gate_acc[here, :], up_acc[here, :]
        open_gate = jax.nn.sigmoid(gate)
        silu = gate * open_gate
        hid_ref[here, :] = (silu * up).astype(BF16)
        gate_acc[here, :] = up * open_gate * (1.0 + gate * (1.0 - open_gate))
        up_acc[here, :] = silu
        return carry

    lax.fori_loop(0, rows // size, hid_rows, 0)

    def down_step(step, carry):
        downs.forward(step)
        grow_back(step)
        return carry

    lax.fori_loop(1, n - 2, down_step, 0)
    downs.forward(n - 2)

    def down_term(owner, tag):
        return dot(dy_ref[rows_of(owner), :], hid_ref[:, tag * hw : (tag + 1) * hw])

    down_ref = accs.at[0, pl.ds(0, shard), :]
    gate_ref = accs.at[0, pl.ds(shard, shard), :]
    up_ref = accs.at[1, pl.ds(0, shard), :]

    def down_write(tag, value):
        down_ref[:, tag * hw : (tag + 1) * hw] = value

    def early_term(owner, tag):
        which, c0 = tag
        return dot(normed_ref[rows_of(owner), :], (dgt_ref, dup_ref)[which][:, c0 : c0 + hw])

    def early_write(tag, value):
        which, c0 = tag
        (gate_ref, up_ref)[which][:, c0 : c0 + hw] = value

    backs = ScatterRing(
        n, [[(hw, 0)], [(hw, 1)]], down_term, (dslot_r, dslot_l), (dfirst_r, dfirst_l), down_write,
        dsend, drecv, place, sides, tp,
    )
    earlies = [
        ScatterRing(
            n, [[(hw, (i, part * hw))] for i in range(2)], early_term, (eslot_r.at[part], eslot_l.at[part]),
            (efirst_r.at[part], efirst_l.at[part]), early_write, esend.at[part], erecv.at[part], place, sides, tp,
        )
        for part in range(2)
    ]
    backs.begin()
    grow_back(n - 2)
    downs.last()
    grow_back(n - 1)

    def grad_rows(i, carry):
        here = pl.ds(pl.multiple_of(i * size, size), size)
        dhid = dhid_acc[here, :]
        dgt_ref[here, :] = (dhid * gate_acc[here, :]).astype(BF16)
        dup_ref[here, :] = (dhid * up_acc[here, :]).astype(BF16)
        return carry

    lax.fori_loop(0, rows // size, grad_rows, 0)

    def dw_part(which, c):
        mine = pl.ds(pl.multiple_of(which * half, half), half)
        back = pl.ds(c * span, span)
        return contract_cols(dgt_ref[mine, :], gate_all[back, :]) + contract_cols(dup_ref[mine, :], up_all[back, :])

    def layer_part(which_chip, which_core):
        back = pl.ds(pl.multiple_of((2 * which_chip + which_core) * span, span), span)
        return contract_cols(hid_ref[...], down_all[back, :])

    total = TpSum(dw_part, dw_ref, (a0, a1, a2, b3), bsend, brecv, core, sibling, across)
    layer = TpSplit(layer_part, (s0, s1, s2, s3), ssend, srecv, chip, core, sibling, across)
    total.first()
    backs.advance(1)
    earlies[0].begin()
    earlies[1].begin()
    total.second()
    gates.sent()
    if attention:
        pairs = heads // 2

        def kv_copies(it):
            part, pair = lax.div(it, pairs), lax.rem(it, pairs)
            source = pl.ds(pl.multiple_of(part * rows, rows), rows)
            target = pl.ds(pl.multiple_of(pair * rows, rows), rows)
            lanes = pl.ds(pl.multiple_of(part * LANES, LANES), LANES)
            return [
                pltpu.make_async_copy(ref.at[pair, source, :], held.at[target, lanes], kv_sem.at[i, it])
                for i, (ref, held) in enumerate(((k_in, gate_all), (v_in, up_all)))
            ]

        def bring(it, carry):
            for copy in kv_copies(it):
                copy.start()
            return carry

        lax.fori_loop(0, n * pairs, bring, 0)
    layer.first()
    layer.second()
    for _ in range(2):
        backs.advance(1)
        earlies[0].advance(1)
        earlies[1].advance(1)
    total.third()
    total.fourth()

    def middle_rows(i, acc):
        here = pl.ds(pl.multiple_of(i * size, size), size)
        middle = mid_ref[here, :]
        inverse = lax.rsqrt(jnp.mean(middle * middle, axis=-1, keepdims=True) + EPS)
        normal = middle * inverse
        dw = dw_ref[here, :].astype(F32)
        back = dw * gain_ref[...]
        back = inverse * (back - normal * jnp.mean(back * normal, axis=-1, keepdims=True))
        dmid = x_ref[here, :].astype(F32) + back
        mid_ref[here, :] = dmid
        branch_ref[here, :] = dmid.astype(BF16)
        return acc + jnp.sum((dw * normal).reshape(size // 8, 8, width), axis=0)

    moves.wait("again")
    gain_out[...] = lax.fori_loop(0, rows // size, middle_rows, jnp.zeros((8, width), F32))
    if attention:
        narrow = q_in.shape[1]
        q_ref = x_ref.at[:, pl.ds(0, narrow)]
        moves.start("q", q_in, q_ref)
        for i in range(n):
            moves.start(
                ("aug", i),
                aug_in.at[pl.ds(i * rows, rows), :],
                x_ref.at[:, pl.ds(narrow + i * LANES, LANES)],
            )
    moves.start("dmid", mid_ref, dmid_out)
    if attention:
        moves.start("dm", branch_ref, dm_out)
    da = dot(branch_ref[...], outw_ref[...])
    open_gate = jax.nn.sigmoid(gl_ref[...])
    do_ref[...] = (da * open_gate).astype(BF16)
    dgl_ref[...] = (da * att_ref[...] * open_gate * (1.0 - open_gate)).astype(BF16)
    moves.start("do", do_ref, do_out)
    moves.start("dgl", dgl_ref, dgl_out)
    backs.advance(1)
    earlies[0].advance(1)
    earlies[1].advance(1)
    layer_ref[...] += layer.third()

    if attention:
        moves.wait("q", "term", *[("aug", i) for i in range(n)])
        first, second = group_map[2 * me], group_map[2 * me + 1]
        in_order = first < second
        query_groups = (jnp.minimum(first, second), jnp.maximum(first, second))

        def put_in(ref):
            def put(h, value, extra):
                ref[:, 2 * h * LANES : (2 * h + 1) * LANES] = value
                ref[:, (2 * h + 1) * LANES : (2 * h + 2) * LANES] = extra

            return put

        spread_heads(q_ref, row_pieces(term_ref[...], True), put_in(dw_ref), heads, in_order)
        delta = head_sums(do_ref[...].astype(F32) * att_ref[...], heads)
        moves.wait("dm")
        spread_heads(do_ref, row_pieces(-delta, False), put_in(branch_ref), heads, in_order)
        accs[...] = jnp.zeros_like(accs)
        query_at = lax.broadcasted_iota(jnp.int32, (half, half), 1)
        key_at = lax.broadcasted_iota(jnp.int32, (half, half), 0)
        diff_ref[...] = key_at - query_at
        for i, group in enumerate(query_groups):
            span_ref[i] = document_start(group * half + query_at, doc_lengths) - key_at
        dcol_acc = dhid_acc.at[:, pl.ds(0, LANES)]

        def stage_copies(it):
            part, pair = lax.div(it, pairs), lax.rem(it, pairs)
            lanes = pl.ds(pl.multiple_of(pair * LANES, LANES), LANES)
            slot = lax.rem(it, 2)
            return [
                pltpu.make_async_copy(stage.at[slot, i], out.at[part, :, lanes], stage_sem.at[slot, i])
                for i, out in enumerate((dk_out, dv_out))
            ]

        def attend(it, carry):
            part, pair = lax.div(it, pairs), lax.rem(it, pairs)
            for copy in kv_copies(it):
                copy.wait()
            one, two = group_map[2 * part], group_map[2 * part + 1]
            forward = one < two
            key_groups = (jnp.minimum(one, two), jnp.maximum(one, two))
            lanes = pl.ds(pl.multiple_of(part * LANES, LANES), LANES)

            def ordered(ref, base, where):
                top = pl.ds(pl.multiple_of(base * rows, rows), half)
                bottom = pl.ds(pl.multiple_of(base * rows + half, half), half)
                return in_pack_order(forward, ref[top, where], ref[bottom, where])

            key_blocks = ordered(gate_all, pair, lanes)
            value_blocks = ordered(up_all, pair, lanes)
            aug_lanes = pl.ds(pl.multiple_of(narrow + part * LANES, LANES), LANES)
            aug_blocks = ordered(x_ref, 0, aug_lanes)
            masks = block_masks(diff_ref, span_ref, skip, query_groups, key_groups, half)
            keys = [jnp.concatenate([key_blocks[ki], aug_blocks[ki]], axis=1) for ki in range(2)]
            values = [jnp.concatenate([value_blocks[ki], aug_blocks[ki]], axis=1) for ki in range(2)]
            both_keys = jnp.concatenate(keys, axis=0)
            queries, douts, probs, grads = [], [], ([], []), ([], [])
            for e in range(2):
                h = 2 * pair + e
                spot = pl.ds(pl.multiple_of(h * 2 * LANES, 2 * LANES), 2 * LANES)
                query, dout = dw_ref[:, spot], branch_ref[:, spot]
                early = contract_cols(keys[0], query)
                scores = (early[:, :half], early[:, half:], contract_cols(keys[1], query[half:]))
                early = contract_cols(values[0], dout)
                backs_out = (early[:, :half], early[:, half:], contract_cols(values[1], dout[half:]))
                prob = [jnp.where(mask, jnp.exp(score), 0.0) for mask, score in zip(masks, scores)]
                grad = [(p * back).astype(BF16) for p, back in zip(prob, backs_out)]
                prob = [p.astype(BF16) for p in prob]
                queries.append(query)
                douts.append(dout[:, :LANES])
                probs[0].extend(prob[:2])
                probs[1].append(prob[2])
                grads[0].extend(grad[:2])
                grads[1].append(grad[2])
                quarter = pl.ds(pl.multiple_of(lax.rem(h, 4) * 2 * LANES, 2 * LANES), 2 * LANES)
                accs[lax.div(h, 4), :half, quarter] += contract_rows(grad[0], keys[0])
                accs[lax.div(h, 4), half:, quarter] += contract_rows(jnp.concatenate(grad[1:], axis=0), both_keys)
            late_queries = jnp.concatenate([query[half:] for query in queries], axis=0)
            late_douts = jnp.concatenate([dout[half:] for dout in douts], axis=0)
            queries, douts = jnp.concatenate(queries, axis=0), jnp.concatenate(douts, axis=0)
            sums = [
                dot(jnp.concatenate(grads[0], axis=1), queries),
                dot(jnp.concatenate(grads[1], axis=1), late_queries),
            ]
            value_sums = [
                dot(jnp.concatenate(probs[0], axis=1), douts),
                dot(jnp.concatenate(probs[1], axis=1), late_douts),
            ]
            columns = jnp.concatenate([part_sum[:, LANES:] for part_sum in sums], axis=0)
            dcol_acc[...] = jnp.where(pair == 0, 0.0, dcol_acc[...]) + columns

            @pl.when(it >= 2)
            def _():
                for copy in stage_copies(it - 2):
                    copy.wait()

            slot = lax.rem(it, 2)
            for i, part_sums in enumerate(([part_sum[:, :LANES] for part_sum in sums], value_sums)):
                stage[slot, i] = jnp.concatenate(in_pack_order(forward, *part_sums), axis=0).astype(BF16)
            for copy in stage_copies(it):
                copy.start()

            @pl.when(pair == pairs - 1)
            def _():
                columns = jnp.concatenate(
                    in_pack_order(forward, dcol_acc[pl.ds(0, half), :], dcol_acc[pl.ds(half, half), :]), axis=0
                )
                dcol_ref[part] = -(columns.T[:8])

            return carry

        turns = (*earlies, backs)
        starts = [ring.next for ring in turns]
        services = sum(n - 1 - start for start in starts)
        assert starts[0] == starts[1] == starts[2] - 1
        share = n * pairs // services

        def serve(k, carry):
            lax.fori_loop(k * share, (k + 1) * share, attend, 0)
            for i, ring in enumerate(turns):

                @pl.when(lax.rem(k, 3) == i)
                def _(i=i, ring=ring):
                    ring.forward(starts[i] + lax.div(k, 3))

            return carry

        lax.fori_loop(0, services, serve, 0)
        for ring in turns:
            ring.next = n - 1
        if services * share < n * pairs:
            lax.fori_loop(services * share, n * pairs, attend, 0)
        for it in (n * pairs - 2, n * pairs - 1):
            for copy in stage_copies(it):
                copy.wait()

        lane = lax.broadcasted_iota(jnp.int32, (rows, LANES), 1)
        low = low_lanes(rows)
        sums = jnp.zeros((rows, LANES), F32)
        for pair in range(pairs):
            parts = []
            for h in (2 * pair, 2 * pair + 1):
                spot = pl.ds((h % 4) * 2 * LANES, 2 * LANES)
                value = jnp.concatenate(
                    in_pack_order(in_order, accs[h // 4, :half, spot], accs[h // 4, half:, spot]), axis=0
                )
                parts.append(value)
                sums = jnp.where(lane == 24 + h, value[:, LANES:], sums)
            dhid_acc[:, (3 + pair) * LANES : (4 + pair) * LANES] = jnp.where(
                low, parts[0][:, :LANES], parts[1][:, :LANES]
            )
        moves.start("dq", dhid_acc.at[:, pl.ds(3 * LANES, pairs * LANES)], dq_out)
        drow_ref[...] = pltpu.roll(sums, LANES - 24, 1).T[:8]

        moves.wait("dq")
    backs.end()
    moves.start("down", down_ref, down_out)
    earlies[0].end()
    earlies[1].end()
    moves.start("gate", gate_ref, gate_out)
    moves.start("up", up_ref, up_out)
    downs.sent()
    moves.wait()


def feed_forward(
    n, collective_id, heads, attended, gate_logit, out_weight, x, gain, dy, w_gate, w_up, w_down, attention=None
):
    rows, width = x.shape
    shard, hidden = w_gate.shape
    heads_width = attended.shape[1]
    own = width // 4
    half = rows // 2
    dma = pltpu.SemaphoreType.DMA
    vmem = pl.BlockSpec(memory_space=VMEM)
    anywhere = pl.BlockSpec(memory_space=pl.ANY)
    wide, narrow, deep = (rows, width), (rows, heads_width), (rows, hidden)
    turned = (n * shard, rows)
    weight = (shard, hidden)
    shapes = [
        (narrow, BF16),
        ((rows, own), F32),
        (weight, F32),
        (weight, F32),
        (weight, F32),
        (wide, F32),
        (narrow, BF16),
        (narrow, BF16),
        ((8, width), F32),
    ]
    kept = [1, 8]
    extra_specs, extra_scratch = [], []
    if attention is not None:
        assert heads // 2 * rows == n * shard and n * LANES == hidden and heads_width + hidden <= width
        shapes += [
            (wide, BF16),
            (narrow, F32),
            ((8, rows), F32),
            ((n, rows, heads_width), BF16),
            ((n, rows, heads_width), BF16),
            ((n, 8, rows), F32),
        ]
        kept += [11, 14]
        extra_specs = [smem()] * 3 + [anywhere] * 5
        extra_scratch = [
            VMEM((rows, LANES), F32),
            VMEM((half, half), jnp.int32),
            VMEM((2, half, half), jnp.int32),
            VMEM((2, 2, rows, LANES), BF16),
            dma((2, n * heads // 2)),
            dma((2, 2)),
        ]
    return pl.pallas_call(
        functools.partial(feed_kernel, n, heads, attention is not None),
        out_shape=[jax.ShapeDtypeStruct(*shape) for shape in shapes],
        in_specs=extra_specs + [anywhere] * 4 + [vmem] + [anywhere] * 4,
        out_specs=[vmem if i in kept else anywhere for i in range(len(shapes))],
        scratch_shapes=[
            VMEM(narrow, F32),
            VMEM(narrow, F32),
            VMEM(out_weight.shape, BF16),
            VMEM(wide, BF16),
            VMEM(narrow, BF16),
            VMEM(turned, BF16),
            VMEM(deep, BF16),
            VMEM(deep, BF16),
            VMEM(narrow, BF16),
            VMEM(narrow, BF16),
            *[VMEM((n * shard, hidden), BF16)] * 3,
            VMEM((2,) + deep, F32),
            VMEM(deep, F32),
            VMEM(deep, BF16),
            VMEM(wide, BF16),
            VMEM(wide, F32),
            VMEM(wide, BF16),
            VMEM(turned, BF16),
            *tp_buffers(rows, width),
            VMEM((rows // 2, width), BF16),
            VMEM((2, rows, own), BF16),
            VMEM((2, rows, own), BF16),
            VMEM((rows, own), BF16),
            VMEM((rows, own), BF16),
            *ring_scratch(n, shard, [hidden // 2] * 2),
            *[VMEM((2, n - 1, shard, hidden // 2), BF16)] * 2,
            *[VMEM((2, shard, hidden // 2), BF16)] * 2,
            *[dma((4, n - 1))] * 4,
            *[dma((3, TP_CHUNKS))] * 4,
            *[dma((3,))] * 2,
            *[dma((2, 1, n - 1))] * 2,
            *[dma((2, 2, 1, n - 1))] * 2,
            dma((28,)),
            *extra_scratch,
        ],
        compiler_params=pltpu.CompilerParams(
            collective_id=collective_id, has_side_effects=True, vmem_limit_bytes=VMEM_LIMIT
        ),
    )(*(attention or ()), attended, gate_logit, out_weight, x, gain, dy, w_gate, w_up, w_down)


def ring_scratch(n, height, widths):
    return [VMEM((n - 1, height, w), BF16) for w in widths] + [VMEM((height, w), BF16) for w in widths]


def head_means(value, heads):
    width = value.shape[1]
    size = width // heads
    left = lax.div(lax.broadcasted_iota(jnp.int32, (width, width), 0), size)
    right = lax.div(lax.broadcasted_iota(jnp.int32, (width, width), 1), size)
    member = (left == right).astype(BF16)
    high = value.astype(BF16)
    return (dot(high, member) + dot((value - high.astype(F32)).astype(BF16), member)) * (1.0 / size)


STAGED = (0, 1, 4, 5, 16, 11, 14, 17, 18, 19, 6, 12, 13, 20)


def finish_kernel(n, heads, gate_plan, attn_plan, *refs):
    operands, refs = list(refs[:24]), refs[24:]
    (q_out, k_out, v_out, g_out, o_out, small_out, input_out), refs = refs[:7], refs[7:]
    staged, refs = refs[: len(STAGED)], refs[len(STAGED) :]
    (
        dmt_ref, pslot_r, pslot_l, gslot_r, gslot_l, gfirst_r, gfirst_l, aslot_r, aslot_l, afirst_r, afirst_l,
        dk_sum, dv_sum, dqr_ref, dkr_ref, dvl_ref, du_ref, sum_ref, t0, t1, t2, t3,
        off_ref, tot_ref, off_land, tot_land, small_ref, small_land,
        psend, precv, gsend, grecv, asend, arecv, osend, orecv, qsend, qrecv, xsend, xrecv, tsend, trecv, local,
    ) = refs
    moves = Moves(local)
    dk_hbm, dv_hbm = operands[:2]
    for target, index in zip(staged, STAGED):
        moves.start(index, operands[index], target)
        operands[index] = target
    (
        dk_ref, dv_ref, col_ref, row_ref, dq_ref, qr_ref, kr_ref, qgain_ref, kgain_ref, fz_ref, group_map,
        wq_ref, wk_ref, wv_ref, wg_ref, wf_ref, dgl_ref, u_ref, dm_ref, gated_ref,
        x_ref, gain_ref, dmid_ref, gain_two_ref,
    ) = operands
    me, tp, place, sides = ring_setup(n)
    chip, core, sibling, across = tp_setup()
    rows, width = dq_ref.shape
    cols = x_ref.shape[1]
    shard = u_ref.shape[0] // n
    half = rows // 2
    head_dim = width // heads

    def rows_of(owner):
        return pl.ds(pl.multiple_of(owner * shard, 16), shard)

    small_ref[...] = jnp.zeros_like(small_ref)
    greet(ctx_peers(me, tp, n) + [sibling, across])

    def pair_term(owner, tag):
        which, c0 = tag
        return (dk_ref, dv_ref)[which][owner, :, c0 : c0 + LANES].astype(F32)

    def pair_write(tag, value):
        which, c0 = tag
        (dk_sum, dv_sum)[which][:, c0 : c0 + LANES] = value

    pairs = ScatterRing(
        n, [[(w, (i, c)) for c, w in pieces(width, LANES)] for i in range(2)], pair_term,
        (pslot_r, pslot_l), None, pair_write, psend, precv, place, sides, tp,
        source=lambda target, side, window: (dk_hbm, dv_hbm)[side].at[target, :, window],
    )
    pairs.begin()
    off_ref[...] = col_ref[...]
    off_ref[me] += row_ref[...]
    tot_ref[...] = jnp.zeros_like(tot_ref)
    for i in range(n):
        for g in range(2):
            tot_ref[:, 2 * i + g : 2 * i + g + 1] = jnp.sum(
                off_ref[i, :, g * half : (g + 1) * half], axis=1, keepdims=True
            )
    exchange_start(n, me, tp, lambda peer: off_ref.at[peer], off_land, osend, orecv)
    exchange_start(n, me, tp, lambda peer: tot_ref, tot_land, qsend, qrecv)
    moves.start("off", off_ref.at[me], off_land.at[me])
    moves.start("tot", tot_ref, tot_land.at[me])

    def raw_grad(grad, raw, gain):
        inverse = lax.rsqrt(head_means(raw * raw, heads) + EPS)
        normal = raw * inverse
        back = grad * gain
        back = inverse * (back - normal * head_means(back * normal, heads))
        return back.astype(BF16), jnp.sum(grad * normal, axis=0, keepdims=True)

    def gain_rows(row, first):
        count = 2 * head_dim // n
        for i in range(n // 2):
            for h in range(heads):
                lane = h * head_dim + i * count
                small_ref[first + i, 2 + h : 3 + h, 0:count] = row[:, lane : lane + count]

    moves.wait(0, 1, 4, 5)
    pairs.advance(1)
    dqr, row = raw_grad(dq_ref[...], qr_ref[...], qgain_ref[...] * 0.125)
    dqr_ref[...] = dqr
    gain_rows(row * 0.125, 0)
    pairs.advance(1)
    moves.wait(16, 11, 14)
    span = cols // TP_CHUNKS
    for c in range(TP_CHUNKS):
        back = pl.ds(c * span, span)
        du_ref[:, back] = contract_cols(dqr_ref[...], wq_ref[back, :]) + contract_cols(dgl_ref[...], wg_ref[back, :])
    moves.wait(18)
    for c in range(TP_CHUNKS):
        back = pl.ds(c * span, span)
        dmt_ref[back, :] = dm_ref[:, back].astype(F32).T.astype(BF16)
    pairs.advance(n)
    moves.wait(17, 19)

    def gate_term(owner, tag):
        right, c0, cw = tag
        left = dmt_ref if right == 2 else u_ref
        return dot(left[rows_of(owner), :], (dqr_ref, dgl_ref, gated_ref)[right][:, c0 : c0 + cw])

    def gate_write(tag, value):
        right, c0, cw = tag
        (q_out, g_out, o_out)[right][:, c0 : c0 + cw] = value

    gates = ScatterRing(
        n, gate_plan, gate_term, (gslot_r, gslot_l), (gfirst_r, gfirst_l), gate_write, gsend, grecv, place, sides, tp,
    )
    gates.begin()
    pairs.end()

    moves.wait(6)
    dkr, row = raw_grad(dk_sum[...], kr_ref[...], kgain_ref[...])
    dkr_ref[...] = dkr
    gain_rows(row, n // 2)
    dvl_ref[...] = dv_sum[...].astype(BF16)

    def attn_term(owner, tag):
        c0, cw = tag[1], tag[2]
        return dot(u_ref[rows_of(owner), :], (dkr_ref, dvl_ref)[tag[0]][:, c0 : c0 + cw])

    def attn_write(tag, value):
        c0, cw = tag[1], tag[2]
        (k_out, v_out)[tag[0]][:, c0 : c0 + cw] = value

    attns = ScatterRing(
        n, attn_plan, attn_term, (aslot_r, aslot_l), (afirst_r, afirst_l), attn_write, asend, arecv, place, sides, tp,
    )
    attns.begin()
    gates.advance(1)
    moves.wait("off", "tot")
    exchange_wait(n, me, tp, lambda peer: off_ref.at[peer], off_land, osend, orecv)
    exchange_wait(n, me, tp, lambda peer: tot_ref, tot_land, qsend, qrecv)
    off_sum = ordered_sum(n, off_land)
    tot_sum = ordered_sum(n, tot_land)
    onward = (
        lax.broadcasted_iota(jnp.int32, (half, half), 0) >= lax.broadcasted_iota(jnp.int32, (half, half), 1)
    ).astype(F32)
    parts = []
    for g in range(2):
        suffix = jnp.dot(
            off_sum[:, g * half : (g + 1) * half], onward, precision=HIGHEST, preferred_element_type=F32
        )
        later = groups_along(group_map, 1, -1, (8, LANES)) > group_map[2 * me + g]
        parts.append(suffix + jnp.sum(jnp.where(later, tot_sum, 0.0), axis=1, keepdims=True))
    dfz = (jnp.concatenate(parts, axis=1) * jax.nn.sigmoid(-fz_ref[...])).astype(BF16).astype(F32)
    head = lax.broadcasted_iota(jnp.int32, dfz.shape, 0)
    dfz = jnp.where(head < heads, dfz, 0.0)
    bias = jnp.sum(dfz, axis=1, keepdims=True)
    dfz_cols = turn(dfz).astype(BF16)
    dfz_low = dfz.astype(BF16)
    for i in range(n):
        small_ref[i, 8:16, :shard] = contract_cols(dfz_low, u_ref[i * shard : (i + 1) * shard, :])
        small_ref[i, 8:16, 224:225] = bias
        small_ref[i, 1:2, :shard] = jnp.sum(gain_two_ref[:, i * shard : (i + 1) * shard], axis=0, keepdims=True)

    moves.wait(12, 13)
    forget = jnp.concatenate([wf_ref[...], jnp.zeros((LANES - 8, cols), F32)], axis=0).astype(BF16)
    for c in range(TP_CHUNKS):
        back = pl.ds(c * span, span)
        du_ref[:, back] += (
            contract_cols(dkr_ref[...], wk_ref[back, :])
            + contract_cols(dvl_ref[...], wv_ref[back, :])
            + dot(dfz_cols, forget[:, c * span : (c + 1) * span])
        )

    def part(which, c):
        return du_ref[pl.ds(pl.multiple_of(which * half, half), half), c * span : (c + 1) * span]

    total = TpSum(part, sum_ref, (t0, t1, t2, t3), tsend, trecv, core, sibling, across)
    total.first()
    attns.advance(1)
    total.second()
    moves.start("dmid", dmid_ref, du_ref)
    gates.advance(1)
    attns.advance(1)
    gates.advance(1)
    total.third()
    attns.advance(1)
    total.fourth()
    moves.wait("dmid", 20)
    size = 64

    def input_rows(i, acc):
        here = pl.ds(pl.multiple_of(i * size, size), size)
        value = x_ref[here, :].astype(F32)
        inverse = lax.rsqrt(jnp.mean(value * value, axis=-1, keepdims=True) + EPS)
        normal = value * inverse
        grad = sum_ref[here, :].astype(F32)
        back = grad * gain_ref[...]
        back = inverse * (back - normal * jnp.mean(back * normal, axis=-1, keepdims=True))
        du_ref[here, :] += back
        return acc + jnp.sum((grad * normal).reshape(size // 8, 8, cols), axis=0)

    gains = lax.fori_loop(0, rows // size, input_rows, jnp.zeros((8, cols), F32))
    moves.start("input", du_ref, input_out)
    for i in range(n):
        small_ref[i, 0:1, :shard] = jnp.sum(gains[:, i * shard : (i + 1) * shard], axis=0, keepdims=True)
    exchange_start(n, me, tp, lambda peer: small_ref.at[peer], small_land, xsend, xrecv)
    moves.start("small", small_ref.at[me], small_land.at[me])
    while gates.next < n - 1:
        gates.advance(1)
        attns.advance(1)
    gates.end()
    attns.end()
    moves.wait("small")
    exchange_wait(n, me, tp, lambda peer: small_ref.at[peer], small_land, xsend, xrecv)
    small_out[...] = ordered_sum(n, small_land)
    pairs.sent()
    moves.wait()


def finish_backward(n, collective_id, heads, gate_plan, attn_plan, *operands):
    dq, u, x = operands[4], operands[17], operands[20]
    rows, width = dq.shape
    cols = x.shape[1]
    shard = u.shape[0] // n
    dma = pltpu.SemaphoreType.DMA
    vmem = pl.BlockSpec(memory_space=VMEM)
    anywhere = pl.BlockSpec(memory_space=pl.ANY)
    outside = STAGED + (22,)
    gate_widths = [sum(w for w, _ in side) for side in gate_plan]
    attn_widths = [sum(w for w, _ in side) for side in attn_plan]

    def ring_semaphores(plan):
        return [dma((2, max(len(side) for side in plan), n - 1))] * 2

    shapes = [(shard, width)] * 5 + [(16, 256), (rows, cols)]
    return pl.pallas_call(
        functools.partial(finish_kernel, n, heads, gate_plan, attn_plan),
        out_shape=[jax.ShapeDtypeStruct(shape, F32) for shape in shapes],
        in_specs=[anywhere if i in outside else smem() if i == 10 else vmem for i in range(len(operands))],
        out_specs=[vmem] * 6 + [anywhere],
        scratch_shapes=[
            *[VMEM(operands[i].shape, operands[i].dtype) for i in STAGED],
            VMEM(u.shape, BF16),
            *[VMEM((n - 1, rows, width), BF16)] * 2,
            *ring_scratch(n, shard, gate_widths),
            *ring_scratch(n, shard, attn_widths),
            VMEM((rows, width), F32),
            VMEM((rows, width), F32),
            *[VMEM((rows, width), BF16)] * 3,
            VMEM((rows, cols), F32),
            VMEM((rows, cols), BF16),
            *tp_buffers(rows, cols),
            VMEM((n, 8, rows), F32),
            VMEM((8, LANES), F32),
            VMEM((n, 8, rows), F32),
            VMEM((n, 8, LANES), F32),
            VMEM((n, 16, 256), F32),
            VMEM((n, 16, 256), F32),
            *[dma((2, len(pieces(width, LANES)), n - 1))] * 2,
            *ring_semaphores(gate_plan),
            *ring_semaphores(attn_plan),
            *[dma((n - 1,))] * 6,
            *[dma((3, TP_CHUNKS))] * 2,
            dma((len(STAGED) + 5,)),
        ],
        compiler_params=pltpu.CompilerParams(
            collective_id=collective_id, has_side_effects=True, vmem_limit_bytes=VMEM_LIMIT
        ),
    )(*operands)


LANES = 128


def block_state(group_map, doc_lengths, skip, query_group, key_group, rows, docs):
    first_q = query_group * rows
    last_q = first_q + rows - 1
    first_k = key_group * rows
    last_k = first_k + rows - 1
    zero = jnp.int32(0)
    doc_qf, doc_ql, doc_kf, doc_kl, end = zero, zero, zero, zero, zero
    for d in range(docs):
        end = end + doc_lengths[d]
        doc_qf += (first_q >= end).astype(jnp.int32)
        doc_ql += (last_q >= end).astype(jnp.int32)
        doc_kf += (first_k >= end).astype(jnp.int32)
        doc_kl += (last_k >= end).astype(jnp.int32)
    earlier = key_group < query_group
    same = key_group == query_group
    kept = skip[query_group, key_group] != 1
    active = jnp.logical_or(same, earlier & kept & (doc_kl == doc_qf))
    full = earlier & (doc_kf == doc_ql)
    return active, full


def block_mask(doc_lengths, query_group, key_group, rows, docs, query_dim):
    shape = (rows, rows)
    pos_q = query_group * rows + lax.broadcasted_iota(jnp.int32, shape, query_dim)
    pos_k = key_group * rows + lax.broadcasted_iota(jnp.int32, shape, 1 - query_dim)
    start = jnp.zeros(shape, jnp.int32)
    end = jnp.int32(0)
    for d in range(docs):
        end = end + doc_lengths[d]
        start = jnp.where(pos_q >= end, end, start)
    return (pos_k <= pos_q) & (pos_k >= start)


def document_start(position, doc_lengths):
    start, end = jnp.zeros_like(position), jnp.int32(0)
    for d in range(doc_lengths.shape[0]):
        end = end + doc_lengths[d]
        start = jnp.where(position >= end, end, start)
    return start


def block_masks(diff_ref, span_ref, skip, query_groups, key_groups, rows):
    masks = []
    for qi, ki in ((0, 0), (1, 0), (1, 1)):
        query_group, key_group = query_groups[qi], key_groups[ki]
        skipped = jnp.where(key_group < query_group, skip[query_group, key_group], 0)
        reach = key_group * rows - (skipped == 1).astype(jnp.int32) * (1 << 30)
        mask = span_ref[qi] <= reach
        if qi == ki:
            mask = mask & (diff_ref[...] <= (query_group - key_group) * rows)
        masks.append(mask)
    return masks


def in_pack_order(forward, one, two):
    return jnp.where(forward, one, two), jnp.where(forward, two, one)


def low_lanes(rows):
    return lax.broadcasted_iota(jnp.int32, (rows, LANES), 1) < LANES // 2


def three_pieces(value):
    high = value.astype(BF16).astype(F32)
    rest = value - high
    middle = rest.astype(BF16).astype(F32)
    return high, middle, rest - middle


def turn(value):
    rows = value.shape[1]
    return jnp.concatenate([value, jnp.zeros((LANES - 8, rows), F32)], axis=0).T


def row_pieces(term, with_ones):
    lane = lax.broadcasted_iota(jnp.int32, term.shape, 1)
    term = jnp.where(lane < 8, term, 0.0)
    high, middle, low = three_pieces(term)
    result = pltpu.roll(high, 24, 1) + pltpu.roll(middle, 32, 1) + pltpu.roll(low, 40, 1)
    if with_ones:
        result = jnp.where(lane < 24, 1.0, result)
    return result


def key_pieces(offsets):
    rows = offsets.shape[1]
    high, middle, low = three_pieces(offsets)
    stack = jnp.concatenate(
        [-high, -middle, -low, jnp.ones((24, rows), F32), jnp.zeros((LANES - 48, rows), F32)], axis=0
    )
    return stack.T.astype(BF16)


def spread_heads(wide_ref, common, put, heads, forward=None):
    rows = wide_ref.shape[0]
    low = low_lanes(rows)
    lane = lax.broadcasted_iota(jnp.int32, (rows, LANES), 1)

    def ordered(value):
        if forward is None:
            return value
        return jnp.concatenate(in_pack_order(forward, value[: rows // 2], value[rows // 2 :]), axis=0)

    common = ordered(common)
    for h in range(heads):
        pair = h // 2
        block = ordered(wide_ref[:, pair * LANES : (pair + 1) * LANES])
        keep = low if h % 2 == 0 else jnp.logical_not(low)
        put(
            h,
            jnp.where(keep, block, jnp.zeros_like(block)),
            jnp.where(lax.rem(lane, 8) == h, common, 0.0).astype(BF16),
        )


def put_rows(cat_ref):
    def put(h, value, extra):
        cat_ref[h, :, :LANES] = value
        cat_ref[h, :, LANES:] = extra

    return put


def smem():
    return pl.BlockSpec(memory_space=pltpu.SMEM)


def whole(shape):
    return pl.BlockSpec(shape, lambda i: (0,) * len(shape))


def head_sums(value, heads):
    width = value.shape[1]
    feature = lax.broadcasted_iota(jnp.int32, (width, LANES), 0)
    lane = lax.broadcasted_iota(jnp.int32, (width, LANES), 1)
    member = (lax.div(feature, width // heads) == lane).astype(BF16)
    high = value.astype(BF16)
    return dot(high, member) + dot((value - high.astype(F32)).astype(BF16), member)


def backward_kernel(
    heads, rows, docs, me, group_map, doc_lengths, skip, q_ref, d_ref, out_ref, term_ref, k_ref, v_ref, kaug_ref,
    dq_ref, drow_ref, dk_ref, dv_ref, dcol_ref, acc_ref, qcat_ref, dcat_ref, dk_acc, dv_acc, dcol_acc,
):
    step = pl.program_id(0)

    @pl.when(step == 0)
    def _():
        acc_ref[...] = jnp.zeros_like(acc_ref)
        spread_heads(q_ref, row_pieces(term_ref[...], True), put_rows(qcat_ref), heads)
        delta = head_sums(d_ref[...].astype(F32) * out_ref[...], heads)
        spread_heads(d_ref, row_pieces(-delta, False), put_rows(dcat_ref), heads)

    dk_acc[...] = jnp.zeros_like(dk_acc)
    dv_acc[...] = jnp.zeros_like(dv_acc)
    dcol_acc[...] = jnp.zeros_like(dcol_acc)

    def tile(qi, ki, mask):
        q_rows = pl.ds(qi * rows, rows)
        k_rows = pl.ds(ki * rows, rows)
        aug = kaug_ref[k_rows, :]
        for pair in range(heads // 2):
            lanes = pl.ds(pair * LANES, LANES)
            keys = jnp.concatenate([k_ref[pair, k_rows, :], aug], axis=1)
            values = jnp.concatenate([v_ref[pair, k_rows, :], aug], axis=1)
            for h in (2 * pair, 2 * pair + 1):
                probs = jnp.exp(contract_cols(keys, qcat_ref[h, q_rows, :]))
                if mask is not None:
                    probs = jnp.where(mask, probs, 0.0)
                grads = (probs * contract_cols(values, dcat_ref[h, q_rows, :])).astype(BF16)
                dv_acc[k_rows, lanes] += dot(probs.astype(BF16), dcat_ref[h, q_rows, :LANES])
                both = dot(grads, qcat_ref[h, q_rows, :])
                dk_acc[k_rows, lanes] += both[:, :LANES]
                dcol_acc[k_rows, :] += both[:, LANES:]
                acc_ref[h, q_rows, :] += contract_rows(grads, keys)

    for ki in range(2):
        key_group = group_map[2 * step + ki]
        for qi in range(2):
            query_group = group_map[2 * me[0] + qi]
            active, full = block_state(group_map, doc_lengths, skip, query_group, key_group, rows, docs)

            @pl.when(active & full)
            def _(qi=qi, ki=ki):
                tile(qi, ki, None)

            @pl.when(active & jnp.logical_not(full))
            def _(qi=qi, ki=ki, query_group=query_group, key_group=key_group):
                tile(qi, ki, block_mask(doc_lengths, query_group, key_group, rows, docs, 1))

    dk_ref[0] = dk_acc[...].astype(BF16)
    dv_ref[0] = dv_acc[...].astype(BF16)
    dcol_ref[0] = -(dcol_acc[...].T[:8])

    @pl.when(step == pl.num_programs(0) - 1)
    def _():
        total_rows = dq_ref.shape[0]
        low = low_lanes(total_rows)
        lane = lax.broadcasted_iota(jnp.int32, (total_rows, LANES), 1)
        sums = jnp.zeros((total_rows, LANES), F32)
        for pair in range(heads // 2):
            a, b = 2 * pair, 2 * pair + 1
            dq_ref[:, pair * LANES : (pair + 1) * LANES] = jnp.where(
                low, acc_ref[a, :, :LANES], acc_ref[b, :, :LANES]
            )
            sums = jnp.where(
                lane == 24 + a, acc_ref[a, :, LANES:], jnp.where(lane == 24 + b, acc_ref[b, :, LANES:], sums)
            )
        drow_ref[...] = pltpu.roll(sums, LANES - 24, 1).T[:8]


def backward_attention(me, group_map, doc_lengths, skip, queries, grads, attended, term, keys, values, key_aug, heads):
    total = keys.shape[1]
    own, width = queries.shape
    rows = own // 2
    n = total // own
    docs = doc_lengths.shape[0]
    return pl.pallas_call(
        functools.partial(backward_kernel, heads, rows, docs),
        grid=(n,),
        out_shape=[
            jax.ShapeDtypeStruct((own, width), F32),
            jax.ShapeDtypeStruct((8, own), F32),
            jax.ShapeDtypeStruct((n, own, width), BF16),
            jax.ShapeDtypeStruct((n, own, width), BF16),
            jax.ShapeDtypeStruct((n, 8, own), F32),
        ],
        in_specs=[smem(), smem(), smem(), smem()]
        + [
            whole((own, width)),
            whole((own, width)),
            whole((own, width)),
            whole((own, LANES)),
            pl.BlockSpec((heads // 2, own, LANES), lambda i: (0, i, 0)),
            pl.BlockSpec((heads // 2, own, LANES), lambda i: (0, i, 0)),
            pl.BlockSpec((own, LANES), lambda i: (i, 0)),
        ],
        out_specs=[
            whole((own, width)),
            whole((8, own)),
            pl.BlockSpec((1, own, width), lambda i: (i, 0, 0)),
            pl.BlockSpec((1, own, width), lambda i: (i, 0, 0)),
            pl.BlockSpec((1, 8, own), lambda i: (i, 0, 0)),
        ],
        scratch_shapes=[
            VMEM((heads, own, 2 * LANES), F32),
            VMEM((heads, own, 2 * LANES), BF16),
            VMEM((heads, own, 2 * LANES), BF16),
            VMEM((own, width), F32),
            VMEM((own, width), F32),
            VMEM((own, LANES), F32),
        ],
        compiler_params=pltpu.CompilerParams(vmem_limit_bytes=VMEM_LIMIT),
        cost_estimate=pl.CostEstimate(
            flops=own * total * width * 10, bytes_accessed=total * width * 8, transcendentals=own * total * heads
        ),
    )(me, group_map, doc_lengths, skip, queries, grads, attended, term, keys, values, key_aug)


def deliver_kernel(heads, count, small_ref, *refs):
    sources, refs = refs[:count], refs[count:]
    targets, refs = refs[:count], refs[count:]
    (first_ref, second_ref, forget_ref, bias_ref, gains_ref), refs = refs[:5], refs[5:]
    held, local = refs[:count], refs[count]
    moves = Moves(local)
    for i in range(count):
        moves.start(i, sources[i], held[i])
    shard, gain_rows = first_ref.shape[0], gains_ref.shape[1]
    first_ref[...] = small_ref[0:1, :shard].reshape(shard)
    second_ref[...] = small_ref[1:2, :shard].reshape(shard)
    turned = jnp.concatenate([small_ref[...], jnp.zeros((LANES - 16, 256), F32)], axis=0).T
    forget_ref[...] = small_ref[8 : 8 + heads, :shard]
    gains_ref[...] = small_ref[2 : 2 + heads, :gain_rows]
    bias_ref[...] = turned[224:225, 8 : 8 + heads].reshape(heads)
    for i in range(count):
        moves.wait(i)
        moves.start(i, held[i], targets[i])
    moves.wait()


def deliver(heads, shard, gain_rows, small, arrays):
    vmem = pl.BlockSpec(memory_space=VMEM)
    anywhere = pl.BlockSpec(memory_space=pl.ANY)
    shapes = [array.shape for array in arrays]
    shapes += [(shard,), (shard,), (heads, shard), (heads,), (heads, gain_rows)]
    (layer, input_grad, query, key, value, gate_out, output, gate, up, down, one, two, forget, bias, gains) = (
        pl.pallas_call(
            functools.partial(deliver_kernel, heads, len(arrays)),
            out_shape=[jax.ShapeDtypeStruct(shape, F32) for shape in shapes],
            in_specs=[vmem] + [anywhere] * len(arrays),
            out_specs=[anywhere] * len(arrays) + [vmem] * 5,
            scratch_shapes=[VMEM(array.shape, F32) for array in arrays]
            + [pltpu.SemaphoreType.DMA((2 * len(arrays),))],
            compiler_params=pltpu.CompilerParams(vmem_limit_bytes=VMEM_LIMIT),
        )(small, *arrays)
    )
    return (
        layer, input_grad, one, query, key, value, gate_out, forget.T, bias, gains.T, output, two, gate, up, down,
    )


def on_device(
    hidden_in,
    norm_one,
    w_query,
    w_key,
    w_value,
    w_gate_out,
    w_forget,
    forget_bias,
    head_gains,
    w_output,
    norm_two,
    w_gate,
    w_up,
    w_down,
    out_grad,
    doc_lengths,
    group_map,
    skip_list,
):
    device_ctx = lax.axis_index("ctx")
    device_tp = lax.axis_index("tp")
    n = lax.axis_size("ctx")
    row_count, model_width = hidden_in.shape
    group_rows = row_count // 2
    heads = forget_bias.shape[0]
    shard = norm_one.shape[0]
    gain_rows = head_gains.shape[0]
    head_dim = gain_rows * n // 2
    width = heads * head_dim
    hidden_width = w_gate.shape[1]

    slots = 2 * n
    (
        query_weight,
        key_weight,
        value_weight,
        gate_out_weight,
        output_weight,
        normed_shards,
        query_rows,
        query_raw,
        key_raw,
        gate_logit,
        forget_logit,
        keys_all,
        values_all,
        key_aug,
        attended_flat,
        row_term,
        gain_one,
        gain_two,
        query_gain,
        key_gain,
        forget_weight,
    ) = start_forward(
        n,
        1,
        group_map,
        doc_lengths,
        skip_list,
        forget_bias,
        hidden_in,
        [norm_one, norm_two, head_gains.T, w_forget.T],
        [w_query, w_key, w_value, w_gate_out],
        w_output,
    )
    half = width // 256 * 128
    fused = n <= 8
    (
        gated,
        layer_out,
        down_share,
        gate_share,
        up_share,
        grad_middle,
        grad_attended,
        grad_gate_logit,
        gain_two_parts,
        *attention_grads,
    ) = feed_forward(
        n,
        3,
        heads,
        attended_flat,
        gate_logit,
        output_weight,
        hidden_in,
        gain_two,
        out_grad,
        w_gate,
        w_up,
        w_down,
        (group_map, doc_lengths, skip_list, query_rows, row_term, keys_all, values_all, key_aug) if fused else None,
    )
    halves = [(0, half), (half, width - half)]
    attn_plan = [[(cw, (i, c0, cw)) for c0, cw in halves] for i in (0, 1)]
    if fused:
        grad_branch, grad_query, row_sums, key_part, value_part, column_sums = attention_grads
        early_plan = [side + [(cw, (2, c0, cw))] for side, (c0, cw) in zip(attn_plan, halves)]
        query_share, key_share, value_share, gate_out_share, output_share, small_share, input_grad = finish_backward(
            n,
            7,
            heads,
            early_plan,
            attn_plan,
            key_part,
            value_part,
            column_sums,
            row_sums,
            grad_query,
            query_raw,
            key_raw,
            query_gain,
            key_gain,
            forget_logit,
            group_map,
            query_weight,
            key_weight,
            value_weight,
            gate_out_weight,
            forget_weight,
            grad_gate_logit,
            normed_shards,
            grad_branch,
            gated,
            hidden_in,
            gain_one,
            grad_middle,
            gain_two_parts,
        )
    else:
        grad_branch = grad_middle.astype(BF16).reshape(row_count, n, shard).transpose(1, 0, 2)
        normed_shards = normed_shards.reshape(n, shard, row_count).transpose(0, 2, 1)
        grad_query, row_sums, key_part, value_part, column_sums = backward_attention(
            device_ctx.astype(jnp.int32).reshape(1),
            group_map,
            doc_lengths,
            skip_list,
            query_rows,
            grad_attended,
            attended_flat,
            row_term,
            keys_all,
            values_all,
            key_aug,
            heads,
        )
        own_groups = lax.dynamic_slice_in_dim(group_map, device_ctx * 2, 2, 0)
        later = (group_map[None, :] > own_groups[:, None]).astype(F32)
        query_gain, key_gain = (gain.reshape(heads, head_dim) for gain in (query_gain, key_gain))
        query_raw, key_raw = (raw.reshape(row_count, heads, head_dim) for raw in (query_raw, key_raw))
        query_norm, key_norm = rms_scale(query_raw), rms_scale(key_raw)
        forget_logit = forget_logit[:heads].T
        forget_weight = forget_weight[:heads].astype(BF16)
        normed_one = normed_shards.transpose(1, 0, 2).reshape(row_count, model_width)
        place = jnp.arange(group_rows, dtype=jnp.int32)
        upper = (place[:, None] <= place[None, :]).astype(F32)
        grad_key, grad_value, off_sum, tot_sum = pair_scatter(n, 7, key_part, value_part, column_sums, row_sums)
        after = contract_cols_exact(tot_sum[:heads, :slots], later)
        suffix = lax.dot_general(
            off_sum[:heads].reshape(heads, 2, group_rows), upper, (((2,), (1,)), ((), ())), precision=HIGHEST
        )
        grad_log_forget = (suffix + after[:, :, None]).reshape(heads, row_count).T
        grad_key3 = grad_key.reshape(row_count, heads, head_dim)
        grad_query3 = grad_query.reshape(row_count, heads, head_dim)
        key_raw_grad = rms_back(grad_key3 * key_gain, key_raw).astype(BF16).reshape(row_count, width)
        query_raw_grad = (
            rms_back(grad_query3 * query_gain * 0.125, query_raw).astype(BF16).reshape(row_count, width)
        )
        value_low = grad_value.astype(BF16)
        query_gain_grad = jnp.sum(grad_query3 * query_norm * 0.125, axis=0)
        key_gain_grad = jnp.sum(grad_key3 * key_norm, axis=0)
        head_gain_grad = jnp.concatenate([query_gain_grad, key_gain_grad], axis=1)
        grad_forget_logit = (grad_log_forget * jax.nn.sigmoid(-forget_logit)).astype(BF16)
        bias_part = jnp.sum(grad_forget_logit.astype(F32), axis=0)
        normed_one_part = (
            contract_cols(query_raw_grad, query_weight)
            + contract_cols(key_raw_grad, key_weight)
            + contract_cols(value_low, value_weight)
            + contract_cols(grad_gate_logit, gate_out_weight)
            + dot(grad_forget_logit, forget_weight)
        )
        forget_grad = contract_rows(grad_forget_logit, normed_one)

        def wide(value):
            return jnp.pad(value, ((0, 0), (0, 0), (0, 256 - value.shape[2])))

        forget_rows = wide(forget_grad.reshape(heads, n, shard).transpose(1, 0, 2))
        forget_rows = forget_rows.at[:, :, 224].set(bias_part[None, :])
        small_grad = jnp.concatenate(
            [
                jnp.zeros((n, 1, 256), F32),
                wide(jnp.sum(gain_two_parts, axis=0).reshape(n, 1, shard)),
                wide(head_gain_grad.reshape(heads, n, gain_rows).transpose(1, 0, 2)),
                jnp.pad(forget_rows, ((0, 0), (0, 8 - heads), (0, 0))),
            ],
            axis=1,
        )
        plan = [
            [(cw, (0, right, c0, cw)) for right in rights for c0, cw in halves] + [(cw, (1, 4, c0, cw))]
            for rights, (c0, cw) in zip(((0, 1), (2, 3)), halves)
        ]
        (
            query_share,
            key_share,
            value_share,
            gate_out_share,
            output_share,
            small_share,
            input_grad,
        ) = weight_scatter(
            n,
            8,
            plan,
            [normed_shards, grad_branch],
            [query_raw_grad, key_raw_grad, value_low, grad_gate_logit, gated],
            small_grad,
            normed_one_part,
            hidden_in,
            gain_one,
            grad_middle,
        )
    return deliver(
        heads,
        shard,
        gain_rows,
        small_share,
        [
            layer_out,
            input_grad,
            query_share,
            key_share,
            value_share,
            gate_out_share,
            output_share,
            gate_share,
            up_share,
            down_share,
        ],
    )


def solution(mesh):
    split = P("ctx", "tp")
    in_specs = (
        P("ctx", None),
        P("ctx"),
        split,
        split,
        split,
        split,
        split,
        P("tp"),
        split,
        split,
        P("ctx"),
        split,
        split,
        split,
        P("ctx", None),
        P(),
        P(),
        P(),
    )
    out_specs = (
        split,
        P("ctx", None),
        P("ctx"),
        split,
        split,
        split,
        split,
        split,
        P("tp"),
        split,
        split,
        P("ctx"),
        split,
        split,
        split,
    )
    return jax.shard_map(on_device, mesh=mesh, in_specs=in_specs, out_specs=out_specs, check_vma=False)
```

```python
import functools

import jax
import jax.numpy as jnp
from jax import lax
from jax.experimental import pallas as pl
from jax.experimental.pallas import tpu as pltpu
from jax.sharding import PartitionSpec as P

EPS = 1e-06
HIGHEST = lax.Precision.HIGHEST
MESH = pl.DeviceIdType.MESH
VMEM = pltpu.VMEM
VMEM_LIMIT = 62 * 1024 * 1024
F32 = jnp.float32
BF16 = jnp.bfloat16


def rms_scale(value):
    return value * lax.rsqrt(jnp.mean(value * value, axis=-1, keepdims=True) + EPS)


def rms_back(grad_in, value):
    inverse = lax.rsqrt(jnp.mean(value * value, axis=-1, keepdims=True) + EPS)
    normal = value * inverse
    return inverse * (grad_in - normal * jnp.mean(grad_in * normal, axis=-1, keepdims=True))


def dot(left, right):
    return jnp.dot(left, right, preferred_element_type=F32)


def contract_cols(left, right):
    return lax.dot_general(left, right, (((1,), (1,)), ((), ())), preferred_element_type=F32)


def contract_cols_exact(left, right):
    return lax.dot_general(left, right, (((1,), (1,)), ((), ())), precision=HIGHEST)


def contract_rows(left, right):
    return lax.dot_general(left, right, (((0,), (0,)), ((), ())), preferred_element_type=F32)


def ring_place(ctx, n):
    odd = lax.rem(ctx, 2)
    half = lax.div(ctx, 2)
    return (1 - odd) * half + odd * (n - 1 - half)


def ring_owner(place, n):
    late = lax.div(place, n // 2)
    return (1 - late) * (2 * place) + late * (2 * (n - 1 - place) + 1)


def wrap(place, n):
    return lax.rem(place + 2 * n, n)


def ring_setup(n):
    me = lax.axis_index("ctx")
    tp = lax.axis_index("tp")
    place = ring_place(me, n)
    right = ring_owner(wrap(place + 1, n), n)
    left = ring_owner(wrap(place - 1, n), n)
    return me, tp, place, (right, left)


def greet(peers):
    barrier = pltpu.get_barrier_semaphore()
    for peer in peers:
        pl.semaphore_signal(barrier, inc=1, device_id=peer, device_id_type=MESH)
    pl.semaphore_wait(barrier, len(peers))


def ctx_peers(me, tp, n):
    return [(lax.rem(me + i, n), tp) for i in range(1, n)]


def remote(src, dst, send, recv, device):
    return pltpu.make_async_remote_copy(
        src_ref=src, dst_ref=dst, send_sem=send, recv_sem=recv, device_id=device, device_id_type=MESH
    )


class Gather:
    def __init__(self, n, place, sides, tp, chunks, send, recv):
        self.n, self.place, self.sides, self.tp = n, place, sides, tp
        self.chunks, self.send, self.recv = chunks, send, recv
        self.arrived = None

    def owner(self, side, back):
        return ring_owner(wrap(self.place - back if side == 0 else self.place + back, self.n), self.n)

    def copy(self, index, step, first):
        side, source, target = self.chunks[index]
        target = target(self.owner(side, step))
        return remote(
            source if first else target, target, self.send.at[index, step], self.recv.at[index, step],
            (self.sides[side], self.tp),
        )

    def arrive(self, index, step):
        side, _, target = self.chunks[index]
        target = target(self.owner(side, step + 1))
        remote(
            target, target, self.send.at[index, step], self.recv.at[index, step], (self.sides[side], self.tp)
        ).wait_recv()
        if self.arrived is not None:
            self.arrived(index, step)

    def begin(self, indices=None):
        for index in indices if indices is not None else range(len(self.chunks)):
            self.copy(index, 0, True).start()

    def forward(self, step):
        for index in range(len(self.chunks)):
            self.arrive(index, step - 1)
            self.copy(index, step, False).start()

    def last(self):
        for index in range(len(self.chunks)):
            self.arrive(index, self.n - 2)

    def sent(self):
        def finish(step, carry):
            for index in range(len(self.chunks)):
                self.copy(index, step, False).wait_send()
            return carry

        lax.fori_loop(0, self.n - 1, finish, 0)


class Moves:
    def __init__(self, semaphores):
        self.semaphores, self.count, self.open = semaphores, 0, {}

    def start(self, name, source, target):
        copy = pltpu.make_async_copy(source, target, self.semaphores.at[self.count])
        self.count += 1
        copy.start()
        self.open[name] = copy

    def wait(self, *names):
        for name in names or list(self.open):
            self.open.pop(name).wait()


def start_kernel(
    n, heads, group_map, doc_lengths, skip, bias_ref, x_ref, norm_one, norm_two, gains_in, forget_in,
    wq_in, wk_in, wv_in, wg_in, wo_in,
    wq_out, wk_out, wv_out, wg_out, wo_ref, u_out, q_out, qr_out, kr_out, gl_out, fz_ref, k_out, v_out, aug_out,
    att_out, term_ref, gain_one, gain_two, qgain_ref, kgain_ref, wf_ref,
    x_vmem, wq_ref, wk_ref, wv_ref, wg_ref, u_ref, turned_ref, q_ref, k_all, v_all, aug_ref, att_ref, acc_ref, cat_ref,
    diff_ref, span_ref, tot_ref, before_ref, inside_all, small_wide, small_in,
    small_all, acc_r, acc_l, inside_src,
    wsend, wrecv, osend, orecv, ksend, krecv, ssend, srecv, isend, irecv, spill, local,
):
    me, tp, place, sides = ring_setup(n)
    moves = Moves(local)
    moves.start("x", x_ref, x_vmem)
    shard, width = wq_in.shape
    small_wide[...] = jnp.zeros_like(small_wide)
    small_wide[0:1, :shard] = norm_one[...].astype(F32).reshape(1, shard)
    small_wide[1:2, :shard] = norm_two[...].astype(F32).reshape(1, shard)
    for ref, first in ((gains_in, 2), (forget_in, 8)):
        small_wide[first : first + heads, : ref.shape[1]] = ref[...].astype(F32)
    small_in[...] = small_wide[...].astype(BF16)
    greet(ctx_peers(me, tp, n))
    rows, cols = x_ref.shape
    half = rows // 2
    head_dim = width // heads

    def shard_rows(owner):
        return pl.ds(pl.multiple_of(owner * shard, 16), shard)

    def window(ref, c0, cw):
        return lambda owner: ref.at[shard_rows(owner), pl.ds(c0, cw)]

    def token_rows(owner):
        return pl.ds(pl.multiple_of(owner * rows, rows), rows)

    def block(ref, pair):
        return lambda owner: ref.at[pair, token_rows(owner), :]

    ring = (n, place, sides, tp)
    projections = Gather(
        *ring,
        [
            (side, source, window(target, 0, width))
            for side, source, target in ((0, wq_in, wq_ref), (1, wv_in, wv_ref), (0, wk_in, wk_ref), (1, wg_in, wg_ref))
        ],
        wsend, wrecv,
    )
    middle = width // 256 * 128
    outputs = Gather(
        *ring,
        [
            (side, wo_in.at[:, pl.ds(c0, cw)], window(wo_ref, c0, cw))
            for side, c0, cw in ((0, 0, middle), (1, middle, width - middle))
        ],
        osend, orecv,
    )
    members = [(0, k_all, k_out, 0), (1, k_all, k_out, 2), (0, v_all, v_out, 0), (1, v_all, v_out, 2)]
    members += [(0, k_all, k_out, 1), (1, v_all, v_out, 1)]
    pairs = Gather(
        *ring, [(side, block(ref, pair)(me), block(ref, pair)) for side, ref, _, pair in members], ksend, krecv
    )

    def spill_copy(index, step):
        side, ref, out, pair = members[index]
        owner = pairs.owner(side, step + 1)
        return pltpu.make_async_copy(
            block(ref, pair)(owner), block(out, pair)(owner), spill.at[index, step]
        )

    pairs.arrived = lambda index, step: spill_copy(index, step).start()

    projections.begin()
    exchange_start(n, me, tp, lambda peer: small_in, small_all, ssend, srecv)
    gathered = ((wq_in, wq_ref), (wk_in, wk_ref), (wv_in, wv_ref), (wg_in, wg_ref), (wo_in, wo_ref))
    for i, (source, target) in enumerate(gathered):
        moves.start(i, source, target.at[shard_rows(me)])
    moves.start("small", small_in, small_all.at[me])
    moves.wait("small")
    exchange_wait(n, me, tp, lambda peer: small_in, small_all, ssend, srecv)
    projections.forward(1)

    count = 2 * head_dim // n
    for i in range(n):
        block_small = small_all[i].astype(F32)
        gain_one[:, i * shard : (i + 1) * shard] = block_small[0:1, :shard]
        gain_two[:, i * shard : (i + 1) * shard] = block_small[1:2, :shard]
        wf_ref[:, i * shard : (i + 1) * shard] = block_small[8:16, :shard]
        target, at = (qgain_ref, i) if i < n // 2 else (kgain_ref, i - n // 2)
        for h in range(heads):
            lane = h * head_dim + at * count
            target[:, lane : lane + count] = block_small[2 + h : 3 + h, :count]

    size = LANES

    def norm_rows(i, carry):
        here = pl.ds(pl.multiple_of(i * size, size), size)
        normed = (rms_scale(x_vmem[here, :].astype(F32)) * gain_one[...]).astype(BF16)
        for j in range(n):
            u_ref[j, here, :] = normed[:, j * shard : (j + 1) * shard]
        turned_ref[:, here] = normed.astype(F32).T.astype(BF16)
        return carry

    moves.wait("x")
    lax.fori_loop(0, rows // size, norm_rows, 0)
    moves.start("u", turned_ref, u_out)

    def grow(back):
        for side, acc, sources in ((0, acc_r, (wq_ref, wk_ref)), (1, acc_l, (wv_ref, wg_ref))):
            owner = projections.owner(side, back)
            for i, source in enumerate(sources):
                acc[:, i * width : (i + 1) * width] += dot(u_ref[owner], source[shard_rows(owner), :])

    acc_r[...] = jnp.zeros_like(acc_r)
    acc_l[...] = jnp.zeros_like(acc_l)
    moves.wait(0, 1, 2, 3, 4)
    grow(0)
    projections.forward(2)
    grow(1)
    grow(2)
    forget = jnp.zeros((16, rows), F32)
    for j in range(n):
        forget += contract_cols(small_all[j, :, :shard], u_ref[j])
    head = lax.broadcasted_iota(jnp.int32, (8, rows), 0)
    fz = forget[8:16]
    for h in range(heads):
        fz = jnp.where(head == h, fz + bias_ref[h], fz)
    fz_ref[...] = fz
    logs = jnp.minimum(fz, 0.0) - jnp.log1p(jnp.exp(-jnp.abs(fz)))
    logs = jnp.where(head < heads, logs, 0.0)
    upto = (
        lax.broadcasted_iota(jnp.int32, (half, half), 0) <= lax.broadcasted_iota(jnp.int32, (half, half), 1)
    ).astype(F32)
    for g in range(2):
        inside_src[:, g * half : (g + 1) * half] = jnp.dot(
            logs[:, g * half : (g + 1) * half], upto, precision=HIGHEST, preferred_element_type=F32
        )
    exchange_start(n, me, tp, lambda peer: inside_src, inside_all, isend, irecv)
    moves.start("inside", inside_src, inside_all.at[me])

    def step_on(step, carry):
        projections.forward(step)
        grow(step)
        return carry

    lax.fori_loop(3, n - 2, step_on, 0)
    outputs.begin()
    projections.forward(n - 2)
    grow(n - 2)
    outputs.forward(1)
    projections.last()
    grow(n - 1)

    def head_norm(value):
        return value * lax.rsqrt(head_means(value * value, heads) + EPS)

    my_rows = token_rows(me)
    for pair in range(heads // 2):
        v_all[pair, my_rows, :] = acc_l[:, pair * LANES : (pair + 1) * LANES].astype(BF16)
    pairs.begin([2, 3, 5])
    keys = (head_norm(acc_r[:, width:]) * kgain_ref[...]).astype(BF16)
    for pair in range(heads // 2):
        k_all[pair, my_rows, :] = keys[:, pair * LANES : (pair + 1) * LANES]
    pairs.begin([0, 1, 4])
    for i, (source, target) in enumerate(
        ((wq_ref, wq_out), (wk_ref, wk_out), (wv_ref, wv_out), (wg_ref, wg_out))
    ):
        moves.start(i, source, target)
    moves.start("qr", acc_r.at[:, pl.ds(0, width)], qr_out)
    moves.start("kr", acc_r.at[:, pl.ds(width, width)], kr_out)
    moves.start("gl", acc_l.at[:, pl.ds(width, width)], gl_out)
    for i, (ref, out) in enumerate(((k_all, k_out), (v_all, v_out))):
        for pair in range(heads // 2):
            moves.start((i, pair), block(ref, pair)(me), block(out, pair)(me))
    q_ref[...] = (head_norm(acc_r[:, :width]) * qgain_ref[...] * 0.125).astype(BF16)
    moves.start("q", q_ref, q_out)

    moves.wait("inside")
    exchange_wait(n, me, tp, lambda peer: inside_src, inside_all, isend, irecv)
    tot_ref[...] = jnp.zeros_like(tot_ref)
    for i in range(n):
        for g in range(2):
            tot_ref[:, 2 * i + g : 2 * i + g + 1] = inside_all[i, :, (g + 1) * half - 1 : (g + 1) * half]
    earlier = groups_along(group_map, 0, 1 << 20) < groups_along(group_map, 1, 1 << 20)
    before_ref[...] = jnp.dot(
        tot_ref[...], earlier.astype(F32), precision=HIGHEST, preferred_element_type=F32
    )
    lane8 = lax.broadcasted_iota(jnp.int32, (8, LANES), 1)

    def offsets_of(shard_index):
        parts = []
        for g in range(2):
            before = jnp.sum(jnp.where(lane8 == 2 * shard_index + g, before_ref[...], 0.0), axis=1, keepdims=True)
            parts.append(inside_all[shard_index, :, g * half : (g + 1) * half] + before)
        return jnp.concatenate(parts, axis=1)

    def aug_rows(i, carry):
        aug_ref[token_rows(i), :] = key_pieces(offsets_of(i))
        return carry

    lax.fori_loop(0, n, aug_rows, 0)
    moves.start("aug", aug_ref, aug_out)
    pairs.forward(1)

    first, second = group_map[2 * me], group_map[2 * me + 1]
    in_order = first < second
    query_groups = (jnp.minimum(first, second), jnp.maximum(first, second))
    mine = turn(offsets_of(me))
    term_ref[...] = mine
    spread_heads(q_ref, row_pieces(mine, True), put_rows(cat_ref), heads, in_order)
    acc_ref[...] = jnp.zeros_like(acc_ref)
    query_at = lax.broadcasted_iota(jnp.int32, (half, half), 0)
    key_at = lax.broadcasted_iota(jnp.int32, (half, half), 1)
    diff_ref[...] = key_at - query_at
    for i, group in enumerate(query_groups):
        span_ref[i] = document_start(group * half + query_at, doc_lengths) - key_at
    ones = jnp.ones((half, LANES), BF16)

    def attend(i, back):
        late = lax.div(i, 2)
        pair = (1 - late) * 2 * i + late
        side = lax.rem(i, 2)
        owner = ring_owner(wrap(place + (2 * side - 1) * back, n), n)
        one, two = group_map[2 * owner], group_map[2 * owner + 1]
        forward = one < two
        key_groups = (jnp.minimum(one, two), jnp.maximum(one, two))
        top = pl.ds(pl.multiple_of(owner * rows, rows), half)
        bottom = pl.ds(pl.multiple_of(owner * rows + half, half), half)
        blocks = []
        for ref in (k_all.at[pair], v_all.at[pair], aug_ref):
            blocks.append(in_pack_order(forward, ref[top, :], ref[bottom, :]))
        masks = block_masks(diff_ref, span_ref, skip, query_groups, key_groups, half)
        keys = [jnp.concatenate([blocks[0][ki], blocks[2][ki]], axis=1) for ki in range(2)]
        values = [jnp.concatenate([blocks[1][ki], ones], axis=1) for ki in range(2)]
        both_values = jnp.concatenate(values, axis=0)
        for e in range(2):
            h = 2 * pair + e
            queries = cat_ref[h]
            early = contract_cols(queries, keys[0])
            weights = [
                jnp.where(mask, jnp.exp(score), 0.0).astype(BF16)
                for mask, score in zip(masks, (early[:half], early[half:], contract_cols(queries[half:], keys[1])))
            ]
            acc_ref[h, :half, :] += dot(weights[0], values[0])
            acc_ref[h, half:, :] += dot(jnp.concatenate(weights[1:], axis=1), both_values)

    def attend_all(count, back):
        def body(i, carry):
            attend(i, back)
            return carry

        lax.fori_loop(0, count, body, 0)

    attend_all(3, 0)

    def pair_step(step, count):
        outputs.forward(step)
        pairs.forward(step)
        attend_all(count, step)

    outputs.forward(2)
    pairs.forward(2)
    attend_all(2, 1)
    attend_all(2, 2)

    def early_step(step, carry):
        pair_step(step, 2)
        return carry

    def late_step(step, carry):
        pair_step(step, 4)
        return carry

    lax.fori_loop(3, n // 2, early_step, 0)
    pair_step(n // 2, 3)
    lax.fori_loop(n // 2 + 1, n - 1, late_step, 0)
    outputs.last()
    pairs.last()
    attend_all(4, n - 1)

    lane = lax.broadcasted_iota(jnp.int32, (rows, LANES), 1)
    low = low_lanes(rows)
    totals = jnp.ones((rows, LANES), F32)
    for pair in range(heads // 2):
        parts = []
        for h in (2 * pair, 2 * pair + 1):
            value = jnp.concatenate(in_pack_order(in_order, acc_ref[h, :half, :], acc_ref[h, half:, :]), axis=0)
            parts.append(value)
            totals = jnp.where(lane == h, value[:, LANES:], totals)
        att_ref[:, pair * LANES : (pair + 1) * LANES] = jnp.where(
            low, parts[0][:, :LANES], parts[1][:, :LANES]
        ) / jnp.where(low, parts[0][:, LANES:], parts[1][:, LANES:])
    moves.start("att", att_ref, att_out)
    term_ref[...] -= jnp.log(totals)

    def spilled(step, carry):
        for index in range(len(members)):
            spill_copy(index, step).wait()
        return carry

    lax.fori_loop(0, n - 1, spilled, 0)
    moves.wait()
    projections.sent()
    outputs.sent()
    pairs.sent()


def groups_along(group_map, dim, fill, shape=(128, 128)):
    slot = lax.broadcasted_iota(jnp.int32, shape, dim)
    groups = jnp.full(shape, fill, jnp.int32)
    for i in range(group_map.shape[0]):
        groups = jnp.where(slot == i, group_map[i], groups)
    return groups


def start_forward(n, collective_id, group_map, doc_lengths, skip, bias, x, vectors, weights, out_weight):
    rows, cols = x.shape
    shard, width = out_weight.shape
    heads = bias.shape[0]
    half = rows // 2
    dma = pltpu.SemaphoreType.DMA
    vmem = pl.BlockSpec(memory_space=VMEM)
    anywhere = pl.BlockSpec(memory_space=pl.ANY)
    by_pair = (heads // 2, n * rows, LANES)
    weight, wide, narrow = (n * shard, width), (rows, cols), (rows, width)
    shapes = (
        [(weight, BF16)] * 5
        + [((n * shard, rows), BF16), (narrow, BF16)]
        + [(narrow, F32)] * 3
        + [((8, rows), F32)]
        + [(by_pair, BF16)] * 2
        + [((n * rows, LANES), BF16), (narrow, F32), ((rows, LANES), F32)]
        + [((1, cols), F32)] * 2
        + [((1, width), F32)] * 2
        + [((8, cols), F32)]
    )
    return pl.pallas_call(
        functools.partial(start_kernel, n, heads),
        out_shape=[jax.ShapeDtypeStruct(*shape) for shape in shapes],
        in_specs=[smem(), smem(), smem(), smem(), anywhere] + [vmem] * 4 + [anywhere] * 5,
        out_specs=[anywhere if i < 10 or 11 <= i <= 14 else vmem for i in range(len(shapes))],
        scratch_shapes=[
            VMEM(wide, BF16),
            *[VMEM(weight, BF16)] * 4,
            VMEM((n, rows, shard), BF16),
            VMEM((n * shard, rows), BF16),
            VMEM(narrow, BF16),
            *[VMEM(by_pair, BF16)] * 2,
            VMEM((n * rows, LANES), BF16),
            VMEM(narrow, F32),
            VMEM((heads, rows, 2 * LANES), F32),
            VMEM((heads, rows, 2 * LANES), BF16),
            VMEM((half, half), jnp.int32),
            VMEM((2, half, half), jnp.int32),
            VMEM((8, LANES), F32),
            VMEM((8, LANES), F32),
            VMEM((n, 8, rows), F32),
            VMEM((16, 256), F32),
            VMEM((16, 256), BF16),
            VMEM((n, 16, 256), BF16),
            VMEM((rows, 2 * width), F32),
            VMEM((rows, 2 * width), F32),
            VMEM((8, rows), F32),
            *[dma((4, n - 1))] * 2,
            *[dma((2, n - 1))] * 2,
            *[dma((6, n - 1))] * 2,
            *[dma((n - 1,))] * 4,
            dma((6, n - 1)),
            dma((26,)),
        ],
        compiler_params=pltpu.CompilerParams(
            collective_id=collective_id, has_side_effects=True, vmem_limit_bytes=VMEM_LIMIT
        ),
    )(group_map, doc_lengths, skip, bias, x, *vectors, *weights, out_weight)


class ScatterRing:
    def __init__(self, n, plan, local_term, slots, firsts, write, send, recv, place, sides, tp, source=None):
        self.n, self.place, self.sides, self.tp = n, place, sides, tp
        self.source, self.next = source, 1
        self.local_term, self.write = local_term, write
        self.slots, self.firsts, self.send, self.recv = slots, firsts, send, recv
        self.order = []
        starts = [0, 0]
        for index in range(max(len(plan[0]), len(plan[1]))):
            for side in (0, 1):
                if index < len(plan[side]):
                    width, tag = plan[side][index]
                    self.order.append((side, index, starts[side], width, tag))
                    starts[side] += width

    def target(self, side, step):
        step = -1 - step if side == 0 else 1 + step
        return ring_owner(wrap(self.place + step, self.n), self.n)

    def hop(self, side, index, start, width, step, first):
        cols = pl.ds(start, width)
        slots = self.slots[side]
        if not first:
            source = slots.at[step - 1, :, cols]
        elif self.source is None:
            source = self.firsts[side].at[:, cols]
        else:
            source = self.source(self.target(side, 0), side, cols)
        return remote(
            source,
            slots.at[step, :, cols],
            self.send.at[side, index, step],
            self.recv.at[side, index, step],
            (self.sides[side], self.tp),
        )

    def begin(self):
        for side, index, start, width, tag in self.order:
            if self.source is None:
                term = self.local_term(self.target(side, 0), tag)
                self.firsts[side][:, start : start + width] = term.astype(BF16)
            self.hop(side, index, start, width, 0, True).start()

    def forward(self, step):
        for side, index, start, width, tag in self.order:
            term = self.local_term(self.target(side, step), tag)
            slot = self.slots[side].at[step - 1, :, pl.ds(start, width)]
            self.hop(side, index, start, width, step - 1, True).wait_recv()
            slot[...] = (slot[...].astype(F32) + term).astype(BF16)
            self.hop(side, index, start, width, step, False).start()

    def span(self, first, last):
        def body(step, carry):
            self.forward(step)
            return carry

        if last > first:
            lax.fori_loop(first, last, body, 0)

    def advance(self, count):
        last = min(self.next + count, self.n - 1)
        self.span(self.next, last)
        self.next = last

    def end(self):
        n = self.n
        self.advance(n)
        for side, index, start, width, tag in self.order:
            term = self.local_term(self.target(side, n - 1), tag)
            self.hop(side, index, start, width, n - 2, True).wait_recv()
            self.write(tag, self.slots[side][n - 2, :, start : start + width].astype(F32) + term)
        if self.source is None:
            self.sent()

    def sent(self):
        for side, index, start, width, tag in self.order:
            self.hop(side, index, start, width, 0, True).wait_send()

        def finish(step, carry):
            for side, index, start, width, tag in self.order:
                self.hop(side, index, start, width, step, False).wait_send()
            return carry

        lax.fori_loop(1, self.n - 1, finish, 0)


def exchange_start(n, me, tp, source_of, landing, send, recv):
    for i in range(1, n):
        peer = lax.rem(me + i, n)
        remote(source_of(peer), landing.at[me], send.at[i - 1], recv.at[i - 1], (peer, tp)).start()


def exchange_wait(n, me, tp, source_of, landing, send, recv):
    for i in range(1, n):
        peer = lax.rem(me - i + n, n)
        remote(source_of(peer), landing.at[peer], send.at[i - 1], recv.at[i - 1], (peer, tp)).wait()


def ordered_sum(n, landing):
    total = landing[0]
    for i in range(1, n):
        total = total + landing[i]
    return total


def pair_scatter_kernel(
    n, key_ref, value_ref, col_ref, row_ref, key_out, value_out, off_out, tot_out,
    slot_r, slot_l, first_r, first_l, off_ref, tot_ref, off_land, tot_land,
    send, recv, osend, orecv, tsend, trecv, local,
):
    me, tp, place, sides = ring_setup(n)
    off_ref[...] = col_ref[...]
    off_ref[me] += row_ref[...]
    group_rows = row_ref.shape[1] // 2
    tot_ref[...] = jnp.zeros_like(tot_ref)
    for i in range(n):
        for g in range(2):
            tot_ref[:, 2 * i + g : 2 * i + g + 1] = jnp.sum(
                off_ref[i, :, g * group_rows : (g + 1) * group_rows], axis=1, keepdims=True
            )
    greet(ctx_peers(me, tp, n))
    exchange_start(n, me, tp, lambda peer: off_ref.at[peer], off_land, osend, orecv)
    exchange_start(n, me, tp, lambda peer: tot_ref, tot_land, tsend, trecv)
    mine = pltpu.make_async_copy(off_ref.at[me], off_land.at[me], local.at[0])
    mine_tot = pltpu.make_async_copy(tot_ref, tot_land.at[me], local.at[1])
    mine.start()
    mine_tot.start()
    width = key_ref.shape[2]
    plan = [
        [(w, (0, c)) for c, w in pieces(width, 128)],
        [(w, (1, c)) for c, w in pieces(width, 128)],
    ]

    def local_term(owner, tag):
        which, c0 = tag
        return (key_ref, value_ref)[which][owner, :, c0 : c0 + 128].astype(F32)

    def write(tag, value):
        which, c0 = tag
        (key_out, value_out)[which][:, c0 : c0 + 128] = value

    ring = ScatterRing(
        n, plan, local_term, (slot_r, slot_l), (first_r, first_l), write, send, recv, place, sides, tp
    )
    ring.begin()
    ring.end()
    mine.wait()
    mine_tot.wait()
    exchange_wait(n, me, tp, lambda peer: off_ref.at[peer], off_land, osend, orecv)
    exchange_wait(n, me, tp, lambda peer: tot_ref, tot_land, tsend, trecv)
    off_out[...] = ordered_sum(n, off_land)
    tot_out[...] = ordered_sum(n, tot_land)


def pieces(width, step):
    return [(c, min(step, width - c)) for c in range(0, width, step)]


def pair_scatter(n, collective_id, keys, values, columns, own_rows):
    _, rows, width = keys.shape
    offs, tots = columns, jax.ShapeDtypeStruct((8, LANES), F32)
    chunks = len(pieces(width, 128))
    return pl.pallas_call(
        functools.partial(pair_scatter_kernel, n),
        out_shape=[
            jax.ShapeDtypeStruct((rows, width), F32),
            jax.ShapeDtypeStruct((rows, width), F32),
            jax.ShapeDtypeStruct(offs.shape[1:], F32),
            jax.ShapeDtypeStruct(tots.shape, F32),
        ],
        in_specs=[pl.BlockSpec(memory_space=VMEM)] * 4,
        out_specs=[pl.BlockSpec(memory_space=VMEM)] * 4,
        scratch_shapes=[
            VMEM((n - 1, rows, width), BF16),
            VMEM((n - 1, rows, width), BF16),
            VMEM((rows, width), BF16),
            VMEM((rows, width), BF16),
            VMEM(offs.shape, F32),
            VMEM(tots.shape, F32),
            VMEM(offs.shape, F32),
            VMEM((n,) + tots.shape, F32),
            pltpu.SemaphoreType.DMA((2, chunks, n - 1)),
            pltpu.SemaphoreType.DMA((2, chunks, n - 1)),
            pltpu.SemaphoreType.DMA((n - 1,)),
            pltpu.SemaphoreType.DMA((n - 1,)),
            pltpu.SemaphoreType.DMA((n - 1,)),
            pltpu.SemaphoreType.DMA((n - 1,)),
            pltpu.SemaphoreType.DMA((2,)),
        ],
        compiler_params=pltpu.CompilerParams(
            collective_id=collective_id, has_side_effects=True, vmem_limit_bytes=VMEM_LIMIT
        ),
    )(keys, values, columns, own_rows)


def weight_scatter_kernel(n, plan, left_count, grads, *refs):
    lefts, refs = refs[:left_count], refs[left_count:]
    rights, refs = refs[:grads], refs[grads:]
    small_ref, part_ref, x_ref, gain_ref, dmid_ref, refs = *refs[:5], refs[5:]
    outs, refs = refs[:grads], refs[grads:]
    small_out, input_out, slot_r, slot_l, first_r, first_l, own_small, land, sum_out, refs = *refs[:9], refs[9:]
    tp_bufs, refs = refs[:4], refs[4:]
    send, recv, xsend, xrecv, tsend, trecv, local = refs
    me, tp, place, sides = ring_setup(n)
    chip, core, sibling, across = tp_setup()
    greet(ctx_peers(me, tp, n) + [sibling, across])
    shard = lefts[0].shape[2]
    half = part_ref.shape[0] // 2

    def local_term(owner, tag):
        left, right, c0, cw = tag
        return contract_rows(lefts[left][owner], rights[right][:, c0 : c0 + cw])

    def write(tag, value):
        _, right, c0, cw = tag
        outs[right][:, c0 : c0 + cw] = value

    ring = ScatterRing(
        n, plan, local_term, (slot_r, slot_l), (first_r, first_l), write, send, recv, place, sides, tp
    )

    def part(which, c):
        cols = part_ref.shape[1] // TP_CHUNKS
        return part_ref[pl.ds(pl.multiple_of(which * half, half), half), c * cols : (c + 1) * cols].astype(F32)

    total = TpSum(part, sum_out, tp_bufs, tsend, trecv, core, sibling, across)
    total.first()
    total.second()
    ring.begin()
    total.third()
    ring.advance(1)
    total.fourth()

    own_small[...] = small_ref[...]
    cols = part_ref.shape[1]
    size = 64

    def gain_rows(i, acc):
        rows = pl.ds(pl.multiple_of(i * size, size), size)
        value = x_ref[rows, :].astype(F32)
        inverse = lax.rsqrt(jnp.mean(value * value, axis=-1, keepdims=True) + EPS)
        normal = value * inverse
        grad = sum_out[rows, :].astype(F32)
        back = grad * gain_ref[...]
        back = inverse * (back - normal * jnp.mean(back * normal, axis=-1, keepdims=True))
        input_out[rows, :] = dmid_ref[rows, :] + back
        return acc + jnp.sum((grad * normal).reshape(size // 8, 8, cols), axis=0)

    gains = lax.fori_loop(0, 2 * half // size, gain_rows, jnp.zeros((8, cols), F32))
    gains = jnp.sum(gains, axis=0, keepdims=True)
    for i in range(n):
        own_small[i, 0:1, :shard] = gains[:, i * shard : (i + 1) * shard]
    exchange_start(n, me, tp, lambda peer: own_small.at[peer], land, xsend, xrecv)
    mine = pltpu.make_async_copy(own_small.at[me], land.at[me], local.at[0])
    mine.start()
    ring.end()
    mine.wait()
    exchange_wait(n, me, tp, lambda peer: own_small.at[peer], land, xsend, xrecv)
    small_out[...] = ordered_sum(n, land)


def weight_scatter(n, collective_id, plan, lefts, rights, small, part, x, gain, dmid):
    rows = lefts[0].shape[2]
    chunks = max(len(plan[0]), len(plan[1]))
    totals = [sum(width for width, _ in side) for side in plan]
    return pl.pallas_call(
        functools.partial(weight_scatter_kernel, n, plan, len(lefts), len(rights)),
        out_shape=[jax.ShapeDtypeStruct((rows, right.shape[1]), F32) for right in rights]
        + [jax.ShapeDtypeStruct(small.shape[1:], F32), jax.ShapeDtypeStruct(part.shape, F32)],
        in_specs=[pl.BlockSpec(memory_space=VMEM)] * (len(lefts) + len(rights) + 5),
        out_specs=[pl.BlockSpec(memory_space=VMEM)] * (len(rights) + 2),
        scratch_shapes=[
            VMEM((n - 1, rows, totals[0]), BF16),
            VMEM((n - 1, rows, totals[1]), BF16),
            VMEM((rows, totals[0]), BF16),
            VMEM((rows, totals[1]), BF16),
            VMEM(small.shape, F32),
            VMEM(small.shape, F32),
            VMEM(part.shape, BF16),
            *tp_buffers(*part.shape),
            pltpu.SemaphoreType.DMA((2, chunks, n - 1)),
            pltpu.SemaphoreType.DMA((2, chunks, n - 1)),
            pltpu.SemaphoreType.DMA((n - 1,)),
            pltpu.SemaphoreType.DMA((n - 1,)),
            pltpu.SemaphoreType.DMA((3, TP_CHUNKS)),
            pltpu.SemaphoreType.DMA((3, TP_CHUNKS)),
            pltpu.SemaphoreType.DMA((1,)),
        ],
        compiler_params=pltpu.CompilerParams(
            collective_id=collective_id, has_side_effects=True, vmem_limit_bytes=VMEM_LIMIT
        ),
    )(*lefts, *rights, small, part, x, gain, dmid)


def tp_setup():
    ctx = lax.axis_index("ctx")
    tp = lax.axis_index("tp")
    chip = lax.div(tp, 2)
    core = lax.rem(tp, 2)
    sibling = (ctx, 2 * chip + 1 - core)
    across = (ctx, 2 * (1 - chip) + core)
    return chip, core, sibling, across


TP_CHUNKS = 4


def tp_buffers(rows, width):
    return [VMEM((rows // 2, width), BF16) for _ in range(4)]


class TpSum:
    def __init__(self, part, out, bufs, send, recv, core, sibling, across):
        self.part, self.out, self.send, self.recv = part, out, send, recv
        self.away, self.land_a, self.half_b, self.land_b = bufs
        self.core, self.sibling, self.across = core, sibling, across
        self.half = self.away.shape[0]
        self.size = self.away.shape[1] // TP_CHUNKS

    def cols(self, c):
        return pl.ds(c * self.size, self.size)

    def copy(self, stage, c, which=None):
        cols = self.cols(c)
        if stage == 0:
            source, target, device = self.away.at[:, cols], self.land_a.at[:, cols], self.sibling
        elif stage == 1:
            source, target, device = self.half_b.at[:, cols], self.land_b.at[:, cols], self.across
        else:
            source = target = self.out.at[self.rows(which), cols]
            device = self.sibling
        return remote(source, target, self.send.at[stage, c], self.recv.at[stage, c], device)

    def rows(self, which):
        return pl.ds(pl.multiple_of(which * self.half, self.half), self.half)

    def first(self):
        for c in range(TP_CHUNKS):
            self.away[:, self.cols(c)] = self.part(1 - self.core, c).astype(BF16)
            self.copy(0, c).start()

    def second(self):
        for c in range(TP_CHUNKS):
            cols = self.cols(c)
            mine = self.part(self.core, c)
            self.copy(0, c).wait_recv()
            self.half_b[:, cols] = (mine + self.land_a[:, cols].astype(F32)).astype(BF16)
            self.copy(1, c).start()

    def third(self):
        for c in range(TP_CHUNKS):
            cols = self.cols(c)
            self.copy(1, c).wait_recv()
            both = self.half_b[:, cols].astype(F32) + self.land_b[:, cols].astype(F32)
            self.out[self.rows(self.core), cols] = both.astype(BF16)
            self.copy(2, c, self.core).start()

    def fourth(self):
        for c in range(TP_CHUNKS):
            self.copy(2, c, 1 - self.core).wait_recv()
            self.copy(0, c).wait_send()
            self.copy(1, c).wait_send()
            self.copy(2, c, self.core).wait_send()


class TpSplit:
    def __init__(self, part, bufs, send, recv, chip, core, sibling, across):
        self.part, self.send, self.recv = part, send, recv
        self.away, self.land_a, self.half_b, self.land_b = bufs
        self.chip, self.core, self.sibling, self.across = chip, core, sibling, across

    def copy(self, stage):
        if stage < 2:
            return remote(
                self.away.at[stage], self.land_a.at[stage], self.send.at[stage], self.recv.at[stage], self.sibling
            )
        return remote(self.half_b, self.land_b, self.send.at[2], self.recv.at[2], self.across)

    def first(self):
        for i, chip in enumerate((1 - self.chip, self.chip)):
            self.away[i] = self.part(chip, 1 - self.core).astype(BF16)
            self.copy(i).start()

    def second(self):
        mine = self.part(1 - self.chip, self.core)
        self.copy(0).wait_recv()
        self.half_b[...] = (mine + self.land_a[0].astype(F32)).astype(BF16)
        self.copy(2).start()

    def mine(self):
        return self.part(self.chip, self.core)

    def third(self):
        self.copy(1).wait_recv()
        self.copy(2).wait_recv()
        total = self.land_a[1].astype(F32) + self.land_b[...].astype(F32)
        for stage in range(3):
            self.copy(stage).wait_send()
        return total


def feed_kernel(n, heads, attention, *refs):
    if attention:
        (group_map, doc_lengths, skip, q_in, term_in, k_in, v_in, aug_in), refs = refs[:8], refs[8:]
    (att_in, gl_in, outw_in, x_in, gain_ref, grad_in, wg_in, wu_in, wd_in), refs = refs[:9], refs[9:]
    (gated_out, layer_ref, down_out, gate_out, up_out, dmid_out, do_out, dgl_out, gain_out), refs = refs[:9], refs[9:]
    if attention:
        (dm_out, dq_out, drow_ref, dk_out, dv_out, dcol_ref), refs = refs[:6], refs[6:]
    (
        att_ref, gl_ref, outw_ref, x_ref, gated_ref, normed_ref, dgt_ref, dup_ref, do_ref, dgl_ref,
        gate_all, up_all, down_all, accs, dhid_acc, hid_ref, branch_ref, mid_ref, dw_ref, dy_ref,
        a0, a1, a2, a3, b3, s0, s1, s2, s3, dslot_r, dslot_l, dfirst_r, dfirst_l, eslot_r, eslot_l, efirst_r, efirst_l,
        gsend, grecv, hsend, hrecv, asend, arecv, bsend, brecv, ssend, srecv, dsend, drecv, esend, erecv, local,
    ), refs = refs[:52], refs[52:]
    if attention:
        term_ref, diff_ref, span_ref, stage, kv_sem, stage_sem = refs
    gate_acc, up_acc = accs.at[0], accs.at[1]
    me, tp, place, sides = ring_setup(n)
    chip, core, sibling, across = tp_setup()
    moves = Moves(local)
    for name, source, target in (
        ("att", att_in, att_ref), ("gl", gl_in, gl_ref), ("outw", outw_in, outw_ref), ("grad", grad_in, dw_ref),
        ("x", x_in, x_ref),
    ):
        moves.start(name, source, target)
    if attention:
        moves.start("term", term_in, term_ref)
    greet([(side, tp) for side in sides] + [sibling, across])
    shard, hidden = wg_in.shape
    rows, width = x_in.shape
    half = rows // 2
    hw = hidden // 2
    size = 64
    ring = (n, place, sides, tp)

    def rows_of(owner):
        return pl.ds(pl.multiple_of(owner * shard, 16), shard)

    def window(ref, c0, cw):
        return lambda owner: ref.at[rows_of(owner), pl.ds(c0, cw)]

    def chunks(members):
        return [(side, source.at[:, pl.ds(c0, cw)], window(target, c0, cw)) for side, source, target, c0, cw in members]

    gates = Gather(
        *ring,
        chunks(
            [
                (side, source, target, c0, hw)
                for c0 in (0, hw)
                for side, source, target in ((0, wg_in, gate_all), (1, wu_in, up_all))
            ]
        ),
        gsend, grecv,
    )
    downs = Gather(
        *ring,
        chunks([(side, wd_in, down_all, side * hw + c0, hw // 2) for c0 in (0, hw // 2) for side in (0, 1)]),
        hsend, hrecv,
    )
    gates.begin()
    for i, (source, target) in enumerate(((wg_in, gate_all), (wu_in, up_all), (wd_in, down_all))):
        moves.start(i, source, target.at[rows_of(me)])

    moves.wait("att", "gl")
    gated_ref[...] = (att_ref[...] * jax.nn.sigmoid(gl_ref[...])).astype(BF16)
    moves.start("gated", gated_ref, gated_out)
    moves.wait("outw")
    span = width // TP_CHUNKS

    def branch_part(which, c):
        mine = gated_ref[pl.ds(pl.multiple_of(which * half, half), half), :]
        return contract_cols(mine, outw_ref[c * span : (c + 1) * span, :])

    branch = TpSum(branch_part, branch_ref, (a0, a1, a2, a3), asend, arecv, core, sibling, across)
    branch.first()
    branch.second()
    gates.forward(1)
    moves.wait("grad")
    for c in range(TP_CHUNKS):
        back = pl.ds(c * span, span)
        dy_ref[back, :] = dw_ref[:, back].astype(F32).T.astype(BF16)
    dhid_acc[...] = jnp.zeros_like(dhid_acc)
    gate_acc[...] = jnp.zeros_like(gate_acc)
    up_acc[...] = jnp.zeros_like(up_acc)

    def grow_back(back):
        for side in (0, 1):
            owner = downs.owner(side, back)
            cols = pl.ds(side * hw, hw)
            dhid_acc[:, cols] += contract_rows(dy_ref[rows_of(owner), :], down_all[rows_of(owner), cols])

    def grow(back):
        for side, acc, source in ((0, gate_acc, gate_all), (1, up_acc, up_all)):
            owner = gates.owner(side, back)
            acc[...] += contract_rows(normed_ref[rows_of(owner), :], source[rows_of(owner), :])

    moves.wait(0, 1, 2)
    grow_back(0)
    gates.forward(2)
    branch.third()
    branch.fourth()
    moves.wait("x")

    def norm_rows(i, carry):
        here = pl.ds(pl.multiple_of(i * LANES, LANES), LANES)
        middle = x_ref[here, :].astype(F32) + branch_ref[here, :].astype(F32)
        mid_ref[here, :] = middle
        normed_ref[:, here] = (rms_scale(middle) * gain_ref[...]).T.astype(BF16)
        return carry

    lax.fori_loop(0, rows // LANES, norm_rows, 0)
    own = pl.ds(pl.multiple_of(tp * span, span), span)
    layer_ref[...] = mid_ref[:, own]
    moves.start("again", grad_in, x_ref)
    if attention:
        moves.wait("gated")
        moves.start("q", q_in, gated_ref)
    gates.forward(3)

    def grow_step(step, carry):
        grow(step)
        return carry

    lax.fori_loop(0, 4, grow_step, 0)

    def gate_step(step, carry):
        gates.forward(step)
        grow(step)
        return carry

    lax.fori_loop(4, n - 1, gate_step, 0)
    downs.begin()
    gates.last()
    grow(n - 1)

    def hid_rows(i, carry):
        here = pl.ds(pl.multiple_of(i * size, size), size)
        gate, up = gate_acc[here, :], up_acc[here, :]
        open_gate = jax.nn.sigmoid(gate)
        silu = gate * open_gate
        hid_ref[here, :] = (silu * up).astype(BF16)
        gate_acc[here, :] = up * open_gate * (1.0 + gate * (1.0 - open_gate))
        up_acc[here, :] = silu
        return carry

    lax.fori_loop(0, rows // size, hid_rows, 0)

    def down_step(step, carry):
        downs.forward(step)
        grow_back(step)
        return carry

    lax.fori_loop(1, n - 2, down_step, 0)
    downs.forward(n - 2)

    def down_term(owner, tag):
        return dot(dy_ref[rows_of(owner), :], hid_ref[:, tag * hw : (tag + 1) * hw])

    down_ref = accs.at[0, pl.ds(0, shard), :]
    gate_ref = accs.at[0, pl.ds(shard, shard), :]
    up_ref = accs.at[1, pl.ds(0, shard), :]

    def down_write(tag, value):
        down_ref[:, tag * hw : (tag + 1) * hw] = value

    def early_term(owner, tag):
        which, c0 = tag
        return dot(normed_ref[rows_of(owner), :], (dgt_ref, dup_ref)[which][:, c0 : c0 + hw])

    def early_write(tag, value):
        which, c0 = tag
        (gate_ref, up_ref)[which][:, c0 : c0 + hw] = value

    backs = ScatterRing(
        n, [[(hw, 0)], [(hw, 1)]], down_term, (dslot_r, dslot_l), (dfirst_r, dfirst_l), down_write,
        dsend, drecv, place, sides, tp,
    )
    earlies = [
        ScatterRing(
            n, [[(hw, (i, part * hw))] for i in range(2)], early_term, (eslot_r.at[part], eslot_l.at[part]),
            (efirst_r.at[part], efirst_l.at[part]), early_write, esend.at[part], erecv.at[part], place, sides, tp,
        )
        for part in range(2)
    ]
    backs.begin()
    grow_back(n - 2)
    downs.last()
    grow_back(n - 1)

    def grad_rows(i, carry):
        here = pl.ds(pl.multiple_of(i * size, size), size)
        dhid = dhid_acc[here, :]
        dgt_ref[here, :] = (dhid * gate_acc[here, :]).astype(BF16)
        dup_ref[here, :] = (dhid * up_acc[here, :]).astype(BF16)
        return carry

    lax.fori_loop(0, rows // size, grad_rows, 0)

    def dw_part(which, c):
        mine = pl.ds(pl.multiple_of(which * half, half), half)
        back = pl.ds(c * span, span)
        return contract_cols(dgt_ref[mine, :], gate_all[back, :]) + contract_cols(dup_ref[mine, :], up_all[back, :])

    def layer_part(which_chip, which_core):
        back = pl.ds(pl.multiple_of((2 * which_chip + which_core) * span, span), span)
        return contract_cols(hid_ref[...], down_all[back, :])

    total = TpSum(dw_part, dw_ref, (a0, a1, a2, b3), bsend, brecv, core, sibling, across)
    layer = TpSplit(layer_part, (s0, s1, s2, s3), ssend, srecv, chip, core, sibling, across)
    total.first()
    backs.advance(1)
    earlies[0].begin()
    earlies[1].begin()
    total.second()
    gates.sent()
    if attention:
        pairs = heads // 2

        def kv_copies(it):
            part, pair = lax.div(it, pairs), lax.rem(it, pairs)
            source = pl.ds(pl.multiple_of(part * rows, rows), rows)
            target = pl.ds(pl.multiple_of(pair * rows, rows), rows)
            lanes = pl.ds(pl.multiple_of(part * LANES, LANES), LANES)
            return [
                pltpu.make_async_copy(ref.at[pair, source, :], held.at[target, lanes], kv_sem.at[i, it])
                for i, (ref, held) in enumerate(((k_in, gate_all), (v_in, up_all)))
            ]

        def bring(it, carry):
            for copy in kv_copies(it):
                copy.start()
            return carry

        lax.fori_loop(0, n * pairs, bring, 0)
    layer.first()
    layer.second()
    layer_ref[...] += layer.mine()

    def serve_all():
        backs.advance(1)
        earlies[0].advance(1)
        earlies[1].advance(1)

    serve_all()
    if attention:
        downs.sent()
        moves.wait("q", "term")
        first, second = group_map[2 * me], group_map[2 * me + 1]
        in_order = first < second
        query_groups = (jnp.minimum(first, second), jnp.maximum(first, second))

        def put_query(h, value, extra):
            here, lane = pl.ds(h // 4 * rows, rows), h % 4 * 2 * LANES
            down_all[here, lane : lane + LANES] = value
            down_all[here, lane + LANES : lane + 2 * LANES] = extra

        spread_heads(gated_ref, row_pieces(term_ref[...], True), put_query, heads, in_order)
        accs[...] = jnp.zeros_like(accs)
        query_at = lax.broadcasted_iota(jnp.int32, (half, half), 1)
        key_at = lax.broadcasted_iota(jnp.int32, (half, half), 0)
        diff_ref[...] = key_at - query_at
        for i, group in enumerate(query_groups):
            span_ref[i] = document_start(group * half + query_at, doc_lengths) - key_at
    total.third()
    total.fourth()

    def middle_rows(i, acc):
        here = pl.ds(pl.multiple_of(i * size, size), size)
        middle = mid_ref[here, :]
        inverse = lax.rsqrt(jnp.mean(middle * middle, axis=-1, keepdims=True) + EPS)
        normal = middle * inverse
        dw = dw_ref[here, :].astype(F32)
        back = dw * gain_ref[...]
        back = inverse * (back - normal * jnp.mean(back * normal, axis=-1, keepdims=True))
        dmid = x_ref[here, :].astype(F32) + back
        mid_ref[here, :] = dmid
        branch_ref[here, :] = dmid.astype(BF16)
        return acc + jnp.sum((dw * normal).reshape(size // 8, 8, width), axis=0)

    moves.wait("again")
    gain_out[...] = lax.fori_loop(0, rows // size, middle_rows, jnp.zeros((8, width), F32))
    if attention:
        for i in range(n):
            moves.start(
                ("aug", i), aug_in.at[pl.ds(i * rows, rows), :], x_ref.at[:, pl.ds(i * LANES, LANES)]
            )
    moves.start("dmid", mid_ref, dmid_out)
    if attention:
        moves.start("dm", branch_ref, dm_out)
    serve_all()
    da = dot(branch_ref[...], outw_ref[...])
    open_gate = jax.nn.sigmoid(gl_ref[...])
    do_ref[...] = (da * open_gate).astype(BF16)
    dgl_ref[...] = (da * att_ref[...] * open_gate * (1.0 - open_gate)).astype(BF16)
    moves.start("do", do_ref, do_out)
    moves.start("dgl", dgl_ref, dgl_out)
    serve_all()
    layer_ref[...] += layer.third()

    if attention:
        def put_grad(h, value, extra):
            branch_ref[:, 2 * h * LANES : (2 * h + 1) * LANES] = value
            branch_ref[:, (2 * h + 1) * LANES : (2 * h + 2) * LANES] = extra

        delta = head_sums(do_ref[...].astype(F32) * att_ref[...], heads)
        moves.wait("dm", *[("aug", i) for i in range(n)])
        spread_heads(do_ref, row_pieces(-delta, False), put_grad, heads, in_order)
        dcol_acc = dhid_acc.at[:, pl.ds(0, LANES)]

        def stage_copies(it):
            part, pair = lax.div(it, pairs), lax.rem(it, pairs)
            lanes = pl.ds(pl.multiple_of(pair * LANES, LANES), LANES)
            slot = lax.rem(it, 2)
            return [
                pltpu.make_async_copy(stage.at[slot, i], out.at[part, :, lanes], stage_sem.at[slot, i])
                for i, out in enumerate((dk_out, dv_out))
            ]

        def attend(it, carry):
            part, pair = lax.div(it, pairs), lax.rem(it, pairs)
            for copy in kv_copies(it):
                copy.wait()
            one, two = group_map[2 * part], group_map[2 * part + 1]
            forward = one < two
            key_groups = (jnp.minimum(one, two), jnp.maximum(one, two))
            lanes = pl.ds(pl.multiple_of(part * LANES, LANES), LANES)

            def ordered(ref, base, where):
                top = pl.ds(pl.multiple_of(base * rows, rows), half)
                bottom = pl.ds(pl.multiple_of(base * rows + half, half), half)
                return in_pack_order(forward, ref[top, where], ref[bottom, where])

            key_blocks = ordered(gate_all, pair, lanes)
            value_blocks = ordered(up_all, pair, lanes)
            aug_blocks = ordered(x_ref, 0, lanes)
            masks = block_masks(diff_ref, span_ref, skip, query_groups, key_groups, half)
            keys = [jnp.concatenate([key_blocks[ki], aug_blocks[ki]], axis=1) for ki in range(2)]
            values = [jnp.concatenate([value_blocks[ki], aug_blocks[ki]], axis=1) for ki in range(2)]
            both_keys = jnp.concatenate(keys, axis=0)
            queries, douts, probs, grads = [], [], ([], []), ([], [])
            for e in range(2):
                h = 2 * pair + e
                spot = pl.ds(pl.multiple_of(h * 2 * LANES, 2 * LANES), 2 * LANES)
                quarter = pl.ds(pl.multiple_of(lax.rem(h, 4) * 2 * LANES, 2 * LANES), 2 * LANES)
                query_rows = pl.ds(pl.multiple_of(lax.div(h, 4) * rows, rows), rows)
                query, dout = down_all[query_rows, quarter], branch_ref[:, spot]
                early = contract_cols(keys[0], query)
                scores = (early[:, :half], early[:, half:], contract_cols(keys[1], query[half:]))
                early = contract_cols(values[0], dout)
                backs_out = (early[:, :half], early[:, half:], contract_cols(values[1], dout[half:]))
                prob = [jnp.where(mask, jnp.exp(score), 0.0) for mask, score in zip(masks, scores)]
                grad = [(p * back).astype(BF16) for p, back in zip(prob, backs_out)]
                prob = [p.astype(BF16) for p in prob]
                queries.append(query)
                douts.append(dout[:, :LANES])
                probs[0].extend(prob[:2])
                probs[1].append(prob[2])
                grads[0].extend(grad[:2])
                grads[1].append(grad[2])
                accs[lax.div(h, 4), :half, quarter] += contract_rows(grad[0], keys[0])
                accs[lax.div(h, 4), half:, quarter] += contract_rows(jnp.concatenate(grad[1:], axis=0), both_keys)
            late_queries = jnp.concatenate([query[half:] for query in queries], axis=0)
            late_douts = jnp.concatenate([dout[half:] for dout in douts], axis=0)
            queries, douts = jnp.concatenate(queries, axis=0), jnp.concatenate(douts, axis=0)
            sums = [
                dot(jnp.concatenate(grads[0], axis=1), queries),
                dot(jnp.concatenate(grads[1], axis=1), late_queries),
            ]
            value_sums = [
                dot(jnp.concatenate(probs[0], axis=1), douts),
                dot(jnp.concatenate(probs[1], axis=1), late_douts),
            ]
            columns = jnp.concatenate([part_sum[:, LANES:] for part_sum in sums], axis=0)
            dcol_acc[...] = jnp.where(pair == 0, 0.0, dcol_acc[...]) + columns

            @pl.when(it >= 2)
            def _():
                for copy in stage_copies(it - 2):
                    copy.wait()

            slot = lax.rem(it, 2)
            for i, part_sums in enumerate(([part_sum[:, :LANES] for part_sum in sums], value_sums)):
                stage[slot, i] = jnp.concatenate(in_pack_order(forward, *part_sums), axis=0).astype(BF16)
            for copy in stage_copies(it):
                copy.start()

            @pl.when(pair == pairs - 1)
            def _():
                columns = jnp.concatenate(
                    in_pack_order(forward, dcol_acc[pl.ds(0, half), :], dcol_acc[pl.ds(half, half), :]), axis=0
                )
                dcol_ref[part] = -(columns.T[:8])

            return carry

        turns = (*earlies, backs)
        starts = [ring.next for ring in turns]
        services = sum(n - 1 - start for start in starts)
        assert starts[0] == starts[1] == starts[2] - 1
        share = n * pairs // services

        def serve(k, carry):
            lax.fori_loop(k * share, (k + 1) * share, attend, 0)
            for i, ring in enumerate(turns):

                @pl.when(lax.rem(k, 3) == i)
                def _(i=i, ring=ring):
                    ring.forward(starts[i] + lax.div(k, 3))

            return carry

        lax.fori_loop(0, services, serve, 0)
        for ring in turns:
            ring.next = n - 1
        if services * share < n * pairs:
            lax.fori_loop(services * share, n * pairs, attend, 0)
        for it in (n * pairs - 2, n * pairs - 1):
            for copy in stage_copies(it):
                copy.wait()

        lane = lax.broadcasted_iota(jnp.int32, (rows, LANES), 1)
        low = low_lanes(rows)
        sums = jnp.zeros((rows, LANES), F32)
        for pair in range(pairs):
            parts = []
            for h in (2 * pair, 2 * pair + 1):
                spot = pl.ds((h % 4) * 2 * LANES, 2 * LANES)
                value = jnp.concatenate(
                    in_pack_order(in_order, accs[h // 4, :half, spot], accs[h // 4, half:, spot]), axis=0
                )
                parts.append(value)
                sums = jnp.where(lane == 24 + h, value[:, LANES:], sums)
            dhid_acc[:, (3 + pair) * LANES : (4 + pair) * LANES] = jnp.where(
                low, parts[0][:, :LANES], parts[1][:, :LANES]
            )
        moves.start("dq", dhid_acc.at[:, pl.ds(3 * LANES, pairs * LANES)], dq_out)
        drow_ref[...] = pltpu.roll(sums, LANES - 24, 1).T[:8]

        moves.wait("dq")
    backs.end()
    moves.start("down", down_ref, down_out)
    earlies[0].end()
    earlies[1].end()
    moves.start("gate", gate_ref, gate_out)
    moves.start("up", up_ref, up_out)
    if not attention:
        downs.sent()
    moves.wait()


def feed_forward(
    n, collective_id, heads, attended, gate_logit, out_weight, x, gain, dy, w_gate, w_up, w_down, attention=None
):
    rows, width = x.shape
    shard, hidden = w_gate.shape
    heads_width = attended.shape[1]
    own = width // 4
    half = rows // 2
    dma = pltpu.SemaphoreType.DMA
    vmem = pl.BlockSpec(memory_space=VMEM)
    anywhere = pl.BlockSpec(memory_space=pl.ANY)
    wide, narrow, deep = (rows, width), (rows, heads_width), (rows, hidden)
    turned = (n * shard, rows)
    weight = (shard, hidden)
    shapes = [
        (narrow, BF16),
        ((rows, own), F32),
        (weight, F32),
        (weight, F32),
        (weight, F32),
        (wide, F32),
        (narrow, BF16),
        (narrow, BF16),
        ((8, width), F32),
    ]
    kept = [1, 8]
    extra_specs, extra_scratch = [], []
    if attention is not None:
        assert heads // 2 * rows == n * shard and n * LANES == hidden and 2 * rows <= n * shard
        shapes += [
            (wide, BF16),
            (narrow, F32),
            ((8, rows), F32),
            ((n, rows, heads_width), BF16),
            ((n, rows, heads_width), BF16),
            ((n, 8, rows), F32),
        ]
        kept += [11, 14]
        extra_specs = [smem()] * 3 + [anywhere] * 5
        extra_scratch = [
            VMEM((rows, LANES), F32),
            VMEM((half, half), jnp.int32),
            VMEM((2, half, half), jnp.int32),
            VMEM((2, 2, rows, LANES), BF16),
            dma((2, n * heads // 2)),
            dma((2, 2)),
        ]
    return pl.pallas_call(
        functools.partial(feed_kernel, n, heads, attention is not None),
        out_shape=[jax.ShapeDtypeStruct(*shape) for shape in shapes],
        in_specs=extra_specs + [anywhere] * 4 + [vmem] + [anywhere] * 4,
        out_specs=[vmem if i in kept else anywhere for i in range(len(shapes))],
        scratch_shapes=[
            VMEM(narrow, F32),
            VMEM(narrow, F32),
            VMEM(out_weight.shape, BF16),
            VMEM(wide, BF16),
            VMEM(narrow, BF16),
            VMEM(turned, BF16),
            VMEM(deep, BF16),
            VMEM(deep, BF16),
            VMEM(narrow, BF16),
            VMEM(narrow, BF16),
            *[VMEM((n * shard, hidden), BF16)] * 3,
            VMEM((2,) + deep, F32),
            VMEM(deep, F32),
            VMEM(deep, BF16),
            VMEM(wide, BF16),
            VMEM(wide, F32),
            VMEM(wide, BF16),
            VMEM(turned, BF16),
            *tp_buffers(rows, width),
            VMEM((rows // 2, width), BF16),
            VMEM((2, rows, own), BF16),
            VMEM((2, rows, own), BF16),
            VMEM((rows, own), BF16),
            VMEM((rows, own), BF16),
            *ring_scratch(n, shard, [hidden // 2] * 2),
            *[VMEM((2, n - 1, shard, hidden // 2), BF16)] * 2,
            *[VMEM((2, shard, hidden // 2), BF16)] * 2,
            *[dma((4, n - 1))] * 4,
            *[dma((3, TP_CHUNKS))] * 4,
            *[dma((3,))] * 2,
            *[dma((2, 1, n - 1))] * 2,
            *[dma((2, 2, 1, n - 1))] * 2,
            dma((28,)),
            *extra_scratch,
        ],
        compiler_params=pltpu.CompilerParams(
            collective_id=collective_id, has_side_effects=True, vmem_limit_bytes=VMEM_LIMIT
        ),
    )(*(attention or ()), attended, gate_logit, out_weight, x, gain, dy, w_gate, w_up, w_down)


def ring_scratch(n, height, widths):
    return [VMEM((n - 1, height, w), BF16) for w in widths] + [VMEM((height, w), BF16) for w in widths]


def head_means(value, heads):
    width = value.shape[1]
    size = width // heads
    left = lax.div(lax.broadcasted_iota(jnp.int32, (width, width), 0), size)
    right = lax.div(lax.broadcasted_iota(jnp.int32, (width, width), 1), size)
    member = (left == right).astype(BF16)
    high = value.astype(BF16)
    return (dot(high, member) + dot((value - high.astype(F32)).astype(BF16), member)) * (1.0 / size)


STAGED = (0, 1, 4, 5, 16, 11, 14, 17, 18, 19, 6, 12, 13, 20)


def finish_kernel(n, heads, gate_plan, attn_plan, *refs):
    operands, refs = list(refs[:24]), refs[24:]
    (q_out, k_out, v_out, g_out, o_out, small_out, input_out), refs = refs[:7], refs[7:]
    staged, refs = refs[: len(STAGED)], refs[len(STAGED) :]
    (
        dmt_ref, pslot_r, pslot_l, gslot_r, gslot_l, gfirst_r, gfirst_l, aslot_r, aslot_l, afirst_r, afirst_l,
        dk_sum, dv_sum, dqr_ref, dkr_ref, dvl_ref, du_ref, sum_ref, t0, t1, t2, t3,
        off_ref, tot_ref, off_land, tot_land, small_ref, small_land,
        psend, precv, gsend, grecv, asend, arecv, osend, orecv, qsend, qrecv, xsend, xrecv, tsend, trecv, local,
    ) = refs
    moves = Moves(local)
    dk_hbm, dv_hbm = operands[:2]
    for target, index in zip(staged, STAGED):
        moves.start(index, operands[index], target)
        operands[index] = target
    (
        dk_ref, dv_ref, col_ref, row_ref, dq_ref, qr_ref, kr_ref, qgain_ref, kgain_ref, fz_ref, group_map,
        wq_ref, wk_ref, wv_ref, wg_ref, wf_ref, dgl_ref, u_ref, dm_ref, gated_ref,
        x_ref, gain_ref, dmid_ref, gain_two_ref,
    ) = operands
    me, tp, place, sides = ring_setup(n)
    chip, core, sibling, across = tp_setup()
    rows, width = dq_ref.shape
    cols = x_ref.shape[1]
    shard = u_ref.shape[0] // n
    half = rows // 2
    head_dim = width // heads

    def rows_of(owner):
        return pl.ds(pl.multiple_of(owner * shard, 16), shard)

    small_ref[...] = jnp.zeros_like(small_ref)
    greet(ctx_peers(me, tp, n) + [sibling, across])

    def pair_term(owner, tag):
        which, c0 = tag
        return (dk_ref, dv_ref)[which][owner, :, c0 : c0 + LANES].astype(F32)

    def pair_write(tag, value):
        which, c0 = tag
        (dk_sum, dv_sum)[which][:, c0 : c0 + LANES] = value

    pairs = ScatterRing(
        n, [[(w, (i, c)) for c, w in pieces(width, LANES)] for i in range(2)], pair_term,
        (pslot_r, pslot_l), None, pair_write, psend, precv, place, sides, tp,
        source=lambda target, side, window: (dk_hbm, dv_hbm)[side].at[target, :, window],
    )
    pairs.begin()
    off_ref[...] = col_ref[...]
    off_ref[me] += row_ref[...]
    tot_ref[...] = jnp.zeros_like(tot_ref)
    for i in range(n):
        for g in range(2):
            tot_ref[:, 2 * i + g : 2 * i + g + 1] = jnp.sum(
                off_ref[i, :, g * half : (g + 1) * half], axis=1, keepdims=True
            )
    exchange_start(n, me, tp, lambda peer: off_ref.at[peer], off_land, osend, orecv)
    exchange_start(n, me, tp, lambda peer: tot_ref, tot_land, qsend, qrecv)
    moves.start("off", off_ref.at[me], off_land.at[me])
    moves.start("tot", tot_ref, tot_land.at[me])

    def raw_grad(grad, raw, gain):
        inverse = lax.rsqrt(head_means(raw * raw, heads) + EPS)
        normal = raw * inverse
        back = grad * gain
        back = inverse * (back - normal * head_means(back * normal, heads))
        return back.astype(BF16), jnp.sum(grad * normal, axis=0, keepdims=True)

    def gain_rows(row, first):
        count = 2 * head_dim // n
        for i in range(n // 2):
            for h in range(heads):
                lane = h * head_dim + i * count
                small_ref[first + i, 2 + h : 3 + h, 0:count] = row[:, lane : lane + count]

    moves.wait(0, 1, 4, 5)
    pairs.advance(1)
    dqr, row = raw_grad(dq_ref[...], qr_ref[...], qgain_ref[...] * 0.125)
    dqr_ref[...] = dqr
    gain_rows(row * 0.125, 0)
    pairs.advance(1)
    moves.wait(16, 11, 14)
    span = cols // TP_CHUNKS
    for c in range(TP_CHUNKS):
        back = pl.ds(c * span, span)
        du_ref[:, back] = contract_cols(dqr_ref[...], wq_ref[back, :]) + contract_cols(dgl_ref[...], wg_ref[back, :])
    moves.wait(18)
    for c in range(TP_CHUNKS):
        back = pl.ds(c * span, span)
        dmt_ref[back, :] = dm_ref[:, back].astype(F32).T.astype(BF16)
    pairs.advance(n)
    moves.wait(17, 19)

    def gate_term(owner, tag):
        right, c0, cw = tag
        left = dmt_ref if right == 2 else u_ref
        return dot(left[rows_of(owner), :], (dqr_ref, dgl_ref, gated_ref)[right][:, c0 : c0 + cw])

    def gate_write(tag, value):
        right, c0, cw = tag
        (q_out, g_out, o_out)[right][:, c0 : c0 + cw] = value

    gates = ScatterRing(
        n, gate_plan, gate_term, (gslot_r, gslot_l), (gfirst_r, gfirst_l), gate_write, gsend, grecv, place, sides, tp,
    )
    gates.begin()
    pairs.end()

    moves.wait(6)
    dkr, row = raw_grad(dk_sum[...], kr_ref[...], kgain_ref[...])
    dkr_ref[...] = dkr
    gain_rows(row, n // 2)
    dvl_ref[...] = dv_sum[...].astype(BF16)

    def attn_term(owner, tag):
        c0, cw = tag[1], tag[2]
        return dot(u_ref[rows_of(owner), :], (dkr_ref, dvl_ref)[tag[0]][:, c0 : c0 + cw])

    def attn_write(tag, value):
        c0, cw = tag[1], tag[2]
        (k_out, v_out)[tag[0]][:, c0 : c0 + cw] = value

    attns = ScatterRing(
        n, attn_plan, attn_term, (aslot_r, aslot_l), (afirst_r, afirst_l), attn_write, asend, arecv, place, sides, tp,
    )
    attns.begin()
    gates.advance(1)
    moves.wait("off", "tot")
    exchange_wait(n, me, tp, lambda peer: off_ref.at[peer], off_land, osend, orecv)
    exchange_wait(n, me, tp, lambda peer: tot_ref, tot_land, qsend, qrecv)
    off_sum = ordered_sum(n, off_land)
    tot_sum = ordered_sum(n, tot_land)
    onward = (
        lax.broadcasted_iota(jnp.int32, (half, half), 0) >= lax.broadcasted_iota(jnp.int32, (half, half), 1)
    ).astype(F32)
    parts = []
    for g in range(2):
        suffix = jnp.dot(
            off_sum[:, g * half : (g + 1) * half], onward, precision=HIGHEST, preferred_element_type=F32
        )
        later = groups_along(group_map, 1, -1, (8, LANES)) > group_map[2 * me + g]
        parts.append(suffix + jnp.sum(jnp.where(later, tot_sum, 0.0), axis=1, keepdims=True))
    dfz = (jnp.concatenate(parts, axis=1) * jax.nn.sigmoid(-fz_ref[...])).astype(BF16).astype(F32)
    head = lax.broadcasted_iota(jnp.int32, dfz.shape, 0)
    dfz = jnp.where(head < heads, dfz, 0.0)
    bias = jnp.sum(dfz, axis=1, keepdims=True)
    dfz_cols = turn(dfz).astype(BF16)
    dfz_low = dfz.astype(BF16)
    for i in range(n):
        small_ref[i, 8:16, :shard] = contract_cols(dfz_low, u_ref[i * shard : (i + 1) * shard, :])
        small_ref[i, 8:16, 224:225] = bias
        small_ref[i, 1:2, :shard] = jnp.sum(gain_two_ref[:, i * shard : (i + 1) * shard], axis=0, keepdims=True)

    moves.wait(12, 13)
    forget = jnp.concatenate([wf_ref[...], jnp.zeros((LANES - 8, cols), F32)], axis=0).astype(BF16)
    for c in range(TP_CHUNKS):
        back = pl.ds(c * span, span)
        du_ref[:, back] += (
            contract_cols(dkr_ref[...], wk_ref[back, :])
            + contract_cols(dvl_ref[...], wv_ref[back, :])
            + dot(dfz_cols, forget[:, c * span : (c + 1) * span])
        )

    def part(which, c):
        return du_ref[pl.ds(pl.multiple_of(which * half, half), half), c * span : (c + 1) * span]

    total = TpSum(part, sum_ref, (t0, t1, t2, t3), tsend, trecv, core, sibling, across)
    total.first()
    attns.advance(1)
    total.second()
    moves.start("dmid", dmid_ref, du_ref)
    for _ in range(3):
        gates.advance(1)
        attns.advance(1)
    total.third()
    gates.advance(1)
    attns.advance(1)
    total.fourth()
    moves.wait("dmid", 20)
    size = 64

    def input_rows(i, acc):
        here = pl.ds(pl.multiple_of(i * size, size), size)
        value = x_ref[here, :].astype(F32)
        inverse = lax.rsqrt(jnp.mean(value * value, axis=-1, keepdims=True) + EPS)
        normal = value * inverse
        grad = sum_ref[here, :].astype(F32)
        back = grad * gain_ref[...]
        back = inverse * (back - normal * jnp.mean(back * normal, axis=-1, keepdims=True))
        du_ref[here, :] += back
        return acc + jnp.sum((grad * normal).reshape(size // 8, 8, cols), axis=0)

    gains = lax.fori_loop(0, rows // size, input_rows, jnp.zeros((8, cols), F32))
    moves.start("input", du_ref, input_out)
    for i in range(n):
        small_ref[i, 0:1, :shard] = jnp.sum(gains[:, i * shard : (i + 1) * shard], axis=0, keepdims=True)
    exchange_start(n, me, tp, lambda peer: small_ref.at[peer], small_land, xsend, xrecv)
    moves.start("small", small_ref.at[me], small_land.at[me])
    while gates.next < n - 1:
        gates.advance(1)
        attns.advance(1)
    gates.end()
    attns.end()
    moves.wait("small")
    exchange_wait(n, me, tp, lambda peer: small_ref.at[peer], small_land, xsend, xrecv)
    small_out[...] = ordered_sum(n, small_land)
    pairs.sent()
    moves.wait()


def finish_backward(n, collective_id, heads, gate_plan, attn_plan, *operands):
    dq, u, x = operands[4], operands[17], operands[20]
    rows, width = dq.shape
    cols = x.shape[1]
    shard = u.shape[0] // n
    dma = pltpu.SemaphoreType.DMA
    vmem = pl.BlockSpec(memory_space=VMEM)
    anywhere = pl.BlockSpec(memory_space=pl.ANY)
    outside = STAGED + (22,)
    gate_widths = [sum(w for w, _ in side) for side in gate_plan]
    attn_widths = [sum(w for w, _ in side) for side in attn_plan]

    def ring_semaphores(plan):
        return [dma((2, max(len(side) for side in plan), n - 1))] * 2

    shapes = [(shard, width)] * 5 + [(16, 256), (rows, cols)]
    return pl.pallas_call(
        functools.partial(finish_kernel, n, heads, gate_plan, attn_plan),
        out_shape=[jax.ShapeDtypeStruct(shape, F32) for shape in shapes],
        in_specs=[anywhere if i in outside else smem() if i == 10 else vmem for i in range(len(operands))],
        out_specs=[vmem] * 6 + [anywhere],
        scratch_shapes=[
            *[VMEM(operands[i].shape, operands[i].dtype) for i in STAGED],
            VMEM(u.shape, BF16),
            *[VMEM((n - 1, rows, width), BF16)] * 2,
            *ring_scratch(n, shard, gate_widths),
            *ring_scratch(n, shard, attn_widths),
            VMEM((rows, width), F32),
            VMEM((rows, width), F32),
            *[VMEM((rows, width), BF16)] * 3,
            VMEM((rows, cols), F32),
            VMEM((rows, cols), BF16),
            *tp_buffers(rows, cols),
            VMEM((n, 8, rows), F32),
            VMEM((8, LANES), F32),
            VMEM((n, 8, rows), F32),
            VMEM((n, 8, LANES), F32),
            VMEM((n, 16, 256), F32),
            VMEM((n, 16, 256), F32),
            *[dma((2, len(pieces(width, LANES)), n - 1))] * 2,
            *ring_semaphores(gate_plan),
            *ring_semaphores(attn_plan),
            *[dma((n - 1,))] * 6,
            *[dma((3, TP_CHUNKS))] * 2,
            dma((len(STAGED) + 5,)),
        ],
        compiler_params=pltpu.CompilerParams(
            collective_id=collective_id, has_side_effects=True, vmem_limit_bytes=VMEM_LIMIT
        ),
    )(*operands)


LANES = 128


def block_state(group_map, doc_lengths, skip, query_group, key_group, rows, docs):
    first_q = query_group * rows
    last_q = first_q + rows - 1
    first_k = key_group * rows
    last_k = first_k + rows - 1
    zero = jnp.int32(0)
    doc_qf, doc_ql, doc_kf, doc_kl, end = zero, zero, zero, zero, zero
    for d in range(docs):
        end = end + doc_lengths[d]
        doc_qf += (first_q >= end).astype(jnp.int32)
        doc_ql += (last_q >= end).astype(jnp.int32)
        doc_kf += (first_k >= end).astype(jnp.int32)
        doc_kl += (last_k >= end).astype(jnp.int32)
    earlier = key_group < query_group
    same = key_group == query_group
    kept = skip[query_group, key_group] != 1
    active = jnp.logical_or(same, earlier & kept & (doc_kl == doc_qf))
    full = earlier & (doc_kf == doc_ql)
    return active, full


def block_mask(doc_lengths, query_group, key_group, rows, docs, query_dim):
    shape = (rows, rows)
    pos_q = query_group * rows + lax.broadcasted_iota(jnp.int32, shape, query_dim)
    pos_k = key_group * rows + lax.broadcasted_iota(jnp.int32, shape, 1 - query_dim)
    start = jnp.zeros(shape, jnp.int32)
    end = jnp.int32(0)
    for d in range(docs):
        end = end + doc_lengths[d]
        start = jnp.where(pos_q >= end, end, start)
    return (pos_k <= pos_q) & (pos_k >= start)


def document_start(position, doc_lengths):
    start, end = jnp.zeros_like(position), jnp.int32(0)
    for d in range(doc_lengths.shape[0]):
        end = end + doc_lengths[d]
        start = jnp.where(position >= end, end, start)
    return start


def block_masks(diff_ref, span_ref, skip, query_groups, key_groups, rows):
    masks = []
    for qi, ki in ((0, 0), (1, 0), (1, 1)):
        query_group, key_group = query_groups[qi], key_groups[ki]
        skipped = jnp.where(key_group < query_group, skip[query_group, key_group], 0)
        reach = key_group * rows - (skipped == 1).astype(jnp.int32) * (1 << 30)
        mask = span_ref[qi] <= reach
        if qi == ki:
            mask = mask & (diff_ref[...] <= (query_group - key_group) * rows)
        masks.append(mask)
    return masks


def in_pack_order(forward, one, two):
    return jnp.where(forward, one, two), jnp.where(forward, two, one)


def low_lanes(rows):
    return lax.broadcasted_iota(jnp.int32, (rows, LANES), 1) < LANES // 2


def three_pieces(value):
    high = value.astype(BF16).astype(F32)
    rest = value - high
    middle = rest.astype(BF16).astype(F32)
    return high, middle, rest - middle


def turn(value):
    rows = value.shape[1]
    return jnp.concatenate([value, jnp.zeros((LANES - 8, rows), F32)], axis=0).T


def row_pieces(term, with_ones):
    lane = lax.broadcasted_iota(jnp.int32, term.shape, 1)
    term = jnp.where(lane < 8, term, 0.0)
    high, middle, low = three_pieces(term)
    result = pltpu.roll(high, 24, 1) + pltpu.roll(middle, 32, 1) + pltpu.roll(low, 40, 1)
    if with_ones:
        result = jnp.where(lane < 24, 1.0, result)
    return result


def key_pieces(offsets):
    rows = offsets.shape[1]
    high, middle, low = three_pieces(offsets)
    stack = jnp.concatenate(
        [-high, -middle, -low, jnp.ones((24, rows), F32), jnp.zeros((LANES - 48, rows), F32)], axis=0
    )
    return stack.T.astype(BF16)


def spread_heads(wide_ref, common, put, heads, forward=None):
    rows = wide_ref.shape[0]
    low = low_lanes(rows)
    lane = lax.broadcasted_iota(jnp.int32, (rows, LANES), 1)

    def ordered(value):
        if forward is None:
            return value
        return jnp.concatenate(in_pack_order(forward, value[: rows // 2], value[rows // 2 :]), axis=0)

    common = ordered(common)
    for h in range(heads):
        pair = h // 2
        block = ordered(wide_ref[:, pair * LANES : (pair + 1) * LANES])
        keep = low if h % 2 == 0 else jnp.logical_not(low)
        put(
            h,
            jnp.where(keep, block, jnp.zeros_like(block)),
            jnp.where(lax.rem(lane, 8) == h, common, 0.0).astype(BF16),
        )


def put_rows(cat_ref):
    def put(h, value, extra):
        cat_ref[h, :, :LANES] = value
        cat_ref[h, :, LANES:] = extra

    return put


def smem():
    return pl.BlockSpec(memory_space=pltpu.SMEM)


def whole(shape):
    return pl.BlockSpec(shape, lambda i: (0,) * len(shape))


def head_sums(value, heads):
    width = value.shape[1]
    feature = lax.broadcasted_iota(jnp.int32, (width, LANES), 0)
    lane = lax.broadcasted_iota(jnp.int32, (width, LANES), 1)
    member = (lax.div(feature, width // heads) == lane).astype(BF16)
    high = value.astype(BF16)
    return dot(high, member) + dot((value - high.astype(F32)).astype(BF16), member)


def backward_kernel(
    heads, rows, docs, me, group_map, doc_lengths, skip, q_ref, d_ref, out_ref, term_ref, k_ref, v_ref, kaug_ref,
    dq_ref, drow_ref, dk_ref, dv_ref, dcol_ref, acc_ref, qcat_ref, dcat_ref, dk_acc, dv_acc, dcol_acc,
):
    step = pl.program_id(0)

    @pl.when(step == 0)
    def _():
        acc_ref[...] = jnp.zeros_like(acc_ref)
        spread_heads(q_ref, row_pieces(term_ref[...], True), put_rows(qcat_ref), heads)
        delta = head_sums(d_ref[...].astype(F32) * out_ref[...], heads)
        spread_heads(d_ref, row_pieces(-delta, False), put_rows(dcat_ref), heads)

    dk_acc[...] = jnp.zeros_like(dk_acc)
    dv_acc[...] = jnp.zeros_like(dv_acc)
    dcol_acc[...] = jnp.zeros_like(dcol_acc)

    def tile(qi, ki, mask):
        q_rows = pl.ds(qi * rows, rows)
        k_rows = pl.ds(ki * rows, rows)
        aug = kaug_ref[k_rows, :]
        for pair in range(heads // 2):
            lanes = pl.ds(pair * LANES, LANES)
            keys = jnp.concatenate([k_ref[pair, k_rows, :], aug], axis=1)
            values = jnp.concatenate([v_ref[pair, k_rows, :], aug], axis=1)
            for h in (2 * pair, 2 * pair + 1):
                probs = jnp.exp(contract_cols(keys, qcat_ref[h, q_rows, :]))
                if mask is not None:
                    probs = jnp.where(mask, probs, 0.0)
                grads = (probs * contract_cols(values, dcat_ref[h, q_rows, :])).astype(BF16)
                dv_acc[k_rows, lanes] += dot(probs.astype(BF16), dcat_ref[h, q_rows, :LANES])
                both = dot(grads, qcat_ref[h, q_rows, :])
                dk_acc[k_rows, lanes] += both[:, :LANES]
                dcol_acc[k_rows, :] += both[:, LANES:]
                acc_ref[h, q_rows, :] += contract_rows(grads, keys)

    for ki in range(2):
        key_group = group_map[2 * step + ki]
        for qi in range(2):
            query_group = group_map[2 * me[0] + qi]
            active, full = block_state(group_map, doc_lengths, skip, query_group, key_group, rows, docs)

            @pl.when(active & full)
            def _(qi=qi, ki=ki):
                tile(qi, ki, None)

            @pl.when(active & jnp.logical_not(full))
            def _(qi=qi, ki=ki, query_group=query_group, key_group=key_group):
                tile(qi, ki, block_mask(doc_lengths, query_group, key_group, rows, docs, 1))

    dk_ref[0] = dk_acc[...].astype(BF16)
    dv_ref[0] = dv_acc[...].astype(BF16)
    dcol_ref[0] = -(dcol_acc[...].T[:8])

    @pl.when(step == pl.num_programs(0) - 1)
    def _():
        total_rows = dq_ref.shape[0]
        low = low_lanes(total_rows)
        lane = lax.broadcasted_iota(jnp.int32, (total_rows, LANES), 1)
        sums = jnp.zeros((total_rows, LANES), F32)
        for pair in range(heads // 2):
            a, b = 2 * pair, 2 * pair + 1
            dq_ref[:, pair * LANES : (pair + 1) * LANES] = jnp.where(
                low, acc_ref[a, :, :LANES], acc_ref[b, :, :LANES]
            )
            sums = jnp.where(
                lane == 24 + a, acc_ref[a, :, LANES:], jnp.where(lane == 24 + b, acc_ref[b, :, LANES:], sums)
            )
        drow_ref[...] = pltpu.roll(sums, LANES - 24, 1).T[:8]


def backward_attention(me, group_map, doc_lengths, skip, queries, grads, attended, term, keys, values, key_aug, heads):
    total = keys.shape[1]
    own, width = queries.shape
    rows = own // 2
    n = total // own
    docs = doc_lengths.shape[0]
    return pl.pallas_call(
        functools.partial(backward_kernel, heads, rows, docs),
        grid=(n,),
        out_shape=[
            jax.ShapeDtypeStruct((own, width), F32),
            jax.ShapeDtypeStruct((8, own), F32),
            jax.ShapeDtypeStruct((n, own, width), BF16),
            jax.ShapeDtypeStruct((n, own, width), BF16),
            jax.ShapeDtypeStruct((n, 8, own), F32),
        ],
        in_specs=[smem(), smem(), smem(), smem()]
        + [
            whole((own, width)),
            whole((own, width)),
            whole((own, width)),
            whole((own, LANES)),
            pl.BlockSpec((heads // 2, own, LANES), lambda i: (0, i, 0)),
            pl.BlockSpec((heads // 2, own, LANES), lambda i: (0, i, 0)),
            pl.BlockSpec((own, LANES), lambda i: (i, 0)),
        ],
        out_specs=[
            whole((own, width)),
            whole((8, own)),
            pl.BlockSpec((1, own, width), lambda i: (i, 0, 0)),
            pl.BlockSpec((1, own, width), lambda i: (i, 0, 0)),
            pl.BlockSpec((1, 8, own), lambda i: (i, 0, 0)),
        ],
        scratch_shapes=[
            VMEM((heads, own, 2 * LANES), F32),
            VMEM((heads, own, 2 * LANES), BF16),
            VMEM((heads, own, 2 * LANES), BF16),
            VMEM((own, width), F32),
            VMEM((own, width), F32),
            VMEM((own, LANES), F32),
        ],
        compiler_params=pltpu.CompilerParams(vmem_limit_bytes=VMEM_LIMIT),
        cost_estimate=pl.CostEstimate(
            flops=own * total * width * 10, bytes_accessed=total * width * 8, transcendentals=own * total * heads
        ),
    )(me, group_map, doc_lengths, skip, queries, grads, attended, term, keys, values, key_aug)


def deliver_kernel(heads, count, small_ref, *refs):
    sources, refs = refs[:count], refs[count:]
    targets, refs = refs[:count], refs[count:]
    (first_ref, second_ref, forget_ref, bias_ref, gains_ref), refs = refs[:5], refs[5:]
    held, local = refs[:count], refs[count]
    moves = Moves(local)
    for i in range(count):
        moves.start(i, sources[i], held[i])
    shard, gain_rows = first_ref.shape[0], gains_ref.shape[1]
    first_ref[...] = small_ref[0:1, :shard].reshape(shard)
    second_ref[...] = small_ref[1:2, :shard].reshape(shard)
    turned = jnp.concatenate([small_ref[...], jnp.zeros((LANES - 16, 256), F32)], axis=0).T
    forget_ref[...] = small_ref[8 : 8 + heads, :shard]
    gains_ref[...] = small_ref[2 : 2 + heads, :gain_rows]
    bias_ref[...] = turned[224:225, 8 : 8 + heads].reshape(heads)
    for i in range(count):
        moves.wait(i)
        moves.start(i, held[i], targets[i])
    moves.wait()


def deliver(heads, shard, gain_rows, small, arrays):
    vmem = pl.BlockSpec(memory_space=VMEM)
    anywhere = pl.BlockSpec(memory_space=pl.ANY)
    shapes = [array.shape for array in arrays]
    shapes += [(shard,), (shard,), (heads, shard), (heads,), (heads, gain_rows)]
    (layer, input_grad, query, key, value, gate_out, output, gate, up, down, one, two, forget, bias, gains) = (
        pl.pallas_call(
            functools.partial(deliver_kernel, heads, len(arrays)),
            out_shape=[jax.ShapeDtypeStruct(shape, F32) for shape in shapes],
            in_specs=[vmem] + [anywhere] * len(arrays),
            out_specs=[anywhere] * len(arrays) + [vmem] * 5,
            scratch_shapes=[VMEM(array.shape, F32) for array in arrays]
            + [pltpu.SemaphoreType.DMA((2 * len(arrays),))],
            compiler_params=pltpu.CompilerParams(vmem_limit_bytes=VMEM_LIMIT),
        )(small, *arrays)
    )
    return (
        layer, input_grad, one, query, key, value, gate_out, forget.T, bias, gains.T, output, two, gate, up, down,
    )


def on_device(
    hidden_in,
    norm_one,
    w_query,
    w_key,
    w_value,
    w_gate_out,
    w_forget,
    forget_bias,
    head_gains,
    w_output,
    norm_two,
    w_gate,
    w_up,
    w_down,
    out_grad,
    doc_lengths,
    group_map,
    skip_list,
):
    device_ctx = lax.axis_index("ctx")
    device_tp = lax.axis_index("tp")
    n = lax.axis_size("ctx")
    row_count, model_width = hidden_in.shape
    group_rows = row_count // 2
    heads = forget_bias.shape[0]
    shard = norm_one.shape[0]
    gain_rows = head_gains.shape[0]
    head_dim = gain_rows * n // 2
    width = heads * head_dim
    hidden_width = w_gate.shape[1]

    slots = 2 * n
    (
        query_weight,
        key_weight,
        value_weight,
        gate_out_weight,
        output_weight,
        normed_shards,
        query_rows,
        query_raw,
        key_raw,
        gate_logit,
        forget_logit,
        keys_all,
        values_all,
        key_aug,
        attended_flat,
        row_term,
        gain_one,
        gain_two,
        query_gain,
        key_gain,
        forget_weight,
    ) = start_forward(
        n,
        1,
        group_map,
        doc_lengths,
        skip_list,
        forget_bias,
        hidden_in,
        [norm_one, norm_two, head_gains.T, w_forget.T],
        [w_query, w_key, w_value, w_gate_out],
        w_output,
    )
    half = width // 256 * 128
    fused = n <= 8
    (
        gated,
        layer_out,
        down_share,
        gate_share,
        up_share,
        grad_middle,
        grad_attended,
        grad_gate_logit,
        gain_two_parts,
        *attention_grads,
    ) = feed_forward(
        n,
        3,
        heads,
        attended_flat,
        gate_logit,
        output_weight,
        hidden_in,
        gain_two,
        out_grad,
        w_gate,
        w_up,
        w_down,
        (group_map, doc_lengths, skip_list, query_rows, row_term, keys_all, values_all, key_aug) if fused else None,
    )
    halves = [(0, half), (half, width - half)]
    attn_plan = [[(cw, (i, c0, cw)) for c0, cw in halves] for i in (0, 1)]
    if fused:
        grad_branch, grad_query, row_sums, key_part, value_part, column_sums = attention_grads
        early_plan = [side + [(cw, (2, c0, cw))] for side, (c0, cw) in zip(attn_plan, halves)]
        query_share, key_share, value_share, gate_out_share, output_share, small_share, input_grad = finish_backward(
            n,
            7,
            heads,
            early_plan,
            attn_plan,
            key_part,
            value_part,
            column_sums,
            row_sums,
            grad_query,
            query_raw,
            key_raw,
            query_gain,
            key_gain,
            forget_logit,
            group_map,
            query_weight,
            key_weight,
            value_weight,
            gate_out_weight,
            forget_weight,
            grad_gate_logit,
            normed_shards,
            grad_branch,
            gated,
            hidden_in,
            gain_one,
            grad_middle,
            gain_two_parts,
        )
    else:
        grad_branch = grad_middle.astype(BF16).reshape(row_count, n, shard).transpose(1, 0, 2)
        normed_shards = normed_shards.reshape(n, shard, row_count).transpose(0, 2, 1)
        grad_query, row_sums, key_part, value_part, column_sums = backward_attention(
            device_ctx.astype(jnp.int32).reshape(1),
            group_map,
            doc_lengths,
            skip_list,
            query_rows,
            grad_attended,
            attended_flat,
            row_term,
            keys_all,
            values_all,
            key_aug,
            heads,
        )
        own_groups = lax.dynamic_slice_in_dim(group_map, device_ctx * 2, 2, 0)
        later = (group_map[None, :] > own_groups[:, None]).astype(F32)
        query_gain, key_gain = (gain.reshape(heads, head_dim) for gain in (query_gain, key_gain))
        query_raw, key_raw = (raw.reshape(row_count, heads, head_dim) for raw in (query_raw, key_raw))
        query_norm, key_norm = rms_scale(query_raw), rms_scale(key_raw)
        forget_logit = forget_logit[:heads].T
        forget_weight = forget_weight[:heads].astype(BF16)
        normed_one = normed_shards.transpose(1, 0, 2).reshape(row_count, model_width)
        place = jnp.arange(group_rows, dtype=jnp.int32)
        upper = (place[:, None] <= place[None, :]).astype(F32)
        grad_key, grad_value, off_sum, tot_sum = pair_scatter(n, 7, key_part, value_part, column_sums, row_sums)
        after = contract_cols_exact(tot_sum[:heads, :slots], later)
        suffix = lax.dot_general(
            off_sum[:heads].reshape(heads, 2, group_rows), upper, (((2,), (1,)), ((), ())), precision=HIGHEST
        )
        grad_log_forget = (suffix + after[:, :, None]).reshape(heads, row_count).T
        grad_key3 = grad_key.reshape(row_count, heads, head_dim)
        grad_query3 = grad_query.reshape(row_count, heads, head_dim)
        key_raw_grad = rms_back(grad_key3 * key_gain, key_raw).astype(BF16).reshape(row_count, width)
        query_raw_grad = (
            rms_back(grad_query3 * query_gain * 0.125, query_raw).astype(BF16).reshape(row_count, width)
        )
        value_low = grad_value.astype(BF16)
        query_gain_grad = jnp.sum(grad_query3 * query_norm * 0.125, axis=0)
        key_gain_grad = jnp.sum(grad_key3 * key_norm, axis=0)
        head_gain_grad = jnp.concatenate([query_gain_grad, key_gain_grad], axis=1)
        grad_forget_logit = (grad_log_forget * jax.nn.sigmoid(-forget_logit)).astype(BF16)
        bias_part = jnp.sum(grad_forget_logit.astype(F32), axis=0)
        normed_one_part = (
            contract_cols(query_raw_grad, query_weight)
            + contract_cols(key_raw_grad, key_weight)
            + contract_cols(value_low, value_weight)
            + contract_cols(grad_gate_logit, gate_out_weight)
            + dot(grad_forget_logit, forget_weight)
        )
        forget_grad = contract_rows(grad_forget_logit, normed_one)

        def wide(value):
            return jnp.pad(value, ((0, 0), (0, 0), (0, 256 - value.shape[2])))

        forget_rows = wide(forget_grad.reshape(heads, n, shard).transpose(1, 0, 2))
        forget_rows = forget_rows.at[:, :, 224].set(bias_part[None, :])
        small_grad = jnp.concatenate(
            [
                jnp.zeros((n, 1, 256), F32),
                wide(jnp.sum(gain_two_parts, axis=0).reshape(n, 1, shard)),
                wide(head_gain_grad.reshape(heads, n, gain_rows).transpose(1, 0, 2)),
                jnp.pad(forget_rows, ((0, 0), (0, 8 - heads), (0, 0))),
            ],
            axis=1,
        )
        plan = [
            [(cw, (0, right, c0, cw)) for right in rights for c0, cw in halves] + [(cw, (1, 4, c0, cw))]
            for rights, (c0, cw) in zip(((0, 1), (2, 3)), halves)
        ]
        (
            query_share,
            key_share,
            value_share,
            gate_out_share,
            output_share,
            small_share,
            input_grad,
        ) = weight_scatter(
            n,
            8,
            plan,
            [normed_shards, grad_branch],
            [query_raw_grad, key_raw_grad, value_low, grad_gate_logit, gated],
            small_grad,
            normed_one_part,
            hidden_in,
            gain_one,
            grad_middle,
        )
    return deliver(
        heads,
        shard,
        gain_rows,
        small_share,
        [
            layer_out,
            input_grad,
            query_share,
            key_share,
            value_share,
            gate_out_share,
            output_share,
            gate_share,
            up_share,
            down_share,
        ],
    )


def solution(mesh):
    split = P("ctx", "tp")
    in_specs = (
        P("ctx", None),
        P("ctx"),
        split,
        split,
        split,
        split,
        split,
        P("tp"),
        split,
        split,
        P("ctx"),
        split,
        split,
        split,
        P("ctx", None),
        P(),
        P(),
        P(),
    )
    out_specs = (
        split,
        P("ctx", None),
        P("ctx"),
        split,
        split,
        split,
        split,
        split,
        P("tp"),
        split,
        split,
        P("ctx"),
        split,
        split,
        split,
    )
    return jax.shard_map(on_device, mesh=mesh, in_specs=in_specs, out_specs=out_specs, check_vma=False)
```

```python
import functools

import jax
import jax.numpy as jnp
from jax import lax
from jax.experimental import pallas as pl
from jax.experimental.pallas import tpu as pltpu
from jax.sharding import PartitionSpec as P

EPS = 1e-06
HIGHEST = lax.Precision.HIGHEST
MESH = pl.DeviceIdType.MESH
VMEM = pltpu.VMEM
VMEM_LIMIT = 62 * 1024 * 1024
F32 = jnp.float32
BF16 = jnp.bfloat16


def rms_scale(value):
    return value * lax.rsqrt(jnp.mean(value * value, axis=-1, keepdims=True) + EPS)


def rms_back(grad_in, value):
    inverse = lax.rsqrt(jnp.mean(value * value, axis=-1, keepdims=True) + EPS)
    normal = value * inverse
    return inverse * (grad_in - normal * jnp.mean(grad_in * normal, axis=-1, keepdims=True))


def dot(left, right):
    return jnp.dot(left, right, preferred_element_type=F32)


def contract_cols(left, right):
    return lax.dot_general(left, right, (((1,), (1,)), ((), ())), preferred_element_type=F32)


def contract_cols_exact(left, right):
    return lax.dot_general(left, right, (((1,), (1,)), ((), ())), precision=HIGHEST)


def contract_rows(left, right):
    return lax.dot_general(left, right, (((0,), (0,)), ((), ())), preferred_element_type=F32)


def ring_place(ctx, n):
    odd = lax.rem(ctx, 2)
    half = lax.div(ctx, 2)
    return (1 - odd) * half + odd * (n - 1 - half)


def ring_owner(place, n):
    late = lax.div(place, n // 2)
    return (1 - late) * (2 * place) + late * (2 * (n - 1 - place) + 1)


def wrap(place, n):
    return lax.rem(place + 2 * n, n)


def ring_setup(n):
    me = lax.axis_index("ctx")
    tp = lax.axis_index("tp")
    place = ring_place(me, n)
    right = ring_owner(wrap(place + 1, n), n)
    left = ring_owner(wrap(place - 1, n), n)
    return me, tp, place, (right, left)


def greet(peers):
    barrier = pltpu.get_barrier_semaphore()
    for peer in peers:
        pl.semaphore_signal(barrier, inc=1, device_id=peer, device_id_type=MESH)
    pl.semaphore_wait(barrier, len(peers))


def ctx_peers(me, tp, n):
    return [(lax.rem(me + i, n), tp) for i in range(1, n)]


def remote(src, dst, send, recv, device):
    return pltpu.make_async_remote_copy(
        src_ref=src, dst_ref=dst, send_sem=send, recv_sem=recv, device_id=device, device_id_type=MESH
    )


class Gather:
    def __init__(self, n, place, sides, tp, chunks, send, recv):
        self.n, self.place, self.sides, self.tp = n, place, sides, tp
        self.chunks, self.send, self.recv = chunks, send, recv
        self.arrived = None

    def owner(self, side, back):
        return ring_owner(wrap(self.place - back if side == 0 else self.place + back, self.n), self.n)

    def copy(self, index, step, first):
        side, source, target = self.chunks[index]
        target = target(self.owner(side, step))
        return remote(
            source if first else target, target, self.send.at[index, step], self.recv.at[index, step],
            (self.sides[side], self.tp),
        )

    def arrive(self, index, step):
        side, _, target = self.chunks[index]
        target = target(self.owner(side, step + 1))
        remote(
            target, target, self.send.at[index, step], self.recv.at[index, step], (self.sides[side], self.tp)
        ).wait_recv()
        if self.arrived is not None:
            self.arrived(index, step)

    def begin(self, indices=None):
        for index in indices if indices is not None else range(len(self.chunks)):
            self.copy(index, 0, True).start()

    def forward(self, step):
        for index in range(len(self.chunks)):
            self.arrive(index, step - 1)
            self.copy(index, step, False).start()

    def last(self):
        for index in range(len(self.chunks)):
            self.arrive(index, self.n - 2)

    def sent(self):
        def finish(step, carry):
            for index in range(len(self.chunks)):
                self.copy(index, step, False).wait_send()
            return carry

        lax.fori_loop(0, self.n - 1, finish, 0)


class Moves:
    def __init__(self, semaphores):
        self.semaphores, self.count, self.open = semaphores, 0, {}

    def start(self, name, source, target):
        copy = pltpu.make_async_copy(source, target, self.semaphores.at[self.count])
        self.count += 1
        copy.start()
        self.open[name] = copy

    def wait(self, *names):
        for name in names or list(self.open):
            self.open.pop(name).wait()


def start_kernel(
    n, heads, group_map, doc_lengths, skip, bias_ref, x_ref, norm_one, norm_two, gains_in, forget_in,
    wq_in, wk_in, wv_in, wg_in, wo_in,
    wq_out, wk_out, wv_out, wg_out, wo_ref, u_out, q_out, qr_out, kr_out, gl_out, fz_ref, k_out, v_out, aug_out,
    att_out, term_ref, gain_one, gain_two, qgain_ref, kgain_ref, wf_ref,
    x_vmem, wq_ref, wk_ref, wv_ref, wg_ref, u_ref, turned_ref, q_ref, k_all, v_all, aug_ref, att_ref, acc_ref, cat_ref,
    diff_ref, span_ref, tot_ref, before_ref, inside_all, small_wide, small_in,
    small_all, acc_r, acc_l, inside_src,
    wsend, wrecv, osend, orecv, ksend, krecv, ssend, srecv, isend, irecv, spill, local,
):
    me, tp, place, sides = ring_setup(n)
    moves = Moves(local)
    moves.start("x", x_ref, x_vmem)
    shard, width = wq_in.shape
    small_wide[...] = jnp.zeros_like(small_wide)
    small_wide[0:1, :shard] = norm_one[...].astype(F32).reshape(1, shard)
    small_wide[1:2, :shard] = norm_two[...].astype(F32).reshape(1, shard)
    for ref, first in ((gains_in, 2), (forget_in, 8)):
        small_wide[first : first + heads, : ref.shape[1]] = ref[...].astype(F32)
    small_in[...] = small_wide[...].astype(BF16)
    greet(ctx_peers(me, tp, n))
    rows, cols = x_ref.shape
    half = rows // 2
    head_dim = width // heads

    def shard_rows(owner):
        return pl.ds(pl.multiple_of(owner * shard, 16), shard)

    def window(ref, c0, cw):
        return lambda owner: ref.at[shard_rows(owner), pl.ds(c0, cw)]

    def token_rows(owner):
        return pl.ds(pl.multiple_of(owner * rows, rows), rows)

    def block(ref, pair):
        return lambda owner: ref.at[pair, token_rows(owner), :]

    ring = (n, place, sides, tp)
    projections = Gather(
        *ring,
        [
            (side, source, window(target, 0, width))
            for side, source, target in ((0, wq_in, wq_ref), (1, wv_in, wv_ref), (0, wk_in, wk_ref), (1, wg_in, wg_ref))
        ],
        wsend, wrecv,
    )
    middle = width // 256 * 128
    outputs = Gather(
        *ring,
        [
            (side, wo_in.at[:, pl.ds(c0, cw)], window(wo_ref, c0, cw))
            for side, c0, cw in ((0, 0, middle), (1, middle, width - middle))
        ],
        osend, orecv,
    )
    members = [(0, k_all, k_out, 0), (1, k_all, k_out, 2), (0, v_all, v_out, 0), (1, v_all, v_out, 2)]
    members += [(0, k_all, k_out, 1), (1, v_all, v_out, 1)]
    pairs = Gather(
        *ring, [(side, block(ref, pair)(me), block(ref, pair)) for side, ref, _, pair in members], ksend, krecv
    )

    def spill_copy(index, step):
        side, ref, out, pair = members[index]
        owner = pairs.owner(side, step + 1)
        return pltpu.make_async_copy(
            block(ref, pair)(owner), block(out, pair)(owner), spill.at[index, step]
        )

    pairs.arrived = lambda index, step: spill_copy(index, step).start()

    projections.begin()
    exchange_start(n, me, tp, lambda peer: small_in, small_all, ssend, srecv)
    gathered = ((wq_in, wq_ref), (wk_in, wk_ref), (wv_in, wv_ref), (wg_in, wg_ref), (wo_in, wo_ref))
    for i, (source, target) in enumerate(gathered):
        moves.start(i, source, target.at[shard_rows(me)])
    moves.start("small", small_in, small_all.at[me])
    moves.wait("small")
    exchange_wait(n, me, tp, lambda peer: small_in, small_all, ssend, srecv)
    projections.forward(1)

    count = 2 * head_dim // n
    for i in range(n):
        block_small = small_all[i].astype(F32)
        gain_one[:, i * shard : (i + 1) * shard] = block_small[0:1, :shard]
        gain_two[:, i * shard : (i + 1) * shard] = block_small[1:2, :shard]
        wf_ref[:, i * shard : (i + 1) * shard] = block_small[8:16, :shard]
        target, at = (qgain_ref, i) if i < n // 2 else (kgain_ref, i - n // 2)
        for h in range(heads):
            lane = h * head_dim + at * count
            target[:, lane : lane + count] = block_small[2 + h : 3 + h, :count]

    size = 64

    def norm_rows(i, carry):
        here = pl.ds(pl.multiple_of(i * size, size), size)
        normed = (rms_scale(x_vmem[here, :].astype(F32)) * gain_one[...]).astype(BF16)
        for j in range(n):
            u_ref[j, here, :] = normed[:, j * shard : (j + 1) * shard]
        return carry

    moves.wait("x")
    lax.fori_loop(0, rows // size, norm_rows, 0)

    def grow(back):
        for side, acc, sources in ((0, acc_r, (wq_ref, wk_ref)), (1, acc_l, (wv_ref, wg_ref))):
            owner = projections.owner(side, back)
            for i, source in enumerate(sources):
                acc[:, i * width : (i + 1) * width] += dot(u_ref[owner], source[shard_rows(owner), :])

    acc_r[...] = jnp.zeros_like(acc_r)
    acc_l[...] = jnp.zeros_like(acc_l)
    moves.wait(0, 1, 2, 3, 4)
    grow(0)
    projections.forward(2)
    grow(1)
    grow(2)
    projections.forward(3)
    grow(3)
    forget = jnp.zeros((16, rows), F32)
    for j in range(n):
        forget += contract_cols(small_all[j, :, :shard], u_ref[j])
    head = lax.broadcasted_iota(jnp.int32, (8, rows), 0)
    fz = forget[8:16]
    for h in range(heads):
        fz = jnp.where(head == h, fz + bias_ref[h], fz)
    fz_ref[...] = fz
    logs = jnp.minimum(fz, 0.0) - jnp.log1p(jnp.exp(-jnp.abs(fz)))
    logs = jnp.where(head < heads, logs, 0.0)
    upto = (
        lax.broadcasted_iota(jnp.int32, (half, half), 0) <= lax.broadcasted_iota(jnp.int32, (half, half), 1)
    ).astype(F32)
    for g in range(2):
        inside_src[:, g * half : (g + 1) * half] = jnp.dot(
            logs[:, g * half : (g + 1) * half], upto, precision=HIGHEST, preferred_element_type=F32
        )
    exchange_start(n, me, tp, lambda peer: inside_src, inside_all, isend, irecv)
    moves.start("inside", inside_src, inside_all.at[me])

    def step_on(step, carry):
        projections.forward(step)
        grow(step)
        return carry

    lax.fori_loop(4, n - 2, step_on, 0)
    outputs.begin()
    projections.forward(n - 2)
    grow(n - 2)
    outputs.forward(1)
    projections.last()
    grow(n - 1)

    def head_norm(value):
        return value * lax.rsqrt(head_means(value * value, heads) + EPS)

    my_rows = token_rows(me)
    for pair in range(heads // 2):
        v_all[pair, my_rows, :] = acc_l[:, pair * LANES : (pair + 1) * LANES].astype(BF16)
    pairs.begin([2, 3, 5])
    keys = (head_norm(acc_r[:, width:]) * kgain_ref[...]).astype(BF16)
    for pair in range(heads // 2):
        k_all[pair, my_rows, :] = keys[:, pair * LANES : (pair + 1) * LANES]
    pairs.begin([0, 1, 4])
    for i, (source, target) in enumerate(
        ((wq_ref, wq_out), (wk_ref, wk_out), (wv_ref, wv_out), (wg_ref, wg_out))
    ):
        moves.start(i, source, target)
    moves.start("qr", acc_r.at[:, pl.ds(0, width)], qr_out)
    moves.start("kr", acc_r.at[:, pl.ds(width, width)], kr_out)
    moves.start("gl", acc_l.at[:, pl.ds(width, width)], gl_out)
    for i, (ref, out) in enumerate(((k_all, k_out), (v_all, v_out))):
        for pair in range(heads // 2):
            moves.start((i, pair), block(ref, pair)(me), block(out, pair)(me))
    q_ref[...] = (head_norm(acc_r[:, :width]) * qgain_ref[...] * 0.125).astype(BF16)
    moves.start("q", q_ref, q_out)

    moves.wait("inside")
    exchange_wait(n, me, tp, lambda peer: inside_src, inside_all, isend, irecv)
    tot_ref[...] = jnp.zeros_like(tot_ref)
    for i in range(n):
        for g in range(2):
            tot_ref[:, 2 * i + g : 2 * i + g + 1] = inside_all[i, :, (g + 1) * half - 1 : (g + 1) * half]
    earlier = groups_along(group_map, 0, 1 << 20) < groups_along(group_map, 1, 1 << 20)
    before_ref[...] = jnp.dot(
        tot_ref[...], earlier.astype(F32), precision=HIGHEST, preferred_element_type=F32
    )
    lane8 = lax.broadcasted_iota(jnp.int32, (8, LANES), 1)

    def offsets_of(shard_index):
        parts = []
        for g in range(2):
            before = jnp.sum(jnp.where(lane8 == 2 * shard_index + g, before_ref[...], 0.0), axis=1, keepdims=True)
            parts.append(inside_all[shard_index, :, g * half : (g + 1) * half] + before)
        return jnp.concatenate(parts, axis=1)

    def aug_rows(i, carry):
        aug_ref[token_rows(i), :] = key_pieces(offsets_of(i))
        return carry

    lax.fori_loop(0, n, aug_rows, 0)
    moves.start("aug", aug_ref, aug_out)
    pairs.forward(1)

    first, second = group_map[2 * me], group_map[2 * me + 1]
    in_order = first < second
    query_groups = (jnp.minimum(first, second), jnp.maximum(first, second))
    mine = turn(offsets_of(me))
    term_ref[...] = mine
    spread_heads(q_ref, row_pieces(mine, True), put_rows(cat_ref), heads, in_order)
    acc_ref[...] = jnp.zeros_like(acc_ref)
    query_at = lax.broadcasted_iota(jnp.int32, (half, half), 0)
    key_at = lax.broadcasted_iota(jnp.int32, (half, half), 1)
    diff_ref[...] = key_at - query_at
    for i, group in enumerate(query_groups):
        span_ref[i] = document_start(group * half + query_at, doc_lengths) - key_at
    ones = jnp.ones((half, LANES), BF16)

    def attend(i, back):
        late = lax.div(i, 2)
        pair = (1 - late) * 2 * i + late
        side = lax.rem(i, 2)
        owner = ring_owner(wrap(place + (2 * side - 1) * back, n), n)
        one, two = group_map[2 * owner], group_map[2 * owner + 1]
        forward = one < two
        key_groups = (jnp.minimum(one, two), jnp.maximum(one, two))
        top = pl.ds(pl.multiple_of(owner * rows, rows), half)
        bottom = pl.ds(pl.multiple_of(owner * rows + half, half), half)
        blocks = []
        for ref in (k_all.at[pair], v_all.at[pair], aug_ref):
            blocks.append(in_pack_order(forward, ref[top, :], ref[bottom, :]))
        masks = block_masks(diff_ref, span_ref, skip, query_groups, key_groups, half)
        keys = [jnp.concatenate([blocks[0][ki], blocks[2][ki]], axis=1) for ki in range(2)]
        values = [jnp.concatenate([blocks[1][ki], ones], axis=1) for ki in range(2)]
        both_values = jnp.concatenate(values, axis=0)
        for e in range(2):
            h = 2 * pair + e
            queries = cat_ref[h]
            early = contract_cols(queries, keys[0])
            weights = [
                jnp.where(mask, jnp.exp(score), 0.0).astype(BF16)
                for mask, score in zip(masks, (early[:half], early[half:], contract_cols(queries[half:], keys[1])))
            ]
            acc_ref[h, :half, :] += dot(weights[0], values[0])
            acc_ref[h, half:, :] += dot(jnp.concatenate(weights[1:], axis=1), both_values)

    def attend_all(count, back):
        def body(i, carry):
            attend(i, back)
            return carry

        lax.fori_loop(0, count, body, 0)

    attend_all(3, 0)

    def pair_step(step, count):
        outputs.forward(step)
        pairs.forward(step)
        attend_all(count, step)

    outputs.forward(2)
    pairs.forward(2)
    attend_all(2, 1)
    attend_all(2, 2)

    def turn_shard(i, carry):
        turned_ref[shard_rows(i), :] = u_ref[i].astype(F32).T.astype(BF16)
        return carry

    lax.fori_loop(0, n, turn_shard, 0)
    moves.start("u", turned_ref, u_out)

    def early_step(step, carry):
        pair_step(step, 2)
        return carry

    def late_step(step, carry):
        pair_step(step, 4)
        return carry

    lax.fori_loop(3, n // 2, early_step, 0)
    pair_step(n // 2, 3)
    lax.fori_loop(n // 2 + 1, n - 1, late_step, 0)
    outputs.last()
    pairs.last()
    attend_all(4, n - 1)

    lane = lax.broadcasted_iota(jnp.int32, (rows, LANES), 1)
    low = low_lanes(rows)
    totals = jnp.ones((rows, LANES), F32)
    for pair in range(heads // 2):
        parts = []
        for h in (2 * pair, 2 * pair + 1):
            value = jnp.concatenate(in_pack_order(in_order, acc_ref[h, :half, :], acc_ref[h, half:, :]), axis=0)
            parts.append(value)
            totals = jnp.where(lane == h, value[:, LANES:], totals)
        att_ref[:, pair * LANES : (pair + 1) * LANES] = jnp.where(
            low, parts[0][:, :LANES], parts[1][:, :LANES]
        ) / jnp.where(low, parts[0][:, LANES:], parts[1][:, LANES:])
    moves.start("att", att_ref, att_out)
    term_ref[...] -= jnp.log(totals)

    def spilled(step, carry):
        for index in range(len(members)):
            spill_copy(index, step).wait()
        return carry

    lax.fori_loop(0, n - 1, spilled, 0)
    moves.wait()
    projections.sent()
    outputs.sent()
    pairs.sent()


def groups_along(group_map, dim, fill, shape=(128, 128)):
    slot = lax.broadcasted_iota(jnp.int32, shape, dim)
    groups = jnp.full(shape, fill, jnp.int32)
    for i in range(group_map.shape[0]):
        groups = jnp.where(slot == i, group_map[i], groups)
    return groups


def start_forward(n, collective_id, group_map, doc_lengths, skip, bias, x, vectors, weights, out_weight):
    rows, cols = x.shape
    shard, width = out_weight.shape
    heads = bias.shape[0]
    half = rows // 2
    dma = pltpu.SemaphoreType.DMA
    vmem = pl.BlockSpec(memory_space=VMEM)
    anywhere = pl.BlockSpec(memory_space=pl.ANY)
    by_pair = (heads // 2, n * rows, LANES)
    weight, wide, narrow = (n * shard, width), (rows, cols), (rows, width)
    shapes = (
        [(weight, BF16)] * 5
        + [((n * shard, rows), BF16), (narrow, BF16)]
        + [(narrow, F32)] * 3
        + [((8, rows), F32)]
        + [(by_pair, BF16)] * 2
        + [((n * rows, LANES), BF16), (narrow, F32), ((rows, LANES), F32)]
        + [((1, cols), F32)] * 2
        + [((1, width), F32)] * 2
        + [((8, cols), F32)]
    )
    return pl.pallas_call(
        functools.partial(start_kernel, n, heads),
        out_shape=[jax.ShapeDtypeStruct(*shape) for shape in shapes],
        in_specs=[smem(), smem(), smem(), smem(), anywhere] + [vmem] * 4 + [anywhere] * 5,
        out_specs=[anywhere if i < 10 or 11 <= i <= 14 else vmem for i in range(len(shapes))],
        scratch_shapes=[
            VMEM(wide, BF16),
            *[VMEM(weight, BF16)] * 4,
            VMEM((n, rows, shard), BF16),
            VMEM((n * shard, rows), BF16),
            VMEM(narrow, BF16),
            *[VMEM(by_pair, BF16)] * 2,
            VMEM((n * rows, LANES), BF16),
            VMEM(narrow, F32),
            VMEM((heads, rows, 2 * LANES), F32),
            VMEM((heads, rows, 2 * LANES), BF16),
            VMEM((half, half), jnp.int32),
            VMEM((2, half, half), jnp.int32),
            VMEM((8, LANES), F32),
            VMEM((8, LANES), F32),
            VMEM((n, 8, rows), F32),
            VMEM((16, 256), F32),
            VMEM((16, 256), BF16),
            VMEM((n, 16, 256), BF16),
            VMEM((rows, 2 * width), F32),
            VMEM((rows, 2 * width), F32),
            VMEM((8, rows), F32),
            *[dma((4, n - 1))] * 2,
            *[dma((2, n - 1))] * 2,
            *[dma((6, n - 1))] * 2,
            *[dma((n - 1,))] * 4,
            dma((6, n - 1)),
            dma((26,)),
        ],
        compiler_params=pltpu.CompilerParams(
            collective_id=collective_id, has_side_effects=True, vmem_limit_bytes=VMEM_LIMIT
        ),
    )(group_map, doc_lengths, skip, bias, x, *vectors, *weights, out_weight)


class ScatterRing:
    def __init__(self, n, plan, local_term, slots, firsts, write, send, recv, place, sides, tp, source=None):
        self.n, self.place, self.sides, self.tp = n, place, sides, tp
        self.source, self.next = source, 1
        self.local_term, self.write = local_term, write
        self.slots, self.firsts, self.send, self.recv = slots, firsts, send, recv
        self.order = []
        starts = [0, 0]
        for index in range(max(len(plan[0]), len(plan[1]))):
            for side in (0, 1):
                if index < len(plan[side]):
                    width, tag = plan[side][index]
                    self.order.append((side, index, starts[side], width, tag))
                    starts[side] += width

    def target(self, side, step):
        step = -1 - step if side == 0 else 1 + step
        return ring_owner(wrap(self.place + step, self.n), self.n)

    def hop(self, side, index, start, width, step, first):
        cols = pl.ds(start, width)
        slots = self.slots[side]
        if not first:
            source = slots.at[step - 1, :, cols]
        elif self.source is None:
            source = self.firsts[side].at[:, cols]
        else:
            source = self.source(self.target(side, 0), side, cols)
        return remote(
            source,
            slots.at[step, :, cols],
            self.send.at[side, index, step],
            self.recv.at[side, index, step],
            (self.sides[side], self.tp),
        )

    def begin(self):
        for side, index, start, width, tag in self.order:
            if self.source is None:
                term = self.local_term(self.target(side, 0), tag)
                self.firsts[side][:, start : start + width] = term.astype(BF16)
            self.hop(side, index, start, width, 0, True).start()

    def forward(self, step):
        for side, index, start, width, tag in self.order:
            term = self.local_term(self.target(side, step), tag)
            slot = self.slots[side].at[step - 1, :, pl.ds(start, width)]
            self.hop(side, index, start, width, step - 1, True).wait_recv()
            slot[...] = (slot[...].astype(F32) + term).astype(BF16)
            self.hop(side, index, start, width, step, False).start()

    def span(self, first, last):
        def body(step, carry):
            self.forward(step)
            return carry

        if last > first:
            lax.fori_loop(first, last, body, 0)

    def advance(self, count):
        last = min(self.next + count, self.n - 1)
        self.span(self.next, last)
        self.next = last

    def end(self):
        n = self.n
        self.advance(n)
        for side, index, start, width, tag in self.order:
            term = self.local_term(self.target(side, n - 1), tag)
            self.hop(side, index, start, width, n - 2, True).wait_recv()
            self.write(tag, self.slots[side][n - 2, :, start : start + width].astype(F32) + term)
        if self.source is None:
            self.sent()

    def sent(self):
        for side, index, start, width, tag in self.order:
            self.hop(side, index, start, width, 0, True).wait_send()

        def finish(step, carry):
            for side, index, start, width, tag in self.order:
                self.hop(side, index, start, width, step, False).wait_send()
            return carry

        lax.fori_loop(1, self.n - 1, finish, 0)


def exchange_start(n, me, tp, source_of, landing, send, recv):
    for i in range(1, n):
        peer = lax.rem(me + i, n)
        remote(source_of(peer), landing.at[me], send.at[i - 1], recv.at[i - 1], (peer, tp)).start()


def exchange_wait(n, me, tp, source_of, landing, send, recv):
    for i in range(1, n):
        peer = lax.rem(me - i + n, n)
        remote(source_of(peer), landing.at[peer], send.at[i - 1], recv.at[i - 1], (peer, tp)).wait()


def ordered_sum(n, landing):
    total = landing[0]
    for i in range(1, n):
        total = total + landing[i]
    return total


def pair_scatter_kernel(
    n, key_ref, value_ref, col_ref, row_ref, key_out, value_out, off_out, tot_out,
    slot_r, slot_l, first_r, first_l, off_ref, tot_ref, off_land, tot_land,
    send, recv, osend, orecv, tsend, trecv, local,
):
    me, tp, place, sides = ring_setup(n)
    off_ref[...] = col_ref[...]
    off_ref[me] += row_ref[...]
    group_rows = row_ref.shape[1] // 2
    tot_ref[...] = jnp.zeros_like(tot_ref)
    for i in range(n):
        for g in range(2):
            tot_ref[:, 2 * i + g : 2 * i + g + 1] = jnp.sum(
                off_ref[i, :, g * group_rows : (g + 1) * group_rows], axis=1, keepdims=True
            )
    greet(ctx_peers(me, tp, n))
    exchange_start(n, me, tp, lambda peer: off_ref.at[peer], off_land, osend, orecv)
    exchange_start(n, me, tp, lambda peer: tot_ref, tot_land, tsend, trecv)
    mine = pltpu.make_async_copy(off_ref.at[me], off_land.at[me], local.at[0])
    mine_tot = pltpu.make_async_copy(tot_ref, tot_land.at[me], local.at[1])
    mine.start()
    mine_tot.start()
    width = key_ref.shape[2]
    plan = [
        [(w, (0, c)) for c, w in pieces(width, 128)],
        [(w, (1, c)) for c, w in pieces(width, 128)],
    ]

    def local_term(owner, tag):
        which, c0 = tag
        return (key_ref, value_ref)[which][owner, :, c0 : c0 + 128].astype(F32)

    def write(tag, value):
        which, c0 = tag
        (key_out, value_out)[which][:, c0 : c0 + 128] = value

    ring = ScatterRing(
        n, plan, local_term, (slot_r, slot_l), (first_r, first_l), write, send, recv, place, sides, tp
    )
    ring.begin()
    ring.end()
    mine.wait()
    mine_tot.wait()
    exchange_wait(n, me, tp, lambda peer: off_ref.at[peer], off_land, osend, orecv)
    exchange_wait(n, me, tp, lambda peer: tot_ref, tot_land, tsend, trecv)
    off_out[...] = ordered_sum(n, off_land)
    tot_out[...] = ordered_sum(n, tot_land)


def pieces(width, step):
    return [(c, min(step, width - c)) for c in range(0, width, step)]


def pair_scatter(n, collective_id, keys, values, columns, own_rows):
    _, rows, width = keys.shape
    offs, tots = columns, jax.ShapeDtypeStruct((8, LANES), F32)
    chunks = len(pieces(width, 128))
    return pl.pallas_call(
        functools.partial(pair_scatter_kernel, n),
        out_shape=[
            jax.ShapeDtypeStruct((rows, width), F32),
            jax.ShapeDtypeStruct((rows, width), F32),
            jax.ShapeDtypeStruct(offs.shape[1:], F32),
            jax.ShapeDtypeStruct(tots.shape, F32),
        ],
        in_specs=[pl.BlockSpec(memory_space=VMEM)] * 4,
        out_specs=[pl.BlockSpec(memory_space=VMEM)] * 4,
        scratch_shapes=[
            VMEM((n - 1, rows, width), BF16),
            VMEM((n - 1, rows, width), BF16),
            VMEM((rows, width), BF16),
            VMEM((rows, width), BF16),
            VMEM(offs.shape, F32),
            VMEM(tots.shape, F32),
            VMEM(offs.shape, F32),
            VMEM((n,) + tots.shape, F32),
            pltpu.SemaphoreType.DMA((2, chunks, n - 1)),
            pltpu.SemaphoreType.DMA((2, chunks, n - 1)),
            pltpu.SemaphoreType.DMA((n - 1,)),
            pltpu.SemaphoreType.DMA((n - 1,)),
            pltpu.SemaphoreType.DMA((n - 1,)),
            pltpu.SemaphoreType.DMA((n - 1,)),
            pltpu.SemaphoreType.DMA((2,)),
        ],
        compiler_params=pltpu.CompilerParams(
            collective_id=collective_id, has_side_effects=True, vmem_limit_bytes=VMEM_LIMIT
        ),
    )(keys, values, columns, own_rows)


def weight_scatter_kernel(n, plan, left_count, grads, *refs):
    lefts, refs = refs[:left_count], refs[left_count:]
    rights, refs = refs[:grads], refs[grads:]
    small_ref, part_ref, x_ref, gain_ref, dmid_ref, refs = *refs[:5], refs[5:]
    outs, refs = refs[:grads], refs[grads:]
    small_out, input_out, slot_r, slot_l, first_r, first_l, own_small, land, sum_out, refs = *refs[:9], refs[9:]
    tp_bufs, refs = refs[:4], refs[4:]
    send, recv, xsend, xrecv, tsend, trecv, local = refs
    me, tp, place, sides = ring_setup(n)
    chip, core, sibling, across = tp_setup()
    greet(ctx_peers(me, tp, n) + [sibling, across])
    shard = lefts[0].shape[2]
    half = part_ref.shape[0] // 2

    def local_term(owner, tag):
        left, right, c0, cw = tag
        return contract_rows(lefts[left][owner], rights[right][:, c0 : c0 + cw])

    def write(tag, value):
        _, right, c0, cw = tag
        outs[right][:, c0 : c0 + cw] = value

    ring = ScatterRing(
        n, plan, local_term, (slot_r, slot_l), (first_r, first_l), write, send, recv, place, sides, tp
    )

    def part(which, c):
        cols = part_ref.shape[1] // TP_CHUNKS
        return part_ref[pl.ds(pl.multiple_of(which * half, half), half), c * cols : (c + 1) * cols].astype(F32)

    total = TpSum(part, sum_out, tp_bufs, tsend, trecv, core, sibling, across)
    total.first()
    total.second()
    ring.begin()
    total.third()
    ring.advance(1)
    total.fourth()

    own_small[...] = small_ref[...]
    cols = part_ref.shape[1]
    size = 64

    def gain_rows(i, acc):
        rows = pl.ds(pl.multiple_of(i * size, size), size)
        value = x_ref[rows, :].astype(F32)
        inverse = lax.rsqrt(jnp.mean(value * value, axis=-1, keepdims=True) + EPS)
        normal = value * inverse
        grad = sum_out[rows, :].astype(F32)
        back = grad * gain_ref[...]
        back = inverse * (back - normal * jnp.mean(back * normal, axis=-1, keepdims=True))
        input_out[rows, :] = dmid_ref[rows, :] + back
        return acc + jnp.sum((grad * normal).reshape(size // 8, 8, cols), axis=0)

    gains = lax.fori_loop(0, 2 * half // size, gain_rows, jnp.zeros((8, cols), F32))
    gains = jnp.sum(gains, axis=0, keepdims=True)
    for i in range(n):
        own_small[i, 0:1, :shard] = gains[:, i * shard : (i + 1) * shard]
    exchange_start(n, me, tp, lambda peer: own_small.at[peer], land, xsend, xrecv)
    mine = pltpu.make_async_copy(own_small.at[me], land.at[me], local.at[0])
    mine.start()
    ring.end()
    mine.wait()
    exchange_wait(n, me, tp, lambda peer: own_small.at[peer], land, xsend, xrecv)
    small_out[...] = ordered_sum(n, land)


def weight_scatter(n, collective_id, plan, lefts, rights, small, part, x, gain, dmid):
    rows = lefts[0].shape[2]
    chunks = max(len(plan[0]), len(plan[1]))
    totals = [sum(width for width, _ in side) for side in plan]
    return pl.pallas_call(
        functools.partial(weight_scatter_kernel, n, plan, len(lefts), len(rights)),
        out_shape=[jax.ShapeDtypeStruct((rows, right.shape[1]), F32) for right in rights]
        + [jax.ShapeDtypeStruct(small.shape[1:], F32), jax.ShapeDtypeStruct(part.shape, F32)],
        in_specs=[pl.BlockSpec(memory_space=VMEM)] * (len(lefts) + len(rights) + 5),
        out_specs=[pl.BlockSpec(memory_space=VMEM)] * (len(rights) + 2),
        scratch_shapes=[
            VMEM((n - 1, rows, totals[0]), BF16),
            VMEM((n - 1, rows, totals[1]), BF16),
            VMEM((rows, totals[0]), BF16),
            VMEM((rows, totals[1]), BF16),
            VMEM(small.shape, F32),
            VMEM(small.shape, F32),
            VMEM(part.shape, BF16),
            *tp_buffers(*part.shape),
            pltpu.SemaphoreType.DMA((2, chunks, n - 1)),
            pltpu.SemaphoreType.DMA((2, chunks, n - 1)),
            pltpu.SemaphoreType.DMA((n - 1,)),
            pltpu.SemaphoreType.DMA((n - 1,)),
            pltpu.SemaphoreType.DMA((3, TP_CHUNKS)),
            pltpu.SemaphoreType.DMA((3, TP_CHUNKS)),
            pltpu.SemaphoreType.DMA((1,)),
        ],
        compiler_params=pltpu.CompilerParams(
            collective_id=collective_id, has_side_effects=True, vmem_limit_bytes=VMEM_LIMIT
        ),
    )(*lefts, *rights, small, part, x, gain, dmid)


def tp_setup():
    ctx = lax.axis_index("ctx")
    tp = lax.axis_index("tp")
    chip = lax.div(tp, 2)
    core = lax.rem(tp, 2)
    sibling = (ctx, 2 * chip + 1 - core)
    across = (ctx, 2 * (1 - chip) + core)
    return chip, core, sibling, across


TP_CHUNKS = 4


def tp_buffers(rows, width):
    return [VMEM((rows // 2, width), BF16) for _ in range(4)]


class TpSum:
    def __init__(self, part, out, bufs, send, recv, core, sibling, across):
        self.part, self.out, self.send, self.recv = part, out, send, recv
        self.away, self.land_a, self.half_b, self.land_b = bufs
        self.core, self.sibling, self.across = core, sibling, across
        self.half = self.away.shape[0]
        self.size = self.away.shape[1] // TP_CHUNKS

    def cols(self, c):
        return pl.ds(c * self.size, self.size)

    def copy(self, stage, c, which=None):
        cols = self.cols(c)
        if stage == 0:
            source, target, device = self.away.at[:, cols], self.land_a.at[:, cols], self.sibling
        elif stage == 1:
            source, target, device = self.half_b.at[:, cols], self.land_b.at[:, cols], self.across
        else:
            source = target = self.out.at[self.rows(which), cols]
            device = self.sibling
        return remote(source, target, self.send.at[stage, c], self.recv.at[stage, c], device)

    def rows(self, which):
        return pl.ds(pl.multiple_of(which * self.half, self.half), self.half)

    def first(self):
        for c in range(TP_CHUNKS):
            self.away[:, self.cols(c)] = self.part(1 - self.core, c).astype(BF16)
            self.copy(0, c).start()

    def second(self):
        for c in range(TP_CHUNKS):
            cols = self.cols(c)
            mine = self.part(self.core, c)
            self.copy(0, c).wait_recv()
            self.half_b[:, cols] = (mine + self.land_a[:, cols].astype(F32)).astype(BF16)
            self.copy(1, c).start()

    def third(self):
        for c in range(TP_CHUNKS):
            cols = self.cols(c)
            self.copy(1, c).wait_recv()
            both = self.half_b[:, cols].astype(F32) + self.land_b[:, cols].astype(F32)
            self.out[self.rows(self.core), cols] = both.astype(BF16)
            self.copy(2, c, self.core).start()

    def fourth(self):
        for c in range(TP_CHUNKS):
            self.copy(2, c, 1 - self.core).wait_recv()
            self.copy(0, c).wait_send()
            self.copy(1, c).wait_send()
            self.copy(2, c, self.core).wait_send()


class TpSplit:
    def __init__(self, part, bufs, send, recv, chip, core, sibling, across):
        self.part, self.send, self.recv = part, send, recv
        self.away, self.land_a, self.half_b, self.land_b = bufs
        self.chip, self.core, self.sibling, self.across = chip, core, sibling, across

    def copy(self, stage):
        if stage < 2:
            return remote(
                self.away.at[stage], self.land_a.at[stage], self.send.at[stage], self.recv.at[stage], self.sibling
            )
        return remote(self.half_b, self.land_b, self.send.at[2], self.recv.at[2], self.across)

    def first(self):
        for i, chip in enumerate((1 - self.chip, self.chip)):
            self.away[i] = self.part(chip, 1 - self.core).astype(BF16)
            self.copy(i).start()

    def second(self):
        mine = self.part(1 - self.chip, self.core)
        self.copy(0).wait_recv()
        self.half_b[...] = (mine + self.land_a[0].astype(F32)).astype(BF16)
        self.copy(2).start()

    def mine(self):
        return self.part(self.chip, self.core)

    def third(self):
        self.copy(1).wait_recv()
        self.copy(2).wait_recv()
        total = self.land_a[1].astype(F32) + self.land_b[...].astype(F32)
        for stage in range(3):
            self.copy(stage).wait_send()
        return total


def feed_kernel(n, heads, attention, *refs):
    if attention:
        (group_map, doc_lengths, skip, q_in, term_in, k_in, v_in, aug_in), refs = refs[:8], refs[8:]
    (att_in, gl_in, outw_in, x_in, gain_ref, grad_in, wg_in, wu_in, wd_in), refs = refs[:9], refs[9:]
    (gated_out, layer_ref, down_out, gate_out, up_out, dmid_out, do_out, dgl_out, gain_out), refs = refs[:9], refs[9:]
    if attention:
        (dm_out, dq_out, drow_ref, dk_out, dv_out, dcol_ref), refs = refs[:6], refs[6:]
    (
        att_ref, gl_ref, outw_ref, x_ref, gated_ref, normed_ref, dgt_ref, dup_ref, do_ref, dgl_ref,
        gate_all, up_all, down_all, accs, dhid_acc, hid_ref, branch_ref, mid_ref, dw_ref, dy_ref,
        a0, a1, a2, a3, b3, s0, s1, s2, s3, dslot_r, dslot_l, dfirst_r, dfirst_l, eslot_r, eslot_l, efirst_r, efirst_l,
        gsend, grecv, hsend, hrecv, asend, arecv, bsend, brecv, ssend, srecv, dsend, drecv, esend, erecv, local,
    ), refs = refs[:52], refs[52:]
    if attention:
        term_ref, diff_ref, span_ref, stage, kv_sem, stage_sem = refs
    gate_acc, up_acc = accs.at[0], accs.at[1]
    me, tp, place, sides = ring_setup(n)
    chip, core, sibling, across = tp_setup()
    moves = Moves(local)
    for name, source, target in (
        ("att", att_in, att_ref), ("gl", gl_in, gl_ref), ("outw", outw_in, outw_ref), ("grad", grad_in, dw_ref),
        ("x", x_in, x_ref),
    ):
        moves.start(name, source, target)
    if attention:
        moves.start("term", term_in, term_ref)
    greet([(side, tp) for side in sides] + [sibling, across])
    shard, hidden = wg_in.shape
    rows, width = x_in.shape
    half = rows // 2
    hw = hidden // 2
    size = 64
    ring = (n, place, sides, tp)

    def rows_of(owner):
        return pl.ds(pl.multiple_of(owner * shard, 16), shard)

    def window(ref, c0, cw):
        return lambda owner: ref.at[rows_of(owner), pl.ds(c0, cw)]

    def chunks(members):
        return [(side, source.at[:, pl.ds(c0, cw)], window(target, c0, cw)) for side, source, target, c0, cw in members]

    gates = Gather(
        *ring,
        chunks(
            [
                (side, source, target, c0, hw)
                for c0 in (0, hw)
                for side, source, target in ((0, wg_in, gate_all), (1, wu_in, up_all))
            ]
        ),
        gsend, grecv,
    )
    downs = Gather(
        *ring,
        chunks([(side, wd_in, down_all, side * hw + c0, hw // 2) for c0 in (0, hw // 2) for side in (0, 1)]),
        hsend, hrecv,
    )
    gates.begin()
    for i, (source, target) in enumerate(((wg_in, gate_all), (wu_in, up_all), (wd_in, down_all))):
        moves.start(i, source, target.at[rows_of(me)])

    moves.wait("att", "gl")
    gated_ref[...] = (att_ref[...] * jax.nn.sigmoid(gl_ref[...])).astype(BF16)
    moves.start("gated", gated_ref, gated_out)
    moves.wait("outw")
    span = width // TP_CHUNKS

    def branch_part(which, c):
        mine = gated_ref[pl.ds(pl.multiple_of(which * half, half), half), :]
        return contract_cols(mine, outw_ref[c * span : (c + 1) * span, :])

    branch = TpSum(branch_part, branch_ref, (a0, a1, a2, a3), asend, arecv, core, sibling, across)
    branch.first()
    branch.second()
    gates.forward(1)
    moves.wait("grad")
    for c in range(TP_CHUNKS):
        back = pl.ds(c * span, span)
        dy_ref[back, :] = dw_ref[:, back].astype(F32).T.astype(BF16)
    dhid_acc[...] = jnp.zeros_like(dhid_acc)
    gate_acc[...] = jnp.zeros_like(gate_acc)
    up_acc[...] = jnp.zeros_like(up_acc)

    def grow_back(back):
        for side in (0, 1):
            owner = downs.owner(side, back)
            cols = pl.ds(side * hw, hw)
            dhid_acc[:, cols] += contract_rows(dy_ref[rows_of(owner), :], down_all[rows_of(owner), cols])

    def grow(back):
        for side, acc, source in ((0, gate_acc, gate_all), (1, up_acc, up_all)):
            owner = gates.owner(side, back)
            acc[...] += contract_rows(normed_ref[rows_of(owner), :], source[rows_of(owner), :])

    moves.wait(0, 1, 2)
    grow_back(0)
    gates.forward(2)
    branch.third()
    branch.fourth()
    moves.wait("x")

    def norm_rows(i, carry):
        here = pl.ds(pl.multiple_of(i * LANES, LANES), LANES)
        middle = x_ref[here, :].astype(F32) + branch_ref[here, :].astype(F32)
        mid_ref[here, :] = middle
        normed_ref[:, here] = (rms_scale(middle) * gain_ref[...]).T.astype(BF16)
        return carry

    lax.fori_loop(0, rows // LANES, norm_rows, 0)
    own = pl.ds(pl.multiple_of(tp * span, span), span)
    layer_ref[...] = mid_ref[:, own]
    moves.start("again", grad_in, x_ref)
    if attention:
        moves.wait("gated")
        moves.start("q", q_in, gated_ref)
    gates.forward(3)

    def grow_step(step, carry):
        grow(step)
        return carry

    lax.fori_loop(0, 4, grow_step, 0)

    def gate_step(step, carry):
        gates.forward(step)
        grow(step)
        return carry

    lax.fori_loop(4, n - 1, gate_step, 0)
    downs.begin()
    gates.last()
    grow(n - 1)

    def hid_rows(i, carry):
        here = pl.ds(pl.multiple_of(i * size, size), size)
        gate, up = gate_acc[here, :], up_acc[here, :]
        open_gate = jax.nn.sigmoid(gate)
        silu = gate * open_gate
        hid_ref[here, :] = (silu * up).astype(BF16)
        gate_acc[here, :] = up * open_gate * (1.0 + gate * (1.0 - open_gate))
        up_acc[here, :] = silu
        return carry

    lax.fori_loop(0, rows // size, hid_rows, 0)

    def down_step(step, carry):
        downs.forward(step)
        grow_back(step)
        return carry

    lax.fori_loop(1, n - 2, down_step, 0)
    downs.forward(n - 2)

    def down_term(owner, tag):
        return dot(dy_ref[rows_of(owner), :], hid_ref[:, tag * hw : (tag + 1) * hw])

    down_ref = accs.at[0, pl.ds(0, shard), :]
    gate_ref = accs.at[0, pl.ds(shard, shard), :]
    up_ref = accs.at[1, pl.ds(0, shard), :]

    def down_write(tag, value):
        down_ref[:, tag * hw : (tag + 1) * hw] = value

    def early_term(owner, tag):
        which, c0 = tag
        return dot(normed_ref[rows_of(owner), :], (dgt_ref, dup_ref)[which][:, c0 : c0 + hw])

    def early_write(tag, value):
        which, c0 = tag
        (gate_ref, up_ref)[which][:, c0 : c0 + hw] = value

    backs = ScatterRing(
        n, [[(hw, 0)], [(hw, 1)]], down_term, (dslot_r, dslot_l), (dfirst_r, dfirst_l), down_write,
        dsend, drecv, place, sides, tp,
    )
    earlies = [
        ScatterRing(
            n, [[(hw, (i, part * hw))] for i in range(2)], early_term, (eslot_r.at[part], eslot_l.at[part]),
            (efirst_r.at[part], efirst_l.at[part]), early_write, esend.at[part], erecv.at[part], place, sides, tp,
        )
        for part in range(2)
    ]
    backs.begin()
    grow_back(n - 2)
    downs.last()
    grow_back(n - 1)

    def grad_rows(i, carry):
        here = pl.ds(pl.multiple_of(i * size, size), size)
        dhid = dhid_acc[here, :]
        dgt_ref[here, :] = (dhid * gate_acc[here, :]).astype(BF16)
        dup_ref[here, :] = (dhid * up_acc[here, :]).astype(BF16)
        return carry

    lax.fori_loop(0, rows // size, grad_rows, 0)

    def dw_part(which, c):
        mine = pl.ds(pl.multiple_of(which * half, half), half)
        back = pl.ds(c * span, span)
        return contract_cols(dgt_ref[mine, :], gate_all[back, :]) + contract_cols(dup_ref[mine, :], up_all[back, :])

    def layer_part(which_chip, which_core):
        back = pl.ds(pl.multiple_of((2 * which_chip + which_core) * span, span), span)
        return contract_cols(hid_ref[...], down_all[back, :])

    total = TpSum(dw_part, dw_ref, (a0, a1, a2, b3), bsend, brecv, core, sibling, across)
    layer = TpSplit(layer_part, (s0, s1, s2, s3), ssend, srecv, chip, core, sibling, across)
    total.first()
    backs.advance(1)
    earlies[0].begin()
    earlies[1].begin()
    total.second()
    gates.sent()
    if attention:
        pairs = heads // 2

        def kv_copies(it):
            part, pair = lax.div(it, pairs), lax.rem(it, pairs)
            source = pl.ds(pl.multiple_of(part * rows, rows), rows)
            target = pl.ds(pl.multiple_of(pair * rows, rows), rows)
            lanes = pl.ds(pl.multiple_of(part * LANES, LANES), LANES)
            return [
                pltpu.make_async_copy(ref.at[pair, source, :], held.at[target, lanes], kv_sem.at[i, it])
                for i, (ref, held) in enumerate(((k_in, gate_all), (v_in, up_all)))
            ]

        def bring(it, carry):
            for copy in kv_copies(it):
                copy.start()
            return carry

        lax.fori_loop(0, n * pairs, bring, 0)
    layer.first()
    layer.second()
    layer_ref[...] += layer.mine()

    def serve_all():
        backs.advance(1)
        earlies[0].advance(1)
        earlies[1].advance(1)

    serve_all()
    if attention:
        downs.sent()
        moves.wait("q", "term")
        first, second = group_map[2 * me], group_map[2 * me + 1]
        in_order = first < second
        query_groups = (jnp.minimum(first, second), jnp.maximum(first, second))

        def put_query(h, value, extra):
            here, lane = pl.ds(h // 4 * rows, rows), h % 4 * 2 * LANES
            down_all[here, lane : lane + LANES] = value
            down_all[here, lane + LANES : lane + 2 * LANES] = extra

        spread_heads(gated_ref, row_pieces(term_ref[...], True), put_query, heads, in_order)
        accs[...] = jnp.zeros_like(accs)
        query_at = lax.broadcasted_iota(jnp.int32, (half, half), 1)
        key_at = lax.broadcasted_iota(jnp.int32, (half, half), 0)
        diff_ref[...] = key_at - query_at
        for i, group in enumerate(query_groups):
            span_ref[i] = document_start(group * half + query_at, doc_lengths) - key_at
    serve_all()
    total.third()
    total.fourth()

    def middle_rows(i, acc):
        here = pl.ds(pl.multiple_of(i * size, size), size)
        middle = mid_ref[here, :]
        inverse = lax.rsqrt(jnp.mean(middle * middle, axis=-1, keepdims=True) + EPS)
        normal = middle * inverse
        dw = dw_ref[here, :].astype(F32)
        back = dw * gain_ref[...]
        back = inverse * (back - normal * jnp.mean(back * normal, axis=-1, keepdims=True))
        dmid = x_ref[here, :].astype(F32) + back
        mid_ref[here, :] = dmid
        branch_ref[here, :] = dmid.astype(BF16)
        return acc + jnp.sum((dw * normal).reshape(size // 8, 8, width), axis=0)

    moves.wait("again")
    gain_out[...] = lax.fori_loop(0, rows // size, middle_rows, jnp.zeros((8, width), F32))
    if attention:
        for i in range(n):
            moves.start(
                ("aug", i), aug_in.at[pl.ds(i * rows, rows), :], x_ref.at[:, pl.ds(i * LANES, LANES)]
            )
    moves.start("dmid", mid_ref, dmid_out)
    if attention:
        moves.start("dm", branch_ref, dm_out)
    da = dot(branch_ref[...], outw_ref[...])
    open_gate = jax.nn.sigmoid(gl_ref[...])
    do_ref[...] = (da * open_gate).astype(BF16)
    dgl_ref[...] = (da * att_ref[...] * open_gate * (1.0 - open_gate)).astype(BF16)
    moves.start("do", do_ref, do_out)
    moves.start("dgl", dgl_ref, dgl_out)
    serve_all()
    layer_ref[...] += layer.third()

    if attention:
        def put_grad(h, value, extra):
            branch_ref[:, 2 * h * LANES : (2 * h + 1) * LANES] = value
            branch_ref[:, (2 * h + 1) * LANES : (2 * h + 2) * LANES] = extra

        delta = head_sums(do_ref[...].astype(F32) * att_ref[...], heads)
        moves.wait("dm", *[("aug", i) for i in range(n)])
        spread_heads(do_ref, row_pieces(-delta, False), put_grad, heads, in_order)
        dcol_acc = dhid_acc.at[:, pl.ds(0, LANES)]

        def stage_copies(it):
            part, pair = lax.div(it, pairs), lax.rem(it, pairs)
            lanes = pl.ds(pl.multiple_of(pair * LANES, LANES), LANES)
            slot = lax.rem(it, 2)
            return [
                pltpu.make_async_copy(stage.at[slot, i], out.at[part, :, lanes], stage_sem.at[slot, i])
                for i, out in enumerate((dk_out, dv_out))
            ]

        def attend(it, carry):
            part, pair = lax.div(it, pairs), lax.rem(it, pairs)
            for copy in kv_copies(it):
                copy.wait()
            one, two = group_map[2 * part], group_map[2 * part + 1]
            forward = one < two
            key_groups = (jnp.minimum(one, two), jnp.maximum(one, two))
            lanes = pl.ds(pl.multiple_of(part * LANES, LANES), LANES)

            def ordered(ref, base, where):
                top = pl.ds(pl.multiple_of(base * rows, rows), half)
                bottom = pl.ds(pl.multiple_of(base * rows + half, half), half)
                return in_pack_order(forward, ref[top, where], ref[bottom, where])

            key_blocks = ordered(gate_all, pair, lanes)
            value_blocks = ordered(up_all, pair, lanes)
            aug_blocks = ordered(x_ref, 0, lanes)
            masks = block_masks(diff_ref, span_ref, skip, query_groups, key_groups, half)
            keys = [jnp.concatenate([key_blocks[ki], aug_blocks[ki]], axis=1) for ki in range(2)]
            values = [jnp.concatenate([value_blocks[ki], aug_blocks[ki]], axis=1) for ki in range(2)]
            both_keys = jnp.concatenate(keys, axis=0)
            queries, douts, probs, grads = [], [], ([], []), ([], [])
            for e in range(2):
                h = 2 * pair + e
                spot = pl.ds(pl.multiple_of(h * 2 * LANES, 2 * LANES), 2 * LANES)
                quarter = pl.ds(pl.multiple_of(lax.rem(h, 4) * 2 * LANES, 2 * LANES), 2 * LANES)
                query_rows = pl.ds(pl.multiple_of(lax.div(h, 4) * rows, rows), rows)
                query, dout = down_all[query_rows, quarter], branch_ref[:, spot]
                early = contract_cols(keys[0], query)
                scores = (early[:, :half], early[:, half:], contract_cols(keys[1], query[half:]))
                early = contract_cols(values[0], dout)
                backs_out = (early[:, :half], early[:, half:], contract_cols(values[1], dout[half:]))
                prob = [jnp.where(mask, jnp.exp(score), 0.0) for mask, score in zip(masks, scores)]
                grad = [(p * back).astype(BF16) for p, back in zip(prob, backs_out)]
                prob = [p.astype(BF16) for p in prob]
                queries.append(query)
                douts.append(dout[:, :LANES])
                probs[0].extend(prob[:2])
                probs[1].append(prob[2])
                grads[0].extend(grad[:2])
                grads[1].append(grad[2])
                accs[lax.div(h, 4), :half, quarter] += contract_rows(grad[0], keys[0])
                accs[lax.div(h, 4), half:, quarter] += contract_rows(jnp.concatenate(grad[1:], axis=0), both_keys)
            late_queries = jnp.concatenate([query[half:] for query in queries], axis=0)
            late_douts = jnp.concatenate([dout[half:] for dout in douts], axis=0)
            queries, douts = jnp.concatenate(queries, axis=0), jnp.concatenate(douts, axis=0)
            sums = [
                dot(jnp.concatenate(grads[0], axis=1), queries),
                dot(jnp.concatenate(grads[1], axis=1), late_queries),
            ]
            value_sums = [
                dot(jnp.concatenate(probs[0], axis=1), douts),
                dot(jnp.concatenate(probs[1], axis=1), late_douts),
            ]
            columns = jnp.concatenate([part_sum[:, LANES:] for part_sum in sums], axis=0)
            dcol_acc[...] = jnp.where(pair == 0, 0.0, dcol_acc[...]) + columns

            @pl.when(it >= 2)
            def _():
                for copy in stage_copies(it - 2):
                    copy.wait()

            slot = lax.rem(it, 2)
            for i, part_sums in enumerate(([part_sum[:, :LANES] for part_sum in sums], value_sums)):
                stage[slot, i] = jnp.concatenate(in_pack_order(forward, *part_sums), axis=0).astype(BF16)
            for copy in stage_copies(it):
                copy.start()

            @pl.when(pair == pairs - 1)
            def _():
                columns = jnp.concatenate(
                    in_pack_order(forward, dcol_acc[pl.ds(0, half), :], dcol_acc[pl.ds(half, half), :]), axis=0
                )
                dcol_ref[part] = -(columns.T[:8])

            return carry

        turns = (*earlies, backs)
        starts = [ring.next for ring in turns]
        services = sum(n - 1 - start for start in starts)
        assert starts[0] == starts[1] == starts[2] - 1
        share = 2 * n * pairs // (3 * services)

        def serve(k, carry):
            lax.fori_loop(k * share, (k + 1) * share, attend, 0)
            for i, ring in enumerate(turns):

                @pl.when(lax.rem(k, 3) == i)
                def _(i=i, ring=ring):
                    ring.forward(starts[i] + lax.div(k, 3))

            return carry

        lax.fori_loop(0, services, serve, 0)
        for ring in turns:
            ring.next = n - 1
        if services * share < n * pairs:
            lax.fori_loop(services * share, n * pairs, attend, 0)
        for it in (n * pairs - 2, n * pairs - 1):
            for copy in stage_copies(it):
                copy.wait()

        lane = lax.broadcasted_iota(jnp.int32, (rows, LANES), 1)
        low = low_lanes(rows)
        sums = jnp.zeros((rows, LANES), F32)
        for pair in range(pairs):
            parts = []
            for h in (2 * pair, 2 * pair + 1):
                spot = pl.ds((h % 4) * 2 * LANES, 2 * LANES)
                value = jnp.concatenate(
                    in_pack_order(in_order, accs[h // 4, :half, spot], accs[h // 4, half:, spot]), axis=0
                )
                parts.append(value)
                sums = jnp.where(lane == 24 + h, value[:, LANES:], sums)
            dhid_acc[:, (3 + pair) * LANES : (4 + pair) * LANES] = jnp.where(
                low, parts[0][:, :LANES], parts[1][:, :LANES]
            )
        moves.start("dq", dhid_acc.at[:, pl.ds(3 * LANES, pairs * LANES)], dq_out)
        drow_ref[...] = pltpu.roll(sums, LANES - 24, 1).T[:8]

        moves.wait("dq")
    backs.end()
    moves.start("down", down_ref, down_out)
    earlies[0].end()
    earlies[1].end()
    moves.start("gate", gate_ref, gate_out)
    moves.start("up", up_ref, up_out)
    if not attention:
        downs.sent()
    moves.wait()


def feed_forward(
    n, collective_id, heads, attended, gate_logit, out_weight, x, gain, dy, w_gate, w_up, w_down, attention=None
):
    rows, width = x.shape
    shard, hidden = w_gate.shape
    heads_width = attended.shape[1]
    own = width // 4
    half = rows // 2
    dma = pltpu.SemaphoreType.DMA
    vmem = pl.BlockSpec(memory_space=VMEM)
    anywhere = pl.BlockSpec(memory_space=pl.ANY)
    wide, narrow, deep = (rows, width), (rows, heads_width), (rows, hidden)
    turned = (n * shard, rows)
    weight = (shard, hidden)
    shapes = [
        (narrow, BF16),
        ((rows, own), F32),
        (weight, F32),
        (weight, F32),
        (weight, F32),
        (wide, F32),
        (narrow, BF16),
        (narrow, BF16),
        ((8, width), F32),
    ]
    kept = [1, 8]
    extra_specs, extra_scratch = [], []
    if attention is not None:
        assert heads // 2 * rows == n * shard and n * LANES == hidden and 2 * rows <= n * shard
        shapes += [
            (wide, BF16),
            (narrow, F32),
            ((8, rows), F32),
            ((n, rows, heads_width), BF16),
            ((n, rows, heads_width), BF16),
            ((n, 8, rows), F32),
        ]
        kept += [11, 14]
        extra_specs = [smem()] * 3 + [anywhere] * 5
        extra_scratch = [
            VMEM((rows, LANES), F32),
            VMEM((half, half), jnp.int32),
            VMEM((2, half, half), jnp.int32),
            VMEM((2, 2, rows, LANES), BF16),
            dma((2, n * heads // 2)),
            dma((2, 2)),
        ]
    return pl.pallas_call(
        functools.partial(feed_kernel, n, heads, attention is not None),
        out_shape=[jax.ShapeDtypeStruct(*shape) for shape in shapes],
        in_specs=extra_specs + [anywhere] * 4 + [vmem] + [anywhere] * 4,
        out_specs=[vmem if i in kept else anywhere for i in range(len(shapes))],
        scratch_shapes=[
            VMEM(narrow, F32),
            VMEM(narrow, F32),
            VMEM(out_weight.shape, BF16),
            VMEM(wide, BF16),
            VMEM(narrow, BF16),
            VMEM(turned, BF16),
            VMEM(deep, BF16),
            VMEM(deep, BF16),
            VMEM(narrow, BF16),
            VMEM(narrow, BF16),
            *[VMEM((n * shard, hidden), BF16)] * 3,
            VMEM((2,) + deep, F32),
            VMEM(deep, F32),
            VMEM(deep, BF16),
            VMEM(wide, BF16),
            VMEM(wide, F32),
            VMEM(wide, BF16),
            VMEM(turned, BF16),
            *tp_buffers(rows, width),
            VMEM((rows // 2, width), BF16),
            VMEM((2, rows, own), BF16),
            VMEM((2, rows, own), BF16),
            VMEM((rows, own), BF16),
            VMEM((rows, own), BF16),
            *ring_scratch(n, shard, [hidden // 2] * 2),
            *[VMEM((2, n - 1, shard, hidden // 2), BF16)] * 2,
            *[VMEM((2, shard, hidden // 2), BF16)] * 2,
            *[dma((4, n - 1))] * 4,
            *[dma((3, TP_CHUNKS))] * 4,
            *[dma((3,))] * 2,
            *[dma((2, 1, n - 1))] * 2,
            *[dma((2, 2, 1, n - 1))] * 2,
            dma((28,)),
            *extra_scratch,
        ],
        compiler_params=pltpu.CompilerParams(
            collective_id=collective_id, has_side_effects=True, vmem_limit_bytes=VMEM_LIMIT
        ),
    )(*(attention or ()), attended, gate_logit, out_weight, x, gain, dy, w_gate, w_up, w_down)


def ring_scratch(n, height, widths):
    return [VMEM((n - 1, height, w), BF16) for w in widths] + [VMEM((height, w), BF16) for w in widths]


def head_means(value, heads):
    width = value.shape[1]
    size = width // heads
    left = lax.div(lax.broadcasted_iota(jnp.int32, (width, width), 0), size)
    right = lax.div(lax.broadcasted_iota(jnp.int32, (width, width), 1), size)
    member = (left == right).astype(BF16)
    high = value.astype(BF16)
    return (dot(high, member) + dot((value - high.astype(F32)).astype(BF16), member)) * (1.0 / size)


STAGED = (0, 1, 4, 5, 16, 11, 14, 17, 18, 19, 6, 12, 13, 20)


def finish_kernel(n, heads, gate_plan, attn_plan, *refs):
    operands, refs = list(refs[:24]), refs[24:]
    (q_out, k_out, v_out, g_out, o_out, small_out, input_out), refs = refs[:7], refs[7:]
    staged, refs = refs[: len(STAGED)], refs[len(STAGED) :]
    (
        dmt_ref, pslot_r, pslot_l, gslot_r, gslot_l, gfirst_r, gfirst_l, aslot_r, aslot_l, afirst_r, afirst_l,
        dk_sum, dv_sum, dqr_ref, dkr_ref, dvl_ref, du_ref, sum_ref, t0, t1, t2, t3,
        off_ref, tot_ref, off_land, tot_land, small_ref, small_land,
        psend, precv, gsend, grecv, asend, arecv, osend, orecv, qsend, qrecv, xsend, xrecv, tsend, trecv, local,
    ) = refs
    moves = Moves(local)
    dk_hbm, dv_hbm = operands[:2]
    for target, index in zip(staged, STAGED):
        moves.start(index, operands[index], target)
        operands[index] = target
    (
        dk_ref, dv_ref, col_ref, row_ref, dq_ref, qr_ref, kr_ref, qgain_ref, kgain_ref, fz_ref, group_map,
        wq_ref, wk_ref, wv_ref, wg_ref, wf_ref, dgl_ref, u_ref, dm_ref, gated_ref,
        x_ref, gain_ref, dmid_ref, gain_two_ref,
    ) = operands
    me, tp, place, sides = ring_setup(n)
    chip, core, sibling, across = tp_setup()
    rows, width = dq_ref.shape
    cols = x_ref.shape[1]
    shard = u_ref.shape[0] // n
    half = rows // 2
    head_dim = width // heads

    def rows_of(owner):
        return pl.ds(pl.multiple_of(owner * shard, 16), shard)

    small_ref[...] = jnp.zeros_like(small_ref)
    greet(ctx_peers(me, tp, n) + [sibling, across])

    def pair_term(owner, tag):
        which, c0 = tag
        return (dk_ref, dv_ref)[which][owner, :, c0 : c0 + LANES].astype(F32)

    def pair_write(tag, value):
        which, c0 = tag
        (dk_sum, dv_sum)[which][:, c0 : c0 + LANES] = value

    pairs = ScatterRing(
        n, [[(w, (i, c)) for c, w in pieces(width, LANES)] for i in range(2)], pair_term,
        (pslot_r, pslot_l), None, pair_write, psend, precv, place, sides, tp,
        source=lambda target, side, window: (dk_hbm, dv_hbm)[side].at[target, :, window],
    )
    pairs.begin()
    off_ref[...] = col_ref[...]
    off_ref[me] += row_ref[...]
    tot_ref[...] = jnp.zeros_like(tot_ref)
    for i in range(n):
        for g in range(2):
            tot_ref[:, 2 * i + g : 2 * i + g + 1] = jnp.sum(
                off_ref[i, :, g * half : (g + 1) * half], axis=1, keepdims=True
            )
    exchange_start(n, me, tp, lambda peer: off_ref.at[peer], off_land, osend, orecv)
    exchange_start(n, me, tp, lambda peer: tot_ref, tot_land, qsend, qrecv)
    moves.start("off", off_ref.at[me], off_land.at[me])
    moves.start("tot", tot_ref, tot_land.at[me])

    def raw_grad(grad, raw, gain):
        inverse = lax.rsqrt(head_means(raw * raw, heads) + EPS)
        normal = raw * inverse
        back = grad * gain
        back = inverse * (back - normal * head_means(back * normal, heads))
        return back.astype(BF16), jnp.sum(grad * normal, axis=0, keepdims=True)

    def gain_rows(row, first):
        count = 2 * head_dim // n
        for i in range(n // 2):
            for h in range(heads):
                lane = h * head_dim + i * count
                small_ref[first + i, 2 + h : 3 + h, 0:count] = row[:, lane : lane + count]

    moves.wait(0, 1, 4, 5)
    pairs.advance(1)
    dqr, row = raw_grad(dq_ref[...], qr_ref[...], qgain_ref[...] * 0.125)
    dqr_ref[...] = dqr
    gain_rows(row * 0.125, 0)
    pairs.advance(1)
    moves.wait(16, 11, 14)
    span = cols // TP_CHUNKS
    for c in range(TP_CHUNKS):
        back = pl.ds(c * span, span)
        du_ref[:, back] = contract_cols(dqr_ref[...], wq_ref[back, :]) + contract_cols(dgl_ref[...], wg_ref[back, :])
    moves.wait(18)
    for c in range(TP_CHUNKS):
        back = pl.ds(c * span, span)
        dmt_ref[back, :] = dm_ref[:, back].astype(F32).T.astype(BF16)
    pairs.advance(n)
    moves.wait(17, 19)

    def gate_term(owner, tag):
        right, c0, cw = tag
        left = dmt_ref if right == 2 else u_ref
        return dot(left[rows_of(owner), :], (dqr_ref, dgl_ref, gated_ref)[right][:, c0 : c0 + cw])

    def gate_write(tag, value):
        right, c0, cw = tag
        (q_out, g_out, o_out)[right][:, c0 : c0 + cw] = value

    gates = ScatterRing(
        n, gate_plan, gate_term, (gslot_r, gslot_l), (gfirst_r, gfirst_l), gate_write, gsend, grecv, place, sides, tp,
    )
    gates.begin()
    pairs.end()

    moves.wait(6)
    dkr, row = raw_grad(dk_sum[...], kr_ref[...], kgain_ref[...])
    dkr_ref[...] = dkr
    gain_rows(row, n // 2)
    dvl_ref[...] = dv_sum[...].astype(BF16)

    def attn_term(owner, tag):
        c0, cw = tag[1], tag[2]
        return dot(u_ref[rows_of(owner), :], (dkr_ref, dvl_ref)[tag[0]][:, c0 : c0 + cw])

    def attn_write(tag, value):
        c0, cw = tag[1], tag[2]
        (k_out, v_out)[tag[0]][:, c0 : c0 + cw] = value

    attns = ScatterRing(
        n, attn_plan, attn_term, (aslot_r, aslot_l), (afirst_r, afirst_l), attn_write, asend, arecv, place, sides, tp,
    )
    attns.begin()
    gates.advance(1)
    moves.wait("off", "tot")
    exchange_wait(n, me, tp, lambda peer: off_ref.at[peer], off_land, osend, orecv)
    exchange_wait(n, me, tp, lambda peer: tot_ref, tot_land, qsend, qrecv)
    off_sum = ordered_sum(n, off_land)
    tot_sum = ordered_sum(n, tot_land)
    onward = (
        lax.broadcasted_iota(jnp.int32, (half, half), 0) >= lax.broadcasted_iota(jnp.int32, (half, half), 1)
    ).astype(F32)
    parts = []
    for g in range(2):
        suffix = jnp.dot(
            off_sum[:, g * half : (g + 1) * half], onward, precision=HIGHEST, preferred_element_type=F32
        )
        later = groups_along(group_map, 1, -1, (8, LANES)) > group_map[2 * me + g]
        parts.append(suffix + jnp.sum(jnp.where(later, tot_sum, 0.0), axis=1, keepdims=True))
    dfz = (jnp.concatenate(parts, axis=1) * jax.nn.sigmoid(-fz_ref[...])).astype(BF16).astype(F32)
    head = lax.broadcasted_iota(jnp.int32, dfz.shape, 0)
    dfz = jnp.where(head < heads, dfz, 0.0)
    bias = jnp.sum(dfz, axis=1, keepdims=True)
    dfz_cols = turn(dfz).astype(BF16)
    dfz_low = dfz.astype(BF16)
    for i in range(n):
        small_ref[i, 8:16, :shard] = contract_cols(dfz_low, u_ref[i * shard : (i + 1) * shard, :])
        small_ref[i, 8:16, 224:225] = bias
        small_ref[i, 1:2, :shard] = jnp.sum(gain_two_ref[:, i * shard : (i + 1) * shard], axis=0, keepdims=True)

    moves.wait(12, 13)
    forget = jnp.concatenate([wf_ref[...], jnp.zeros((LANES - 8, cols), F32)], axis=0).astype(BF16)
    for c in range(TP_CHUNKS):
        back = pl.ds(c * span, span)
        du_ref[:, back] += (
            contract_cols(dkr_ref[...], wk_ref[back, :])
            + contract_cols(dvl_ref[...], wv_ref[back, :])
            + dot(dfz_cols, forget[:, c * span : (c + 1) * span])
        )

    def part(which, c):
        return du_ref[pl.ds(pl.multiple_of(which * half, half), half), c * span : (c + 1) * span]

    total = TpSum(part, sum_ref, (t0, t1, t2, t3), tsend, trecv, core, sibling, across)
    total.first()
    attns.advance(1)
    total.second()
    moves.start("dmid", dmid_ref, du_ref)
    for _ in range(3):
        gates.advance(1)
        attns.advance(1)
    total.third()
    gates.advance(1)
    attns.advance(1)
    total.fourth()
    moves.wait("dmid", 20)
    size = 64

    def input_rows(i, acc):
        here = pl.ds(pl.multiple_of(i * size, size), size)
        value = x_ref[here, :].astype(F32)
        inverse = lax.rsqrt(jnp.mean(value * value, axis=-1, keepdims=True) + EPS)
        normal = value * inverse
        grad = sum_ref[here, :].astype(F32)
        back = grad * gain_ref[...]
        back = inverse * (back - normal * jnp.mean(back * normal, axis=-1, keepdims=True))
        du_ref[here, :] += back
        return acc + jnp.sum((grad * normal).reshape(size // 8, 8, cols), axis=0)

    gains = lax.fori_loop(0, rows // size, input_rows, jnp.zeros((8, cols), F32))
    moves.start("input", du_ref, input_out)
    for i in range(n):
        small_ref[i, 0:1, :shard] = jnp.sum(gains[:, i * shard : (i + 1) * shard], axis=0, keepdims=True)
    exchange_start(n, me, tp, lambda peer: small_ref.at[peer], small_land, xsend, xrecv)
    moves.start("small", small_ref.at[me], small_land.at[me])
    while gates.next < n - 1:
        gates.advance(1)
        attns.advance(1)
    gates.end()
    attns.end()
    moves.wait("small")
    exchange_wait(n, me, tp, lambda peer: small_ref.at[peer], small_land, xsend, xrecv)
    small_out[...] = ordered_sum(n, small_land)
    pairs.sent()
    moves.wait()


def finish_backward(n, collective_id, heads, gate_plan, attn_plan, *operands):
    dq, u, x = operands[4], operands[17], operands[20]
    rows, width = dq.shape
    cols = x.shape[1]
    shard = u.shape[0] // n
    dma = pltpu.SemaphoreType.DMA
    vmem = pl.BlockSpec(memory_space=VMEM)
    anywhere = pl.BlockSpec(memory_space=pl.ANY)
    outside = STAGED + (22,)
    gate_widths = [sum(w for w, _ in side) for side in gate_plan]
    attn_widths = [sum(w for w, _ in side) for side in attn_plan]

    def ring_semaphores(plan):
        return [dma((2, max(len(side) for side in plan), n - 1))] * 2

    shapes = [(shard, width)] * 5 + [(16, 256), (rows, cols)]
    return pl.pallas_call(
        functools.partial(finish_kernel, n, heads, gate_plan, attn_plan),
        out_shape=[jax.ShapeDtypeStruct(shape, F32) for shape in shapes],
        in_specs=[anywhere if i in outside else smem() if i == 10 else vmem for i in range(len(operands))],
        out_specs=[vmem] * 6 + [anywhere],
        scratch_shapes=[
            *[VMEM(operands[i].shape, operands[i].dtype) for i in STAGED],
            VMEM(u.shape, BF16),
            *[VMEM((n - 1, rows, width), BF16)] * 2,
            *ring_scratch(n, shard, gate_widths),
            *ring_scratch(n, shard, attn_widths),
            VMEM((rows, width), F32),
            VMEM((rows, width), F32),
            *[VMEM((rows, width), BF16)] * 3,
            VMEM((rows, cols), F32),
            VMEM((rows, cols), BF16),
            *tp_buffers(rows, cols),
            VMEM((n, 8, rows), F32),
            VMEM((8, LANES), F32),
            VMEM((n, 8, rows), F32),
            VMEM((n, 8, LANES), F32),
            VMEM((n, 16, 256), F32),
            VMEM((n, 16, 256), F32),
            *[dma((2, len(pieces(width, LANES)), n - 1))] * 2,
            *ring_semaphores(gate_plan),
            *ring_semaphores(attn_plan),
            *[dma((n - 1,))] * 6,
            *[dma((3, TP_CHUNKS))] * 2,
            dma((len(STAGED) + 5,)),
        ],
        compiler_params=pltpu.CompilerParams(
            collective_id=collective_id, has_side_effects=True, vmem_limit_bytes=VMEM_LIMIT
        ),
    )(*operands)


LANES = 128


def block_state(group_map, doc_lengths, skip, query_group, key_group, rows, docs):
    first_q = query_group * rows
    last_q = first_q + rows - 1
    first_k = key_group * rows
    last_k = first_k + rows - 1
    zero = jnp.int32(0)
    doc_qf, doc_ql, doc_kf, doc_kl, end = zero, zero, zero, zero, zero
    for d in range(docs):
        end = end + doc_lengths[d]
        doc_qf += (first_q >= end).astype(jnp.int32)
        doc_ql += (last_q >= end).astype(jnp.int32)
        doc_kf += (first_k >= end).astype(jnp.int32)
        doc_kl += (last_k >= end).astype(jnp.int32)
    earlier = key_group < query_group
    same = key_group == query_group
    kept = skip[query_group, key_group] != 1
    active = jnp.logical_or(same, earlier & kept & (doc_kl == doc_qf))
    full = earlier & (doc_kf == doc_ql)
    return active, full


def block_mask(doc_lengths, query_group, key_group, rows, docs, query_dim):
    shape = (rows, rows)
    pos_q = query_group * rows + lax.broadcasted_iota(jnp.int32, shape, query_dim)
    pos_k = key_group * rows + lax.broadcasted_iota(jnp.int32, shape, 1 - query_dim)
    start = jnp.zeros(shape, jnp.int32)
    end = jnp.int32(0)
    for d in range(docs):
        end = end + doc_lengths[d]
        start = jnp.where(pos_q >= end, end, start)
    return (pos_k <= pos_q) & (pos_k >= start)


def document_start(position, doc_lengths):
    start, end = jnp.zeros_like(position), jnp.int32(0)
    for d in range(doc_lengths.shape[0]):
        end = end + doc_lengths[d]
        start = jnp.where(position >= end, end, start)
    return start


def block_masks(diff_ref, span_ref, skip, query_groups, key_groups, rows):
    masks = []
    for qi, ki in ((0, 0), (1, 0), (1, 1)):
        query_group, key_group = query_groups[qi], key_groups[ki]
        skipped = jnp.where(key_group < query_group, skip[query_group, key_group], 0)
        reach = key_group * rows - (skipped == 1).astype(jnp.int32) * (1 << 30)
        mask = span_ref[qi] <= reach
        if qi == ki:
            mask = mask & (diff_ref[...] <= (query_group - key_group) * rows)
        masks.append(mask)
    return masks


def in_pack_order(forward, one, two):
    return jnp.where(forward, one, two), jnp.where(forward, two, one)


def low_lanes(rows):
    return lax.broadcasted_iota(jnp.int32, (rows, LANES), 1) < LANES // 2


def three_pieces(value):
    high = value.astype(BF16).astype(F32)
    rest = value - high
    middle = rest.astype(BF16).astype(F32)
    return high, middle, rest - middle


def turn(value):
    rows = value.shape[1]
    return jnp.concatenate([value, jnp.zeros((LANES - 8, rows), F32)], axis=0).T


def row_pieces(term, with_ones):
    lane = lax.broadcasted_iota(jnp.int32, term.shape, 1)
    term = jnp.where(lane < 8, term, 0.0)
    high, middle, low = three_pieces(term)
    result = pltpu.roll(high, 24, 1) + pltpu.roll(middle, 32, 1) + pltpu.roll(low, 40, 1)
    if with_ones:
        result = jnp.where(lane < 24, 1.0, result)
    return result


def key_pieces(offsets):
    rows = offsets.shape[1]
    high, middle, low = three_pieces(offsets)
    stack = jnp.concatenate(
        [-high, -middle, -low, jnp.ones((24, rows), F32), jnp.zeros((LANES - 48, rows), F32)], axis=0
    )
    return stack.T.astype(BF16)


def spread_heads(wide_ref, common, put, heads, forward=None):
    rows = wide_ref.shape[0]
    low = low_lanes(rows)
    lane = lax.broadcasted_iota(jnp.int32, (rows, LANES), 1)

    def ordered(value):
        if forward is None:
            return value
        return jnp.concatenate(in_pack_order(forward, value[: rows // 2], value[rows // 2 :]), axis=0)

    common = ordered(common)
    for h in range(heads):
        pair = h // 2
        block = ordered(wide_ref[:, pair * LANES : (pair + 1) * LANES])
        keep = low if h % 2 == 0 else jnp.logical_not(low)
        put(
            h,
            jnp.where(keep, block, jnp.zeros_like(block)),
            jnp.where(lax.rem(lane, 8) == h, common, 0.0).astype(BF16),
        )


def put_rows(cat_ref):
    def put(h, value, extra):
        cat_ref[h, :, :LANES] = value
        cat_ref[h, :, LANES:] = extra

    return put


def smem():
    return pl.BlockSpec(memory_space=pltpu.SMEM)


def whole(shape):
    return pl.BlockSpec(shape, lambda i: (0,) * len(shape))


def head_sums(value, heads):
    width = value.shape[1]
    feature = lax.broadcasted_iota(jnp.int32, (width, LANES), 0)
    lane = lax.broadcasted_iota(jnp.int32, (width, LANES), 1)
    member = (lax.div(feature, width // heads) == lane).astype(BF16)
    high = value.astype(BF16)
    return dot(high, member) + dot((value - high.astype(F32)).astype(BF16), member)


def backward_kernel(
    heads, rows, docs, me, group_map, doc_lengths, skip, q_ref, d_ref, out_ref, term_ref, k_ref, v_ref, kaug_ref,
    dq_ref, drow_ref, dk_ref, dv_ref, dcol_ref, acc_ref, qcat_ref, dcat_ref, dk_acc, dv_acc, dcol_acc,
):
    step = pl.program_id(0)

    @pl.when(step == 0)
    def _():
        acc_ref[...] = jnp.zeros_like(acc_ref)
        spread_heads(q_ref, row_pieces(term_ref[...], True), put_rows(qcat_ref), heads)
        delta = head_sums(d_ref[...].astype(F32) * out_ref[...], heads)
        spread_heads(d_ref, row_pieces(-delta, False), put_rows(dcat_ref), heads)

    dk_acc[...] = jnp.zeros_like(dk_acc)
    dv_acc[...] = jnp.zeros_like(dv_acc)
    dcol_acc[...] = jnp.zeros_like(dcol_acc)

    def tile(qi, ki, mask):
        q_rows = pl.ds(qi * rows, rows)
        k_rows = pl.ds(ki * rows, rows)
        aug = kaug_ref[k_rows, :]
        for pair in range(heads // 2):
            lanes = pl.ds(pair * LANES, LANES)
            keys = jnp.concatenate([k_ref[pair, k_rows, :], aug], axis=1)
            values = jnp.concatenate([v_ref[pair, k_rows, :], aug], axis=1)
            for h in (2 * pair, 2 * pair + 1):
                probs = jnp.exp(contract_cols(keys, qcat_ref[h, q_rows, :]))
                if mask is not None:
                    probs = jnp.where(mask, probs, 0.0)
                grads = (probs * contract_cols(values, dcat_ref[h, q_rows, :])).astype(BF16)
                dv_acc[k_rows, lanes] += dot(probs.astype(BF16), dcat_ref[h, q_rows, :LANES])
                both = dot(grads, qcat_ref[h, q_rows, :])
                dk_acc[k_rows, lanes] += both[:, :LANES]
                dcol_acc[k_rows, :] += both[:, LANES:]
                acc_ref[h, q_rows, :] += contract_rows(grads, keys)

    for ki in range(2):
        key_group = group_map[2 * step + ki]
        for qi in range(2):
            query_group = group_map[2 * me[0] + qi]
            active, full = block_state(group_map, doc_lengths, skip, query_group, key_group, rows, docs)

            @pl.when(active & full)
            def _(qi=qi, ki=ki):
                tile(qi, ki, None)

            @pl.when(active & jnp.logical_not(full))
            def _(qi=qi, ki=ki, query_group=query_group, key_group=key_group):
                tile(qi, ki, block_mask(doc_lengths, query_group, key_group, rows, docs, 1))

    dk_ref[0] = dk_acc[...].astype(BF16)
    dv_ref[0] = dv_acc[...].astype(BF16)
    dcol_ref[0] = -(dcol_acc[...].T[:8])

    @pl.when(step == pl.num_programs(0) - 1)
    def _():
        total_rows = dq_ref.shape[0]
        low = low_lanes(total_rows)
        lane = lax.broadcasted_iota(jnp.int32, (total_rows, LANES), 1)
        sums = jnp.zeros((total_rows, LANES), F32)
        for pair in range(heads // 2):
            a, b = 2 * pair, 2 * pair + 1
            dq_ref[:, pair * LANES : (pair + 1) * LANES] = jnp.where(
                low, acc_ref[a, :, :LANES], acc_ref[b, :, :LANES]
            )
            sums = jnp.where(
                lane == 24 + a, acc_ref[a, :, LANES:], jnp.where(lane == 24 + b, acc_ref[b, :, LANES:], sums)
            )
        drow_ref[...] = pltpu.roll(sums, LANES - 24, 1).T[:8]


def backward_attention(me, group_map, doc_lengths, skip, queries, grads, attended, term, keys, values, key_aug, heads):
    total = keys.shape[1]
    own, width = queries.shape
    rows = own // 2
    n = total // own
    docs = doc_lengths.shape[0]
    return pl.pallas_call(
        functools.partial(backward_kernel, heads, rows, docs),
        grid=(n,),
        out_shape=[
            jax.ShapeDtypeStruct((own, width), F32),
            jax.ShapeDtypeStruct((8, own), F32),
            jax.ShapeDtypeStruct((n, own, width), BF16),
            jax.ShapeDtypeStruct((n, own, width), BF16),
            jax.ShapeDtypeStruct((n, 8, own), F32),
        ],
        in_specs=[smem(), smem(), smem(), smem()]
        + [
            whole((own, width)),
            whole((own, width)),
            whole((own, width)),
            whole((own, LANES)),
            pl.BlockSpec((heads // 2, own, LANES), lambda i: (0, i, 0)),
            pl.BlockSpec((heads // 2, own, LANES), lambda i: (0, i, 0)),
            pl.BlockSpec((own, LANES), lambda i: (i, 0)),
        ],
        out_specs=[
            whole((own, width)),
            whole((8, own)),
            pl.BlockSpec((1, own, width), lambda i: (i, 0, 0)),
            pl.BlockSpec((1, own, width), lambda i: (i, 0, 0)),
            pl.BlockSpec((1, 8, own), lambda i: (i, 0, 0)),
        ],
        scratch_shapes=[
            VMEM((heads, own, 2 * LANES), F32),
            VMEM((heads, own, 2 * LANES), BF16),
            VMEM((heads, own, 2 * LANES), BF16),
            VMEM((own, width), F32),
            VMEM((own, width), F32),
            VMEM((own, LANES), F32),
        ],
        compiler_params=pltpu.CompilerParams(vmem_limit_bytes=VMEM_LIMIT),
        cost_estimate=pl.CostEstimate(
            flops=own * total * width * 10, bytes_accessed=total * width * 8, transcendentals=own * total * heads
        ),
    )(me, group_map, doc_lengths, skip, queries, grads, attended, term, keys, values, key_aug)


def deliver_kernel(heads, count, small_ref, *refs):
    sources, refs = refs[:count], refs[count:]
    targets, refs = refs[:count], refs[count:]
    (first_ref, second_ref, forget_ref, bias_ref, gains_ref), refs = refs[:5], refs[5:]
    held, local = refs[:count], refs[count]
    moves = Moves(local)
    for i in range(count):
        moves.start(i, sources[i], held[i])
    shard, gain_rows = first_ref.shape[0], gains_ref.shape[1]
    first_ref[...] = small_ref[0:1, :shard].reshape(shard)
    second_ref[...] = small_ref[1:2, :shard].reshape(shard)
    turned = jnp.concatenate([small_ref[...], jnp.zeros((LANES - 16, 256), F32)], axis=0).T
    forget_ref[...] = small_ref[8 : 8 + heads, :shard]
    gains_ref[...] = small_ref[2 : 2 + heads, :gain_rows]
    bias_ref[...] = turned[224:225, 8 : 8 + heads].reshape(heads)
    for i in range(count):
        moves.wait(i)
        moves.start(i, held[i], targets[i])
    moves.wait()


def deliver(heads, shard, gain_rows, small, arrays):
    vmem = pl.BlockSpec(memory_space=VMEM)
    anywhere = pl.BlockSpec(memory_space=pl.ANY)
    shapes = [array.shape for array in arrays]
    shapes += [(shard,), (shard,), (heads, shard), (heads,), (heads, gain_rows)]
    (layer, input_grad, query, key, value, gate_out, output, gate, up, down, one, two, forget, bias, gains) = (
        pl.pallas_call(
            functools.partial(deliver_kernel, heads, len(arrays)),
            out_shape=[jax.ShapeDtypeStruct(shape, F32) for shape in shapes],
            in_specs=[vmem] + [anywhere] * len(arrays),
            out_specs=[anywhere] * len(arrays) + [vmem] * 5,
            scratch_shapes=[VMEM(array.shape, F32) for array in arrays]
            + [pltpu.SemaphoreType.DMA((2 * len(arrays),))],
            compiler_params=pltpu.CompilerParams(vmem_limit_bytes=VMEM_LIMIT),
        )(small, *arrays)
    )
    return (
        layer, input_grad, one, query, key, value, gate_out, forget.T, bias, gains.T, output, two, gate, up, down,
    )


def on_device(
    hidden_in,
    norm_one,
    w_query,
    w_key,
    w_value,
    w_gate_out,
    w_forget,
    forget_bias,
    head_gains,
    w_output,
    norm_two,
    w_gate,
    w_up,
    w_down,
    out_grad,
    doc_lengths,
    group_map,
    skip_list,
):
    device_ctx = lax.axis_index("ctx")
    device_tp = lax.axis_index("tp")
    n = lax.axis_size("ctx")
    row_count, model_width = hidden_in.shape
    group_rows = row_count // 2
    heads = forget_bias.shape[0]
    shard = norm_one.shape[0]
    gain_rows = head_gains.shape[0]
    head_dim = gain_rows * n // 2
    width = heads * head_dim
    hidden_width = w_gate.shape[1]

    slots = 2 * n
    (
        query_weight,
        key_weight,
        value_weight,
        gate_out_weight,
        output_weight,
        normed_shards,
        query_rows,
        query_raw,
        key_raw,
        gate_logit,
        forget_logit,
        keys_all,
        values_all,
        key_aug,
        attended_flat,
        row_term,
        gain_one,
        gain_two,
        query_gain,
        key_gain,
        forget_weight,
    ) = start_forward(
        n,
        1,
        group_map,
        doc_lengths,
        skip_list,
        forget_bias,
        hidden_in,
        [norm_one, norm_two, head_gains.T, w_forget.T],
        [w_query, w_key, w_value, w_gate_out],
        w_output,
    )
    half = width // 256 * 128
    fused = n <= 8
    (
        gated,
        layer_out,
        down_share,
        gate_share,
        up_share,
        grad_middle,
        grad_attended,
        grad_gate_logit,
        gain_two_parts,
        *attention_grads,
    ) = feed_forward(
        n,
        3,
        heads,
        attended_flat,
        gate_logit,
        output_weight,
        hidden_in,
        gain_two,
        out_grad,
        w_gate,
        w_up,
        w_down,
        (group_map, doc_lengths, skip_list, query_rows, row_term, keys_all, values_all, key_aug) if fused else None,
    )
    halves = [(0, half), (half, width - half)]
    attn_plan = [[(cw, (i, c0, cw)) for c0, cw in halves] for i in (0, 1)]
    if fused:
        grad_branch, grad_query, row_sums, key_part, value_part, column_sums = attention_grads
        early_plan = [side + [(cw, (2, c0, cw))] for side, (c0, cw) in zip(attn_plan, halves)]
        query_share, key_share, value_share, gate_out_share, output_share, small_share, input_grad = finish_backward(
            n,
            7,
            heads,
            early_plan,
            attn_plan,
            key_part,
            value_part,
            column_sums,
            row_sums,
            grad_query,
            query_raw,
            key_raw,
            query_gain,
            key_gain,
            forget_logit,
            group_map,
            query_weight,
            key_weight,
            value_weight,
            gate_out_weight,
            forget_weight,
            grad_gate_logit,
            normed_shards,
            grad_branch,
            gated,
            hidden_in,
            gain_one,
            grad_middle,
            gain_two_parts,
        )
    else:
        grad_branch = grad_middle.astype(BF16).reshape(row_count, n, shard).transpose(1, 0, 2)
        normed_shards = normed_shards.reshape(n, shard, row_count).transpose(0, 2, 1)
        grad_query, row_sums, key_part, value_part, column_sums = backward_attention(
            device_ctx.astype(jnp.int32).reshape(1),
            group_map,
            doc_lengths,
            skip_list,
            query_rows,
            grad_attended,
            attended_flat,
            row_term,
            keys_all,
            values_all,
            key_aug,
            heads,
        )
        own_groups = lax.dynamic_slice_in_dim(group_map, device_ctx * 2, 2, 0)
        later = (group_map[None, :] > own_groups[:, None]).astype(F32)
        query_gain, key_gain = (gain.reshape(heads, head_dim) for gain in (query_gain, key_gain))
        query_raw, key_raw = (raw.reshape(row_count, heads, head_dim) for raw in (query_raw, key_raw))
        query_norm, key_norm = rms_scale(query_raw), rms_scale(key_raw)
        forget_logit = forget_logit[:heads].T
        forget_weight = forget_weight[:heads].astype(BF16)
        normed_one = normed_shards.transpose(1, 0, 2).reshape(row_count, model_width)
        place = jnp.arange(group_rows, dtype=jnp.int32)
        upper = (place[:, None] <= place[None, :]).astype(F32)
        grad_key, grad_value, off_sum, tot_sum = pair_scatter(n, 7, key_part, value_part, column_sums, row_sums)
        after = contract_cols_exact(tot_sum[:heads, :slots], later)
        suffix = lax.dot_general(
            off_sum[:heads].reshape(heads, 2, group_rows), upper, (((2,), (1,)), ((), ())), precision=HIGHEST
        )
        grad_log_forget = (suffix + after[:, :, None]).reshape(heads, row_count).T
        grad_key3 = grad_key.reshape(row_count, heads, head_dim)
        grad_query3 = grad_query.reshape(row_count, heads, head_dim)
        key_raw_grad = rms_back(grad_key3 * key_gain, key_raw).astype(BF16).reshape(row_count, width)
        query_raw_grad = (
            rms_back(grad_query3 * query_gain * 0.125, query_raw).astype(BF16).reshape(row_count, width)
        )
        value_low = grad_value.astype(BF16)
        query_gain_grad = jnp.sum(grad_query3 * query_norm * 0.125, axis=0)
        key_gain_grad = jnp.sum(grad_key3 * key_norm, axis=0)
        head_gain_grad = jnp.concatenate([query_gain_grad, key_gain_grad], axis=1)
        grad_forget_logit = (grad_log_forget * jax.nn.sigmoid(-forget_logit)).astype(BF16)
        bias_part = jnp.sum(grad_forget_logit.astype(F32), axis=0)
        normed_one_part = (
            contract_cols(query_raw_grad, query_weight)
            + contract_cols(key_raw_grad, key_weight)
            + contract_cols(value_low, value_weight)
            + contract_cols(grad_gate_logit, gate_out_weight)
            + dot(grad_forget_logit, forget_weight)
        )
        forget_grad = contract_rows(grad_forget_logit, normed_one)

        def wide(value):
            return jnp.pad(value, ((0, 0), (0, 0), (0, 256 - value.shape[2])))

        forget_rows = wide(forget_grad.reshape(heads, n, shard).transpose(1, 0, 2))
        forget_rows = forget_rows.at[:, :, 224].set(bias_part[None, :])
        small_grad = jnp.concatenate(
            [
                jnp.zeros((n, 1, 256), F32),
                wide(jnp.sum(gain_two_parts, axis=0).reshape(n, 1, shard)),
                wide(head_gain_grad.reshape(heads, n, gain_rows).transpose(1, 0, 2)),
                jnp.pad(forget_rows, ((0, 0), (0, 8 - heads), (0, 0))),
            ],
            axis=1,
        )
        plan = [
            [(cw, (0, right, c0, cw)) for right in rights for c0, cw in halves] + [(cw, (1, 4, c0, cw))]
            for rights, (c0, cw) in zip(((0, 1), (2, 3)), halves)
        ]
        (
            query_share,
            key_share,
            value_share,
            gate_out_share,
            output_share,
            small_share,
            input_grad,
        ) = weight_scatter(
            n,
            8,
            plan,
            [normed_shards, grad_branch],
            [query_raw_grad, key_raw_grad, value_low, grad_gate_logit, gated],
            small_grad,
            normed_one_part,
            hidden_in,
            gain_one,
            grad_middle,
        )
    return deliver(
        heads,
        shard,
        gain_rows,
        small_share,
        [
            layer_out,
            input_grad,
            query_share,
            key_share,
            value_share,
            gate_out_share,
            output_share,
            gate_share,
            up_share,
            down_share,
        ],
    )


def solution(mesh):
    split = P("ctx", "tp")
    in_specs = (
        P("ctx", None),
        P("ctx"),
        split,
        split,
        split,
        split,
        split,
        P("tp"),
        split,
        split,
        P("ctx"),
        split,
        split,
        split,
        P("ctx", None),
        P(),
        P(),
        P(),
    )
    out_specs = (
        split,
        P("ctx", None),
        P("ctx"),
        split,
        split,
        split,
        split,
        split,
        P("tp"),
        split,
        split,
        P("ctx"),
        split,
        split,
        split,
    )
    return jax.shard_map(on_device, mesh=mesh, in_specs=in_specs, out_specs=out_specs, check_vma=False)
```

```python
import functools

import jax
import jax.numpy as jnp
from jax import lax
from jax.experimental import pallas as pl
from jax.experimental.pallas import tpu as pltpu
from jax.sharding import PartitionSpec as P

EPS = 1e-06
HIGHEST = lax.Precision.HIGHEST
MESH = pl.DeviceIdType.MESH
VMEM = pltpu.VMEM
VMEM_LIMIT = 62 * 1024 * 1024
F32 = jnp.float32
BF16 = jnp.bfloat16


def rms_scale(value):
    return value * lax.rsqrt(jnp.mean(value * value, axis=-1, keepdims=True) + EPS)


def rms_back(grad_in, value):
    inverse = lax.rsqrt(jnp.mean(value * value, axis=-1, keepdims=True) + EPS)
    normal = value * inverse
    return inverse * (grad_in - normal * jnp.mean(grad_in * normal, axis=-1, keepdims=True))


def dot(left, right):
    return jnp.dot(left, right, preferred_element_type=F32)


def contract_cols(left, right):
    return lax.dot_general(left, right, (((1,), (1,)), ((), ())), preferred_element_type=F32)


def contract_cols_exact(left, right):
    return lax.dot_general(left, right, (((1,), (1,)), ((), ())), precision=HIGHEST)


def contract_rows(left, right):
    return lax.dot_general(left, right, (((0,), (0,)), ((), ())), preferred_element_type=F32)


def ring_place(ctx, n):
    odd = lax.rem(ctx, 2)
    half = lax.div(ctx, 2)
    return (1 - odd) * half + odd * (n - 1 - half)


def ring_owner(place, n):
    late = lax.div(place, n // 2)
    return (1 - late) * (2 * place) + late * (2 * (n - 1 - place) + 1)


def wrap(place, n):
    return lax.rem(place + 2 * n, n)


def ring_setup(n):
    me = lax.axis_index("ctx")
    tp = lax.axis_index("tp")
    place = ring_place(me, n)
    right = ring_owner(wrap(place + 1, n), n)
    left = ring_owner(wrap(place - 1, n), n)
    return me, tp, place, (right, left)


def greet(peers):
    barrier = pltpu.get_barrier_semaphore()
    for peer in peers:
        pl.semaphore_signal(barrier, inc=1, device_id=peer, device_id_type=MESH)
    pl.semaphore_wait(barrier, len(peers))


def ctx_peers(me, tp, n):
    return [(lax.rem(me + i, n), tp) for i in range(1, n)]


def remote(src, dst, send, recv, device):
    return pltpu.make_async_remote_copy(
        src_ref=src, dst_ref=dst, send_sem=send, recv_sem=recv, device_id=device, device_id_type=MESH
    )


class Gather:
    def __init__(self, n, place, sides, tp, chunks, send, recv):
        self.n, self.place, self.sides, self.tp = n, place, sides, tp
        self.chunks, self.send, self.recv = chunks, send, recv
        self.arrived = None

    def owner(self, side, back):
        return ring_owner(wrap(self.place - back if side == 0 else self.place + back, self.n), self.n)

    def copy(self, index, step, first):
        side, source, target = self.chunks[index]
        target = target(self.owner(side, step))
        return remote(
            source if first else target, target, self.send.at[index, step], self.recv.at[index, step],
            (self.sides[side], self.tp),
        )

    def arrive(self, index, step):
        side, _, target = self.chunks[index]
        target = target(self.owner(side, step + 1))
        remote(
            target, target, self.send.at[index, step], self.recv.at[index, step], (self.sides[side], self.tp)
        ).wait_recv()
        if self.arrived is not None:
            self.arrived(index, step)

    def begin(self, indices=None):
        for index in indices if indices is not None else range(len(self.chunks)):
            self.copy(index, 0, True).start()

    def forward(self, step):
        for index in range(len(self.chunks)):
            self.arrive(index, step - 1)
            self.copy(index, step, False).start()

    def last(self):
        for index in range(len(self.chunks)):
            self.arrive(index, self.n - 2)

    def sent(self):
        def finish(step, carry):
            for index in range(len(self.chunks)):
                self.copy(index, step, False).wait_send()
            return carry

        lax.fori_loop(0, self.n - 1, finish, 0)


class Moves:
    def __init__(self, semaphores):
        self.semaphores, self.count, self.open = semaphores, 0, {}

    def start(self, name, source, target):
        copy = pltpu.make_async_copy(source, target, self.semaphores.at[self.count])
        self.count += 1
        copy.start()
        self.open[name] = copy

    def wait(self, *names):
        for name in names or list(self.open):
            self.open.pop(name).wait()


def start_kernel(
    n, heads, group_map, doc_lengths, skip, bias_ref, x_ref, norm_one, norm_two, gains_in, forget_in,
    wq_in, wk_in, wv_in, wg_in, wo_in,
    wq_out, wk_out, wv_out, wg_out, wo_ref, u_out, q_out, qr_out, kr_out, gl_out, fz_ref, k_out, v_out, aug_out,
    att_out, term_ref, gain_one, gain_two, qgain_ref, kgain_ref, wf_ref,
    x_vmem, wq_ref, wk_ref, wv_ref, wg_ref, u_ref, turned_ref, q_ref, k_all, v_all, aug_ref, att_ref, acc_ref, cat_ref,
    diff_ref, span_ref, tot_ref, before_ref, inside_all, small_wide, small_in,
    small_all, acc_r, acc_l, inside_src,
    wsend, wrecv, osend, orecv, ksend, krecv, ssend, srecv, isend, irecv, spill, local,
):
    me, tp, place, sides = ring_setup(n)
    moves = Moves(local)
    moves.start("x", x_ref, x_vmem)
    shard, width = wq_in.shape
    small_wide[...] = jnp.zeros_like(small_wide)
    small_wide[0:1, :shard] = norm_one[...].astype(F32).reshape(1, shard)
    small_wide[1:2, :shard] = norm_two[...].astype(F32).reshape(1, shard)
    for ref, first in ((gains_in, 2), (forget_in, 8)):
        small_wide[first : first + heads, : ref.shape[1]] = ref[...].astype(F32)
    small_in[...] = small_wide[...].astype(BF16)
    greet(ctx_peers(me, tp, n))
    rows, cols = x_ref.shape
    half = rows // 2
    head_dim = width // heads

    def shard_rows(owner):
        return pl.ds(pl.multiple_of(owner * shard, 16), shard)

    def window(ref, c0, cw):
        return lambda owner: ref.at[shard_rows(owner), pl.ds(c0, cw)]

    def token_rows(owner):
        return pl.ds(pl.multiple_of(owner * rows, rows), rows)

    def block(ref, pair):
        return lambda owner: ref.at[pair, token_rows(owner), :]

    ring = (n, place, sides, tp)
    projections = Gather(
        *ring,
        [
            (side, source, window(target, 0, width))
            for side, source, target in ((0, wq_in, wq_ref), (1, wv_in, wv_ref), (0, wk_in, wk_ref), (1, wg_in, wg_ref))
        ],
        wsend, wrecv,
    )
    middle = width // 256 * 128
    outputs = Gather(
        *ring,
        [
            (side, wo_in.at[:, pl.ds(c0, cw)], window(wo_ref, c0, cw))
            for side, c0, cw in ((0, 0, middle), (1, middle, width - middle))
        ],
        osend, orecv,
    )
    members = [(0, k_all, k_out, 0), (1, k_all, k_out, 2), (0, v_all, v_out, 0), (1, v_all, v_out, 2)]
    members += [(0, k_all, k_out, 1), (1, v_all, v_out, 1)]
    pairs = Gather(
        *ring, [(side, block(ref, pair)(me), block(ref, pair)) for side, ref, _, pair in members], ksend, krecv
    )

    def spill_copy(index, step):
        side, ref, out, pair = members[index]
        owner = pairs.owner(side, step + 1)
        return pltpu.make_async_copy(
            block(ref, pair)(owner), block(out, pair)(owner), spill.at[index, step]
        )

    pairs.arrived = lambda index, step: spill_copy(index, step).start()

    projections.begin()
    exchange_start(n, me, tp, lambda peer: small_in, small_all, ssend, srecv)
    gathered = ((wq_in, wq_ref), (wk_in, wk_ref), (wv_in, wv_ref), (wg_in, wg_ref), (wo_in, wo_ref))
    for i, (source, target) in enumerate(gathered):
        moves.start(i, source, target.at[shard_rows(me)])
    moves.start("small", small_in, small_all.at[me])
    moves.wait("small")
    exchange_wait(n, me, tp, lambda peer: small_in, small_all, ssend, srecv)
    projections.forward(1)

    count = 2 * head_dim // n
    for i in range(n):
        block_small = small_all[i].astype(F32)
        gain_one[:, i * shard : (i + 1) * shard] = block_small[0:1, :shard]
        gain_two[:, i * shard : (i + 1) * shard] = block_small[1:2, :shard]
        wf_ref[:, i * shard : (i + 1) * shard] = block_small[8:16, :shard]
        target, at = (qgain_ref, i) if i < n // 2 else (kgain_ref, i - n // 2)
        for h in range(heads):
            lane = h * head_dim + at * count
            target[:, lane : lane + count] = block_small[2 + h : 3 + h, :count]

    size = 64

    def norm_rows(i, carry):
        here = pl.ds(pl.multiple_of(i * size, size), size)
        normed = (rms_scale(x_vmem[here, :].astype(F32)) * gain_one[...]).astype(BF16)
        for j in range(n):
            u_ref[j, here, :] = normed[:, j * shard : (j + 1) * shard]
        return carry

    moves.wait("x")
    lax.fori_loop(0, rows // size, norm_rows, 0)

    def grow(back):
        for side, acc, sources in ((0, acc_r, (wq_ref, wk_ref)), (1, acc_l, (wv_ref, wg_ref))):
            owner = projections.owner(side, back)
            for i, source in enumerate(sources):
                acc[:, i * width : (i + 1) * width] += dot(u_ref[owner], source[shard_rows(owner), :])

    acc_r[...] = jnp.zeros_like(acc_r)
    acc_l[...] = jnp.zeros_like(acc_l)
    moves.wait(0, 1, 2, 3, 4)
    grow(0)
    projections.forward(2)
    grow(1)
    grow(2)
    projections.forward(3)
    grow(3)
    forget = jnp.zeros((16, rows), F32)
    for j in range(n):
        forget += contract_cols(small_all[j, :, :shard], u_ref[j])
    head = lax.broadcasted_iota(jnp.int32, (8, rows), 0)
    fz = forget[8:16]
    for h in range(heads):
        fz = jnp.where(head == h, fz + bias_ref[h], fz)
    fz_ref[...] = fz
    logs = jnp.minimum(fz, 0.0) - jnp.log1p(jnp.exp(-jnp.abs(fz)))
    logs = jnp.where(head < heads, logs, 0.0)
    upto = (
        lax.broadcasted_iota(jnp.int32, (half, half), 0) <= lax.broadcasted_iota(jnp.int32, (half, half), 1)
    ).astype(F32)
    for g in range(2):
        inside_src[:, g * half : (g + 1) * half] = jnp.dot(
            logs[:, g * half : (g + 1) * half], upto, precision=HIGHEST, preferred_element_type=F32
        )
    exchange_start(n, me, tp, lambda peer: inside_src, inside_all, isend, irecv)
    moves.start("inside", inside_src, inside_all.at[me])

    def step_on(step, carry):
        projections.forward(step)
        grow(step)
        return carry

    lax.fori_loop(4, n - 2, step_on, 0)
    outputs.begin()
    projections.forward(n - 2)
    grow(n - 2)
    outputs.forward(1)
    projections.last()
    grow(n - 1)

    def head_norm(value):
        return value * lax.rsqrt(head_means(value * value, heads) + EPS)

    my_rows = token_rows(me)
    for pair in range(heads // 2):
        v_all[pair, my_rows, :] = acc_l[:, pair * LANES : (pair + 1) * LANES].astype(BF16)
    pairs.begin([2, 3, 5])
    keys = (head_norm(acc_r[:, width:]) * kgain_ref[...]).astype(BF16)
    for pair in range(heads // 2):
        k_all[pair, my_rows, :] = keys[:, pair * LANES : (pair + 1) * LANES]
    pairs.begin([0, 1, 4])
    for i, (source, target) in enumerate(
        ((wq_ref, wq_out), (wk_ref, wk_out), (wv_ref, wv_out), (wg_ref, wg_out))
    ):
        moves.start(i, source, target)
    moves.start("qr", acc_r.at[:, pl.ds(0, width)], qr_out)
    moves.start("kr", acc_r.at[:, pl.ds(width, width)], kr_out)
    moves.start("gl", acc_l.at[:, pl.ds(width, width)], gl_out)
    for i, (ref, out) in enumerate(((k_all, k_out), (v_all, v_out))):
        for pair in range(heads // 2):
            moves.start((i, pair), block(ref, pair)(me), block(out, pair)(me))
    q_ref[...] = (head_norm(acc_r[:, :width]) * qgain_ref[...] * 0.125).astype(BF16)
    moves.start("q", q_ref, q_out)

    moves.wait("inside")
    exchange_wait(n, me, tp, lambda peer: inside_src, inside_all, isend, irecv)
    tot_ref[...] = jnp.zeros_like(tot_ref)
    for i in range(n):
        for g in range(2):
            tot_ref[:, 2 * i + g : 2 * i + g + 1] = inside_all[i, :, (g + 1) * half - 1 : (g + 1) * half]
    earlier = groups_along(group_map, 0, 1 << 20) < groups_along(group_map, 1, 1 << 20)
    before_ref[...] = jnp.dot(
        tot_ref[...], earlier.astype(F32), precision=HIGHEST, preferred_element_type=F32
    )
    lane8 = lax.broadcasted_iota(jnp.int32, (8, LANES), 1)

    def offsets_of(shard_index):
        parts = []
        for g in range(2):
            before = jnp.sum(jnp.where(lane8 == 2 * shard_index + g, before_ref[...], 0.0), axis=1, keepdims=True)
            parts.append(inside_all[shard_index, :, g * half : (g + 1) * half] + before)
        return jnp.concatenate(parts, axis=1)

    def aug_rows(i, carry):
        aug_ref[token_rows(i), :] = key_pieces(offsets_of(i))
        return carry

    lax.fori_loop(0, n, aug_rows, 0)
    moves.start("aug", aug_ref, aug_out)
    pairs.forward(1)

    first, second = group_map[2 * me], group_map[2 * me + 1]
    in_order = first < second
    query_groups = (jnp.minimum(first, second), jnp.maximum(first, second))
    mine = turn(offsets_of(me))
    term_ref[...] = mine
    spread_heads(q_ref, row_pieces(mine, True), put_rows(cat_ref), heads, in_order)
    acc_ref[...] = jnp.zeros_like(acc_ref)
    query_at = lax.broadcasted_iota(jnp.int32, (half, half), 0)
    key_at = lax.broadcasted_iota(jnp.int32, (half, half), 1)
    diff_ref[...] = key_at - query_at
    for i, group in enumerate(query_groups):
        span_ref[i] = document_start(group * half + query_at, doc_lengths) - key_at
    ones = jnp.ones((half, LANES), BF16)

    def attend(i, back):
        late = lax.div(i, 2)
        pair = (1 - late) * 2 * i + late
        side = lax.rem(i, 2)
        owner = ring_owner(wrap(place + (2 * side - 1) * back, n), n)
        one, two = group_map[2 * owner], group_map[2 * owner + 1]
        forward = one < two
        key_groups = (jnp.minimum(one, two), jnp.maximum(one, two))
        top = pl.ds(pl.multiple_of(owner * rows, rows), half)
        bottom = pl.ds(pl.multiple_of(owner * rows + half, half), half)
        blocks = []
        for ref in (k_all.at[pair], v_all.at[pair], aug_ref):
            blocks.append(in_pack_order(forward, ref[top, :], ref[bottom, :]))
        masks = block_masks(diff_ref, span_ref, skip, query_groups, key_groups, half)
        keys = [jnp.concatenate([blocks[0][ki], blocks[2][ki]], axis=1) for ki in range(2)]
        values = [jnp.concatenate([blocks[1][ki], ones], axis=1) for ki in range(2)]
        both_values = jnp.concatenate(values, axis=0)
        for e in range(2):
            h = 2 * pair + e
            queries = cat_ref[h]
            early = contract_cols(queries, keys[0])
            weights = [
                jnp.where(mask, jnp.exp(score), 0.0).astype(BF16)
                for mask, score in zip(masks, (early[:half], early[half:], contract_cols(queries[half:], keys[1])))
            ]
            acc_ref[h, :half, :] += dot(weights[0], values[0])
            acc_ref[h, half:, :] += dot(jnp.concatenate(weights[1:], axis=1), both_values)

    def attend_all(count, back, first=0):
        def body(i, carry):
            attend(i, back)
            return carry

        lax.fori_loop(first, count, body, 0)

    attend_all(3, 0)

    def pair_step(step, count):
        outputs.forward(step)
        pairs.forward(step)
        attend_all(count, step)

    outputs.forward(2)
    pairs.forward(2)
    attend_all(2, 1)
    attend_all(2, 2)

    def turn_shard(i, carry):
        turned_ref[shard_rows(i), :] = u_ref[i].astype(F32).T.astype(BF16)
        return carry

    lax.fori_loop(0, n, turn_shard, 0)
    moves.start("u", turned_ref, u_out)

    def early_step(step, carry):
        pair_step(step, 2)
        return carry

    def late_step(step, carry):
        pair_step(step, 4)
        return carry

    lax.fori_loop(3, n // 2, early_step, 0)
    pair_step(n // 2, 3)
    lax.fori_loop(n // 2 + 1, n - 1, late_step, 0)
    for index in range(4):
        pairs.arrive(index, n - 2)
    attend_all(2, n - 1)
    outputs.last()
    for index in (4, 5):
        pairs.arrive(index, n - 2)
    attend_all(4, n - 1, 2)

    lane = lax.broadcasted_iota(jnp.int32, (rows, LANES), 1)
    low = low_lanes(rows)
    totals = jnp.ones((rows, LANES), F32)
    for pair in range(heads // 2):
        parts = []
        for h in (2 * pair, 2 * pair + 1):
            value = jnp.concatenate(in_pack_order(in_order, acc_ref[h, :half, :], acc_ref[h, half:, :]), axis=0)
            parts.append(value)
            totals = jnp.where(lane == h, value[:, LANES:], totals)
        att_ref[:, pair * LANES : (pair + 1) * LANES] = jnp.where(
            low, parts[0][:, :LANES], parts[1][:, :LANES]
        ) / jnp.where(low, parts[0][:, LANES:], parts[1][:, LANES:])
    moves.start("att", att_ref, att_out)
    term_ref[...] -= jnp.log(totals)

    def spilled(step, carry):
        for index in range(len(members)):
            spill_copy(index, step).wait()
        return carry

    lax.fori_loop(0, n - 1, spilled, 0)
    moves.wait()
    projections.sent()
    outputs.sent()
    pairs.sent()


def groups_along(group_map, dim, fill, shape=(128, 128)):
    slot = lax.broadcasted_iota(jnp.int32, shape, dim)
    groups = jnp.full(shape, fill, jnp.int32)
    for i in range(group_map.shape[0]):
        groups = jnp.where(slot == i, group_map[i], groups)
    return groups


def start_forward(n, collective_id, group_map, doc_lengths, skip, bias, x, vectors, weights, out_weight):
    rows, cols = x.shape
    shard, width = out_weight.shape
    heads = bias.shape[0]
    half = rows // 2
    dma = pltpu.SemaphoreType.DMA
    vmem = pl.BlockSpec(memory_space=VMEM)
    anywhere = pl.BlockSpec(memory_space=pl.ANY)
    by_pair = (heads // 2, n * rows, LANES)
    weight, wide, narrow = (n * shard, width), (rows, cols), (rows, width)
    shapes = (
        [(weight, BF16)] * 5
        + [((n * shard, rows), BF16), (narrow, BF16)]
        + [(narrow, F32)] * 3
        + [((8, rows), F32)]
        + [(by_pair, BF16)] * 2
        + [((n * rows, LANES), BF16), (narrow, F32), ((rows, LANES), F32)]
        + [((1, cols), F32)] * 2
        + [((1, width), F32)] * 2
        + [((8, cols), F32)]
    )
    return pl.pallas_call(
        functools.partial(start_kernel, n, heads),
        out_shape=[jax.ShapeDtypeStruct(*shape) for shape in shapes],
        in_specs=[smem(), smem(), smem(), smem(), anywhere] + [vmem] * 4 + [anywhere] * 5,
        out_specs=[anywhere if i < 10 or 11 <= i <= 14 else vmem for i in range(len(shapes))],
        scratch_shapes=[
            VMEM(wide, BF16),
            *[VMEM(weight, BF16)] * 4,
            VMEM((n, rows, shard), BF16),
            VMEM((n * shard, rows), BF16),
            VMEM(narrow, BF16),
            *[VMEM(by_pair, BF16)] * 2,
            VMEM((n * rows, LANES), BF16),
            VMEM(narrow, F32),
            VMEM((heads, rows, 2 * LANES), F32),
            VMEM((heads, rows, 2 * LANES), BF16),
            VMEM((half, half), jnp.int32),
            VMEM((2, half, half), jnp.int32),
            VMEM((8, LANES), F32),
            VMEM((8, LANES), F32),
            VMEM((n, 8, rows), F32),
            VMEM((16, 256), F32),
            VMEM((16, 256), BF16),
            VMEM((n, 16, 256), BF16),
            VMEM((rows, 2 * width), F32),
            VMEM((rows, 2 * width), F32),
            VMEM((8, rows), F32),
            *[dma((4, n - 1))] * 2,
            *[dma((2, n - 1))] * 2,
            *[dma((6, n - 1))] * 2,
            *[dma((n - 1,))] * 4,
            dma((6, n - 1)),
            dma((26,)),
        ],
        compiler_params=pltpu.CompilerParams(
            collective_id=collective_id, has_side_effects=True, vmem_limit_bytes=VMEM_LIMIT
        ),
    )(group_map, doc_lengths, skip, bias, x, *vectors, *weights, out_weight)


class ScatterRing:
    def __init__(self, n, plan, local_term, slots, firsts, write, send, recv, place, sides, tp, source=None):
        self.n, self.place, self.sides, self.tp = n, place, sides, tp
        self.source, self.next = source, 1
        self.local_term, self.write = local_term, write
        self.slots, self.firsts, self.send, self.recv = slots, firsts, send, recv
        self.order = []
        starts = [0, 0]
        for index in range(max(len(plan[0]), len(plan[1]))):
            for side in (0, 1):
                if index < len(plan[side]):
                    width, tag = plan[side][index]
                    self.order.append((side, index, starts[side], width, tag))
                    starts[side] += width

    def target(self, side, step):
        step = -1 - step if side == 0 else 1 + step
        return ring_owner(wrap(self.place + step, self.n), self.n)

    def hop(self, side, index, start, width, step, first):
        cols = pl.ds(start, width)
        slots = self.slots[side]
        if not first:
            source = slots.at[step - 1, :, cols]
        elif self.source is None:
            source = self.firsts[side].at[:, cols]
        else:
            source = self.source(self.target(side, 0), side, cols)
        return remote(
            source,
            slots.at[step, :, cols],
            self.send.at[side, index, step],
            self.recv.at[side, index, step],
            (self.sides[side], self.tp),
        )

    def begin(self):
        for side, index, start, width, tag in self.order:
            if self.source is None:
                term = self.local_term(self.target(side, 0), tag)
                self.firsts[side][:, start : start + width] = term.astype(BF16)
            self.hop(side, index, start, width, 0, True).start()

    def forward(self, step):
        for side, index, start, width, tag in self.order:
            term = self.local_term(self.target(side, step), tag)
            slot = self.slots[side].at[step - 1, :, pl.ds(start, width)]
            self.hop(side, index, start, width, step - 1, True).wait_recv()
            slot[...] = (slot[...].astype(F32) + term).astype(BF16)
            self.hop(side, index, start, width, step, False).start()

    def span(self, first, last):
        def body(step, carry):
            self.forward(step)
            return carry

        if last > first:
            lax.fori_loop(first, last, body, 0)

    def advance(self, count):
        last = min(self.next + count, self.n - 1)
        self.span(self.next, last)
        self.next = last

    def end(self):
        n = self.n
        self.advance(n)
        for side, index, start, width, tag in self.order:
            term = self.local_term(self.target(side, n - 1), tag)
            self.hop(side, index, start, width, n - 2, True).wait_recv()
            self.write(tag, self.slots[side][n - 2, :, start : start + width].astype(F32) + term)
        if self.source is None:
            self.sent()

    def sent(self):
        for side, index, start, width, tag in self.order:
            self.hop(side, index, start, width, 0, True).wait_send()

        def finish(step, carry):
            for side, index, start, width, tag in self.order:
                self.hop(side, index, start, width, step, False).wait_send()
            return carry

        lax.fori_loop(1, self.n - 1, finish, 0)


def exchange_start(n, me, tp, source_of, landing, send, recv):
    for i in range(1, n):
        peer = lax.rem(me + i, n)
        remote(source_of(peer), landing.at[me], send.at[i - 1], recv.at[i - 1], (peer, tp)).start()


def exchange_wait(n, me, tp, source_of, landing, send, recv):
    for i in range(1, n):
        peer = lax.rem(me - i + n, n)
        remote(source_of(peer), landing.at[peer], send.at[i - 1], recv.at[i - 1], (peer, tp)).wait()


def ordered_sum(n, landing):
    total = landing[0]
    for i in range(1, n):
        total = total + landing[i]
    return total


def pair_scatter_kernel(
    n, key_ref, value_ref, col_ref, row_ref, key_out, value_out, off_out, tot_out,
    slot_r, slot_l, first_r, first_l, off_ref, tot_ref, off_land, tot_land,
    send, recv, osend, orecv, tsend, trecv, local,
):
    me, tp, place, sides = ring_setup(n)
    off_ref[...] = col_ref[...]
    off_ref[me] += row_ref[...]
    group_rows = row_ref.shape[1] // 2
    tot_ref[...] = jnp.zeros_like(tot_ref)
    for i in range(n):
        for g in range(2):
            tot_ref[:, 2 * i + g : 2 * i + g + 1] = jnp.sum(
                off_ref[i, :, g * group_rows : (g + 1) * group_rows], axis=1, keepdims=True
            )
    greet(ctx_peers(me, tp, n))
    exchange_start(n, me, tp, lambda peer: off_ref.at[peer], off_land, osend, orecv)
    exchange_start(n, me, tp, lambda peer: tot_ref, tot_land, tsend, trecv)
    mine = pltpu.make_async_copy(off_ref.at[me], off_land.at[me], local.at[0])
    mine_tot = pltpu.make_async_copy(tot_ref, tot_land.at[me], local.at[1])
    mine.start()
    mine_tot.start()
    width = key_ref.shape[2]
    plan = [
        [(w, (0, c)) for c, w in pieces(width, 128)],
        [(w, (1, c)) for c, w in pieces(width, 128)],
    ]

    def local_term(owner, tag):
        which, c0 = tag
        return (key_ref, value_ref)[which][owner, :, c0 : c0 + 128].astype(F32)

    def write(tag, value):
        which, c0 = tag
        (key_out, value_out)[which][:, c0 : c0 + 128] = value

    ring = ScatterRing(
        n, plan, local_term, (slot_r, slot_l), (first_r, first_l), write, send, recv, place, sides, tp
    )
    ring.begin()
    ring.end()
    mine.wait()
    mine_tot.wait()
    exchange_wait(n, me, tp, lambda peer: off_ref.at[peer], off_land, osend, orecv)
    exchange_wait(n, me, tp, lambda peer: tot_ref, tot_land, tsend, trecv)
    off_out[...] = ordered_sum(n, off_land)
    tot_out[...] = ordered_sum(n, tot_land)


def pieces(width, step):
    return [(c, min(step, width - c)) for c in range(0, width, step)]


def pair_scatter(n, collective_id, keys, values, columns, own_rows):
    _, rows, width = keys.shape
    offs, tots = columns, jax.ShapeDtypeStruct((8, LANES), F32)
    chunks = len(pieces(width, 128))
    return pl.pallas_call(
        functools.partial(pair_scatter_kernel, n),
        out_shape=[
            jax.ShapeDtypeStruct((rows, width), F32),
            jax.ShapeDtypeStruct((rows, width), F32),
            jax.ShapeDtypeStruct(offs.shape[1:], F32),
            jax.ShapeDtypeStruct(tots.shape, F32),
        ],
        in_specs=[pl.BlockSpec(memory_space=VMEM)] * 4,
        out_specs=[pl.BlockSpec(memory_space=VMEM)] * 4,
        scratch_shapes=[
            VMEM((n - 1, rows, width), BF16),
            VMEM((n - 1, rows, width), BF16),
            VMEM((rows, width), BF16),
            VMEM((rows, width), BF16),
            VMEM(offs.shape, F32),
            VMEM(tots.shape, F32),
            VMEM(offs.shape, F32),
            VMEM((n,) + tots.shape, F32),
            pltpu.SemaphoreType.DMA((2, chunks, n - 1)),
            pltpu.SemaphoreType.DMA((2, chunks, n - 1)),
            pltpu.SemaphoreType.DMA((n - 1,)),
            pltpu.SemaphoreType.DMA((n - 1,)),
            pltpu.SemaphoreType.DMA((n - 1,)),
            pltpu.SemaphoreType.DMA((n - 1,)),
            pltpu.SemaphoreType.DMA((2,)),
        ],
        compiler_params=pltpu.CompilerParams(
            collective_id=collective_id, has_side_effects=True, vmem_limit_bytes=VMEM_LIMIT
        ),
    )(keys, values, columns, own_rows)


def weight_scatter_kernel(n, plan, left_count, grads, *refs):
    lefts, refs = refs[:left_count], refs[left_count:]
    rights, refs = refs[:grads], refs[grads:]
    small_ref, part_ref, x_ref, gain_ref, dmid_ref, refs = *refs[:5], refs[5:]
    outs, refs = refs[:grads], refs[grads:]
    small_out, input_out, slot_r, slot_l, first_r, first_l, own_small, land, sum_out, refs = *refs[:9], refs[9:]
    tp_bufs, refs = refs[:4], refs[4:]
    send, recv, xsend, xrecv, tsend, trecv, local = refs
    me, tp, place, sides = ring_setup(n)
    chip, core, sibling, across = tp_setup()
    greet(ctx_peers(me, tp, n) + [sibling, across])
    shard = lefts[0].shape[2]
    half = part_ref.shape[0] // 2

    def local_term(owner, tag):
        left, right, c0, cw = tag
        return contract_rows(lefts[left][owner], rights[right][:, c0 : c0 + cw])

    def write(tag, value):
        _, right, c0, cw = tag
        outs[right][:, c0 : c0 + cw] = value

    ring = ScatterRing(
        n, plan, local_term, (slot_r, slot_l), (first_r, first_l), write, send, recv, place, sides, tp
    )

    def part(which, c):
        cols = part_ref.shape[1] // TP_CHUNKS
        return part_ref[pl.ds(pl.multiple_of(which * half, half), half), c * cols : (c + 1) * cols].astype(F32)

    total = TpSum(part, sum_out, tp_bufs, tsend, trecv, core, sibling, across)
    total.first()
    total.second()
    ring.begin()
    total.third()
    ring.advance(1)
    total.fourth()

    own_small[...] = small_ref[...]
    cols = part_ref.shape[1]
    size = 64

    def gain_rows(i, acc):
        rows = pl.ds(pl.multiple_of(i * size, size), size)
        value = x_ref[rows, :].astype(F32)
        inverse = lax.rsqrt(jnp.mean(value * value, axis=-1, keepdims=True) + EPS)
        normal = value * inverse
        grad = sum_out[rows, :].astype(F32)
        back = grad * gain_ref[...]
        back = inverse * (back - normal * jnp.mean(back * normal, axis=-1, keepdims=True))
        input_out[rows, :] = dmid_ref[rows, :] + back
        return acc + jnp.sum((grad * normal).reshape(size // 8, 8, cols), axis=0)

    gains = lax.fori_loop(0, 2 * half // size, gain_rows, jnp.zeros((8, cols), F32))
    gains = jnp.sum(gains, axis=0, keepdims=True)
    for i in range(n):
        own_small[i, 0:1, :shard] = gains[:, i * shard : (i + 1) * shard]
    exchange_start(n, me, tp, lambda peer: own_small.at[peer], land, xsend, xrecv)
    mine = pltpu.make_async_copy(own_small.at[me], land.at[me], local.at[0])
    mine.start()
    ring.end()
    mine.wait()
    exchange_wait(n, me, tp, lambda peer: own_small.at[peer], land, xsend, xrecv)
    small_out[...] = ordered_sum(n, land)


def weight_scatter(n, collective_id, plan, lefts, rights, small, part, x, gain, dmid):
    rows = lefts[0].shape[2]
    chunks = max(len(plan[0]), len(plan[1]))
    totals = [sum(width for width, _ in side) for side in plan]
    return pl.pallas_call(
        functools.partial(weight_scatter_kernel, n, plan, len(lefts), len(rights)),
        out_shape=[jax.ShapeDtypeStruct((rows, right.shape[1]), F32) for right in rights]
        + [jax.ShapeDtypeStruct(small.shape[1:], F32), jax.ShapeDtypeStruct(part.shape, F32)],
        in_specs=[pl.BlockSpec(memory_space=VMEM)] * (len(lefts) + len(rights) + 5),
        out_specs=[pl.BlockSpec(memory_space=VMEM)] * (len(rights) + 2),
        scratch_shapes=[
            VMEM((n - 1, rows, totals[0]), BF16),
            VMEM((n - 1, rows, totals[1]), BF16),
            VMEM((rows, totals[0]), BF16),
            VMEM((rows, totals[1]), BF16),
            VMEM(small.shape, F32),
            VMEM(small.shape, F32),
            VMEM(part.shape, BF16),
            *tp_buffers(*part.shape),
            pltpu.SemaphoreType.DMA((2, chunks, n - 1)),
            pltpu.SemaphoreType.DMA((2, chunks, n - 1)),
            pltpu.SemaphoreType.DMA((n - 1,)),
            pltpu.SemaphoreType.DMA((n - 1,)),
            pltpu.SemaphoreType.DMA((3, TP_CHUNKS)),
            pltpu.SemaphoreType.DMA((3, TP_CHUNKS)),
            pltpu.SemaphoreType.DMA((1,)),
        ],
        compiler_params=pltpu.CompilerParams(
            collective_id=collective_id, has_side_effects=True, vmem_limit_bytes=VMEM_LIMIT
        ),
    )(*lefts, *rights, small, part, x, gain, dmid)


def tp_setup():
    ctx = lax.axis_index("ctx")
    tp = lax.axis_index("tp")
    chip = lax.div(tp, 2)
    core = lax.rem(tp, 2)
    sibling = (ctx, 2 * chip + 1 - core)
    across = (ctx, 2 * (1 - chip) + core)
    return chip, core, sibling, across


TP_CHUNKS = 4


def tp_buffers(rows, width):
    return [VMEM((rows // 2, width), BF16) for _ in range(4)]


class TpSum:
    def __init__(self, part, out, bufs, send, recv, core, sibling, across):
        self.part, self.out, self.send, self.recv = part, out, send, recv
        self.away, self.land_a, self.half_b, self.land_b = bufs
        self.core, self.sibling, self.across = core, sibling, across
        self.half = self.away.shape[0]
        self.size = self.away.shape[1] // TP_CHUNKS

    def cols(self, c):
        return pl.ds(c * self.size, self.size)

    def copy(self, stage, c, which=None):
        cols = self.cols(c)
        if stage == 0:
            source, target, device = self.away.at[:, cols], self.land_a.at[:, cols], self.sibling
        elif stage == 1:
            source, target, device = self.half_b.at[:, cols], self.land_b.at[:, cols], self.across
        else:
            source = target = self.out.at[self.rows(which), cols]
            device = self.sibling
        return remote(source, target, self.send.at[stage, c], self.recv.at[stage, c], device)

    def rows(self, which):
        return pl.ds(pl.multiple_of(which * self.half, self.half), self.half)

    def first(self):
        for c in range(TP_CHUNKS):
            self.away[:, self.cols(c)] = self.part(1 - self.core, c).astype(BF16)
            self.copy(0, c).start()

    def second(self):
        for c in range(TP_CHUNKS):
            cols = self.cols(c)
            mine = self.part(self.core, c)
            self.copy(0, c).wait_recv()
            self.half_b[:, cols] = (mine + self.land_a[:, cols].astype(F32)).astype(BF16)
            self.copy(1, c).start()

    def third(self):
        for c in range(TP_CHUNKS):
            cols = self.cols(c)
            self.copy(1, c).wait_recv()
            both = self.half_b[:, cols].astype(F32) + self.land_b[:, cols].astype(F32)
            self.out[self.rows(self.core), cols] = both.astype(BF16)
            self.copy(2, c, self.core).start()

    def fourth(self):
        for c in range(TP_CHUNKS):
            self.copy(2, c, 1 - self.core).wait_recv()
            self.copy(0, c).wait_send()
            self.copy(1, c).wait_send()
            self.copy(2, c, self.core).wait_send()


class TpSplit:
    def __init__(self, part, bufs, send, recv, chip, core, sibling, across):
        self.part, self.send, self.recv = part, send, recv
        self.away, self.land_a, self.half_b, self.land_b = bufs
        self.chip, self.core, self.sibling, self.across = chip, core, sibling, across

    def copy(self, stage):
        if stage < 2:
            return remote(
                self.away.at[stage], self.land_a.at[stage], self.send.at[stage], self.recv.at[stage], self.sibling
            )
        return remote(self.half_b, self.land_b, self.send.at[2], self.recv.at[2], self.across)

    def first(self):
        for i, chip in enumerate((1 - self.chip, self.chip)):
            self.away[i] = self.part(chip, 1 - self.core).astype(BF16)
            self.copy(i).start()

    def second(self):
        mine = self.part(1 - self.chip, self.core)
        self.copy(0).wait_recv()
        self.half_b[...] = (mine + self.land_a[0].astype(F32)).astype(BF16)
        self.copy(2).start()

    def mine(self):
        return self.part(self.chip, self.core)

    def third(self):
        self.copy(1).wait_recv()
        self.copy(2).wait_recv()
        total = self.land_a[1].astype(F32) + self.land_b[...].astype(F32)
        for stage in range(3):
            self.copy(stage).wait_send()
        return total


def feed_kernel(n, heads, attention, *refs):
    if attention:
        (group_map, doc_lengths, skip, q_in, term_in, k_in, v_in, aug_in), refs = refs[:8], refs[8:]
    (att_in, gl_in, outw_in, x_in, gain_ref, grad_in, wg_in, wu_in, wd_in), refs = refs[:9], refs[9:]
    (gated_out, layer_ref, down_out, gate_out, up_out, dmid_out, do_out, dgl_out, gain_out), refs = refs[:9], refs[9:]
    if attention:
        (dm_out, dq_out, drow_ref, dk_out, dv_out, dcol_ref), refs = refs[:6], refs[6:]
    (
        att_ref, gl_ref, outw_ref, x_ref, gated_ref, normed_ref, dgt_ref, dup_ref, do_ref, dgl_ref,
        gate_all, up_all, down_all, accs, dhid_acc, hid_ref, branch_ref, mid_ref, dw_ref, dy_ref,
        a0, a1, a2, a3, b3, s0, s1, s2, s3, dslot_r, dslot_l, dfirst_r, dfirst_l, eslot_r, eslot_l, efirst_r, efirst_l,
        gsend, grecv, hsend, hrecv, asend, arecv, bsend, brecv, ssend, srecv, dsend, drecv, esend, erecv, local,
    ), refs = refs[:52], refs[52:]
    if attention:
        term_ref, diff_ref, span_ref, stage, kv_sem, stage_sem = refs
    gate_acc, up_acc = accs.at[0], accs.at[1]
    me, tp, place, sides = ring_setup(n)
    chip, core, sibling, across = tp_setup()
    moves = Moves(local)
    for name, source, target in (
        ("att", att_in, att_ref), ("gl", gl_in, gl_ref), ("outw", outw_in, outw_ref), ("grad", grad_in, dw_ref),
        ("x", x_in, x_ref),
    ):
        moves.start(name, source, target)
    if attention:
        moves.start("term", term_in, term_ref)
    greet([(side, tp) for side in sides] + [sibling, across])
    shard, hidden = wg_in.shape
    rows, width = x_in.shape
    half = rows // 2
    hw = hidden // 2
    size = 64
    ring = (n, place, sides, tp)

    def rows_of(owner):
        return pl.ds(pl.multiple_of(owner * shard, 16), shard)

    def window(ref, c0, cw):
        return lambda owner: ref.at[rows_of(owner), pl.ds(c0, cw)]

    def chunks(members):
        return [(side, source.at[:, pl.ds(c0, cw)], window(target, c0, cw)) for side, source, target, c0, cw in members]

    gates = Gather(
        *ring,
        chunks(
            [
                (side, source, target, c0, hw)
                for c0 in (0, hw)
                for side, source, target in ((0, wg_in, gate_all), (1, wu_in, up_all))
            ]
        ),
        gsend, grecv,
    )
    downs = Gather(
        *ring,
        chunks([(side, wd_in, down_all, side * hw + c0, hw // 2) for c0 in (0, hw // 2) for side in (0, 1)]),
        hsend, hrecv,
    )
    gates.begin()
    for i, (source, target) in enumerate(((wg_in, gate_all), (wu_in, up_all), (wd_in, down_all))):
        moves.start(i, source, target.at[rows_of(me)])

    moves.wait("att", "gl")
    gated_ref[...] = (att_ref[...] * jax.nn.sigmoid(gl_ref[...])).astype(BF16)
    moves.start("gated", gated_ref, gated_out)
    moves.wait("outw")
    span = width // TP_CHUNKS

    def branch_part(which, c):
        mine = gated_ref[pl.ds(pl.multiple_of(which * half, half), half), :]
        return contract_cols(mine, outw_ref[c * span : (c + 1) * span, :])

    branch = TpSum(branch_part, branch_ref, (a0, a1, a2, a3), asend, arecv, core, sibling, across)
    branch.first()
    branch.second()
    gates.forward(1)
    moves.wait("grad")
    for c in range(TP_CHUNKS):
        back = pl.ds(c * span, span)
        dy_ref[back, :] = dw_ref[:, back].astype(F32).T.astype(BF16)
    dhid_acc[...] = jnp.zeros_like(dhid_acc)
    gate_acc[...] = jnp.zeros_like(gate_acc)
    up_acc[...] = jnp.zeros_like(up_acc)

    def grow_back(back):
        for side in (0, 1):
            owner = downs.owner(side, back)
            cols = pl.ds(side * hw, hw)
            dhid_acc[:, cols] += contract_rows(dy_ref[rows_of(owner), :], down_all[rows_of(owner), cols])

    def grow(back):
        for side, acc, source in ((0, gate_acc, gate_all), (1, up_acc, up_all)):
            owner = gates.owner(side, back)
            acc[...] += contract_rows(normed_ref[rows_of(owner), :], source[rows_of(owner), :])

    moves.wait(0, 1, 2)
    grow_back(0)
    gates.forward(2)
    branch.third()
    branch.fourth()
    moves.wait("x")

    def norm_rows(i, carry):
        here = pl.ds(pl.multiple_of(i * LANES, LANES), LANES)
        middle = x_ref[here, :].astype(F32) + branch_ref[here, :].astype(F32)
        mid_ref[here, :] = middle
        normed_ref[:, here] = (rms_scale(middle) * gain_ref[...]).T.astype(BF16)
        return carry

    lax.fori_loop(0, rows // LANES, norm_rows, 0)
    own = pl.ds(pl.multiple_of(tp * span, span), span)
    layer_ref[...] = mid_ref[:, own]
    moves.start("again", grad_in, x_ref)
    if attention:
        moves.wait("gated")
        moves.start("q", q_in, gated_ref)
    gates.forward(3)

    def grow_step(step, carry):
        grow(step)
        return carry

    lax.fori_loop(0, 4, grow_step, 0)

    def gate_step(step, carry):
        gates.forward(step)
        grow(step)
        return carry

    lax.fori_loop(4, n - 1, gate_step, 0)
    downs.begin()
    gates.last()
    grow(n - 1)

    def hid_rows(i, carry):
        here = pl.ds(pl.multiple_of(i * size, size), size)
        gate, up = gate_acc[here, :], up_acc[here, :]
        open_gate = jax.nn.sigmoid(gate)
        silu = gate * open_gate
        hid_ref[here, :] = (silu * up).astype(BF16)
        gate_acc[here, :] = up * open_gate * (1.0 + gate * (1.0 - open_gate))
        up_acc[here, :] = silu
        return carry

    lax.fori_loop(0, rows // size, hid_rows, 0)

    def down_step(step, carry):
        downs.forward(step)
        grow_back(step)
        return carry

    lax.fori_loop(1, n - 2, down_step, 0)
    downs.forward(n - 2)

    def down_term(owner, tag):
        return dot(dy_ref[rows_of(owner), :], hid_ref[:, tag * hw : (tag + 1) * hw])

    down_ref = accs.at[0, pl.ds(0, shard), :]
    gate_ref = accs.at[0, pl.ds(shard, shard), :]
    up_ref = accs.at[1, pl.ds(0, shard), :]

    def down_write(tag, value):
        down_ref[:, tag * hw : (tag + 1) * hw] = value

    def early_term(owner, tag):
        which, c0 = tag
        return dot(normed_ref[rows_of(owner), :], (dgt_ref, dup_ref)[which][:, c0 : c0 + hw])

    def early_write(tag, value):
        which, c0 = tag
        (gate_ref, up_ref)[which][:, c0 : c0 + hw] = value

    backs = ScatterRing(
        n, [[(hw, 0)], [(hw, 1)]], down_term, (dslot_r, dslot_l), (dfirst_r, dfirst_l), down_write,
        dsend, drecv, place, sides, tp,
    )
    earlies = [
        ScatterRing(
            n, [[(hw, (i, part * hw))] for i in range(2)], early_term, (eslot_r.at[part], eslot_l.at[part]),
            (efirst_r.at[part], efirst_l.at[part]), early_write, esend.at[part], erecv.at[part], place, sides, tp,
        )
        for part in range(2)
    ]
    backs.begin()
    grow_back(n - 2)
    downs.last()
    grow_back(n - 1)

    def grad_rows(i, carry):
        here = pl.ds(pl.multiple_of(i * size, size), size)
        dhid = dhid_acc[here, :]
        dgt_ref[here, :] = (dhid * gate_acc[here, :]).astype(BF16)
        dup_ref[here, :] = (dhid * up_acc[here, :]).astype(BF16)
        return carry

    lax.fori_loop(0, rows // size, grad_rows, 0)

    def dw_part(which, c):
        mine = pl.ds(pl.multiple_of(which * half, half), half)
        back = pl.ds(c * span, span)
        return contract_cols(dgt_ref[mine, :], gate_all[back, :]) + contract_cols(dup_ref[mine, :], up_all[back, :])

    def layer_part(which_chip, which_core):
        back = pl.ds(pl.multiple_of((2 * which_chip + which_core) * span, span), span)
        return contract_cols(hid_ref[...], down_all[back, :])

    total = TpSum(dw_part, dw_ref, (a0, a1, a2, b3), bsend, brecv, core, sibling, across)
    layer = TpSplit(layer_part, (s0, s1, s2, s3), ssend, srecv, chip, core, sibling, across)
    total.first()
    backs.advance(1)
    earlies[0].begin()
    earlies[1].begin()
    total.second()
    gates.sent()
    if attention:
        pairs = heads // 2

        def kv_copies(it):
            part, pair = lax.div(it, pairs), lax.rem(it, pairs)
            source = pl.ds(pl.multiple_of(part * rows, rows), rows)
            target = pl.ds(pl.multiple_of(pair * rows, rows), rows)
            lanes = pl.ds(pl.multiple_of(part * LANES, LANES), LANES)
            return [
                pltpu.make_async_copy(ref.at[pair, source, :], held.at[target, lanes], kv_sem.at[i, it])
                for i, (ref, held) in enumerate(((k_in, gate_all), (v_in, up_all)))
            ]

        def bring(it, carry):
            for copy in kv_copies(it):
                copy.start()
            return carry

        lax.fori_loop(0, n * pairs, bring, 0)
    layer.first()
    layer.second()
    layer_ref[...] += layer.mine()

    def serve_all():
        backs.advance(1)
        earlies[0].advance(1)
        earlies[1].advance(1)

    serve_all()
    if attention:
        downs.sent()
        moves.wait("q", "term")
        first, second = group_map[2 * me], group_map[2 * me + 1]
        in_order = first < second
        query_groups = (jnp.minimum(first, second), jnp.maximum(first, second))

        def put_query(h, value, extra):
            here, lane = pl.ds(h // 4 * rows, rows), h % 4 * 2 * LANES
            down_all[here, lane : lane + LANES] = value
            down_all[here, lane + LANES : lane + 2 * LANES] = extra

        spread_heads(gated_ref, row_pieces(term_ref[...], True), put_query, heads, in_order)
        accs[...] = jnp.zeros_like(accs)
        query_at = lax.broadcasted_iota(jnp.int32, (half, half), 1)
        key_at = lax.broadcasted_iota(jnp.int32, (half, half), 0)
        diff_ref[...] = key_at - query_at
        for i, group in enumerate(query_groups):
            span_ref[i] = document_start(group * half + query_at, doc_lengths) - key_at
    serve_all()
    total.third()
    total.fourth()

    def middle_rows(i, acc):
        here = pl.ds(pl.multiple_of(i * size, size), size)
        middle = mid_ref[here, :]
        inverse = lax.rsqrt(jnp.mean(middle * middle, axis=-1, keepdims=True) + EPS)
        normal = middle * inverse
        dw = dw_ref[here, :].astype(F32)
        back = dw * gain_ref[...]
        back = inverse * (back - normal * jnp.mean(back * normal, axis=-1, keepdims=True))
        dmid = x_ref[here, :].astype(F32) + back
        mid_ref[here, :] = dmid
        branch_ref[here, :] = dmid.astype(BF16)
        return acc + jnp.sum((dw * normal).reshape(size // 8, 8, width), axis=0)

    moves.wait("again")
    gain_out[...] = lax.fori_loop(0, rows // size, middle_rows, jnp.zeros((8, width), F32))
    if attention:
        for i in range(n):
            moves.start(
                ("aug", i), aug_in.at[pl.ds(i * rows, rows), :], x_ref.at[:, pl.ds(i * LANES, LANES)]
            )
    moves.start("dmid", mid_ref, dmid_out)
    if attention:
        moves.start("dm", branch_ref, dm_out)
    da = dot(branch_ref[...], outw_ref[...])
    open_gate = jax.nn.sigmoid(gl_ref[...])
    do_ref[...] = (da * open_gate).astype(BF16)
    dgl_ref[...] = (da * att_ref[...] * open_gate * (1.0 - open_gate)).astype(BF16)
    moves.start("do", do_ref, do_out)
    moves.start("dgl", dgl_ref, dgl_out)
    serve_all()
    layer_ref[...] += layer.third()

    if attention:
        def put_grad(h, value, extra):
            branch_ref[:, 2 * h * LANES : (2 * h + 1) * LANES] = value
            branch_ref[:, (2 * h + 1) * LANES : (2 * h + 2) * LANES] = extra

        delta = head_sums(do_ref[...].astype(F32) * att_ref[...], heads)
        moves.wait("dm", *[("aug", i) for i in range(n)])
        spread_heads(do_ref, row_pieces(-delta, False), put_grad, heads, in_order)
        dcol_acc = dhid_acc.at[:, pl.ds(0, LANES)]

        def stage_copies(it):
            part, pair = lax.div(it, pairs), lax.rem(it, pairs)
            lanes = pl.ds(pl.multiple_of(pair * LANES, LANES), LANES)
            slot = lax.rem(it, 2)
            return [
                pltpu.make_async_copy(stage.at[slot, i], out.at[part, :, lanes], stage_sem.at[slot, i])
                for i, out in enumerate((dk_out, dv_out))
            ]

        def attend(it, carry):
            part, pair = lax.div(it, pairs), lax.rem(it, pairs)
            for copy in kv_copies(it):
                copy.wait()
            one, two = group_map[2 * part], group_map[2 * part + 1]
            forward = one < two
            key_groups = (jnp.minimum(one, two), jnp.maximum(one, two))
            lanes = pl.ds(pl.multiple_of(part * LANES, LANES), LANES)

            def ordered(ref, base, where):
                top = pl.ds(pl.multiple_of(base * rows, rows), half)
                bottom = pl.ds(pl.multiple_of(base * rows + half, half), half)
                return in_pack_order(forward, ref[top, where], ref[bottom, where])

            key_blocks = ordered(gate_all, pair, lanes)
            value_blocks = ordered(up_all, pair, lanes)
            aug_blocks = ordered(x_ref, 0, lanes)
            masks = block_masks(diff_ref, span_ref, skip, query_groups, key_groups, half)
            keys = [jnp.concatenate([key_blocks[ki], aug_blocks[ki]], axis=1) for ki in range(2)]
            values = [jnp.concatenate([value_blocks[ki], aug_blocks[ki]], axis=1) for ki in range(2)]
            both_keys = jnp.concatenate(keys, axis=0)
            queries, douts, probs, grads = [], [], ([], []), ([], [])
            for e in range(2):
                h = 2 * pair + e
                spot = pl.ds(pl.multiple_of(h * 2 * LANES, 2 * LANES), 2 * LANES)
                quarter = pl.ds(pl.multiple_of(lax.rem(h, 4) * 2 * LANES, 2 * LANES), 2 * LANES)
                query_rows = pl.ds(pl.multiple_of(lax.div(h, 4) * rows, rows), rows)
                query, dout = down_all[query_rows, quarter], branch_ref[:, spot]
                early = contract_cols(keys[0], query)
                scores = (early[:, :half], early[:, half:], contract_cols(keys[1], query[half:]))
                early = contract_cols(values[0], dout)
                backs_out = (early[:, :half], early[:, half:], contract_cols(values[1], dout[half:]))
                prob = [jnp.where(mask, jnp.exp(score), 0.0) for mask, score in zip(masks, scores)]
                grad = [(p * back).astype(BF16) for p, back in zip(prob, backs_out)]
                prob = [p.astype(BF16) for p in prob]
                queries.append(query)
                douts.append(dout[:, :LANES])
                probs[0].extend(prob[:2])
                probs[1].append(prob[2])
                grads[0].extend(grad[:2])
                grads[1].append(grad[2])
                accs[lax.div(h, 4), :half, quarter] += contract_rows(grad[0], keys[0])
                accs[lax.div(h, 4), half:, quarter] += contract_rows(jnp.concatenate(grad[1:], axis=0), both_keys)
            late_queries = jnp.concatenate([query[half:] for query in queries], axis=0)
            late_douts = jnp.concatenate([dout[half:] for dout in douts], axis=0)
            queries, douts = jnp.concatenate(queries, axis=0), jnp.concatenate(douts, axis=0)
            sums = [
                dot(jnp.concatenate(grads[0], axis=1), queries),
                dot(jnp.concatenate(grads[1], axis=1), late_queries),
            ]
            value_sums = [
                dot(jnp.concatenate(probs[0], axis=1), douts),
                dot(jnp.concatenate(probs[1], axis=1), late_douts),
            ]
            columns = jnp.concatenate([part_sum[:, LANES:] for part_sum in sums], axis=0)
            dcol_acc[...] = jnp.where(pair == 0, 0.0, dcol_acc[...]) + columns

            @pl.when(it >= 2)
            def _():
                for copy in stage_copies(it - 2):
                    copy.wait()

            slot = lax.rem(it, 2)
            for i, part_sums in enumerate(([part_sum[:, :LANES] for part_sum in sums], value_sums)):
                stage[slot, i] = jnp.concatenate(in_pack_order(forward, *part_sums), axis=0).astype(BF16)
            for copy in stage_copies(it):
                copy.start()

            @pl.when(pair == pairs - 1)
            def _():
                columns = jnp.concatenate(
                    in_pack_order(forward, dcol_acc[pl.ds(0, half), :], dcol_acc[pl.ds(half, half), :]), axis=0
                )
                dcol_ref[part] = -(columns.T[:8])

            return carry

        turns = (*earlies, backs)
        starts = [ring.next for ring in turns]
        services = sum(n - 1 - start for start in starts)
        assert starts[0] == starts[1] == starts[2] - 1
        share = 2 * n * pairs // (3 * services)

        def serve(k, carry):
            lax.fori_loop(k * share, (k + 1) * share, attend, 0)
            for i, ring in enumerate(turns):

                @pl.when(lax.rem(k, 3) == i)
                def _(i=i, ring=ring):
                    ring.forward(starts[i] + lax.div(k, 3))

            return carry

        lax.fori_loop(0, services, serve, 0)
        for ring in turns:
            ring.next = n - 1
        if services * share < n * pairs:
            lax.fori_loop(services * share, n * pairs, attend, 0)
        for it in (n * pairs - 2, n * pairs - 1):
            for copy in stage_copies(it):
                copy.wait()

        lane = lax.broadcasted_iota(jnp.int32, (rows, LANES), 1)
        low = low_lanes(rows)
        sums = jnp.zeros((rows, LANES), F32)
        for pair in range(pairs):
            parts = []
            for h in (2 * pair, 2 * pair + 1):
                spot = pl.ds((h % 4) * 2 * LANES, 2 * LANES)
                value = jnp.concatenate(
                    in_pack_order(in_order, accs[h // 4, :half, spot], accs[h // 4, half:, spot]), axis=0
                )
                parts.append(value)
                sums = jnp.where(lane == 24 + h, value[:, LANES:], sums)
            dhid_acc[:, (3 + pair) * LANES : (4 + pair) * LANES] = jnp.where(
                low, parts[0][:, :LANES], parts[1][:, :LANES]
            )
        moves.start("dq", dhid_acc.at[:, pl.ds(3 * LANES, pairs * LANES)], dq_out)
        drow_ref[...] = pltpu.roll(sums, LANES - 24, 1).T[:8]

        moves.wait("dq")
    backs.end()
    moves.start("down", down_ref, down_out)
    earlies[0].end()
    earlies[1].end()
    moves.start("gate", gate_ref, gate_out)
    moves.start("up", up_ref, up_out)
    if not attention:
        downs.sent()
    moves.wait()


def feed_forward(
    n, collective_id, heads, attended, gate_logit, out_weight, x, gain, dy, w_gate, w_up, w_down, attention=None
):
    rows, width = x.shape
    shard, hidden = w_gate.shape
    heads_width = attended.shape[1]
    own = width // 4
    half = rows // 2
    dma = pltpu.SemaphoreType.DMA
    vmem = pl.BlockSpec(memory_space=VMEM)
    anywhere = pl.BlockSpec(memory_space=pl.ANY)
    wide, narrow, deep = (rows, width), (rows, heads_width), (rows, hidden)
    turned = (n * shard, rows)
    weight = (shard, hidden)
    shapes = [
        (narrow, BF16),
        ((rows, own), F32),
        (weight, F32),
        (weight, F32),
        (weight, F32),
        (wide, F32),
        (narrow, BF16),
        (narrow, BF16),
        ((8, width), F32),
    ]
    kept = [1, 8]
    extra_specs, extra_scratch = [], []
    if attention is not None:
        assert heads // 2 * rows == n * shard and n * LANES == hidden and 2 * rows <= n * shard
        shapes += [
            (wide, BF16),
            (narrow, F32),
            ((8, rows), F32),
            ((n, rows, heads_width), BF16),
            ((n, rows, heads_width), BF16),
            ((n, 8, rows), F32),
        ]
        kept += [11, 14]
        extra_specs = [smem()] * 3 + [anywhere] * 5
        extra_scratch = [
            VMEM((rows, LANES), F32),
            VMEM((half, half), jnp.int32),
            VMEM((2, half, half), jnp.int32),
            VMEM((2, 2, rows, LANES), BF16),
            dma((2, n * heads // 2)),
            dma((2, 2)),
        ]
    return pl.pallas_call(
        functools.partial(feed_kernel, n, heads, attention is not None),
        out_shape=[jax.ShapeDtypeStruct(*shape) for shape in shapes],
        in_specs=extra_specs + [anywhere] * 4 + [vmem] + [anywhere] * 4,
        out_specs=[vmem if i in kept else anywhere for i in range(len(shapes))],
        scratch_shapes=[
            VMEM(narrow, F32),
            VMEM(narrow, F32),
            VMEM(out_weight.shape, BF16),
            VMEM(wide, BF16),
            VMEM(narrow, BF16),
            VMEM(turned, BF16),
            VMEM(deep, BF16),
            VMEM(deep, BF16),
            VMEM(narrow, BF16),
            VMEM(narrow, BF16),
            *[VMEM((n * shard, hidden), BF16)] * 3,
            VMEM((2,) + deep, F32),
            VMEM(deep, F32),
            VMEM(deep, BF16),
            VMEM(wide, BF16),
            VMEM(wide, F32),
            VMEM(wide, BF16),
            VMEM(turned, BF16),
            *tp_buffers(rows, width),
            VMEM((rows // 2, width), BF16),
            VMEM((2, rows, own), BF16),
            VMEM((2, rows, own), BF16),
            VMEM((rows, own), BF16),
            VMEM((rows, own), BF16),
            *ring_scratch(n, shard, [hidden // 2] * 2),
            *[VMEM((2, n - 1, shard, hidden // 2), BF16)] * 2,
            *[VMEM((2, shard, hidden // 2), BF16)] * 2,
            *[dma((4, n - 1))] * 4,
            *[dma((3, TP_CHUNKS))] * 4,
            *[dma((3,))] * 2,
            *[dma((2, 1, n - 1))] * 2,
            *[dma((2, 2, 1, n - 1))] * 2,
            dma((28,)),
            *extra_scratch,
        ],
        compiler_params=pltpu.CompilerParams(
            collective_id=collective_id, has_side_effects=True, vmem_limit_bytes=VMEM_LIMIT
        ),
    )(*(attention or ()), attended, gate_logit, out_weight, x, gain, dy, w_gate, w_up, w_down)


def ring_scratch(n, height, widths):
    return [VMEM((n - 1, height, w), BF16) for w in widths] + [VMEM((height, w), BF16) for w in widths]


def head_means(value, heads):
    width = value.shape[1]
    size = width // heads
    left = lax.div(lax.broadcasted_iota(jnp.int32, (width, width), 0), size)
    right = lax.div(lax.broadcasted_iota(jnp.int32, (width, width), 1), size)
    member = (left == right).astype(BF16)
    high = value.astype(BF16)
    return (dot(high, member) + dot((value - high.astype(F32)).astype(BF16), member)) * (1.0 / size)


STAGED = (0, 1, 4, 5, 16, 11, 14, 17, 18, 19, 6, 12, 13, 20)


def finish_kernel(n, heads, gate_plan, attn_plan, *refs):
    operands, refs = list(refs[:24]), refs[24:]
    (q_out, k_out, v_out, g_out, o_out, small_out, input_out), refs = refs[:7], refs[7:]
    staged, refs = refs[: len(STAGED)], refs[len(STAGED) :]
    (
        dmt_ref, pslot_r, pslot_l, gslot_r, gslot_l, gfirst_r, gfirst_l, aslot_r, aslot_l, afirst_r, afirst_l,
        dk_sum, dv_sum, dqr_ref, dkr_ref, dvl_ref, du_ref, sum_ref, t0, t1, t2, t3,
        off_ref, tot_ref, off_land, tot_land, small_ref, small_land,
        psend, precv, gsend, grecv, asend, arecv, osend, orecv, qsend, qrecv, xsend, xrecv, tsend, trecv, local,
    ) = refs
    moves = Moves(local)
    dk_hbm, dv_hbm = operands[:2]
    for target, index in zip(staged, STAGED):
        moves.start(index, operands[index], target)
        operands[index] = target
    (
        dk_ref, dv_ref, col_ref, row_ref, dq_ref, qr_ref, kr_ref, qgain_ref, kgain_ref, fz_ref, group_map,
        wq_ref, wk_ref, wv_ref, wg_ref, wf_ref, dgl_ref, u_ref, dm_ref, gated_ref,
        x_ref, gain_ref, dmid_ref, gain_two_ref,
    ) = operands
    me, tp, place, sides = ring_setup(n)
    chip, core, sibling, across = tp_setup()
    rows, width = dq_ref.shape
    cols = x_ref.shape[1]
    shard = u_ref.shape[0] // n
    half = rows // 2
    head_dim = width // heads

    def rows_of(owner):
        return pl.ds(pl.multiple_of(owner * shard, 16), shard)

    small_ref[...] = jnp.zeros_like(small_ref)
    greet(ctx_peers(me, tp, n) + [sibling, across])

    def pair_term(owner, tag):
        which, c0 = tag
        return (dk_ref, dv_ref)[which][owner, :, c0 : c0 + LANES].astype(F32)

    def pair_write(tag, value):
        which, c0 = tag
        (dk_sum, dv_sum)[which][:, c0 : c0 + LANES] = value

    pairs = ScatterRing(
        n, [[(w, (i, c)) for c, w in pieces(width, LANES)] for i in range(2)], pair_term,
        (pslot_r, pslot_l), None, pair_write, psend, precv, place, sides, tp,
        source=lambda target, side, window: (dk_hbm, dv_hbm)[side].at[target, :, window],
    )
    pairs.begin()
    off_ref[...] = col_ref[...]
    off_ref[me] += row_ref[...]
    tot_ref[...] = jnp.zeros_like(tot_ref)
    for i in range(n):
        for g in range(2):
            tot_ref[:, 2 * i + g : 2 * i + g + 1] = jnp.sum(
                off_ref[i, :, g * half : (g + 1) * half], axis=1, keepdims=True
            )
    exchange_start(n, me, tp, lambda peer: off_ref.at[peer], off_land, osend, orecv)
    exchange_start(n, me, tp, lambda peer: tot_ref, tot_land, qsend, qrecv)
    moves.start("off", off_ref.at[me], off_land.at[me])
    moves.start("tot", tot_ref, tot_land.at[me])

    def raw_grad(grad, raw, gain):
        inverse = lax.rsqrt(head_means(raw * raw, heads) + EPS)
        normal = raw * inverse
        back = grad * gain
        back = inverse * (back - normal * head_means(back * normal, heads))
        return back.astype(BF16), jnp.sum(grad * normal, axis=0, keepdims=True)

    def gain_rows(row, first):
        count = 2 * head_dim // n
        for i in range(n // 2):
            for h in range(heads):
                lane = h * head_dim + i * count
                small_ref[first + i, 2 + h : 3 + h, 0:count] = row[:, lane : lane + count]

    moves.wait(0, 1, 4, 5)
    pairs.advance(1)
    dqr, row = raw_grad(dq_ref[...], qr_ref[...], qgain_ref[...] * 0.125)
    dqr_ref[...] = dqr
    gain_rows(row * 0.125, 0)
    pairs.advance(1)
    moves.wait(16, 11, 14)
    span = cols // TP_CHUNKS
    for c in range(TP_CHUNKS):
        back = pl.ds(c * span, span)
        du_ref[:, back] = contract_cols(dqr_ref[...], wq_ref[back, :]) + contract_cols(dgl_ref[...], wg_ref[back, :])
    moves.wait(18)
    for c in range(TP_CHUNKS):
        back = pl.ds(c * span, span)
        dmt_ref[back, :] = dm_ref[:, back].astype(F32).T.astype(BF16)
    pairs.advance(n)
    moves.wait(17, 19)

    def gate_term(owner, tag):
        right, c0, cw = tag
        left = dmt_ref if right == 2 else u_ref
        return dot(left[rows_of(owner), :], (dqr_ref, dgl_ref, gated_ref)[right][:, c0 : c0 + cw])

    def gate_write(tag, value):
        right, c0, cw = tag
        (q_out, g_out, o_out)[right][:, c0 : c0 + cw] = value

    gates = ScatterRing(
        n, gate_plan, gate_term, (gslot_r, gslot_l), (gfirst_r, gfirst_l), gate_write, gsend, grecv, place, sides, tp,
    )
    gates.begin()
    pairs.end()

    moves.wait(6)
    dkr, row = raw_grad(dk_sum[...], kr_ref[...], kgain_ref[...])
    dkr_ref[...] = dkr
    gain_rows(row, n // 2)
    dvl_ref[...] = dv_sum[...].astype(BF16)

    def attn_term(owner, tag):
        c0, cw = tag[1], tag[2]
        return dot(u_ref[rows_of(owner), :], (dkr_ref, dvl_ref)[tag[0]][:, c0 : c0 + cw])

    def attn_write(tag, value):
        c0, cw = tag[1], tag[2]
        (k_out, v_out)[tag[0]][:, c0 : c0 + cw] = value

    attns = ScatterRing(
        n, attn_plan, attn_term, (aslot_r, aslot_l), (afirst_r, afirst_l), attn_write, asend, arecv, place, sides, tp,
    )
    attns.begin()
    gates.advance(1)
    moves.wait("off", "tot")
    exchange_wait(n, me, tp, lambda peer: off_ref.at[peer], off_land, osend, orecv)
    exchange_wait(n, me, tp, lambda peer: tot_ref, tot_land, qsend, qrecv)
    off_sum = ordered_sum(n, off_land)
    tot_sum = ordered_sum(n, tot_land)
    onward = (
        lax.broadcasted_iota(jnp.int32, (half, half), 0) >= lax.broadcasted_iota(jnp.int32, (half, half), 1)
    ).astype(F32)
    parts = []
    for g in range(2):
        suffix = jnp.dot(
            off_sum[:, g * half : (g + 1) * half], onward, precision=HIGHEST, preferred_element_type=F32
        )
        later = groups_along(group_map, 1, -1, (8, LANES)) > group_map[2 * me + g]
        parts.append(suffix + jnp.sum(jnp.where(later, tot_sum, 0.0), axis=1, keepdims=True))
    dfz = (jnp.concatenate(parts, axis=1) * jax.nn.sigmoid(-fz_ref[...])).astype(BF16).astype(F32)
    head = lax.broadcasted_iota(jnp.int32, dfz.shape, 0)
    dfz = jnp.where(head < heads, dfz, 0.0)
    bias = jnp.sum(dfz, axis=1, keepdims=True)
    dfz_cols = turn(dfz).astype(BF16)
    dfz_low = dfz.astype(BF16)
    for i in range(n):
        small_ref[i, 8:16, :shard] = contract_cols(dfz_low, u_ref[i * shard : (i + 1) * shard, :])
        small_ref[i, 8:16, 224:225] = bias
        small_ref[i, 1:2, :shard] = jnp.sum(gain_two_ref[:, i * shard : (i + 1) * shard], axis=0, keepdims=True)

    moves.wait(12, 13)
    forget = jnp.concatenate([wf_ref[...], jnp.zeros((LANES - 8, cols), F32)], axis=0).astype(BF16)
    for c in range(TP_CHUNKS):
        back = pl.ds(c * span, span)
        du_ref[:, back] += (
            contract_cols(dkr_ref[...], wk_ref[back, :])
            + contract_cols(dvl_ref[...], wv_ref[back, :])
            + dot(dfz_cols, forget[:, c * span : (c + 1) * span])
        )

    def part(which, c):
        return du_ref[pl.ds(pl.multiple_of(which * half, half), half), c * span : (c + 1) * span]

    total = TpSum(part, sum_ref, (t0, t1, t2, t3), tsend, trecv, core, sibling, across)
    total.first()
    attns.advance(1)
    total.second()
    moves.start("dmid", dmid_ref, du_ref)
    for _ in range(3):
        gates.advance(1)
        attns.advance(1)
    total.third()
    gates.advance(1)
    attns.advance(1)
    total.fourth()
    moves.wait("dmid", 20)
    size = 64

    def input_rows(i, acc):
        here = pl.ds(pl.multiple_of(i * size, size), size)
        value = x_ref[here, :].astype(F32)
        inverse = lax.rsqrt(jnp.mean(value * value, axis=-1, keepdims=True) + EPS)
        normal = value * inverse
        grad = sum_ref[here, :].astype(F32)
        back = grad * gain_ref[...]
        back = inverse * (back - normal * jnp.mean(back * normal, axis=-1, keepdims=True))
        du_ref[here, :] += back
        return acc + jnp.sum((grad * normal).reshape(size // 8, 8, cols), axis=0)

    gains = lax.fori_loop(0, rows // size, input_rows, jnp.zeros((8, cols), F32))
    moves.start("input", du_ref, input_out)
    for i in range(n):
        small_ref[i, 0:1, :shard] = jnp.sum(gains[:, i * shard : (i + 1) * shard], axis=0, keepdims=True)
    exchange_start(n, me, tp, lambda peer: small_ref.at[peer], small_land, xsend, xrecv)
    moves.start("small", small_ref.at[me], small_land.at[me])
    while gates.next < n - 1:
        gates.advance(1)
        attns.advance(1)
    gates.end()
    attns.end()
    moves.wait("small")
    exchange_wait(n, me, tp, lambda peer: small_ref.at[peer], small_land, xsend, xrecv)
    small_out[...] = ordered_sum(n, small_land)
    pairs.sent()
    moves.wait()


def finish_backward(n, collective_id, heads, gate_plan, attn_plan, *operands):
    dq, u, x = operands[4], operands[17], operands[20]
    rows, width = dq.shape
    cols = x.shape[1]
    shard = u.shape[0] // n
    dma = pltpu.SemaphoreType.DMA
    vmem = pl.BlockSpec(memory_space=VMEM)
    anywhere = pl.BlockSpec(memory_space=pl.ANY)
    outside = STAGED + (22,)
    gate_widths = [sum(w for w, _ in side) for side in gate_plan]
    attn_widths = [sum(w for w, _ in side) for side in attn_plan]

    def ring_semaphores(plan):
        return [dma((2, max(len(side) for side in plan), n - 1))] * 2

    shapes = [(shard, width)] * 5 + [(16, 256), (rows, cols)]
    return pl.pallas_call(
        functools.partial(finish_kernel, n, heads, gate_plan, attn_plan),
        out_shape=[jax.ShapeDtypeStruct(shape, F32) for shape in shapes],
        in_specs=[anywhere if i in outside else smem() if i == 10 else vmem for i in range(len(operands))],
        out_specs=[vmem] * 6 + [anywhere],
        scratch_shapes=[
            *[VMEM(operands[i].shape, operands[i].dtype) for i in STAGED],
            VMEM(u.shape, BF16),
            *[VMEM((n - 1, rows, width), BF16)] * 2,
            *ring_scratch(n, shard, gate_widths),
            *ring_scratch(n, shard, attn_widths),
            VMEM((rows, width), F32),
            VMEM((rows, width), F32),
            *[VMEM((rows, width), BF16)] * 3,
            VMEM((rows, cols), F32),
            VMEM((rows, cols), BF16),
            *tp_buffers(rows, cols),
            VMEM((n, 8, rows), F32),
            VMEM((8, LANES), F32),
            VMEM((n, 8, rows), F32),
            VMEM((n, 8, LANES), F32),
            VMEM((n, 16, 256), F32),
            VMEM((n, 16, 256), F32),
            *[dma((2, len(pieces(width, LANES)), n - 1))] * 2,
            *ring_semaphores(gate_plan),
            *ring_semaphores(attn_plan),
            *[dma((n - 1,))] * 6,
            *[dma((3, TP_CHUNKS))] * 2,
            dma((len(STAGED) + 5,)),
        ],
        compiler_params=pltpu.CompilerParams(
            collective_id=collective_id, has_side_effects=True, vmem_limit_bytes=VMEM_LIMIT
        ),
    )(*operands)


LANES = 128


def block_state(group_map, doc_lengths, skip, query_group, key_group, rows, docs):
    first_q = query_group * rows
    last_q = first_q + rows - 1
    first_k = key_group * rows
    last_k = first_k + rows - 1
    zero = jnp.int32(0)
    doc_qf, doc_ql, doc_kf, doc_kl, end = zero, zero, zero, zero, zero
    for d in range(docs):
        end = end + doc_lengths[d]
        doc_qf += (first_q >= end).astype(jnp.int32)
        doc_ql += (last_q >= end).astype(jnp.int32)
        doc_kf += (first_k >= end).astype(jnp.int32)
        doc_kl += (last_k >= end).astype(jnp.int32)
    earlier = key_group < query_group
    same = key_group == query_group
    kept = skip[query_group, key_group] != 1
    active = jnp.logical_or(same, earlier & kept & (doc_kl == doc_qf))
    full = earlier & (doc_kf == doc_ql)
    return active, full


def block_mask(doc_lengths, query_group, key_group, rows, docs, query_dim):
    shape = (rows, rows)
    pos_q = query_group * rows + lax.broadcasted_iota(jnp.int32, shape, query_dim)
    pos_k = key_group * rows + lax.broadcasted_iota(jnp.int32, shape, 1 - query_dim)
    start = jnp.zeros(shape, jnp.int32)
    end = jnp.int32(0)
    for d in range(docs):
        end = end + doc_lengths[d]
        start = jnp.where(pos_q >= end, end, start)
    return (pos_k <= pos_q) & (pos_k >= start)


def document_start(position, doc_lengths):
    start, end = jnp.zeros_like(position), jnp.int32(0)
    for d in range(doc_lengths.shape[0]):
        end = end + doc_lengths[d]
        start = jnp.where(position >= end, end, start)
    return start


def block_masks(diff_ref, span_ref, skip, query_groups, key_groups, rows):
    masks = []
    for qi, ki in ((0, 0), (1, 0), (1, 1)):
        query_group, key_group = query_groups[qi], key_groups[ki]
        skipped = jnp.where(key_group < query_group, skip[query_group, key_group], 0)
        reach = key_group * rows - (skipped == 1).astype(jnp.int32) * (1 << 30)
        mask = span_ref[qi] <= reach
        if qi == ki:
            mask = mask & (diff_ref[...] <= (query_group - key_group) * rows)
        masks.append(mask)
    return masks


def in_pack_order(forward, one, two):
    return jnp.where(forward, one, two), jnp.where(forward, two, one)


def low_lanes(rows):
    return lax.broadcasted_iota(jnp.int32, (rows, LANES), 1) < LANES // 2


def three_pieces(value):
    high = value.astype(BF16).astype(F32)
    rest = value - high
    middle = rest.astype(BF16).astype(F32)
    return high, middle, rest - middle


def turn(value):
    rows = value.shape[1]
    return jnp.concatenate([value, jnp.zeros((LANES - 8, rows), F32)], axis=0).T


def row_pieces(term, with_ones):
    lane = lax.broadcasted_iota(jnp.int32, term.shape, 1)
    term = jnp.where(lane < 8, term, 0.0)
    high, middle, low = three_pieces(term)
    result = pltpu.roll(high, 24, 1) + pltpu.roll(middle, 32, 1) + pltpu.roll(low, 40, 1)
    if with_ones:
        result = jnp.where(lane < 24, 1.0, result)
    return result


def key_pieces(offsets):
    rows = offsets.shape[1]
    high, middle, low = three_pieces(offsets)
    stack = jnp.concatenate(
        [-high, -middle, -low, jnp.ones((24, rows), F32), jnp.zeros((LANES - 48, rows), F32)], axis=0
    )
    return stack.T.astype(BF16)


def spread_heads(wide_ref, common, put, heads, forward=None):
    rows = wide_ref.shape[0]
    low = low_lanes(rows)
    lane = lax.broadcasted_iota(jnp.int32, (rows, LANES), 1)

    def ordered(value):
        if forward is None:
            return value
        return jnp.concatenate(in_pack_order(forward, value[: rows // 2], value[rows // 2 :]), axis=0)

    common = ordered(common)
    for h in range(heads):
        pair = h // 2
        block = ordered(wide_ref[:, pair * LANES : (pair + 1) * LANES])
        keep = low if h % 2 == 0 else jnp.logical_not(low)
        put(
            h,
            jnp.where(keep, block, jnp.zeros_like(block)),
            jnp.where(lax.rem(lane, 8) == h, common, 0.0).astype(BF16),
        )


def put_rows(cat_ref):
    def put(h, value, extra):
        cat_ref[h, :, :LANES] = value
        cat_ref[h, :, LANES:] = extra

    return put


def smem():
    return pl.BlockSpec(memory_space=pltpu.SMEM)


def whole(shape):
    return pl.BlockSpec(shape, lambda i: (0,) * len(shape))


def head_sums(value, heads):
    width = value.shape[1]
    feature = lax.broadcasted_iota(jnp.int32, (width, LANES), 0)
    lane = lax.broadcasted_iota(jnp.int32, (width, LANES), 1)
    member = (lax.div(feature, width // heads) == lane).astype(BF16)
    high = value.astype(BF16)
    return dot(high, member) + dot((value - high.astype(F32)).astype(BF16), member)


def backward_kernel(
    heads, rows, docs, me, group_map, doc_lengths, skip, q_ref, d_ref, out_ref, term_ref, k_ref, v_ref, kaug_ref,
    dq_ref, drow_ref, dk_ref, dv_ref, dcol_ref, acc_ref, qcat_ref, dcat_ref, dk_acc, dv_acc, dcol_acc,
):
    step = pl.program_id(0)

    @pl.when(step == 0)
    def _():
        acc_ref[...] = jnp.zeros_like(acc_ref)
        spread_heads(q_ref, row_pieces(term_ref[...], True), put_rows(qcat_ref), heads)
        delta = head_sums(d_ref[...].astype(F32) * out_ref[...], heads)
        spread_heads(d_ref, row_pieces(-delta, False), put_rows(dcat_ref), heads)

    dk_acc[...] = jnp.zeros_like(dk_acc)
    dv_acc[...] = jnp.zeros_like(dv_acc)
    dcol_acc[...] = jnp.zeros_like(dcol_acc)

    def tile(qi, ki, mask):
        q_rows = pl.ds(qi * rows, rows)
        k_rows = pl.ds(ki * rows, rows)
        aug = kaug_ref[k_rows, :]
        for pair in range(heads // 2):
            lanes = pl.ds(pair * LANES, LANES)
            keys = jnp.concatenate([k_ref[pair, k_rows, :], aug], axis=1)
            values = jnp.concatenate([v_ref[pair, k_rows, :], aug], axis=1)
            for h in (2 * pair, 2 * pair + 1):
                probs = jnp.exp(contract_cols(keys, qcat_ref[h, q_rows, :]))
                if mask is not None:
                    probs = jnp.where(mask, probs, 0.0)
                grads = (probs * contract_cols(values, dcat_ref[h, q_rows, :])).astype(BF16)
                dv_acc[k_rows, lanes] += dot(probs.astype(BF16), dcat_ref[h, q_rows, :LANES])
                both = dot(grads, qcat_ref[h, q_rows, :])
                dk_acc[k_rows, lanes] += both[:, :LANES]
                dcol_acc[k_rows, :] += both[:, LANES:]
                acc_ref[h, q_rows, :] += contract_rows(grads, keys)

    for ki in range(2):
        key_group = group_map[2 * step + ki]
        for qi in range(2):
            query_group = group_map[2 * me[0] + qi]
            active, full = block_state(group_map, doc_lengths, skip, query_group, key_group, rows, docs)

            @pl.when(active & full)
            def _(qi=qi, ki=ki):
                tile(qi, ki, None)

            @pl.when(active & jnp.logical_not(full))
            def _(qi=qi, ki=ki, query_group=query_group, key_group=key_group):
                tile(qi, ki, block_mask(doc_lengths, query_group, key_group, rows, docs, 1))

    dk_ref[0] = dk_acc[...].astype(BF16)
    dv_ref[0] = dv_acc[...].astype(BF16)
    dcol_ref[0] = -(dcol_acc[...].T[:8])

    @pl.when(step == pl.num_programs(0) - 1)
    def _():
        total_rows = dq_ref.shape[0]
        low = low_lanes(total_rows)
        lane = lax.broadcasted_iota(jnp.int32, (total_rows, LANES), 1)
        sums = jnp.zeros((total_rows, LANES), F32)
        for pair in range(heads // 2):
            a, b = 2 * pair, 2 * pair + 1
            dq_ref[:, pair * LANES : (pair + 1) * LANES] = jnp.where(
                low, acc_ref[a, :, :LANES], acc_ref[b, :, :LANES]
            )
            sums = jnp.where(
                lane == 24 + a, acc_ref[a, :, LANES:], jnp.where(lane == 24 + b, acc_ref[b, :, LANES:], sums)
            )
        drow_ref[...] = pltpu.roll(sums, LANES - 24, 1).T[:8]


def backward_attention(me, group_map, doc_lengths, skip, queries, grads, attended, term, keys, values, key_aug, heads):
    total = keys.shape[1]
    own, width = queries.shape
    rows = own // 2
    n = total // own
    docs = doc_lengths.shape[0]
    return pl.pallas_call(
        functools.partial(backward_kernel, heads, rows, docs),
        grid=(n,),
        out_shape=[
            jax.ShapeDtypeStruct((own, width), F32),
            jax.ShapeDtypeStruct((8, own), F32),
            jax.ShapeDtypeStruct((n, own, width), BF16),
            jax.ShapeDtypeStruct((n, own, width), BF16),
            jax.ShapeDtypeStruct((n, 8, own), F32),
        ],
        in_specs=[smem(), smem(), smem(), smem()]
        + [
            whole((own, width)),
            whole((own, width)),
            whole((own, width)),
            whole((own, LANES)),
            pl.BlockSpec((heads // 2, own, LANES), lambda i: (0, i, 0)),
            pl.BlockSpec((heads // 2, own, LANES), lambda i: (0, i, 0)),
            pl.BlockSpec((own, LANES), lambda i: (i, 0)),
        ],
        out_specs=[
            whole((own, width)),
            whole((8, own)),
            pl.BlockSpec((1, own, width), lambda i: (i, 0, 0)),
            pl.BlockSpec((1, own, width), lambda i: (i, 0, 0)),
            pl.BlockSpec((1, 8, own), lambda i: (i, 0, 0)),
        ],
        scratch_shapes=[
            VMEM((heads, own, 2 * LANES), F32),
            VMEM((heads, own, 2 * LANES), BF16),
            VMEM((heads, own, 2 * LANES), BF16),
            VMEM((own, width), F32),
            VMEM((own, width), F32),
            VMEM((own, LANES), F32),
        ],
        compiler_params=pltpu.CompilerParams(vmem_limit_bytes=VMEM_LIMIT),
        cost_estimate=pl.CostEstimate(
            flops=own * total * width * 10, bytes_accessed=total * width * 8, transcendentals=own * total * heads
        ),
    )(me, group_map, doc_lengths, skip, queries, grads, attended, term, keys, values, key_aug)


def deliver_kernel(heads, count, small_ref, *refs):
    sources, refs = refs[:count], refs[count:]
    targets, refs = refs[:count], refs[count:]
    (first_ref, second_ref, forget_ref, bias_ref, gains_ref), refs = refs[:5], refs[5:]
    held, local = refs[:count], refs[count]
    moves = Moves(local)
    for i in range(count):
        moves.start(i, sources[i], held[i])
    shard, gain_rows = first_ref.shape[0], gains_ref.shape[1]
    first_ref[...] = small_ref[0:1, :shard].reshape(shard)
    second_ref[...] = small_ref[1:2, :shard].reshape(shard)
    turned = jnp.concatenate([small_ref[...], jnp.zeros((LANES - 16, 256), F32)], axis=0).T
    forget_ref[...] = small_ref[8 : 8 + heads, :shard]
    gains_ref[...] = small_ref[2 : 2 + heads, :gain_rows]
    bias_ref[...] = turned[224:225, 8 : 8 + heads].reshape(heads)
    for i in range(count):
        moves.wait(i)
        moves.start(i, held[i], targets[i])
    moves.wait()


def deliver(heads, shard, gain_rows, small, arrays):
    vmem = pl.BlockSpec(memory_space=VMEM)
    anywhere = pl.BlockSpec(memory_space=pl.ANY)
    shapes = [array.shape for array in arrays]
    shapes += [(shard,), (shard,), (heads, shard), (heads,), (heads, gain_rows)]
    (layer, input_grad, query, key, value, gate_out, output, gate, up, down, one, two, forget, bias, gains) = (
        pl.pallas_call(
            functools.partial(deliver_kernel, heads, len(arrays)),
            out_shape=[jax.ShapeDtypeStruct(shape, F32) for shape in shapes],
            in_specs=[vmem] + [anywhere] * len(arrays),
            out_specs=[anywhere] * len(arrays) + [vmem] * 5,
            scratch_shapes=[VMEM(array.shape, F32) for array in arrays]
            + [pltpu.SemaphoreType.DMA((2 * len(arrays),))],
            compiler_params=pltpu.CompilerParams(vmem_limit_bytes=VMEM_LIMIT),
        )(small, *arrays)
    )
    return (
        layer, input_grad, one, query, key, value, gate_out, forget.T, bias, gains.T, output, two, gate, up, down,
    )


def on_device(
    hidden_in,
    norm_one,
    w_query,
    w_key,
    w_value,
    w_gate_out,
    w_forget,
    forget_bias,
    head_gains,
    w_output,
    norm_two,
    w_gate,
    w_up,
    w_down,
    out_grad,
    doc_lengths,
    group_map,
    skip_list,
):
    device_ctx = lax.axis_index("ctx")
    device_tp = lax.axis_index("tp")
    n = lax.axis_size("ctx")
    row_count, model_width = hidden_in.shape
    group_rows = row_count // 2
    heads = forget_bias.shape[0]
    shard = norm_one.shape[0]
    gain_rows = head_gains.shape[0]
    head_dim = gain_rows * n // 2
    width = heads * head_dim
    hidden_width = w_gate.shape[1]

    slots = 2 * n
    (
        query_weight,
        key_weight,
        value_weight,
        gate_out_weight,
        output_weight,
        normed_shards,
        query_rows,
        query_raw,
        key_raw,
        gate_logit,
        forget_logit,
        keys_all,
        values_all,
        key_aug,
        attended_flat,
        row_term,
        gain_one,
        gain_two,
        query_gain,
        key_gain,
        forget_weight,
    ) = start_forward(
        n,
        1,
        group_map,
        doc_lengths,
        skip_list,
        forget_bias,
        hidden_in,
        [norm_one, norm_two, head_gains.T, w_forget.T],
        [w_query, w_key, w_value, w_gate_out],
        w_output,
    )
    half = width // 256 * 128
    fused = n <= 8
    (
        gated,
        layer_out,
        down_share,
        gate_share,
        up_share,
        grad_middle,
        grad_attended,
        grad_gate_logit,
        gain_two_parts,
        *attention_grads,
    ) = feed_forward(
        n,
        3,
        heads,
        attended_flat,
        gate_logit,
        output_weight,
        hidden_in,
        gain_two,
        out_grad,
        w_gate,
        w_up,
        w_down,
        (group_map, doc_lengths, skip_list, query_rows, row_term, keys_all, values_all, key_aug) if fused else None,
    )
    halves = [(0, half), (half, width - half)]
    attn_plan = [[(cw, (i, c0, cw)) for c0, cw in halves] for i in (0, 1)]
    if fused:
        grad_branch, grad_query, row_sums, key_part, value_part, column_sums = attention_grads
        early_plan = [side + [(cw, (2, c0, cw))] for side, (c0, cw) in zip(attn_plan, halves)]
        query_share, key_share, value_share, gate_out_share, output_share, small_share, input_grad = finish_backward(
            n,
            7,
            heads,
            early_plan,
            attn_plan,
            key_part,
            value_part,
            column_sums,
            row_sums,
            grad_query,
            query_raw,
            key_raw,
            query_gain,
            key_gain,
            forget_logit,
            group_map,
            query_weight,
            key_weight,
            value_weight,
            gate_out_weight,
            forget_weight,
            grad_gate_logit,
            normed_shards,
            grad_branch,
            gated,
            hidden_in,
            gain_one,
            grad_middle,
            gain_two_parts,
        )
    else:
        grad_branch = grad_middle.astype(BF16).reshape(row_count, n, shard).transpose(1, 0, 2)
        normed_shards = normed_shards.reshape(n, shard, row_count).transpose(0, 2, 1)
        grad_query, row_sums, key_part, value_part, column_sums = backward_attention(
            device_ctx.astype(jnp.int32).reshape(1),
            group_map,
            doc_lengths,
            skip_list,
            query_rows,
            grad_attended,
            attended_flat,
            row_term,
            keys_all,
            values_all,
            key_aug,
            heads,
        )
        own_groups = lax.dynamic_slice_in_dim(group_map, device_ctx * 2, 2, 0)
        later = (group_map[None, :] > own_groups[:, None]).astype(F32)
        query_gain, key_gain = (gain.reshape(heads, head_dim) for gain in (query_gain, key_gain))
        query_raw, key_raw = (raw.reshape(row_count, heads, head_dim) for raw in (query_raw, key_raw))
        query_norm, key_norm = rms_scale(query_raw), rms_scale(key_raw)
        forget_logit = forget_logit[:heads].T
        forget_weight = forget_weight[:heads].astype(BF16)
        normed_one = normed_shards.transpose(1, 0, 2).reshape(row_count, model_width)
        place = jnp.arange(group_rows, dtype=jnp.int32)
        upper = (place[:, None] <= place[None, :]).astype(F32)
        grad_key, grad_value, off_sum, tot_sum = pair_scatter(n, 7, key_part, value_part, column_sums, row_sums)
        after = contract_cols_exact(tot_sum[:heads, :slots], later)
        suffix = lax.dot_general(
            off_sum[:heads].reshape(heads, 2, group_rows), upper, (((2,), (1,)), ((), ())), precision=HIGHEST
        )
        grad_log_forget = (suffix + after[:, :, None]).reshape(heads, row_count).T
        grad_key3 = grad_key.reshape(row_count, heads, head_dim)
        grad_query3 = grad_query.reshape(row_count, heads, head_dim)
        key_raw_grad = rms_back(grad_key3 * key_gain, key_raw).astype(BF16).reshape(row_count, width)
        query_raw_grad = (
            rms_back(grad_query3 * query_gain * 0.125, query_raw).astype(BF16).reshape(row_count, width)
        )
        value_low = grad_value.astype(BF16)
        query_gain_grad = jnp.sum(grad_query3 * query_norm * 0.125, axis=0)
        key_gain_grad = jnp.sum(grad_key3 * key_norm, axis=0)
        head_gain_grad = jnp.concatenate([query_gain_grad, key_gain_grad], axis=1)
        grad_forget_logit = (grad_log_forget * jax.nn.sigmoid(-forget_logit)).astype(BF16)
        bias_part = jnp.sum(grad_forget_logit.astype(F32), axis=0)
        normed_one_part = (
            contract_cols(query_raw_grad, query_weight)
            + contract_cols(key_raw_grad, key_weight)
            + contract_cols(value_low, value_weight)
            + contract_cols(grad_gate_logit, gate_out_weight)
            + dot(grad_forget_logit, forget_weight)
        )
        forget_grad = contract_rows(grad_forget_logit, normed_one)

        def wide(value):
            return jnp.pad(value, ((0, 0), (0, 0), (0, 256 - value.shape[2])))

        forget_rows = wide(forget_grad.reshape(heads, n, shard).transpose(1, 0, 2))
        forget_rows = forget_rows.at[:, :, 224].set(bias_part[None, :])
        small_grad = jnp.concatenate(
            [
                jnp.zeros((n, 1, 256), F32),
                wide(jnp.sum(gain_two_parts, axis=0).reshape(n, 1, shard)),
                wide(head_gain_grad.reshape(heads, n, gain_rows).transpose(1, 0, 2)),
                jnp.pad(forget_rows, ((0, 0), (0, 8 - heads), (0, 0))),
            ],
            axis=1,
        )
        plan = [
            [(cw, (0, right, c0, cw)) for right in rights for c0, cw in halves] + [(cw, (1, 4, c0, cw))]
            for rights, (c0, cw) in zip(((0, 1), (2, 3)), halves)
        ]
        (
            query_share,
            key_share,
            value_share,
            gate_out_share,
            output_share,
            small_share,
            input_grad,
        ) = weight_scatter(
            n,
            8,
            plan,
            [normed_shards, grad_branch],
            [query_raw_grad, key_raw_grad, value_low, grad_gate_logit, gated],
            small_grad,
            normed_one_part,
            hidden_in,
            gain_one,
            grad_middle,
        )
    return deliver(
        heads,
        shard,
        gain_rows,
        small_share,
        [
            layer_out,
            input_grad,
            query_share,
            key_share,
            value_share,
            gate_out_share,
            output_share,
            gate_share,
            up_share,
            down_share,
        ],
    )


def solution(mesh):
    split = P("ctx", "tp")
    in_specs = (
        P("ctx", None),
        P("ctx"),
        split,
        split,
        split,
        split,
        split,
        P("tp"),
        split,
        split,
        P("ctx"),
        split,
        split,
        split,
        P("ctx", None),
        P(),
        P(),
        P(),
    )
    out_specs = (
        split,
        P("ctx", None),
        P("ctx"),
        split,
        split,
        split,
        split,
        split,
        P("tp"),
        split,
        split,
        P("ctx"),
        split,
        split,
        split,
    )
    return jax.shard_map(on_device, mesh=mesh, in_specs=in_specs, out_specs=out_specs, check_vma=False)
```
